32 devices in a mesh: req: 8 (over y, x, core), head: 4 (over z).
Axes of the slice: x: 2, y: 2, z: 4, core: 2. Of those that a mesh axis runs over, the one named last changes fastest.
Arguments:
- tokens: bfloat16 [32, 7168], P('req'), may hold values from -6 to 6
- norm_gain: float32 [7168], replicated, may hold values from 0.5 to 1.5
- norm_shift: float32 [7168], replicated, may hold values from -3 to 3
- qkv_weight: bfloat16 [7168, 56, 384], P('req', 'head'), may hold values from -0.0625 to 0.0625
- qkv_bias: float32 [56, 384], P('head'), may hold values from -3 to 3
- out_weight: bfloat16 [56, 128, 7168], P('head', 'req'), may hold values from -0.09375 to 0.09375
- out_bias: float32 [7168], replicated, may hold values from -3 to 3
- key_pool: bfloat16 [160, 64, 7168], P('req', None, 'head'), may hold values from -256 to 256
- value_pool: bfloat16 [160, 64, 7168], P('req', None, 'head'), may hold values from -6 to 6
- lengths: int32 [32], P('req'), may hold values from 1 to 1023, as said below
- page_table: int32 [32, 16], P('req'), may hold values from 0 to 19, as said below
- new_slot: int32 [32], P('req'), may hold values from 0 to 31, as said below
- new_page: int32 [32], P('req'), may hold values from 0 to 19, as said below
Outputs:
- hidden_out: bfloat16 [32, 7168], P('req', 'head')
- key_out: bfloat16 [160, 64, 7168], P('req', None, 'head')
- value_out: bfloat16 [160, 64, 7168], P('req', None, 'head')
The draws below stay inside these ranges and needn't reach their ends.
Inputs may be any that keep to these rules, and one draw needn't show every extreme that they name: `lengths`: A request with length under 64 uses one page; the others use 16 pages. A device holds at most one request of length 64 or more. `page_table`: local pages of the request's device; the used entries (the first (lengths + 64) // 64 of a row) of all requests of one device are distinct. `new_slot`: A permutation of the slots. Every device has exactly one request whose new slot lies on another device, and it has length under 64; every device receives exactly one such request into the slot its own leaving request frees; the others keep their slot. `new_page`: for a moving request, a local page of its new device that no request uses before the move; for the others, page_table[s, 0].
All inputs are finite; a program needn't handle non-finite values.
Results may differ from the reference program's by a relative error of at most 0.012.
Values may be sent and summed in bfloat16 or wider, within the bound.
No kernel may reach another device: no remote copies, remote signals or barrier semaphores. Data moves between devices by JAX's collectives and lax.ppermute only.
A program may use at most 192 MiB of HBM per device.

```python
import jax
import jax.numpy as jnp
from jax import lax

D = 7168
HEADS = 56
HD = 128
SLOTS_DEV = 4
PAGE = 64
MAXP = 16
PAGES_DEV = 20
REQUESTS = 32
POOL = 160


def layout(key):
    base = jax.random.fold_in(key, 7)
    groups = REQUESTS // SLOTS_DEV
    keys = jax.random.split(base, 8)
    order = jax.random.permutation(keys[0], groups).astype(jnp.int32)
    rank = jnp.zeros((groups,), jnp.int32).at[order].set(jnp.arange(groups, dtype=jnp.int32))
    has_long = rank < groups // 2
    long_slot = jax.random.randint(keys[1], (groups,), 0, SLOTS_DEV).astype(jnp.int32)
    local = jnp.arange(SLOTS_DEV, dtype=jnp.int32)
    is_long = has_long[:, None] & (local[None, :] == long_slot[:, None])
    long_size = jax.random.randint(keys[2], (groups, SLOTS_DEV), (MAXP - 1) * PAGE, MAXP * PAGE).astype(jnp.int32)
    long_size = jnp.where(rank[:, None] == 0, MAXP * PAGE - 1, long_size)
    short_size = jax.random.randint(keys[3], (groups, SLOTS_DEV), 1, PAGE).astype(jnp.int32)
    sizes = jnp.where(is_long, long_size, short_size)
    needed = jnp.where(is_long, MAXP, 1).astype(jnp.int32)
    offset = jnp.cumsum(needed, axis=1) - needed
    used = jnp.sum(needed, axis=1)
    page_keys = jax.random.split(keys[4], groups)
    orders = jax.vmap(lambda one_key: jax.random.permutation(one_key, PAGES_DEV))(page_keys).astype(jnp.int32)
    index = (offset[:, :, None] + jnp.arange(MAXP, dtype=jnp.int32)[None, None, :]) % PAGES_DEV
    table = jnp.take_along_axis(orders, index.reshape(groups, SLOTS_DEV * MAXP), axis=1).reshape(groups, SLOTS_DEV, MAXP)
    draw_slot = jax.random.randint(keys[5], (groups,), 0, SLOTS_DEV).astype(jnp.int32)
    mover = jnp.where(has_long, (long_slot + 1 + draw_slot % (SLOTS_DEV - 1)) % SLOTS_DEV, draw_slot)
    cycle = jax.random.permutation(keys[6], groups).astype(jnp.int32)
    next_device = jnp.zeros((groups,), jnp.int32).at[cycle].set(jnp.roll(cycle, -1))
    dest_slot = next_device * SLOTS_DEV + mover[next_device]
    slot_ids = jnp.arange(groups * SLOTS_DEV, dtype=jnp.int32).reshape(groups, SLOTS_DEV)
    is_mover = local[None, :] == mover[:, None]
    slots_after = jnp.where(is_mover, dest_slot[:, None], slot_ids)
    pick = jax.random.randint(keys[7], (groups,), 0, 1 << 20).astype(jnp.int32)
    free_count = PAGES_DEV - used[next_device]
    free_page = orders[next_device, (used[next_device] + pick % free_count) % PAGES_DEV]
    pages_after = jnp.where(is_mover, free_page[:, None], table[:, :, 0])
    return (sizes.reshape(-1).astype(jnp.int32), table.reshape(groups * SLOTS_DEV, MAXP).astype(jnp.int32), slots_after.reshape(-1).astype(jnp.int32), pages_after.reshape(-1).astype(jnp.int32))


def draw_lengths(key, part):
    return layout(key)[0]


def draw_page_table(key, part):
    return layout(key)[1]


def draw_new_slot(key, part):
    return layout(key)[2]


def draw_new_page(key, part):
    return layout(key)[3]


def draw_key_pool(key, part):
    base = jax.random.fold_in(key, 11)
    first_key = jax.random.fold_in(base, 0)
    values = jax.random.normal(first_key, (POOL, PAGE, D), jnp.float32)
    values = jnp.clip(values, -6.0, 6.0)
    return values.astype(jnp.bfloat16)


def with_spikes(array, stream_key, source, target, parts, factor):
    def block_of(dim):
        return (jnp.arange(array.shape[dim]) // (array.shape[dim] // parts)).reshape((-1,) + (1,) * (array.ndim - 1 - dim))

    near = jax.random.permutation(stream_key, parts)[block_of(target)]
    far = (block_of(target) + parts // 2) % parts
    return jnp.where((block_of(source) == near) | (block_of(source) == far), factor * array, array)


def steps_of(key, extent, pieces, low, high):
    factor_of, own = 1.0, jax.random.fold_in(key, 6)
    for position, parts in pieces:
        heights = jnp.exp(jax.random.uniform(jax.random.fold_in(own, position), (parts,), jnp.float32, low / len(pieces), high / len(pieces)))
        factor_of = factor_of * jnp.repeat(heights, extent[position] // parts).reshape([-1 if axis == position else 1 for axis in range(len(extent))])
    return factor_of


def noise(own_key, dims, width, most, cuts=(), kind=jnp.bfloat16):
    drawn = width * jax.random.normal(own_key, dims, jnp.float32)
    if cuts:
        drawn = drawn * steps_of(own_key, dims, cuts, -0.22, 0.18)
    return jnp.clip(drawn, -most, most).astype(kind)


def heavy_noise(stream_key, shape, width, reach, pieces, heavy, kind=jnp.bfloat16):
    array = width * jax.random.normal(stream_key, shape, jnp.float32)
    if pieces:
        array = array * steps_of(stream_key, shape, pieces, -0.22, 0.18)
    return jnp.clip(with_spikes(array, jax.random.fold_in(stream_key, 3), *heavy), -reach, reach).astype(kind)


def setup_inputs(seed: int = 0) -> dict:
    key_of = jax.random.split(jax.random.key(seed), 14)
    return {
        "tokens": noise(key_of[0], (REQUESTS, D), 1.0, 6.0, ((0, 8),)),
        "norm_gain": jnp.clip(1.0 + 0.1 * jax.random.normal(key_of[1], (D,), jnp.float32), 0.5, 1.5),
        "norm_shift": noise(key_of[2], (D,), 0.5, 3.0, (), jnp.float32),
        "qkv_weight": noise(key_of[3], (D, HEADS, 3 * HD), D ** -0.5, 0.0625, ((0, 8), (1, 4))),
        "qkv_bias": noise(key_of[4], (HEADS, 3 * HD), 0.5, 3.0, ((0, 4),), jnp.float32),
        "out_weight": heavy_noise(key_of[5], (HEADS, HD, D), D ** -0.5, 0.09375, ((0, 4), (1, 8)), (1, 2, 8, 2.0)),
        "out_bias": noise(key_of[6], (D,), 0.5, 3.0, (), jnp.float32),
        "key_pool": draw_key_pool(jax.random.fold_in(key_of[13], 71), 0),
        "value_pool": noise(key_of[8], (POOL, PAGE, D), 1.0, 6.0, ((0, 8), (2, 4))),
        "lengths": draw_lengths(jax.random.fold_in(key_of[13], 71), 0),
        "page_table": draw_page_table(jax.random.fold_in(key_of[13], 71), 0),
        "new_slot": draw_new_slot(jax.random.fold_in(key_of[13], 71), 0),
        "new_page": draw_new_page(jax.random.fold_in(key_of[13], 71), 0),
    }


EPSILON = 1e-05

def reference(tokens, norm_gain, norm_shift, qkv_weight, qkv_bias, out_weight, out_bias, key_pool, value_pool, lengths, page_table, new_slot, new_page):
    total_slots = REQUESTS
    values_f = tokens.astype(jnp.float32)
    average = lax.optimization_barrier(jnp.mean(values_f, axis=1, keepdims=True))
    centered = values_f - average
    variance = lax.optimization_barrier(jnp.mean(centered * centered, axis=1, keepdims=True))
    normed = (centered * lax.rsqrt(variance + EPSILON) * norm_gain + norm_shift).astype(jnp.bfloat16)
    projected = jnp.dot(normed, qkv_weight.reshape(D, HEADS * 3 * HD), preferred_element_type=jnp.float32)
    projected = projected.reshape(total_slots, HEADS, 3 * HD) + qkv_bias
    query = (projected[:, :, :HD] * HD ** (-0.5)).astype(jnp.bfloat16)
    key_new = projected[:, :, HD:2 * HD].astype(jnp.bfloat16)
    value_new = projected[:, :, 2 * HD:].astype(jnp.bfloat16)
    slot_range = jnp.arange(total_slots, dtype=jnp.int32)
    anchor = jnp.zeros((total_slots,), jnp.int32).at[new_slot].set(slot_range)
    old_device = slot_range // SLOTS_DEV
    new_device = new_slot // SLOTS_DEV
    moving = new_device != old_device
    source_global = old_device * PAGES_DEV + page_table[:, 0]
    dest_global = new_device * PAGES_DEV + new_page
    write_index = jnp.where(moving, dest_global, POOL)
    key_moved = key_pool.at[write_index].set(key_pool[source_global], mode='drop')
    value_moved = value_pool.at[write_index].set(value_pool[source_global], mode='drop')
    size_new = lengths[anchor]
    moved_in = moving[anchor]
    table_local = jnp.where(moved_in[:, None], new_page[anchor][:, None], page_table[anchor])
    table = table_local + (slot_range // SLOTS_DEV)[:, None] * PAGES_DEV
    page_slot = jnp.take_along_axis(table, (size_new // PAGE)[:, None], axis=1)[:, 0]
    offset = size_new % PAGE
    key_out = key_moved.at[page_slot, offset].set(key_new[anchor].reshape(total_slots, D))
    value_out = value_moved.at[page_slot, offset].set(value_new[anchor].reshape(total_slots, D))
    positions = jnp.arange(MAXP * PAGE, dtype=jnp.int32)

    def attend(item):
        row_pages, size_one, query_one = item
        keys = key_out[row_pages].reshape(MAXP * PAGE, HEADS, HD).astype(jnp.float32)
        values = value_out[row_pages].reshape(MAXP * PAGE, HEADS, HD).astype(jnp.float32)
        scores = jnp.einsum('hc,thc->ht', query_one.astype(jnp.float32), keys)
        valid = (positions <= size_one)[None, :]
        masked = jnp.where(valid, scores, -1e+30)
        peak = lax.optimization_barrier(jnp.max(masked, axis=1, keepdims=True))
        weights = jnp.where(valid, jnp.exp(masked - peak), 0.0)
        denom = lax.optimization_barrier(jnp.sum(weights, axis=1))
        probs = lax.optimization_barrier(weights.astype(jnp.bfloat16)).astype(jnp.float32)
        mixed = jnp.einsum('ht,thc->hc', probs, values)
        return (mixed / denom[:, None]).astype(jnp.bfloat16)
    attended = lax.map(attend, (table, size_new, query[anchor]))
    projected_out = jnp.dot(attended.reshape(total_slots, D), out_weight.reshape(D, D), preferred_element_type=jnp.float32)
    hidden_out = (projected_out + out_bias + tokens[anchor].astype(jnp.float32)).astype(jnp.bfloat16)
    return (hidden_out, key_out, value_out)
```

```python
import functools

import jax
import jax.numpy as jnp
from jax import lax
from jax.experimental import pallas as pl
from jax.experimental.pallas import tpu as pltpu
from jax.sharding import PartitionSpec as P

EPSILON = 1e-05
F32 = jnp.float32
BF16 = jnp.bfloat16
LANES = 128
META = 128
PACK = 256
VMEM = pl.BlockSpec(memory_space=pltpu.VMEM)
SMEM = pl.BlockSpec(memory_space=pltpu.SMEM)
ANY = pl.BlockSpec(memory_space=pl.ANY)
LIMIT = 56 * 1024 * 1024


def cost(flops, moved):
    return pl.CostEstimate(flops=flops, bytes_accessed=moved, transcendentals=0)


def layer_norm(tokens, norm_gain, norm_shift):
    values_f = tokens.astype(F32)
    average = jnp.mean(values_f, axis=1, keepdims=True)
    centered = values_f - average
    variance = jnp.mean(centered * centered, axis=1, keepdims=True)
    return (centered * lax.rsqrt(variance + EPSILON) * norm_gain + norm_shift).astype(BF16)


def swap(value, axis, step):
    size = lax.axis_size(axis)
    return lax.ppermute(value, axis, [(i, i ^ step) for i in range(size)])


def relative(blocks, index):
    size = blocks.shape[0]
    tail = blocks.shape[1:]
    bits = size.bit_length() - 1
    split = blocks.reshape((2,) * bits + tail)
    for bit in range(bits):
        axis = bits - 1 - bit
        split = jnp.where((index >> bit) & 1 == 1, jnp.flip(split, axis), split)
    return split.reshape((size,) + tail)


def spread_pairs(keep, send):
    got = swap(send, "req", 1)
    chips = keep.shape[0]
    return [jnp.stack([keep[0], got[0]])] + [
        swap(jnp.stack([keep[d], got[d]]), "req", 2 * d) for d in range(1, chips)
    ]


def copy_pools(key_pool, value_pool):
    pages = key_pool.shape[0]
    parts = 4
    step = pages // parts

    def kernel(key_ref, value_ref, key_out, value_out, sems):
        copies = [
            pltpu.make_async_copy(
                source.at[pl.ds(i * step, step)], target.at[pl.ds(i * step, step)], sems.at[n, i]
            )
            for n, (source, target) in enumerate(((key_ref, key_out), (value_ref, value_out)))
            for i in range(parts)
        ]
        for copy in copies:
            copy.start()
        for copy in copies:
            copy.wait()

    shape = jax.ShapeDtypeStruct(key_pool.shape, key_pool.dtype)
    return pl.pallas_call(
        kernel,
        out_shape=(shape, shape),
        in_specs=[ANY, ANY],
        out_specs=(ANY, ANY),
        scratch_shapes=[pltpu.SemaphoreType.DMA((2, parts))],
        compiler_params=pltpu.CompilerParams(vmem_limit_bytes=LIMIT),
        cost_estimate=cost(0, 4 * key_pool.size * 2),
        name="copy_pools",
    )(key_pool, value_pool)


def pick_page(key_pool, value_pool, page):
    shape = (2,) + key_pool.shape[1:]

    def kernel(page_ref, key_ref, value_ref, out_ref, sems):
        copies = [
            pltpu.make_async_copy(source.at[page_ref[0]], out_ref.at[n], sems.at[n])
            for n, source in enumerate((key_ref, value_ref))
        ]
        for copy in copies:
            copy.start()
        for copy in copies:
            copy.wait()

    return pl.pallas_call(
        kernel,
        out_shape=jax.ShapeDtypeStruct(shape, key_pool.dtype),
        in_specs=[SMEM, ANY, ANY],
        out_specs=ANY,
        scratch_shapes=[pltpu.SemaphoreType.DMA((2,))],
        compiler_params=pltpu.CompilerParams(vmem_limit_bytes=LIMIT),
        cost_estimate=cost(0, 4 * key_pool.shape[1] * key_pool.shape[2] * 2),
        name="pick_page",
    )(page, key_pool, value_pool)


def choose_page(which, candidates):
    def kernel(which_ref, *refs):
        out_ref, sem = refs[-2:]
        for n, candidate in enumerate(refs[:-2]):

            @pl.when(which_ref[0] == n)
            def _():
                copy = pltpu.make_async_copy(candidate, out_ref, sem)
                copy.start()
                copy.wait()

    one = candidates[0]
    return pl.pallas_call(
        kernel,
        out_shape=jax.ShapeDtypeStruct(one.shape, one.dtype),
        in_specs=[SMEM] + [ANY] * len(candidates),
        out_specs=ANY,
        scratch_shapes=[pltpu.SemaphoreType.DMA],
        compiler_params=pltpu.CompilerParams(vmem_limit_bytes=LIMIT),
        cost_estimate=cost(0, 4 * one.size),
        name="choose_page",
    )(which, *candidates)


def project(blocks, weight):
    chips = len(blocks)
    slots = blocks[0].shape[1]
    heads, depth, width = weight.shape
    per = 2 if heads % 2 == 0 else 1
    rows = chips * 2 * slots

    def kernel(*refs):
        block_refs = refs[:chips]
        weight_ref, keep_ref, send_ref, left = refs[chips:]

        @pl.when(pl.program_id(0) == 0)
        def _():
            for d in range(chips):
                for e in range(2):
                    row = (d * 2 + e) * slots
                    left[row : row + slots, :] = block_refs[d][e][:, :depth].astype(F32)

        lhs = left[...].astype(BF16)
        for j in range(per):
            total = jnp.dot(lhs, weight_ref[j], preferred_element_type=F32)
            for d in range(chips):
                row = d * 2 * slots
                columns = slice(j * width, (j + 1) * width)
                keep_ref[d, :, columns] = total[row : row + slots]
                send_ref[d, :, columns] = total[row + slots : row + 2 * slots]

    shape = jax.ShapeDtypeStruct((chips, slots, heads * width), F32)
    out_spec = pl.BlockSpec((chips, slots, per * width), lambda i: (0, 0, i))
    return pl.pallas_call(
        kernel,
        grid=(heads // per,),
        out_shape=(shape, shape),
        in_specs=[VMEM] * chips + [pl.BlockSpec((per, depth, width), lambda i: (i, 0, 0))],
        out_specs=(out_spec, out_spec),
        scratch_shapes=[pltpu.VMEM((rows, depth), F32)],
        compiler_params=pltpu.CompilerParams(vmem_limit_bytes=LIMIT),
        cost_estimate=cost(2 * rows * weight.size, 2 * weight.size),
        name="project",
    )(*blocks, weight)


def attend(numbers, page_table, sums, bias, tokens, key_pool, value_pool, key_out, value_out):
    parts = len(sums)
    slots = sums[0].shape[0]
    pages, page, width = key_pool.shape
    head = LANES
    heads = width // head
    max_pages = page_table.shape[1]
    chunk_pages = 4
    chunk = chunk_pages * page
    chunks = max_pages // chunk_pages
    long_rows = max_pages * page
    short_rows = slots * page
    groups = 2 * parts
    share = head // groups
    per = LANES // share
    tall = 16
    strips = width // PACK
    scale = head ** (-0.5)

    def kernel(*refs):
        numbers_ref, table_ref = refs[:2]
        sum_refs = refs[2 : 2 + parts]
        (bias_ref, token_ref, key_ref, value_ref, _, _, pack_keep, pack_send, key_out_ref, value_out_ref) = refs[
            2 + parts : 12 + parts
        ]
        key_buffer, value_buffer, score_buffer, mix_buffer, sems, out_sems = refs[12 + parts :]
        leaving = numbers_ref[slots]
        here = numbers_ref[slots + 1]
        column_block = numbers_ref[slots + 2]
        lengths = [numbers_ref[s] for s in range(slots)]
        long_slot = jnp.int32(0)
        long_length = jnp.int32(-1)
        for s in range(slots):
            is_long = lengths[s] >= page
            long_slot = jnp.where(is_long, s, long_slot)
            long_length = jnp.where(is_long, lengths[s], long_length)
        turns = (long_length + chunk) // chunk

        pairs = ((key_ref, key_buffer), (value_ref, value_buffer))

        def short_copies(n):
            source, buffer = pairs[n]
            return [
                pltpu.make_async_copy(
                    source.at[table_ref[s, 0]], buffer.at[pl.ds(long_rows + s * page, page)], sems.at[n, chunks]
                )
                for s in range(slots)
            ]

        def long_copies(n, c):
            source, buffer = pairs[n]
            return [
                pltpu.make_async_copy(
                    source.at[table_ref[long_slot, c * chunk_pages + i]],
                    buffer.at[pl.ds((c * chunk_pages + i) * page, page)],
                    sems.at[n, c],
                )
                for i in range(chunk_pages)
            ]

        for n in range(2):
            for copy in short_copies(n):
                copy.start()
            for c in range(chunks):

                @pl.when(c < turns)
                def _():
                    for copy in long_copies(n, c):
                        copy.start()

        total = sum_refs[0][...]
        for ref in sum_refs[1:]:
            total = total + ref[...].astype(F32)
        total = total + bias_ref[...]

        def third(k):
            return jnp.concatenate(
                [total[:, (3 * h + k) * head : (3 * h + k + 1) * head] for h in range(heads)], axis=1
            )

        query = (third(0) * scale).astype(BF16).astype(F32)
        new_rows = (third(1).astype(BF16).astype(F32), third(2).astype(BF16).astype(F32))

        lane_head = lax.broadcasted_iota(jnp.int32, (tall, width), 1) // head
        on_head = lane_head == lax.broadcasted_iota(jnp.int32, (tall, width), 0)

        def blocked(row):
            return jnp.where(on_head, jnp.broadcast_to(row, (tall, width)), 0.0).astype(BF16)

        def append(n, s, base, offset, out_ref):
            _, buffer = pairs[n]
            first = pl.multiple_of(offset // 16 * 16, 16)
            place = pl.ds(pl.multiple_of(base + first, 16), 16)
            old = buffer[place, :].astype(F32)
            row = lax.broadcasted_iota(jnp.int32, (16, width), 0)
            fresh = jnp.where(row == offset - first, jnp.broadcast_to(new_rows[n][s : s + 1], (16, width)), old)
            buffer[place, :] = fresh.astype(BF16)

        def out_copy(n, s):
            _, buffer = pairs[n]
            out_ref = (key_out_ref, value_out_ref)[n]
            length = lengths[s]
            is_long = length >= page
            within = length % page // 16 * 16
            base = jnp.where(is_long, length // page * page, long_rows + s * page)
            return pltpu.make_async_copy(
                buffer.at[pl.ds(pl.multiple_of(base + within, 16), 16)],
                out_ref.at[table_ref[s, length // page], pl.ds(pl.multiple_of(within, 16), 16)],
                out_sems.at[n, s],
            )

        def append_short(n):
            for s in range(slots):

                @pl.when(lengths[s] < page)
                def _():
                    append(n, s, long_rows + s * page, lengths[s], None)

        def append_long(n):
            for s in range(slots):

                @pl.when(lengths[s] >= page)
                def _():
                    append(n, s, 0, lengths[s], None)

        def softmax(scores, valid):
            masked = jnp.where(valid, scores, -1e30)
            peak = jnp.max(masked, axis=1, keepdims=True)
            weights = jnp.where(valid, jnp.exp(masked - peak), 0.0)
            return weights.astype(BF16), jnp.sum(weights, axis=1, keepdims=True)

        across = (((1,), (1,)), ((), ()))
        for copy in short_copies(0):
            copy.wait()
        append_short(0)
        short_query = jnp.concatenate([blocked(query[s : s + 1]) for s in range(slots)], axis=0)
        short_scores = lax.dot_general(
            short_query, key_buffer[long_rows:, :], across, preferred_element_type=F32
        )
        size = (slots * tall, short_rows)
        row_slot = lax.broadcasted_iota(jnp.int32, size, 0) // tall
        column = lax.broadcasted_iota(jnp.int32, size, 1)
        limit = jnp.zeros(size, jnp.int32)
        for s in range(slots):
            limit = jnp.where(row_slot == s, jnp.minimum(lengths[s], page - 1), limit)
        in_slot = row_slot == column // page
        short_probs, short_denom = softmax(short_scores, in_slot & (column % page <= limit))

        long_row = jnp.zeros((1, width), F32)
        for s in range(slots):
            long_row = jnp.where(long_slot == s, query[s : s + 1], long_row)
        long_query = blocked(long_row)
        for c in range(chunks):

            @pl.when(c < turns)
            def _():
                for copy in long_copies(0, c):
                    copy.wait()

        append_long(0)
        score_buffer[...] = jnp.full(score_buffer.shape, -1e30, F32)
        for c in range(chunks):

            @pl.when(c < turns)
            def _():
                score_buffer[:, c * chunk : (c + 1) * chunk] = lax.dot_general(
                    long_query, key_buffer[c * chunk : (c + 1) * chunk, :], across, preferred_element_type=F32
                )

        position = lax.broadcasted_iota(jnp.int32, (tall, long_rows), 1)
        long_probs, long_denom = softmax(score_buffer[...], position <= jnp.maximum(long_length, 0))

        for copy in short_copies(1):
            copy.wait()
        append_short(1)
        short_mix = jnp.dot(short_probs, value_buffer[long_rows:, :], preferred_element_type=F32) / short_denom
        mix_buffer[...] = jnp.zeros(mix_buffer.shape, F32)
        for c in range(chunks):

            @pl.when(c < turns)
            def _():
                for copy in long_copies(1, c):
                    copy.wait()

        append_long(1)
        for n in range(2):
            for s in range(slots):

                @pl.when(leaving != s)
                def _():
                    out_copy(n, s).start()

        for c in range(chunks):

            @pl.when(c < turns)
            def _():
                mix_buffer[...] += jnp.dot(
                    long_probs[:, c * chunk : (c + 1) * chunk],
                    value_buffer[c * chunk : (c + 1) * chunk, :],
                    preferred_element_type=F32,
                )

        def fold(mixed):
            return jnp.sum(jnp.where(on_head, mixed, 0.0), axis=0, keepdims=True)

        long_mix = fold(mix_buffer[...] / long_denom)
        rows = []
        for s in range(slots):
            row = fold(short_mix[s * tall : (s + 1) * tall])
            rows.append(jnp.where(lengths[s] >= page, long_mix, row))
        high = -(-slots // 8) * 8
        attended = jnp.concatenate(rows + [jnp.zeros((high - slots, width), F32)], axis=0)

        token = token_ref[:, pl.ds(pl.multiple_of(column_block * width, LANES), width)].astype(F32)
        extra = []
        for source in new_rows + (token,):
            one = jnp.zeros((1, width), F32)
            for s in range(slots):
                one = jnp.where(leaving == s, source[s : s + 1], one)
            extra += [one[:, i * PACK : (i + 1) * PACK] for i in range(strips)]
        extra = jnp.concatenate(extra + [jnp.zeros((pack_rows(slots, strips) - high - 3 * strips, PACK), F32)], axis=0)

        lane = lax.broadcasted_iota(jnp.int32, (high, LANES), 1) // share
        for k in range(groups):
            wanted = here ^ k
            tiles = [jnp.zeros((high, LANES), F32) for _ in range(PACK // LANES)]
            for h in range(heads):
                place = h % per
                shift = lax.rem((place - wanted) * share + 2 * LANES, LANES)
                turned = pltpu.roll(attended[:, h * head : (h + 1) * head], shift, 1)
                tiles[h // per] = jnp.where(lane == place, turned, tiles[h // per])
            block = jnp.concatenate([jnp.concatenate(tiles, axis=1), extra], axis=0).astype(BF16)
            (pack_keep, pack_send)[k % 2][k // 2] = block

        for n in range(2):
            for s in range(slots):

                @pl.when(leaving != s)
                def _():
                    out_copy(n, s).wait()

    packed = jax.ShapeDtypeStruct((parts, pack_rows(slots, strips), PACK), BF16)
    pool_shape = jax.ShapeDtypeStruct(key_pool.shape, key_pool.dtype)
    return pl.pallas_call(
        kernel,
        out_shape=(packed, packed, pool_shape, pool_shape),
        in_specs=[SMEM, SMEM] + [VMEM] * (parts + 2) + [ANY] * 4,
        out_specs=(VMEM, VMEM, ANY, ANY),
        scratch_shapes=[
            pltpu.VMEM((long_rows + short_rows, width), BF16),
            pltpu.VMEM((long_rows + short_rows, width), BF16),
            pltpu.VMEM((tall, long_rows), F32),
            pltpu.VMEM((tall, width), F32),
            pltpu.SemaphoreType.DMA((2, chunks + 1)),
            pltpu.SemaphoreType.DMA((2, slots)),
        ],
        input_output_aliases={6 + parts: 2, 7 + parts: 3},
        compiler_params=pltpu.CompilerParams(vmem_limit_bytes=LIMIT),
        cost_estimate=cost(4 * tall * (long_rows + short_rows) * width, 4 * (long_rows + short_rows) * width),
        name="attend",
    )(numbers, page_table, *sums, bias, tokens, key_pool, value_pool, key_out, value_out)


def pack_rows(slots, strips):
    need = -(-slots // 8) * 8 + 3 * strips
    return -(-need // 16) * 16


def out_project(column_block, order, blocks, weight, pieces):
    chips = len(blocks)
    depth, width = weight.shape
    rows, high = order.shape[0], order.shape[1] // (2 * chips)
    half = rows // 2
    piece = width // pieces

    def kernel(column_ref, order_ref, *refs):
        block_refs = refs[:chips]
        weight_ref, keep_ref, send_ref, left = refs[chips:]

        @pl.when(pl.program_id(0) == 0)
        def _():
            gathered = jnp.concatenate(
                [block_refs[d][e, :high, :].astype(F32) for d in range(chips) for e in range(2)], axis=0
            ).astype(BF16)
            left[...] = jnp.dot(order_ref[...], gathered, preferred_element_type=F32)

        total = jnp.dot(left[:, :depth].astype(BF16), weight_ref[...], preferred_element_type=F32)
        keep_ref[0] = total[:half]
        send_ref[0] = total[half:]

    shape = jax.ShapeDtypeStruct((pieces, half, piece), F32)
    out_spec = pl.BlockSpec((1, half, piece), lambda j, c: (j, 0, 0))
    whole = lambda shape: pl.BlockSpec(shape, lambda j, c: (0,) * len(shape))
    return pl.pallas_call(
        kernel,
        out_shape=(shape, shape),
        grid_spec=pltpu.PrefetchScalarGridSpec(
            num_scalar_prefetch=1,
            grid=(pieces,),
            in_specs=[whole(order.shape)]
            + [whole(block.shape) for block in blocks]
            + [pl.BlockSpec((depth, piece), lambda j, c: (0, j ^ c[0]))],
            out_specs=(out_spec, out_spec),
            scratch_shapes=[pltpu.VMEM((rows, PACK), F32)],
        ),
        compiler_params=pltpu.CompilerParams(vmem_limit_bytes=LIMIT),
        cost_estimate=cost(2 * rows * weight.size, 2 * weight.size),
        name="out_project",
    )(column_block, order, *blocks, weight)


def place_page(numbers, new_rows, candidates, key_out, value_out):
    count = len(candidates)
    page, width = key_out.shape[1:]

    def kernel(numbers_ref, rows_ref, *refs):
        candidate_refs = refs[:count]
        _, _, key_ref, value_ref, buffer, sem, out_sems = refs[count:]
        for n in range(count):

            @pl.when(numbers_ref[0] == n)
            def _():
                copy = pltpu.make_async_copy(candidate_refs[n], buffer, sem)
                copy.start()
                copy.wait()

        offset = numbers_ref[2]
        first = pl.multiple_of(offset // 16 * 16, 16)
        row = lax.broadcasted_iota(jnp.int32, (16, width), 0)
        for n in range(2):
            old = buffer[n, pl.ds(first, 16), :].astype(F32)
            new = jnp.broadcast_to(rows_ref[n : n + 1, :].astype(F32), (16, width))
            buffer[n, pl.ds(first, 16), :] = jnp.where(row == offset - first, new, old).astype(BF16)
        copies = [
            pltpu.make_async_copy(buffer.at[n], target.at[numbers_ref[1]], out_sems.at[n])
            for n, target in enumerate((key_ref, value_ref))
        ]
        for copy in copies:
            copy.start()
        for copy in copies:
            copy.wait()

    shape = jax.ShapeDtypeStruct(key_out.shape, key_out.dtype)
    return pl.pallas_call(
        kernel,
        out_shape=(shape, shape),
        in_specs=[SMEM, VMEM] + [ANY] * (count + 2),
        out_specs=(ANY, ANY),
        scratch_shapes=[
            pltpu.VMEM((2, page, width), BF16),
            pltpu.SemaphoreType.DMA,
            pltpu.SemaphoreType.DMA((2,)),
        ],
        input_output_aliases={2 + count: 0, 3 + count: 1},
        compiler_params=pltpu.CompilerParams(vmem_limit_bytes=LIMIT),
        cost_estimate=cost(0, 8 * page * width * 2),
        name="place_page",
    )(numbers, new_rows, *candidates, key_out, value_out)


def body(
    tokens,
    norm_gain,
    norm_shift,
    qkv_weight,
    qkv_bias,
    out_weight,
    out_bias,
    key_pool,
    value_pool,
    lengths,
    page_table,
    new_slot,
    new_page,
):
    groups = lax.axis_size("req")
    head_groups = lax.axis_size("head")
    here = lax.axis_index("req")
    column_block = lax.axis_index("head")
    slots = tokens.shape[0]
    chips = groups // 2
    page_size, width = key_pool.shape[1:]
    depth = qkv_weight.shape[0]
    local_heads = qkv_weight.shape[1]
    slot_range = jnp.arange(slots, dtype=jnp.int32)
    target_device = new_slot // slots
    leaving = jnp.sum(jnp.where(target_device != here, slot_range, 0))

    mine = pick_page(key_pool, value_pool, page_table[leaving, :1])

    normed = layer_norm(tokens, norm_gain, norm_shift)
    table = jnp.stack(
        [target_device, new_slot % slots, new_page, lengths % page_size], axis=1
    ).astype(BF16)
    table = jnp.pad(table, ((0, 0), (0, META - table.shape[1])))
    features = normed.reshape(slots, groups, depth).transpose(1, 0, 2)
    blocks = jnp.concatenate(
        [relative(features, here), jnp.broadcast_to(table[None], (groups, slots, META))], axis=2
    ).reshape(chips, 2, slots, depth + META)
    spread = spread_pairs(blocks[:, 0], blocks[:, 1])
    candidates = [mine] + [swap(mine, "req", 2 * d) for d in range(1, chips)]

    told = jnp.stack(spread)[..., depth : depth + 4].astype(jnp.int32).reshape(groups, slots, 4)
    places = jnp.arange(groups, dtype=jnp.int32)
    goal = told[..., 0] ^ here
    for_me = (goal == 0) & (places[:, None] != 0)
    for_other = (goal == 1) & (places[:, None] != 1)
    pick = lambda mask, values: jnp.sum(jnp.where(mask, values, 0))
    source = pick(for_me, places[:, None])
    source_other = pick(for_other, places[:, None])
    arrived_page = pick(for_me, told[..., 2])
    arrived_length = pick(for_me, told[..., 3])
    high = -(-slots // 8) * 8
    goal_row = (goal % 2) * (chips * slots) + (goal // 2) * slots + told[..., 1]
    goal_row = jnp.pad(goal_row, ((0, 0), (0, high - slots)), constant_values=-1).reshape(-1)
    order = (
        jnp.arange(groups * slots, dtype=jnp.int32)[:, None] == goal_row[None, :]
    ).astype(BF16)

    keep, send = project(spread, jnp.transpose(qkv_weight, (1, 0, 2)))
    total = keep + swap(send, "req", 1)
    sums = [total[0]] + [swap(total[d], "req", 2 * d) for d in range(1, chips)]

    key_copy, value_copy = copy_pools(key_pool, value_pool)
    numbers = jnp.concatenate([lengths, jnp.stack([leaving, here, column_block])])
    pack_keep, pack_send, key_out, value_out = attend(
        numbers,
        page_table,
        sums,
        qkv_bias.reshape(1, -1),
        tokens,
        key_pool,
        value_pool,
        key_copy,
        value_copy,
    )
    packs = spread_pairs(pack_keep, pack_send)

    which = jnp.where(source_other % 2 == 0, source_other // 2, 0)
    from_other = swap(choose_page(which[None], candidates), "req", 1)

    strips = width // PACK
    rows = lax.dynamic_index_in_dim(
        jnp.stack(packs).reshape(groups, -1, PACK), source, 0, keepdims=False
    )
    arrived_rows = rows[high : high + 3 * strips].reshape(3, width)
    arrived = jnp.where(source % 2 == 0, source // 2, chips)
    key_out, value_out = place_page(
        jnp.stack([arrived, arrived_page, arrived_length]),
        arrived_rows[:2],
        candidates + [from_other],
        key_out,
        value_out,
    )

    keep, send = out_project(
        column_block[None],
        order,
        packs,
        out_weight.reshape(-1, out_weight.shape[2]),
        head_groups,
    )
    total = (keep + swap(send, "req", 1)).reshape(head_groups, chips, slots, width)
    summed = total[:, 0]
    for d in range(1, chips):
        summed = summed + swap(total[:, d].astype(BF16), "req", 2 * d).astype(F32)
    hidden = summed[0]
    for j in range(1, head_groups):
        hidden = hidden + swap(summed[j].astype(BF16), "head", j).astype(F32)
    token_part = lax.dynamic_slice_in_dim(tokens, column_block * width, width, 1)
    residual = jnp.where((slot_range == leaving)[:, None], arrived_rows[2:3], token_part)
    bias_part = lax.dynamic_slice_in_dim(out_bias, column_block * width, width, 0)
    hidden_out = (hidden + bias_part + residual.astype(F32)).astype(BF16)
    return (hidden_out, key_out, value_out)


def solution(mesh):
    in_specs = (
        P("req", None),
        P(),
        P(),
        P("req", "head", None),
        P("head", None),
        P("head", "req", None),
        P(),
        P("req", None, "head"),
        P("req", None, "head"),
        P("req"),
        P("req", None),
        P("req"),
        P("req"),
    )
    out_specs = (P("req", "head"), P("req", None, "head"), P("req", None, "head"))
    return jax.shard_map(body, mesh=mesh, in_specs=in_specs, out_specs=out_specs, check_vma=False)
```

```python
import functools

import jax
import jax.numpy as jnp
from jax import lax
from jax.experimental import pallas as pl
from jax.experimental.pallas import tpu as pltpu
from jax.sharding import PartitionSpec as P

EPSILON = 1e-05
F32 = jnp.float32
BF16 = jnp.bfloat16
LANES = 128
META = 128
PACK = 256
VMEM = pl.BlockSpec(memory_space=pltpu.VMEM)
SMEM = pl.BlockSpec(memory_space=pltpu.SMEM)
ANY = pl.BlockSpec(memory_space=pl.ANY)
MIB = 1024 * 1024


def cost(flops, moved):
    return pl.CostEstimate(flops=flops, bytes_accessed=moved, transcendentals=0)


def layer_norm(tokens, norm_gain, norm_shift):
    values_f = tokens.astype(F32)
    average = jnp.mean(values_f, axis=1, keepdims=True)
    centered = values_f - average
    variance = jnp.mean(centered * centered, axis=1, keepdims=True)
    return (centered * lax.rsqrt(variance + EPSILON) * norm_gain + norm_shift).astype(BF16)


def swap(value, axis, step):
    size = lax.axis_size(axis)
    return lax.ppermute(value, axis, [(i, i ^ step) for i in range(size)])


def relative(blocks, index):
    size = blocks.shape[0]
    tail = blocks.shape[1:]
    bits = size.bit_length() - 1
    split = blocks.reshape((2,) * bits + tail)
    for bit in range(bits):
        axis = bits - 1 - bit
        split = jnp.where((index >> bit) & 1 == 1, jnp.flip(split, axis), split)
    return split.reshape((size,) + tail)


def spread_pairs(keep, send):
    got = swap(send, "req", 1)
    chips = keep.shape[0]
    return [jnp.stack([keep[0], got[0]])] + [
        swap(jnp.stack([keep[d], got[d]]), "req", 2 * d) for d in range(1, chips)
    ]


def copy_pools(key_pool, value_pool):
    pages = key_pool.shape[0]
    parts = 5 if pages % 5 == 0 else 1
    step = pages // parts

    def kernel(key_ref, value_ref, key_out, value_out, buffer, in_sems, out_sems):
        steps = [(n, i, pl.ds(i * step, step)) for i in range(parts) for n in range(2)]
        sources, targets = (key_ref, value_ref), (key_out, value_out)
        reads = [
            pltpu.make_async_copy(sources[n].at[place], buffer.at[n, place], in_sems.at[n, i])
            for n, i, place in steps
        ]
        writes = [
            pltpu.make_async_copy(buffer.at[n, place], targets[n].at[place], out_sems.at[n, i])
            for n, i, place in steps
        ]
        for read in reads:
            read.start()
        for read, write in zip(reads, writes):
            read.wait()
            write.start()
        for write in writes:
            write.wait()

    shape = jax.ShapeDtypeStruct(key_pool.shape, key_pool.dtype)
    return pl.pallas_call(
        kernel,
        out_shape=(shape, shape),
        in_specs=[ANY, ANY],
        out_specs=(ANY, ANY),
        scratch_shapes=[
            pltpu.VMEM((2,) + key_pool.shape, key_pool.dtype),
            pltpu.SemaphoreType.DMA((2, parts)),
            pltpu.SemaphoreType.DMA((2, parts)),
        ],
        compiler_params=pltpu.CompilerParams(vmem_limit_bytes=11 * MIB),
        cost_estimate=cost(0, 4 * key_pool.size * 2),
        name="copy_pools",
    )(key_pool, value_pool)


def pick_page(key_pool, value_pool, page):
    shape = (2,) + key_pool.shape[1:]

    def kernel(page_ref, key_ref, value_ref, out_ref, sems):
        copies = [
            pltpu.make_async_copy(source.at[page_ref[0]], out_ref.at[n], sems.at[n])
            for n, source in enumerate((key_ref, value_ref))
        ]
        for copy in copies:
            copy.start()
        for copy in copies:
            copy.wait()

    return pl.pallas_call(
        kernel,
        out_shape=jax.ShapeDtypeStruct(shape, key_pool.dtype),
        in_specs=[SMEM, ANY, ANY],
        out_specs=VMEM,
        scratch_shapes=[pltpu.SemaphoreType.DMA((2,))],
        compiler_params=pltpu.CompilerParams(vmem_limit_bytes=2 * MIB),
        cost_estimate=cost(0, 4 * key_pool.shape[1] * key_pool.shape[2] * 2),
        name="pick_page",
    )(page, key_pool, value_pool)


def choose_page(which, candidates):
    def kernel(which_ref, *refs):
        out_ref, sem = refs[-2:]
        for n, candidate in enumerate(refs[:-2]):

            @pl.when(which_ref[0] == n)
            def _():
                copy = pltpu.make_async_copy(candidate, out_ref, sem)
                copy.start()
                copy.wait()

    one = candidates[0]
    return pl.pallas_call(
        kernel,
        out_shape=jax.ShapeDtypeStruct(one.shape, one.dtype),
        in_specs=[SMEM] + [ANY] * len(candidates),
        out_specs=VMEM,
        scratch_shapes=[pltpu.SemaphoreType.DMA],
        compiler_params=pltpu.CompilerParams(vmem_limit_bytes=2 * MIB),
        cost_estimate=cost(0, 4 * one.size),
        name="choose_page",
    )(which, *candidates)


def project(blocks, weight):
    chips = len(blocks)
    slots = blocks[0].shape[1]
    heads, depth, width = weight.shape
    per = 2 if heads % 2 == 0 else 1
    rows = chips * 2 * slots

    def kernel(*refs):
        block_refs = refs[:chips]
        weight_ref, keep_ref, send_ref, left = refs[chips:]

        @pl.when(pl.program_id(0) == 0)
        def _():
            for d in range(chips):
                for e in range(2):
                    row = (d * 2 + e) * slots
                    left[row : row + slots, :] = block_refs[d][e][:, :depth].astype(F32)

        lhs = left[...].astype(BF16)
        for j in range(per):
            total = jnp.dot(lhs, weight_ref[j], preferred_element_type=F32)
            for d in range(chips):
                row = d * 2 * slots
                columns = slice(j * width, (j + 1) * width)
                keep_ref[d, :, columns] = total[row : row + slots]
                send_ref[d, :, columns] = total[row + slots : row + 2 * slots]

    shape = jax.ShapeDtypeStruct((chips, slots, heads * width), F32)
    out_spec = pl.BlockSpec((chips, slots, per * width), lambda i: (0, 0, i))
    return pl.pallas_call(
        kernel,
        grid=(heads // per,),
        out_shape=(shape, shape),
        in_specs=[VMEM] * chips + [pl.BlockSpec((per, depth, width), lambda i: (i, 0, 0))],
        out_specs=(out_spec, out_spec),
        scratch_shapes=[pltpu.VMEM((rows, depth), F32)],
        compiler_params=pltpu.CompilerParams(vmem_limit_bytes=8 * MIB),
        cost_estimate=cost(2 * rows * weight.size, 2 * weight.size),
        name="project",
    )(*blocks, weight)


def attend(numbers, page_table, sums, bias, tokens, key_pool, value_pool, key_out, value_out):
    parts = len(sums)
    slots = sums[0].shape[0]
    pages, page, width = key_pool.shape
    head = LANES
    heads = width // head
    max_pages = page_table.shape[1]
    chunk_pages = 4
    chunk = chunk_pages * page
    chunks = max_pages // chunk_pages
    long_rows = max_pages * page
    short_rows = slots * page
    groups = 2 * parts
    share = head // groups
    per = LANES // share
    tall = 16
    strips = width // PACK
    scale = head ** (-0.5)

    def kernel(*refs):
        numbers_ref, table_ref = refs[:2]
        sum_refs = refs[2 : 2 + parts]
        (bias_ref, token_ref, key_ref, value_ref, _, _, pack_keep, pack_send, key_out_ref, value_out_ref) = refs[
            2 + parts : 12 + parts
        ]
        key_buffer, value_buffer, score_buffer, mix_buffer, sems, out_sems = refs[12 + parts :]
        leaving = numbers_ref[slots]
        here = numbers_ref[slots + 1]
        column_block = numbers_ref[slots + 2]
        lengths = [numbers_ref[s] for s in range(slots)]
        long_slot = jnp.int32(0)
        long_length = jnp.int32(-1)
        for s in range(slots):
            is_long = lengths[s] >= page
            long_slot = jnp.where(is_long, s, long_slot)
            long_length = jnp.where(is_long, lengths[s], long_length)
        turns = (long_length + chunk) // chunk

        pairs = ((key_ref, key_buffer), (value_ref, value_buffer))

        def short_copies(n):
            source, buffer = pairs[n]
            return [
                pltpu.make_async_copy(
                    source.at[table_ref[s, 0]], buffer.at[pl.ds(long_rows + s * page, page)], sems.at[n, chunks]
                )
                for s in range(slots)
            ]

        def long_copies(n, c):
            source, buffer = pairs[n]
            return [
                pltpu.make_async_copy(
                    source.at[table_ref[long_slot, c * chunk_pages + i]],
                    buffer.at[pl.ds((c * chunk_pages + i) * page, page)],
                    sems.at[n, c],
                )
                for i in range(chunk_pages)
            ]

        for n in range(2):
            for copy in short_copies(n):
                copy.start()
            for c in range(chunks):

                @pl.when(c < turns)
                def _():
                    for copy in long_copies(n, c):
                        copy.start()

        total = sum_refs[0][...]
        for ref in sum_refs[1:]:
            total = total + ref[...].astype(F32)
        total = total + bias_ref[...]

        def third(k):
            return jnp.concatenate(
                [total[:, (3 * h + k) * head : (3 * h + k + 1) * head] for h in range(heads)], axis=1
            )

        query = (third(0) * scale).astype(BF16).astype(F32)
        new_rows = (third(1).astype(BF16).astype(F32), third(2).astype(BF16).astype(F32))

        lane_head = lax.broadcasted_iota(jnp.int32, (tall, width), 1) // head
        on_head = lane_head == lax.broadcasted_iota(jnp.int32, (tall, width), 0)

        def blocked(row):
            return jnp.where(on_head, jnp.broadcast_to(row, (tall, width)), 0.0).astype(BF16)

        def append(n, s, base, offset, out_ref):
            _, buffer = pairs[n]
            first = pl.multiple_of(offset // 16 * 16, 16)
            place = pl.ds(pl.multiple_of(base + first, 16), 16)
            old = buffer[place, :].astype(F32)
            row = lax.broadcasted_iota(jnp.int32, (16, width), 0)
            fresh = jnp.where(row == offset - first, jnp.broadcast_to(new_rows[n][s : s + 1], (16, width)), old)
            buffer[place, :] = fresh.astype(BF16)

        def out_copy(n, s):
            _, buffer = pairs[n]
            out_ref = (key_out_ref, value_out_ref)[n]
            length = lengths[s]
            is_long = length >= page
            within = length % page // 16 * 16
            base = jnp.where(is_long, length // page * page, long_rows + s * page)
            return pltpu.make_async_copy(
                buffer.at[pl.ds(pl.multiple_of(base + within, 16), 16)],
                out_ref.at[table_ref[s, length // page], pl.ds(pl.multiple_of(within, 16), 16)],
                out_sems.at[n, s],
            )

        def append_short(n):
            for s in range(slots):

                @pl.when(lengths[s] < page)
                def _():
                    append(n, s, long_rows + s * page, lengths[s], None)

        def append_long(n):
            for s in range(slots):

                @pl.when(lengths[s] >= page)
                def _():
                    append(n, s, 0, lengths[s], None)

        def softmax(scores, valid):
            masked = jnp.where(valid, scores, -1e30)
            peak = jnp.max(masked, axis=1, keepdims=True)
            weights = jnp.where(valid, jnp.exp(masked - peak), 0.0)
            return weights.astype(BF16), jnp.sum(weights, axis=1, keepdims=True)

        across = (((1,), (1,)), ((), ()))
        for copy in short_copies(0):
            copy.wait()
        append_short(0)
        short_query = jnp.concatenate([blocked(query[s : s + 1]) for s in range(slots)], axis=0)
        short_scores = lax.dot_general(
            short_query, key_buffer[long_rows:, :], across, preferred_element_type=F32
        )
        size = (slots * tall, short_rows)
        row_slot = lax.broadcasted_iota(jnp.int32, size, 0) // tall
        column = lax.broadcasted_iota(jnp.int32, size, 1)
        limit = jnp.zeros(size, jnp.int32)
        for s in range(slots):
            limit = jnp.where(row_slot == s, jnp.minimum(lengths[s], page - 1), limit)
        in_slot = row_slot == column // page
        short_probs, short_denom = softmax(short_scores, in_slot & (column % page <= limit))

        long_row = jnp.zeros((1, width), F32)
        for s in range(slots):
            long_row = jnp.where(long_slot == s, query[s : s + 1], long_row)
        long_query = blocked(long_row)
        for c in range(chunks):

            @pl.when(c < turns)
            def _():
                for copy in long_copies(0, c):
                    copy.wait()

        append_long(0)
        score_buffer[...] = jnp.full(score_buffer.shape, -1e30, F32)
        for c in range(chunks):

            @pl.when(c < turns)
            def _():
                score_buffer[:, c * chunk : (c + 1) * chunk] = lax.dot_general(
                    long_query, key_buffer[c * chunk : (c + 1) * chunk, :], across, preferred_element_type=F32
                )

        position = lax.broadcasted_iota(jnp.int32, (tall, long_rows), 1)
        long_probs, long_denom = softmax(score_buffer[...], position <= jnp.maximum(long_length, 0))

        for copy in short_copies(1):
            copy.wait()
        append_short(1)
        short_mix = jnp.dot(short_probs, value_buffer[long_rows:, :], preferred_element_type=F32) / short_denom
        mix_buffer[...] = jnp.zeros(mix_buffer.shape, F32)
        for c in range(chunks):

            @pl.when(c < turns)
            def _():
                for copy in long_copies(1, c):
                    copy.wait()

        append_long(1)
        for n in range(2):
            for s in range(slots):

                @pl.when(leaving != s)
                def _():
                    out_copy(n, s).start()

        for c in range(chunks):

            @pl.when(c < turns)
            def _():
                mix_buffer[...] += jnp.dot(
                    long_probs[:, c * chunk : (c + 1) * chunk],
                    value_buffer[c * chunk : (c + 1) * chunk, :],
                    preferred_element_type=F32,
                )

        def fold(mixed):
            return jnp.sum(jnp.where(on_head, mixed, 0.0), axis=0, keepdims=True)

        long_mix = fold(mix_buffer[...] / long_denom)
        rows = []
        for s in range(slots):
            row = fold(short_mix[s * tall : (s + 1) * tall])
            rows.append(jnp.where(lengths[s] >= page, long_mix, row))
        high = -(-slots // 8) * 8
        attended = jnp.concatenate(rows + [jnp.zeros((high - slots, width), F32)], axis=0)

        token = token_ref[:, pl.ds(pl.multiple_of(column_block * width, LANES), width)].astype(F32)
        extra = []
        for source in new_rows + (token,):
            one = jnp.zeros((1, width), F32)
            for s in range(slots):
                one = jnp.where(leaving == s, source[s : s + 1], one)
            extra += [one[:, i * PACK : (i + 1) * PACK] for i in range(strips)]
        extra = jnp.concatenate(extra + [jnp.zeros((pack_rows(slots, strips) - high - 3 * strips, PACK), F32)], axis=0)

        lane = lax.broadcasted_iota(jnp.int32, (high, LANES), 1) // share
        for k in range(groups):
            wanted = here ^ k
            tiles = [jnp.zeros((high, LANES), F32) for _ in range(PACK // LANES)]
            for h in range(heads):
                place = h % per
                shift = lax.rem((place - wanted) * share + 2 * LANES, LANES)
                turned = pltpu.roll(attended[:, h * head : (h + 1) * head], shift, 1)
                tiles[h // per] = jnp.where(lane == place, turned, tiles[h // per])
            block = jnp.concatenate([jnp.concatenate(tiles, axis=1), extra], axis=0).astype(BF16)
            (pack_keep, pack_send)[k % 2][k // 2] = block

        for n in range(2):
            for s in range(slots):

                @pl.when(leaving != s)
                def _():
                    out_copy(n, s).wait()

    packed = jax.ShapeDtypeStruct((parts, pack_rows(slots, strips), PACK), BF16)
    pool_shape = jax.ShapeDtypeStruct(key_pool.shape, key_pool.dtype)
    return pl.pallas_call(
        kernel,
        out_shape=(packed, packed, pool_shape, pool_shape),
        in_specs=[SMEM, SMEM] + [VMEM] * (parts + 2) + [ANY] * 4,
        out_specs=(VMEM, VMEM, ANY, ANY),
        scratch_shapes=[
            pltpu.VMEM((long_rows + short_rows, width), BF16),
            pltpu.VMEM((long_rows + short_rows, width), BF16),
            pltpu.VMEM((tall, long_rows), F32),
            pltpu.VMEM((tall, width), F32),
            pltpu.SemaphoreType.DMA((2, chunks + 1)),
            pltpu.SemaphoreType.DMA((2, slots)),
        ],
        input_output_aliases={6 + parts: 2, 7 + parts: 3},
        compiler_params=pltpu.CompilerParams(vmem_limit_bytes=18 * MIB),
        cost_estimate=cost(4 * tall * (long_rows + short_rows) * width, 4 * (long_rows + short_rows) * width),
        name="attend",
    )(numbers, page_table, *sums, bias, tokens, key_pool, value_pool, key_out, value_out)


def pack_rows(slots, strips):
    need = -(-slots // 8) * 8 + 3 * strips
    return -(-need // 16) * 16


def out_project(column_block, order, blocks, weight, pieces):
    chips = len(blocks)
    depth, width = weight.shape
    rows, high = order.shape[0], order.shape[1] // (2 * chips)
    half = rows // 2
    piece = width // pieces

    def kernel(column_ref, order_ref, *refs):
        block_refs = refs[:chips]
        weight_ref, keep_ref, send_ref, left = refs[chips:]

        @pl.when(pl.program_id(0) == 0)
        def _():
            gathered = jnp.concatenate(
                [block_refs[d][e, :high, :].astype(F32) for d in range(chips) for e in range(2)], axis=0
            ).astype(BF16)
            left[...] = jnp.dot(order_ref[...], gathered, preferred_element_type=F32)

        total = jnp.dot(left[:, :depth].astype(BF16), weight_ref[...], preferred_element_type=F32)
        keep_ref[0] = total[:half]
        send_ref[0] = total[half:]

    shape = jax.ShapeDtypeStruct((pieces, half, piece), F32)
    out_spec = pl.BlockSpec((1, half, piece), lambda j, c: (j, 0, 0))
    whole = lambda shape: pl.BlockSpec(shape, lambda j, c: (0,) * len(shape))
    return pl.pallas_call(
        kernel,
        out_shape=(shape, shape),
        grid_spec=pltpu.PrefetchScalarGridSpec(
            num_scalar_prefetch=1,
            grid=(pieces,),
            in_specs=[whole(order.shape)]
            + [whole(block.shape) for block in blocks]
            + [pl.BlockSpec((depth, piece), lambda j, c: (0, j ^ c[0]))],
            out_specs=(out_spec, out_spec),
            scratch_shapes=[pltpu.VMEM((rows, PACK), F32)],
        ),
        compiler_params=pltpu.CompilerParams(vmem_limit_bytes=8 * MIB),
        cost_estimate=cost(2 * rows * weight.size, 2 * weight.size),
        name="out_project",
    )(column_block, order, *blocks, weight)


def place_page(numbers, new_rows, candidates, key_out, value_out):
    count = len(candidates)
    page, width = key_out.shape[1:]

    def kernel(numbers_ref, rows_ref, *refs):
        candidate_refs = refs[:count]
        _, _, key_ref, value_ref, buffer, sem, out_sems = refs[count:]
        for n in range(count):

            @pl.when(numbers_ref[0] == n)
            def _():
                copy = pltpu.make_async_copy(candidate_refs[n], buffer, sem)
                copy.start()
                copy.wait()

        offset = numbers_ref[2]
        first = pl.multiple_of(offset // 16 * 16, 16)
        row = lax.broadcasted_iota(jnp.int32, (16, width), 0)
        for n in range(2):
            old = buffer[n, pl.ds(first, 16), :].astype(F32)
            new = jnp.broadcast_to(rows_ref[n : n + 1, :].astype(F32), (16, width))
            buffer[n, pl.ds(first, 16), :] = jnp.where(row == offset - first, new, old).astype(BF16)
        copies = [
            pltpu.make_async_copy(buffer.at[n], target.at[numbers_ref[1]], out_sems.at[n])
            for n, target in enumerate((key_ref, value_ref))
        ]
        for copy in copies:
            copy.start()
        for copy in copies:
            copy.wait()

    shape = jax.ShapeDtypeStruct(key_out.shape, key_out.dtype)
    return pl.pallas_call(
        kernel,
        out_shape=(shape, shape),
        in_specs=[SMEM, VMEM] + [ANY] * (count + 2),
        out_specs=(ANY, ANY),
        scratch_shapes=[
            pltpu.VMEM((2, page, width), BF16),
            pltpu.SemaphoreType.DMA,
            pltpu.SemaphoreType.DMA((2,)),
        ],
        input_output_aliases={2 + count: 0, 3 + count: 1},
        compiler_params=pltpu.CompilerParams(vmem_limit_bytes=2 * MIB),
        cost_estimate=cost(0, 8 * page * width * 2),
        name="place_page",
    )(numbers, new_rows, *candidates, key_out, value_out)


def body(
    tokens,
    norm_gain,
    norm_shift,
    qkv_weight,
    qkv_bias,
    out_weight,
    out_bias,
    key_pool,
    value_pool,
    lengths,
    page_table,
    new_slot,
    new_page,
):
    groups = lax.axis_size("req")
    head_groups = lax.axis_size("head")
    here = lax.axis_index("req")
    column_block = lax.axis_index("head")
    slots = tokens.shape[0]
    chips = groups // 2
    page_size, width = key_pool.shape[1:]
    depth = qkv_weight.shape[0]
    local_heads = qkv_weight.shape[1]
    slot_range = jnp.arange(slots, dtype=jnp.int32)
    target_device = new_slot // slots
    leaving = jnp.sum(jnp.where(target_device != here, slot_range, 0))

    mine = pick_page(key_pool, value_pool, page_table[leaving, :1])

    normed = layer_norm(tokens, norm_gain, norm_shift)
    table = jnp.stack(
        [target_device, new_slot % slots, new_page, lengths % page_size], axis=1
    ).astype(BF16)
    table = jnp.pad(table, ((0, 0), (0, META - table.shape[1])))
    features = normed.reshape(slots, groups, depth).transpose(1, 0, 2)
    blocks = jnp.concatenate(
        [relative(features, here), jnp.broadcast_to(table[None], (groups, slots, META))], axis=2
    ).reshape(chips, 2, slots, depth + META)
    spread = spread_pairs(blocks[:, 0], blocks[:, 1])
    candidates = [mine] + [swap(mine, "req", 2 * d) for d in range(1, chips)]

    told = jnp.stack(spread)[..., depth : depth + 4].astype(jnp.int32).reshape(groups, slots, 4)
    places = jnp.arange(groups, dtype=jnp.int32)
    goal = told[..., 0] ^ here
    for_me = (goal == 0) & (places[:, None] != 0)
    for_other = (goal == 1) & (places[:, None] != 1)
    pick = lambda mask, values: jnp.sum(jnp.where(mask, values, 0))
    source = pick(for_me, places[:, None])
    source_other = pick(for_other, places[:, None])
    arrived_page = pick(for_me, told[..., 2])
    arrived_length = pick(for_me, told[..., 3])
    high = -(-slots // 8) * 8
    goal_row = (goal % 2) * (chips * slots) + (goal // 2) * slots + told[..., 1]
    goal_row = jnp.pad(goal_row, ((0, 0), (0, high - slots)), constant_values=-1).reshape(-1)
    order = (
        jnp.arange(groups * slots, dtype=jnp.int32)[:, None] == goal_row[None, :]
    ).astype(BF16)

    keep, send = project(spread, jnp.transpose(qkv_weight, (1, 0, 2)))
    total = keep + swap(send, "req", 1)
    sums = [total[0]] + [swap(total[d], "req", 2 * d) for d in range(1, chips)]

    key_copy, value_copy = copy_pools(key_pool, value_pool)
    numbers = jnp.concatenate([lengths, jnp.stack([leaving, here, column_block])])
    pack_keep, pack_send, key_out, value_out = attend(
        numbers,
        page_table,
        sums,
        qkv_bias.reshape(1, -1),
        tokens,
        key_pool,
        value_pool,
        key_copy,
        value_copy,
    )
    packs = spread_pairs(pack_keep, pack_send)

    which = jnp.where(source_other % 2 == 0, source_other // 2, 0)
    from_other = swap(choose_page(which[None], candidates), "req", 1)

    strips = width // PACK
    rows = lax.dynamic_index_in_dim(
        jnp.stack(packs).reshape(groups, -1, PACK), source, 0, keepdims=False
    )
    arrived_rows = rows[high : high + 3 * strips].reshape(3, width)
    arrived = jnp.where(source % 2 == 0, source // 2, chips)
    key_out, value_out = place_page(
        jnp.stack([arrived, arrived_page, arrived_length]),
        arrived_rows[:2],
        candidates + [from_other],
        key_out,
        value_out,
    )

    keep, send = out_project(
        column_block[None],
        order,
        packs,
        out_weight.reshape(-1, out_weight.shape[2]),
        head_groups,
    )
    total = (keep + swap(send, "req", 1)).reshape(head_groups, chips, slots, width)
    summed = total[:, 0]
    for d in range(1, chips):
        summed = summed + swap(total[:, d].astype(BF16), "req", 2 * d).astype(F32)
    hidden = summed[0]
    for j in range(1, head_groups):
        hidden = hidden + swap(summed[j].astype(BF16), "head", j).astype(F32)
    token_part = lax.dynamic_slice_in_dim(tokens, column_block * width, width, 1)
    residual = jnp.where((slot_range == leaving)[:, None], arrived_rows[2:3], token_part)
    bias_part = lax.dynamic_slice_in_dim(out_bias, column_block * width, width, 0)
    hidden_out = (hidden + bias_part + residual.astype(F32)).astype(BF16)
    return (hidden_out, key_out, value_out)


def solution(mesh):
    in_specs = (
        P("req", None),
        P(),
        P(),
        P("req", "head", None),
        P("head", None),
        P("head", "req", None),
        P(),
        P("req", None, "head"),
        P("req", None, "head"),
        P("req"),
        P("req", None),
        P("req"),
        P("req"),
    )
    out_specs = (P("req", "head"), P("req", None, "head"), P("req", None, "head"))
    return jax.shard_map(body, mesh=mesh, in_specs=in_specs, out_specs=out_specs, check_vma=False)
```

```python
import functools

import jax
import jax.numpy as jnp
from jax import lax
from jax.experimental import pallas as pl
from jax.experimental.pallas import tpu as pltpu
from jax.sharding import PartitionSpec as P

EPSILON = 1e-05
F32 = jnp.float32
BF16 = jnp.bfloat16
LANES = 128
META = 128
PACK = 256
VMEM = pl.BlockSpec(memory_space=pltpu.VMEM)
SMEM = pl.BlockSpec(memory_space=pltpu.SMEM)
ANY = pl.BlockSpec(memory_space=pl.ANY)
HBM = pl.BlockSpec(memory_space=pltpu.HBM)
MIB = 1024 * 1024


def cost(flops, moved):
    return pl.CostEstimate(flops=flops, bytes_accessed=moved, transcendentals=0)


def swap(value, axis, step):
    size = lax.axis_size(axis)
    return lax.ppermute(value, axis, [(i, i ^ step) for i in range(size)])


def spread_pairs(keep, send):
    got = swap(send, "req", 1)
    chips = keep.shape[0]
    return [jnp.stack([keep[0], got[0]])] + [
        swap(jnp.stack([keep[d], got[d]]), "req", 2 * d) for d in range(1, chips)
    ]


def copy_pool(pool, after):
    pages = pool.shape[0]
    parts = 5 if pages % 5 == 0 else 1
    step = pages // parts

    def kernel(pool_ref, _, out_ref, buffer, in_sems, out_sems):
        places = [pl.ds(i * step, step) for i in range(parts)]
        reads = [
            pltpu.make_async_copy(pool_ref.at[place], buffer.at[place], in_sems.at[i])
            for i, place in enumerate(places)
        ]
        writes = [
            pltpu.make_async_copy(buffer.at[place], out_ref.at[place], out_sems.at[i])
            for i, place in enumerate(places)
        ]
        for read in reads:
            read.start()
        for read, write in zip(reads, writes):
            read.wait()
            write.start()
        for write in writes:
            write.wait()

    return pl.pallas_call(
        kernel,
        out_shape=jax.ShapeDtypeStruct(pool.shape, pool.dtype),
        in_specs=[HBM, ANY],
        out_specs=HBM,
        scratch_shapes=[
            pltpu.VMEM(pool.shape, pool.dtype),
            pltpu.SemaphoreType.DMA((parts,)),
            pltpu.SemaphoreType.DMA((parts,)),
        ],
        compiler_params=pltpu.CompilerParams(vmem_limit_bytes=6 * MIB),
        cost_estimate=cost(0, 2 * pool.size * 2),
        name="copy_pool",
    )(pool, after)


def leaving_slot(new_slot_ref, slots, here):
    leaving = jnp.int32(0)
    for s in range(slots):
        leaving = jnp.where(new_slot_ref[s] // slots != here, s, leaving)
    return leaving


def prepare(tokens, gain, shift, lengths, page_table, new_slot, new_page, key_pool, value_pool):
    groups = lax.axis_size("req")
    chips = groups // 2
    slots, model = tokens.shape
    depth = model // groups
    page, width = key_pool.shape[1:]

    def kernel(
        token_ref, gain_ref, shift_ref, length_ref, table_ref, slot_ref, page_ref, key_ref, value_ref,
        keep_ref, send_ref, out_ref, normed, sems,
    ):
        here = lax.axis_index("req")
        leaving = leaving_slot(slot_ref, slots, here)
        copies = [
            pltpu.make_async_copy(source.at[table_ref[leaving, 0]], out_ref.at[n], sems.at[n])
            for n, source in enumerate((key_ref, value_ref))
        ]
        for copy in copies:
            copy.start()
        values = token_ref[...].astype(F32)
        average = jnp.mean(values, axis=1, keepdims=True)
        centered = values - average
        variance = jnp.mean(centered * centered, axis=1, keepdims=True)
        rows = centered * lax.rsqrt(variance + EPSILON) * gain_ref[...] + shift_ref[...]
        normed[...] = rows.astype(BF16).astype(F32)
        row = lax.broadcasted_iota(jnp.int32, (slots, META), 0)
        lane = lax.broadcasted_iota(jnp.int32, (slots, META), 1)
        told = jnp.zeros((slots, META), F32)
        for s in range(slots):
            slot = slot_ref[s]
            numbers = (slot // slots, slot % slots, page_ref[s], length_ref[s] % page)
            for j, number in enumerate(numbers):
                told = jnp.where((row == s) & (lane == j), number.astype(F32), told)
        told = told.astype(BF16)
        for k in range(groups):
            first = (here ^ k) * depth
            if depth % LANES == 0:
                block = normed[:, pl.ds(pl.multiple_of(first, LANES), depth)]
            else:
                block = pltpu.roll(normed[...], lax.rem(model - first, model), 1)[:, :depth]
            target = (keep_ref, send_ref)[k % 2]
            target[k // 2, :, :META] = told
            target[k // 2, :, META:] = block.astype(BF16)
        for copy in copies:
            copy.wait()

    blocks = jax.ShapeDtypeStruct((chips, slots, META + depth), BF16)
    return pl.pallas_call(
        kernel,
        out_shape=(blocks, blocks, jax.ShapeDtypeStruct((2, page, width), key_pool.dtype)),
        in_specs=[VMEM] * 3 + [SMEM] * 4 + [HBM] * 2,
        out_specs=(VMEM, VMEM, VMEM),
        scratch_shapes=[pltpu.VMEM((slots, model), F32), pltpu.SemaphoreType.DMA((2,))],
        compiler_params=pltpu.CompilerParams(vmem_limit_bytes=4 * MIB),
        cost_estimate=cost(0, 8 * page * width),
        name="prepare",
    )(tokens, gain, shift, lengths, page_table, new_slot, new_page, key_pool, value_pool)


def arrivals(block_refs, here, wanted):
    slots = block_refs[0].shape[1]
    lane = lax.broadcasted_iota(jnp.int32, (slots, META), 1)
    found = jnp.zeros((slots, META), F32)
    goal = (here ^ wanted).astype(F32)
    for d, ref in enumerate(block_refs):
        for e in range(2):
            k = 2 * d + e
            if k == wanted:
                continue
            told = ref[e, :, :META].astype(F32)
            numbered = jnp.where(lane == 4, float(k), told)
            found = jnp.where(told[:, :1] == goal, numbered, found)
    pick = lambda j: jnp.sum(jnp.where(lane == j, found, 0.0)).astype(jnp.int32)
    return pick(4), pick(2), pick(3)


def choose_page(spread, candidates):
    chips = len(spread)

    def kernel(*refs):
        block_refs, candidate_refs = refs[:chips], refs[chips : 2 * chips]
        out_ref, sem = refs[2 * chips :]
        source = arrivals(block_refs, lax.axis_index("req"), 1)[0]
        which = jnp.where(source % 2 == 0, source // 2, 0)
        for n, candidate in enumerate(candidate_refs):

            @pl.when(which == n)
            def _():
                copy = pltpu.make_async_copy(candidate, out_ref, sem)
                copy.start()
                copy.wait()

    one = candidates[0]
    return pl.pallas_call(
        kernel,
        out_shape=jax.ShapeDtypeStruct(one.shape, one.dtype),
        in_specs=[VMEM] * chips + [ANY] * chips,
        out_specs=VMEM,
        scratch_shapes=[pltpu.SemaphoreType.DMA],
        compiler_params=pltpu.CompilerParams(vmem_limit_bytes=2 * MIB),
        cost_estimate=cost(0, 4 * one.size),
        name="choose_page",
    )(*spread, *candidates)


def project(blocks, weight):
    chips = len(blocks)
    slots = blocks[0].shape[1]
    heads, depth, width = weight.shape
    per = 2 if heads % 2 == 0 else 1
    rows = chips * 2 * slots

    def kernel(*refs):
        block_refs = refs[:chips]
        weight_ref, keep_ref, send_ref, left = refs[chips:]

        @pl.when(pl.program_id(0) == 0)
        def _():
            for d in range(chips):
                for e in range(2):
                    row = (d * 2 + e) * slots
                    left[row : row + slots, :] = block_refs[d][e, :, META:].astype(F32)

        lhs = left[...].astype(BF16)
        for j in range(per):
            total = jnp.dot(lhs, weight_ref[j], preferred_element_type=F32)
            for d in range(chips):
                row = d * 2 * slots
                columns = slice(j * width, (j + 1) * width)
                keep_ref[d, :, columns] = total[row : row + slots]
                send_ref[d, :, columns] = total[row + slots : row + 2 * slots]

    shape = jax.ShapeDtypeStruct((chips, slots, heads * width), F32)
    out_spec = pl.BlockSpec((chips, slots, per * width), lambda i: (0, 0, i))
    return pl.pallas_call(
        kernel,
        grid=(heads // per,),
        out_shape=(shape, shape),
        in_specs=[VMEM] * chips + [pl.BlockSpec((per, depth, width), lambda i: (i, 0, 0))],
        out_specs=(out_spec, out_spec),
        scratch_shapes=[pltpu.VMEM((rows, depth), F32)],
        compiler_params=pltpu.CompilerParams(vmem_limit_bytes=8 * MIB),
        cost_estimate=cost(2 * rows * weight.size, 2 * weight.size),
        name="project",
    )(*blocks, weight)


def combine(keep, got):
    chips, slots, width = keep.shape
    heads = width // (3 * LANES)

    def kernel(keep_ref, got_ref, own_ref, *message_refs):
        own_ref[...] = keep_ref[0] + got_ref[0]
        for d in range(1, chips):
            for h in range(heads):
                total = keep_ref[d, :, 3 * h * LANES : 3 * (h + 1) * LANES] + got_ref[d, :, 3 * h * LANES : 3 * (h + 1) * LANES]
                query = total[:, :LANES]
                high = query.astype(BF16)
                low = (query - high.astype(F32)).astype(BF16)
                base = 4 * h * LANES
                message_refs[d - 1][:, base : base + LANES] = high
                message_refs[d - 1][:, base + LANES : base + 2 * LANES] = low
                message_refs[d - 1][:, base + 2 * LANES : base + 4 * LANES] = total[:, LANES:].astype(BF16)

    message = jax.ShapeDtypeStruct((slots, 4 * heads * LANES), BF16)
    return pl.pallas_call(
        kernel,
        out_shape=(jax.ShapeDtypeStruct((slots, width), F32),) + (message,) * (chips - 1),
        in_specs=[VMEM, VMEM],
        out_specs=(VMEM,) * chips,
        compiler_params=pltpu.CompilerParams(vmem_limit_bytes=8 * MIB),
        cost_estimate=cost(0, 8 * keep.size),
        name="combine",
    )(keep, got)


def attend(lengths, new_slot, page_table, sums, bias, tokens, key_pool, value_pool, key_out, value_out):
    parts = len(sums)
    slots = sums[0].shape[0]
    pages, page, width = key_pool.shape
    head = LANES
    heads = width // head
    max_pages = page_table.shape[1]
    chunk_pages = 4
    chunk = chunk_pages * page
    chunks = max_pages // chunk_pages
    long_rows = max_pages * page
    short_rows = slots * page
    groups = 2 * parts
    share = head // groups
    per = LANES // share
    tall = 16
    strips = width // PACK
    scale = head ** (-0.5)

    def kernel(*refs):
        length_ref, slot_ref, table_ref = refs[:3]
        sum_refs = refs[3 : 3 + parts]
        (bias_ref, token_ref, key_ref, value_ref, _, _, pack_keep, pack_send, key_out_ref, value_out_ref) = refs[
            3 + parts : 13 + parts
        ]
        key_buffer, value_buffer, score_buffer, mix_buffer, sems, out_sems = refs[13 + parts :]
        here = lax.axis_index("req")
        column_block = lax.axis_index("head")
        leaving = leaving_slot(slot_ref, slots, here)
        lengths = [length_ref[s] for s in range(slots)]
        long_slot = jnp.int32(0)
        long_length = jnp.int32(-1)
        for s in range(slots):
            is_long = lengths[s] >= page
            long_slot = jnp.where(is_long, s, long_slot)
            long_length = jnp.where(is_long, lengths[s], long_length)
        turns = (long_length + chunk) // chunk

        pairs = ((key_ref, key_buffer), (value_ref, value_buffer))

        def short_copies(n):
            source, buffer = pairs[n]
            return [
                pltpu.make_async_copy(
                    source.at[table_ref[s, 0]], buffer.at[pl.ds(long_rows + s * page, page)], sems.at[n, chunks]
                )
                for s in range(slots)
            ]

        def long_copies(n, c):
            source, buffer = pairs[n]
            return [
                pltpu.make_async_copy(
                    source.at[table_ref[long_slot, c * chunk_pages + i]],
                    buffer.at[pl.ds((c * chunk_pages + i) * page, page)],
                    sems.at[n, c],
                )
                for i in range(chunk_pages)
            ]

        for n in range(2):
            for copy in short_copies(n):
                copy.start()
            for c in range(chunks):

                @pl.when(c < turns)
                def _():
                    for copy in long_copies(n, c):
                        copy.start()

        total = sum_refs[0][...] + bias_ref[...]

        def third(k):
            columns = []
            for h in range(heads):
                one = total[:, (3 * h + k) * head : (3 * h + k + 1) * head]
                for ref in sum_refs[1:]:
                    base = 4 * h * head
                    if k == 0:
                        one = one + ref[:, base : base + head].astype(F32) + ref[:, base + head : base + 2 * head].astype(F32)
                    else:
                        one = one + ref[:, base + (k + 1) * head : base + (k + 2) * head].astype(F32)
                columns.append(one)
            return jnp.concatenate(columns, axis=1)

        query = (third(0) * scale).astype(BF16).astype(F32)
        new_rows = (third(1).astype(BF16).astype(F32), third(2).astype(BF16).astype(F32))

        lane_head = lax.broadcasted_iota(jnp.int32, (tall, width), 1) // head
        on_head = lane_head == lax.broadcasted_iota(jnp.int32, (tall, width), 0)

        def blocked(row):
            return jnp.where(on_head, jnp.broadcast_to(row, (tall, width)), 0.0).astype(BF16)

        def append(n, s, base, offset, out_ref):
            _, buffer = pairs[n]
            first = pl.multiple_of(offset // 16 * 16, 16)
            place = pl.ds(pl.multiple_of(base + first, 16), 16)
            old = buffer[place, :].astype(F32)
            row = lax.broadcasted_iota(jnp.int32, (16, width), 0)
            fresh = jnp.where(row == offset - first, jnp.broadcast_to(new_rows[n][s : s + 1], (16, width)), old)
            buffer[place, :] = fresh.astype(BF16)

        def out_copy(n, s):
            _, buffer = pairs[n]
            out_ref = (key_out_ref, value_out_ref)[n]
            length = lengths[s]
            is_long = length >= page
            within = length % page // 16 * 16
            base = jnp.where(is_long, length // page * page, long_rows + s * page)
            return pltpu.make_async_copy(
                buffer.at[pl.ds(pl.multiple_of(base + within, 16), 16)],
                out_ref.at[table_ref[s, length // page], pl.ds(pl.multiple_of(within, 16), 16)],
                out_sems.at[n, s],
            )

        def append_short(n):
            for s in range(slots):

                @pl.when(lengths[s] < page)
                def _():
                    append(n, s, long_rows + s * page, lengths[s], None)

        def append_long(n):
            for s in range(slots):

                @pl.when(lengths[s] >= page)
                def _():
                    append(n, s, 0, lengths[s], None)

        def softmax(scores, valid):
            masked = jnp.where(valid, scores, -1e30)
            peak = jnp.max(masked, axis=1, keepdims=True)
            weights = jnp.where(valid, jnp.exp(masked - peak), 0.0)
            return weights.astype(BF16), jnp.sum(weights, axis=1, keepdims=True)

        across = (((1,), (1,)), ((), ()))
        for copy in short_copies(0):
            copy.wait()
        append_short(0)
        short_query = jnp.concatenate([blocked(query[s : s + 1]) for s in range(slots)], axis=0)
        short_scores = lax.dot_general(
            short_query, key_buffer[long_rows:, :], across, preferred_element_type=F32
        )
        size = (slots * tall, short_rows)
        row_slot = lax.broadcasted_iota(jnp.int32, size, 0) // tall
        column = lax.broadcasted_iota(jnp.int32, size, 1)
        limit = jnp.zeros(size, jnp.int32)
        for s in range(slots):
            limit = jnp.where(row_slot == s, jnp.minimum(lengths[s], page - 1), limit)
        in_slot = row_slot == column // page
        short_probs, short_denom = softmax(short_scores, in_slot & (column % page <= limit))

        long_row = jnp.zeros((1, width), F32)
        for s in range(slots):
            long_row = jnp.where(long_slot == s, query[s : s + 1], long_row)
        long_query = blocked(long_row)
        for c in range(chunks):

            @pl.when(c < turns)
            def _():
                for copy in long_copies(0, c):
                    copy.wait()

        append_long(0)
        score_buffer[...] = jnp.full(score_buffer.shape, -1e30, F32)
        for c in range(chunks):

            @pl.when(c < turns)
            def _():
                score_buffer[:, c * chunk : (c + 1) * chunk] = lax.dot_general(
                    long_query, key_buffer[c * chunk : (c + 1) * chunk, :], across, preferred_element_type=F32
                )

        position = lax.broadcasted_iota(jnp.int32, (tall, long_rows), 1)
        long_probs, long_denom = softmax(score_buffer[...], position <= jnp.maximum(long_length, 0))

        for copy in short_copies(1):
            copy.wait()
        append_short(1)
        short_mix = jnp.dot(short_probs, value_buffer[long_rows:, :], preferred_element_type=F32) / short_denom
        mix_buffer[...] = jnp.zeros(mix_buffer.shape, F32)
        for c in range(chunks):

            @pl.when(c < turns)
            def _():
                for copy in long_copies(1, c):
                    copy.wait()

        append_long(1)
        for n in range(2):
            for s in range(slots):

                @pl.when(leaving != s)
                def _():
                    out_copy(n, s).start()

        for c in range(chunks):

            @pl.when(c < turns)
            def _():
                mix_buffer[...] += jnp.dot(
                    long_probs[:, c * chunk : (c + 1) * chunk],
                    value_buffer[c * chunk : (c + 1) * chunk, :],
                    preferred_element_type=F32,
                )

        def fold(mixed):
            return jnp.sum(jnp.where(on_head, mixed, 0.0), axis=0, keepdims=True)

        long_mix = fold(mix_buffer[...] / long_denom)
        rows = []
        for s in range(slots):
            row = fold(short_mix[s * tall : (s + 1) * tall])
            rows.append(jnp.where(lengths[s] >= page, long_mix, row))
        high = -(-slots // 8) * 8
        attended = jnp.concatenate(rows + [jnp.zeros((high - slots, width), F32)], axis=0)

        token = token_ref[:, pl.ds(pl.multiple_of(column_block * width, LANES), width)].astype(F32)
        extra = []
        for source in new_rows + (token,):
            one = jnp.zeros((1, width), F32)
            for s in range(slots):
                one = jnp.where(leaving == s, source[s : s + 1], one)
            extra += [one[:, i * PACK : (i + 1) * PACK] for i in range(strips)]
        extra = jnp.concatenate(extra + [jnp.zeros((pack_rows(slots, strips) - high - 3 * strips, PACK), F32)], axis=0)

        row_at = lax.broadcasted_iota(jnp.int32, (high, LANES), 0)
        lane_at = lax.broadcasted_iota(jnp.int32, (high, LANES), 1)
        goal_device = jnp.full((high, LANES), -1.0, F32)
        goal_slot = jnp.zeros((high, LANES), F32)
        for s in range(slots):
            goal_device = jnp.where(row_at == s, (slot_ref[s] // slots).astype(F32), goal_device)
            goal_slot = jnp.where(row_at == s, (slot_ref[s] % slots).astype(F32), goal_slot)
        lane = lane_at // share
        for k in range(groups):
            wanted = here ^ k
            tiles = [jnp.zeros((high, LANES), F32) for _ in range(PACK // LANES)]
            for h in range(heads):
                place = h % per
                shift = lax.rem((place - wanted) * share + 2 * LANES, LANES)
                turned = pltpu.roll(attended[:, h * head : (h + 1) * head], shift, 1)
                tiles[h // per] = jnp.where(lane == place, turned, tiles[h // per])
            tiles[-1] = jnp.where(lane_at == LANES - 2, goal_device, jnp.where(lane_at == LANES - 1, goal_slot, tiles[-1]))
            block = jnp.concatenate([jnp.concatenate(tiles, axis=1), extra], axis=0).astype(BF16)
            (pack_keep, pack_send)[k % 2][k // 2] = block

        for n in range(2):
            for s in range(slots):

                @pl.when(leaving != s)
                def _():
                    out_copy(n, s).wait()

    packed = jax.ShapeDtypeStruct((parts, pack_rows(slots, strips), PACK), BF16)
    pool_shape = jax.ShapeDtypeStruct(key_pool.shape, key_pool.dtype)
    return pl.pallas_call(
        kernel,
        out_shape=(packed, packed, pool_shape, pool_shape),
        in_specs=[SMEM] * 3 + [VMEM] * (parts + 2) + [HBM] * 4,
        out_specs=(VMEM, VMEM, HBM, HBM),
        scratch_shapes=[
            pltpu.VMEM((long_rows + short_rows, width), BF16),
            pltpu.VMEM((long_rows + short_rows, width), BF16),
            pltpu.VMEM((tall, long_rows), F32),
            pltpu.VMEM((tall, width), F32),
            pltpu.SemaphoreType.DMA((2, chunks + 1)),
            pltpu.SemaphoreType.DMA((2, slots)),
        ],
        input_output_aliases={7 + parts: 2, 8 + parts: 3},
        compiler_params=pltpu.CompilerParams(vmem_limit_bytes=18 * MIB),
        cost_estimate=cost(4 * tall * (long_rows + short_rows) * width, 4 * (long_rows + short_rows) * width),
        name="attend",
    )(lengths, new_slot, page_table, *sums, bias, tokens, key_pool, value_pool, key_out, value_out)


def pack_rows(slots, strips):
    need = -(-slots // 8) * 8 + 3 * strips
    return -(-need // 16) * 16


def out_project(column_block, blocks, weight, pieces, slots):
    chips = len(blocks)
    depth, width = weight.shape
    high = -(-slots // 8) * 8
    rows = 2 * chips * slots
    piece = width // pieces

    def kernel(column_ref, *refs):
        block_refs = refs[:chips]
        weight_ref, keep_ref, send_ref, left = refs[chips:]

        @pl.when(pl.program_id(0) == 0)
        def _():
            gathered = jnp.concatenate(
                [block_refs[d][e, :high, :].astype(F32) for d in range(chips) for e in range(2)], axis=0
            )
            goal = gathered[:, PACK - 2 : PACK - 1].astype(jnp.int32)
            place = goal ^ lax.axis_index("req")
            row = (place % 2) * (chips * slots) + (place // 2) * slots + gathered[:, PACK - 1 :].astype(jnp.int32)
            row = jnp.where(goal < 0, -1, row)
            size = (gathered.shape[0], rows)
            order = jnp.where(lax.broadcasted_iota(jnp.int32, size, 1) == row, 1.0, 0.0)
            left[...] = lax.dot_general(
                order.astype(BF16), gathered.astype(BF16), (((0,), (0,)), ((), ())), preferred_element_type=F32
            )

        total = jnp.dot(left[:, :depth].astype(BF16), weight_ref[...], preferred_element_type=F32)
        for d in range(chips):
            keep_ref[d, 0] = total[d * slots : (d + 1) * slots]
            send_ref[d, 0] = total[(chips + d) * slots : (chips + d + 1) * slots].astype(BF16)

    shape = (chips, pieces, slots, piece)
    out_spec = pl.BlockSpec((chips, 1, slots, piece), lambda j, c: (0, j, 0, 0))
    whole = lambda shape: pl.BlockSpec(shape, lambda j, c: (0,) * len(shape))
    return pl.pallas_call(
        kernel,
        out_shape=(jax.ShapeDtypeStruct(shape, F32), jax.ShapeDtypeStruct(shape, BF16)),
        grid_spec=pltpu.PrefetchScalarGridSpec(
            num_scalar_prefetch=1,
            grid=(pieces,),
            in_specs=[whole(block.shape) for block in blocks]
            + [pl.BlockSpec((depth, piece), lambda j, c: (0, j ^ c[0]))],
            out_specs=(out_spec, out_spec),
            scratch_shapes=[pltpu.VMEM((rows, PACK), F32)],
        ),
        compiler_params=pltpu.CompilerParams(vmem_limit_bytes=8 * MIB),
        cost_estimate=cost(2 * rows * weight.size, 2 * weight.size),
        name="out_project",
    )(column_block, *blocks, weight)


def place_page(new_slot, spread, packs, tokens, out_bias, candidates, key_out, value_out):
    chips = len(spread)
    count = len(candidates)
    page, width = key_out.shape[1:]
    slots = tokens.shape[0]
    high = -(-slots // 8) * 8
    strips = width // PACK

    def kernel(slot_ref, *refs):
        block_refs, pack_refs = refs[:chips], refs[chips : 2 * chips]
        token_ref, bias_ref = refs[2 * chips : 2 * chips + 2]
        candidate_refs = refs[2 * chips + 2 : 2 * chips + 2 + count]
        _, _, base_ref, key_ref, value_ref, buffer, arrived, sem, out_sems = refs[2 * chips + 2 + count :]
        here = lax.axis_index("req")
        column = pl.multiple_of(lax.axis_index("head") * width, LANES)
        source, page_at, offset = arrivals(block_refs, here, 0)
        which = jnp.where(source % 2 == 0, source // 2, chips)
        for n in range(count):

            @pl.when(which == n)
            def _():
                copy = pltpu.make_async_copy(candidate_refs[n], buffer, sem)
                copy.start()

        for d in range(chips):
            for e in range(2):

                @pl.when(source == 2 * d + e)
                def _():
                    arrived[...] = pack_refs[d][e].astype(F32)

        def fresh(n):
            strip = high + n * strips
            return jnp.concatenate([arrived[strip + i : strip + i + 1, :] for i in range(strips)], axis=1)

        at = lax.broadcasted_iota(jnp.int32, (slots, width), 0)
        token = jnp.where(
            at == leaving_slot(slot_ref, slots, here),
            jnp.broadcast_to(fresh(2), (slots, width)),
            token_ref[:, pl.ds(column, width)].astype(F32),
        )
        base_ref[...] = token + bias_ref[:, pl.ds(column, width)]
        pltpu.make_async_copy(candidate_refs[0], buffer, sem).wait()
        first = pl.multiple_of(offset // 16 * 16, 16)
        row = lax.broadcasted_iota(jnp.int32, (16, width), 0)
        for n in range(2):
            old = buffer[n, pl.ds(first, 16), :].astype(F32)
            new = jnp.broadcast_to(fresh(n), (16, width))
            buffer[n, pl.ds(first, 16), :] = jnp.where(row == offset - first, new, old).astype(BF16)
        copies = [
            pltpu.make_async_copy(buffer.at[n], target.at[page_at], out_sems.at[n])
            for n, target in enumerate((key_ref, value_ref))
        ]
        for copy in copies:
            copy.start()
        for copy in copies:
            copy.wait()

    shape = jax.ShapeDtypeStruct(key_out.shape, key_out.dtype)
    return pl.pallas_call(
        kernel,
        out_shape=(jax.ShapeDtypeStruct((slots, width), F32), shape, shape),
        in_specs=[SMEM] + [VMEM] * (2 * chips + 2) + [ANY] * count + [HBM] * 2,
        out_specs=(VMEM, HBM, HBM),
        scratch_shapes=[
            pltpu.VMEM((2, page, width), BF16),
            pltpu.VMEM(packs[0].shape[1:], F32),
            pltpu.SemaphoreType.DMA,
            pltpu.SemaphoreType.DMA((2,)),
        ],
        input_output_aliases={2 * chips + 3 + count: 1, 2 * chips + 4 + count: 2},
        compiler_params=pltpu.CompilerParams(vmem_limit_bytes=4 * MIB),
        cost_estimate=cost(0, 8 * page * width),
        name="place_page",
    )(new_slot, *spread, *packs, tokens, out_bias, *candidates, key_out, value_out)


def body(
    tokens,
    norm_gain,
    norm_shift,
    qkv_weight,
    qkv_bias,
    out_weight,
    out_bias,
    key_pool,
    value_pool,
    lengths,
    page_table,
    new_slot,
    new_page,
):
    groups = lax.axis_size("req")
    head_groups = lax.axis_size("head")
    column_block = lax.axis_index("head")
    slots = tokens.shape[0]
    chips = groups // 2

    keep, send, mine = prepare(
        tokens, norm_gain[None], norm_shift[None], lengths, page_table, new_slot, new_page, key_pool, value_pool
    )
    got = swap(send, "req", 1)
    spread = [jnp.stack([keep[0], got[0]])] + [
        swap(jnp.stack([keep[d], got[d]]), "req", 2 * d) for d in range(1, chips)
    ]
    key_copy = copy_pool(key_pool, got)
    candidates = [mine] + [swap(mine, "req", 2 * d) for d in range(1, chips)]

    keep, send = project(spread, jnp.transpose(qkv_weight, (1, 0, 2)))
    got = swap(send, "req", 1)
    own, *messages = combine(keep, got)
    sums = [own] + [swap(messages[d - 1], "req", 2 * d) for d in range(1, chips)]
    value_copy = copy_pool(value_pool, own)

    pack_keep, pack_send, key_out, value_out = attend(
        lengths,
        new_slot,
        page_table,
        sums,
        qkv_bias.reshape(1, -1),
        tokens,
        key_pool,
        value_pool,
        key_copy,
        value_copy,
    )
    packs = spread_pairs(pack_keep, pack_send)

    from_other = swap(choose_page(spread, candidates), "req", 1)

    keep, send = out_project(
        column_block[None], packs, out_weight.reshape(-1, out_weight.shape[2]), head_groups, slots
    )
    base, key_out, value_out = place_page(
        new_slot, spread, packs, tokens, out_bias[None], candidates + [from_other], key_out, value_out
    )
    total = keep + swap(send, "req", 1).astype(F32)
    summed = total[0]
    for d in range(1, chips):
        summed = summed + swap(total[d].astype(BF16), "req", 2 * d).astype(F32)
    hidden = summed[0]
    for j in range(1, head_groups):
        hidden = hidden + swap(summed[j].astype(BF16), "head", j).astype(F32)
    hidden_out = (hidden + base).astype(BF16)
    return (hidden_out, key_out, value_out)


def solution(mesh):
    in_specs = (
        P("req", None),
        P(),
        P(),
        P("req", "head", None),
        P("head", None),
        P("head", "req", None),
        P(),
        P("req", None, "head"),
        P("req", None, "head"),
        P("req"),
        P("req", None),
        P("req"),
        P("req"),
    )
    out_specs = (P("req", "head"), P("req", None, "head"), P("req", None, "head"))
    return jax.shard_map(body, mesh=mesh, in_specs=in_specs, out_specs=out_specs, check_vma=False)
```

```python
import functools

import jax
import jax.numpy as jnp
from jax import lax
from jax.experimental import pallas as pl
from jax.experimental.pallas import tpu as pltpu
from jax.sharding import PartitionSpec as P

EPSILON = 1e-05
F32 = jnp.float32
BF16 = jnp.bfloat16
LANES = 128
META = 128
PACK = 256
VMEM = pl.BlockSpec(memory_space=pltpu.VMEM)
SMEM = pl.BlockSpec(memory_space=pltpu.SMEM)
ANY = pl.BlockSpec(memory_space=pl.ANY)
HBM = pl.BlockSpec(memory_space=pltpu.HBM)
MIB = 1024 * 1024


def cost(flops, moved):
    return pl.CostEstimate(flops=flops, bytes_accessed=moved, transcendentals=0)


def swap(value, axis, step):
    size = lax.axis_size(axis)
    return lax.ppermute(value, axis, [(i, i ^ step) for i in range(size)])


def spread_pairs(keep, send):
    got = swap(send, "req", 1)
    chips = keep.shape[0]
    return [jnp.stack([keep[0], got[0]])] + [
        swap(jnp.stack([keep[d], got[d]]), "req", 2 * d) for d in range(1, chips)
    ]


def in_hbm(*arrays):
    return [pltpu.with_memory_space_constraint(array, pltpu.HBM) for array in arrays]


def stage(arrays, after, name):
    count = len(arrays)
    parts = 4

    def kernel(*refs):
        sources, targets, sems = refs[:count], refs[count + 1 : 2 * count + 1], refs[-1]
        copies = []
        for n in range(count):
            step = -(-arrays[n].shape[0] // parts)
            for i, first in enumerate(range(0, arrays[n].shape[0], step)):
                place = pl.ds(first, min(step, arrays[n].shape[0] - first))
                copies.append(pltpu.make_async_copy(sources[n].at[place], targets[n].at[place], sems.at[n, i]))
        for copy in copies:
            copy.start()
        for copy in copies:
            copy.wait()

    size = sum(array.size * 2 for array in arrays)
    return pl.pallas_call(
        kernel,
        out_shape=tuple(jax.ShapeDtypeStruct(array.shape, array.dtype) for array in arrays),
        in_specs=[HBM] * count + [ANY],
        out_specs=(VMEM,) * count,
        scratch_shapes=[pltpu.SemaphoreType.DMA((count, parts))],
        compiler_params=pltpu.CompilerParams(vmem_limit_bytes=size + 2 * MIB),
        cost_estimate=cost(0, size),
        name=name,
    )(*in_hbm(*arrays), after)


def write_pools(lengths, new_slot, page_table, patches, key_pool, value_pool, after):
    pages, page, width = key_pool.shape
    slots, tall = patches.shape[1:3]
    parts = 4
    step = pages // parts

    def kernel(length_ref, slot_ref, table_ref, patch_ref, key_ref, value_ref, _, key_out, value_out, sems, patch_sems):
        leaving = leaving_slot(slot_ref, slots, lax.axis_index("req"))
        pairs = ((key_ref, key_out), (value_ref, value_out))
        copies = [
            pltpu.make_async_copy(source.at[pl.ds(i * step, step)], target.at[pl.ds(i * step, step)], sems.at[n, i])
            for n, (source, target) in enumerate(pairs)
            for i in range(parts)
        ]
        for copy in copies:
            copy.start()
        for copy in copies:
            copy.wait()

        def patch(n, s):
            length = length_ref[s]
            first = pl.multiple_of(length % page // tall * tall, tall)
            return pltpu.make_async_copy(
                patch_ref.at[n, s], pairs[n][1].at[table_ref[s, length // page], pl.ds(first, tall)], patch_sems.at[n, s]
            )

        for act in ("start", "wait"):
            for n in range(2):
                for s in range(slots):

                    @pl.when(leaving != s)
                    def _():
                        copy = patch(n, s)
                        copy.start() if act == "start" else copy.wait()

    shape = jax.ShapeDtypeStruct(key_pool.shape, key_pool.dtype)
    return pl.pallas_call(
        kernel,
        out_shape=(shape, shape),
        in_specs=[SMEM] * 3 + [VMEM] * 3 + [ANY],
        out_specs=(HBM, HBM),
        scratch_shapes=[pltpu.SemaphoreType.DMA((2, parts)), pltpu.SemaphoreType.DMA((2, slots))],
        compiler_params=pltpu.CompilerParams(vmem_limit_bytes=14 * MIB),
        cost_estimate=cost(0, 4 * key_pool.size),
        name="write_pools",
    )(lengths, new_slot, page_table, patches, key_pool, value_pool, after)


def leaving_slot(new_slot_ref, slots, here):
    leaving = jnp.int32(0)
    for s in range(slots):
        leaving = jnp.where(new_slot_ref[s] // slots != here, s, leaving)
    return leaving


def prepare(tokens, gain, shift, lengths, page_table, new_slot, new_page, key_pool, value_pool):
    groups = lax.axis_size("req")
    chips = groups // 2
    slots, model = tokens.shape
    depth = model // groups
    page, width = key_pool.shape[1:]

    def kernel(
        token_ref, gain_ref, shift_ref, length_ref, table_ref, slot_ref, page_ref, key_ref, value_ref,
        keep_ref, send_ref, out_ref, normed, sems,
    ):
        here = lax.axis_index("req")
        leaving = leaving_slot(slot_ref, slots, here)
        copies = [
            pltpu.make_async_copy(source.at[table_ref[leaving, 0]], out_ref.at[n], sems.at[n])
            for n, source in enumerate((key_ref, value_ref))
        ]
        for copy in copies:
            copy.start()
        values = token_ref[...].astype(F32)
        average = jnp.mean(values, axis=1, keepdims=True)
        centered = values - average
        variance = jnp.mean(centered * centered, axis=1, keepdims=True)
        rows = centered * lax.rsqrt(variance + EPSILON) * gain_ref[...] + shift_ref[...]
        normed[...] = rows.astype(BF16).astype(F32)
        row = lax.broadcasted_iota(jnp.int32, (slots, META), 0)
        lane = lax.broadcasted_iota(jnp.int32, (slots, META), 1)
        told = jnp.zeros((slots, META), F32)
        for s in range(slots):
            slot = slot_ref[s]
            numbers = (slot // slots, slot % slots, page_ref[s], length_ref[s] % page)
            for j, number in enumerate(numbers):
                told = jnp.where((row == s) & (lane == j), number.astype(F32), told)
        told = told.astype(BF16)
        for k in range(groups):
            first = (here ^ k) * depth
            if depth % LANES == 0:
                block = normed[:, pl.ds(pl.multiple_of(first, LANES), depth)]
            else:
                block = pltpu.roll(normed[...], lax.rem(model - first, model), 1)[:, :depth]
            target = (keep_ref, send_ref)[k % 2]
            target[k // 2, :, :META] = told
            target[k // 2, :, META:] = block.astype(BF16)
        for copy in copies:
            copy.wait()

    blocks = jax.ShapeDtypeStruct((chips, slots, META + depth), BF16)
    return pl.pallas_call(
        kernel,
        out_shape=(blocks, blocks, jax.ShapeDtypeStruct((2, page, width), key_pool.dtype)),
        in_specs=[VMEM] * 3 + [SMEM] * 4 + [HBM] * 2,
        out_specs=(VMEM, VMEM, VMEM),
        scratch_shapes=[pltpu.VMEM((slots, model), F32), pltpu.SemaphoreType.DMA((2,))],
        compiler_params=pltpu.CompilerParams(vmem_limit_bytes=4 * MIB),
        cost_estimate=cost(0, 8 * page * width),
        name="prepare",
    )(*in_hbm(tokens, gain, shift, lengths, page_table, new_slot, new_page, key_pool, value_pool))


def arrivals(block_refs, here, wanted):
    slots = block_refs[0].shape[1]
    lane = lax.broadcasted_iota(jnp.int32, (slots, META), 1)
    found = jnp.zeros((slots, META), F32)
    goal = (here ^ wanted).astype(F32)
    for d, ref in enumerate(block_refs):
        for e in range(2):
            k = 2 * d + e
            if k == wanted:
                continue
            told = ref[e, :, :META].astype(F32)
            numbered = jnp.where(lane == 4, float(k), told)
            found = jnp.where(told[:, :1] == goal, numbered, found)
    pick = lambda j: jnp.sum(jnp.where(lane == j, found, 0.0)).astype(jnp.int32)
    return pick(4), pick(2), pick(3)


def choose_page(spread, candidates):
    chips = len(spread)

    def kernel(*refs):
        block_refs, candidate_refs = refs[:chips], refs[chips : 2 * chips]
        out_ref, sem = refs[2 * chips :]
        source = arrivals(block_refs, lax.axis_index("req"), 1)[0]
        which = jnp.where(source % 2 == 0, source // 2, 0)
        for n, candidate in enumerate(candidate_refs):

            @pl.when(which == n)
            def _():
                copy = pltpu.make_async_copy(candidate, out_ref, sem)
                copy.start()
                copy.wait()

    one = candidates[0]
    return pl.pallas_call(
        kernel,
        out_shape=jax.ShapeDtypeStruct(one.shape, one.dtype),
        in_specs=[VMEM] * chips + [ANY] * chips,
        out_specs=VMEM,
        scratch_shapes=[pltpu.SemaphoreType.DMA],
        compiler_params=pltpu.CompilerParams(vmem_limit_bytes=2 * MIB),
        cost_estimate=cost(0, 4 * one.size),
        name="choose_page",
    )(*spread, *candidates)


def project(blocks, weight):
    chips = len(blocks)
    slots = blocks[0].shape[1]
    heads, depth, width = weight.shape
    per = 2 if heads % 2 == 0 else 1
    rows = chips * 2 * slots

    def kernel(*refs):
        block_refs = refs[:chips]
        weight_ref, keep_ref, send_ref, left = refs[chips:]
        for d in range(chips):
            for e in range(2):
                row = (d * 2 + e) * slots
                left[row : row + slots, :] = block_refs[d][e, :, META:].astype(F32)
        lhs = left[...].astype(BF16)

        @pl.loop(0, heads // per)
        def _(i):
            right = jnp.concatenate([weight_ref[i * per + j] for j in range(per)], axis=1)
            total = jnp.dot(lhs, right, preferred_element_type=F32)
            columns = pl.ds(pl.multiple_of(i * (per * width), per * width), per * width)
            for d in range(chips):
                row = d * 2 * slots
                keep_ref[d, :, columns] = total[row : row + slots]
                send_ref[d, :, columns] = total[row + slots : row + 2 * slots]

    shape = jax.ShapeDtypeStruct((chips, slots, heads * width), F32)
    return pl.pallas_call(
        kernel,
        out_shape=(shape, shape),
        in_specs=[VMEM] * (chips + 1),
        out_specs=(VMEM, VMEM),
        scratch_shapes=[pltpu.VMEM((rows, depth), F32)],
        compiler_params=pltpu.CompilerParams(vmem_limit_bytes=weight.size * 2 + 8 * MIB),
        cost_estimate=cost(2 * rows * weight.size, 2 * weight.size),
        name="project",
    )(*blocks, weight)


def combine(keep, got):
    chips, slots, width = keep.shape
    heads = width // (3 * LANES)

    def kernel(keep_ref, got_ref, own_ref, *message_refs):
        own_ref[...] = keep_ref[0] + got_ref[0]
        for d in range(1, chips):
            for h in range(heads):
                total = keep_ref[d, :, 3 * h * LANES : 3 * (h + 1) * LANES] + got_ref[d, :, 3 * h * LANES : 3 * (h + 1) * LANES]
                query = total[:, :LANES]
                high = query.astype(BF16)
                low = (query - high.astype(F32)).astype(BF16)
                base = 4 * h * LANES
                message_refs[d - 1][:, base : base + LANES] = high
                message_refs[d - 1][:, base + LANES : base + 2 * LANES] = low
                message_refs[d - 1][:, base + 2 * LANES : base + 4 * LANES] = total[:, LANES:].astype(BF16)

    message = jax.ShapeDtypeStruct((slots, 4 * heads * LANES), BF16)
    return pl.pallas_call(
        kernel,
        out_shape=(jax.ShapeDtypeStruct((slots, width), F32),) + (message,) * (chips - 1),
        in_specs=[VMEM, VMEM],
        out_specs=(VMEM,) * chips,
        compiler_params=pltpu.CompilerParams(vmem_limit_bytes=8 * MIB),
        cost_estimate=cost(0, 8 * keep.size),
        name="combine",
    )(keep, got)


def attend(lengths, new_slot, page_table, sums, bias, tokens, key_pool, value_pool):
    parts = len(sums)
    slots = sums[0].shape[0]
    pages, page, width = key_pool.shape
    head = LANES
    heads = width // head
    max_pages = page_table.shape[1]
    chunk_pages = 4
    chunk = chunk_pages * page
    chunks = max_pages // chunk_pages
    long_rows = max_pages * page
    short_rows = slots * page
    groups = 2 * parts
    share = head // groups
    per = LANES // share
    tall = 16
    strips = width // PACK
    scale = head ** (-0.5)

    def kernel(*refs):
        length_ref, slot_ref, table_ref = refs[:3]
        sum_refs = refs[3 : 3 + parts]
        (bias_ref, token_ref, key_ref, value_ref, pack_keep, pack_send, patch_ref, score_buffer, mix_buffer) = refs[
            3 + parts :
        ]
        here = lax.axis_index("req")
        column_block = lax.axis_index("head")
        leaving = leaving_slot(slot_ref, slots, here)
        lengths = [length_ref[s] for s in range(slots)]
        long_slot = jnp.int32(0)
        long_length = jnp.int32(0)
        for s in range(slots):
            is_long = lengths[s] >= page
            long_slot = jnp.where(is_long, s, long_slot)
            long_length = jnp.where(is_long, lengths[s], long_length)
        turns = (long_length + chunk - 1) // chunk

        total = sum_refs[0][...] + bias_ref[...]

        def third(k):
            columns = []
            for h in range(heads):
                one = total[:, (3 * h + k) * head : (3 * h + k + 1) * head]
                for ref in sum_refs[1:]:
                    base = 4 * h * head
                    if k == 0:
                        one = one + ref[:, base : base + head].astype(F32) + ref[:, base + head : base + 2 * head].astype(F32)
                    else:
                        one = one + ref[:, base + (k + 1) * head : base + (k + 2) * head].astype(F32)
                columns.append(one)
            return jnp.concatenate(columns, axis=1)

        query = (third(0) * scale).astype(BF16).astype(F32)
        new_rows = (third(1).astype(BF16).astype(F32), third(2).astype(BF16).astype(F32))

        lane_head = lax.broadcasted_iota(jnp.int32, (tall, width), 1) // head
        on_head = lane_head == lax.broadcasted_iota(jnp.int32, (tall, width), 0)

        def blocked(row):
            return jnp.where(on_head, jnp.broadcast_to(row, (tall, width)), 0.0).astype(BF16)

        def for_slot(which, rows):
            found = rows[0]
            for s in range(1, slots):
                found = jnp.where(which == s, rows[s], found)
            return found

        def softmax(scores, valid, new_score):
            masked = jnp.where(valid, scores, -1e30)
            peak = jnp.maximum(jnp.max(masked, axis=1, keepdims=True), new_score)
            weights = jnp.where(valid, jnp.exp(masked - peak), 0.0)
            new_weight = jnp.exp(new_score - peak)
            denom = jnp.sum(weights, axis=1, keepdims=True) + new_weight
            return weights.astype(BF16), new_weight.astype(BF16).astype(F32), denom

        across = (((1,), (1,)), ((), ()))
        short_query = jnp.concatenate([blocked(query[s : s + 1]) for s in range(slots)], axis=0)
        new_keys = jnp.concatenate([new_rows[0], jnp.zeros((tall - slots, width), F32)], axis=0).astype(BF16)
        new_scores = lax.dot_general(short_query, new_keys, across, preferred_element_type=F32)
        size = (slots * tall, tall)
        own_column = lax.broadcasted_iota(jnp.int32, size, 0) // tall == lax.broadcasted_iota(jnp.int32, size, 1)
        new_score = jnp.sum(jnp.where(own_column, new_scores, 0.0), axis=1, keepdims=True)

        first_pages = lambda ref: jnp.concatenate([ref[table_ref[s, 0]] for s in range(slots)], axis=0)
        short_scores = lax.dot_general(short_query, first_pages(key_ref), across, preferred_element_type=F32)
        size = (slots * tall, short_rows)
        row_slot = lax.broadcasted_iota(jnp.int32, size, 0) // tall
        column = lax.broadcasted_iota(jnp.int32, size, 1)
        limit = jnp.zeros(size, jnp.int32)
        for s in range(slots):
            limit = jnp.where(row_slot == s, lengths[s], limit)
        valid = (row_slot == column // page) & (column % page < limit)
        short_probs, new_prob, short_denom = softmax(short_scores, valid, new_score)
        new_values = jnp.concatenate(
            [jnp.broadcast_to(new_rows[1][s : s + 1], (tall, width)) for s in range(slots)], axis=0
        )
        short_mix = jnp.dot(short_probs, first_pages(value_ref), preferred_element_type=F32)
        short_mix = (short_mix + new_prob * new_values) / short_denom

        mix_buffer[...] = jnp.zeros(mix_buffer.shape, F32)

        @pl.when(turns > 0)
        def _():
            some_pages = lambda ref, c: jnp.concatenate(
                [ref[table_ref[long_slot, c * chunk_pages + i]] for i in range(chunk_pages)], axis=0
            )
            long_query = blocked(for_slot(long_slot, [query[s : s + 1] for s in range(slots)]))
            long_new = for_slot(long_slot, [new_score[s * tall : (s + 1) * tall] for s in range(slots)])
            long_value = for_slot(long_slot, [new_rows[1][s : s + 1] for s in range(slots)])
            for c in range(chunks):

                @pl.when(c < turns)
                def _():
                    score_buffer[:, c * chunk : (c + 1) * chunk] = lax.dot_general(
                        long_query, some_pages(key_ref, c), across, preferred_element_type=F32
                    )

                @pl.when(c >= turns)
                def _():
                    score_buffer[:, c * chunk : (c + 1) * chunk] = jnp.zeros((tall, chunk), F32)

            position = lax.broadcasted_iota(jnp.int32, (tall, long_rows), 1)
            long_probs, long_prob, long_denom = softmax(score_buffer[...], position < long_length, long_new)
            for c in range(chunks):

                @pl.when(c < turns)
                def _():
                    mix_buffer[...] += jnp.dot(
                        long_probs[:, c * chunk : (c + 1) * chunk], some_pages(value_ref, c), preferred_element_type=F32
                    )

            mix_buffer[...] = (mix_buffer[...] + long_prob * long_value) / long_denom

        def fold(mixed):
            return jnp.sum(jnp.where(on_head, mixed, 0.0), axis=0, keepdims=True)

        long_mix = fold(mix_buffer[...])
        rows = []
        for s in range(slots):
            row = fold(short_mix[s * tall : (s + 1) * tall])
            rows.append(jnp.where(lengths[s] >= page, long_mix, row))
        high = -(-slots // 8) * 8
        attended = jnp.concatenate(rows + [jnp.zeros((high - slots, width), F32)], axis=0).astype(BF16).astype(F32)

        token = token_ref[:, pl.ds(pl.multiple_of(column_block * width, LANES), width)].astype(F32)
        extra = []
        for source in new_rows + (token,):
            one = jnp.zeros((1, width), F32)
            for s in range(slots):
                one = jnp.where(leaving == s, source[s : s + 1], one)
            extra += [one[:, i * PACK : (i + 1) * PACK] for i in range(strips)]
        extra = jnp.concatenate(extra + [jnp.zeros((pack_rows(slots, strips) - high - 3 * strips, PACK), F32)], axis=0)

        row_at = lax.broadcasted_iota(jnp.int32, (high, LANES), 0)
        lane_at = lax.broadcasted_iota(jnp.int32, (high, LANES), 1)
        goal_device = jnp.full((high, LANES), -1.0, F32)
        goal_slot = jnp.zeros((high, LANES), F32)
        for s in range(slots):
            goal_device = jnp.where(row_at == s, (slot_ref[s] // slots).astype(F32), goal_device)
            goal_slot = jnp.where(row_at == s, (slot_ref[s] % slots).astype(F32), goal_slot)
        lane = lane_at // share
        for k in range(groups):
            wanted = here ^ k
            tiles = [jnp.zeros((high, LANES), F32) for _ in range(PACK // LANES)]
            for h in range(heads):
                place = h % per
                shift = lax.rem((place - wanted) * share + 2 * LANES, LANES)
                turned = pltpu.roll(attended[:, h * head : (h + 1) * head], shift, 1)
                tiles[h // per] = jnp.where(lane == place, turned, tiles[h // per])
            tiles[-1] = jnp.where(lane_at == LANES - 2, goal_device, jnp.where(lane_at == LANES - 1, goal_slot, tiles[-1]))
            block = jnp.concatenate([jnp.concatenate(tiles, axis=1), extra], axis=0).astype(BF16)
            (pack_keep, pack_send)[k % 2][k // 2] = block

        at = lax.broadcasted_iota(jnp.int32, (tall, width), 0)
        for n, ref in enumerate((key_ref, value_ref)):
            for s in range(slots):
                offset = lengths[s] % page
                first = pl.multiple_of(offset // tall * tall, tall)
                old = ref[table_ref[s, lengths[s] // page], pl.ds(first, tall), :].astype(F32)
                new = jnp.broadcast_to(new_rows[n][s : s + 1], (tall, width))
                patch_ref[n, s] = jnp.where(at == offset - first, new, old).astype(BF16)

    packed = jax.ShapeDtypeStruct((parts, pack_rows(slots, strips), PACK), BF16)
    return pl.pallas_call(
        kernel,
        out_shape=(packed, packed, jax.ShapeDtypeStruct((2, slots, tall, width), BF16)),
        in_specs=[SMEM] * 3 + [VMEM] * (parts + 4),
        out_specs=(VMEM, VMEM, VMEM),
        scratch_shapes=[pltpu.VMEM((tall, long_rows), F32), pltpu.VMEM((tall, width), F32)],
        compiler_params=pltpu.CompilerParams(vmem_limit_bytes=18 * MIB),
        cost_estimate=cost(4 * tall * (long_rows + short_rows) * width, 4 * (long_rows + short_rows) * width),
        name="attend",
    )(lengths, new_slot, page_table, *sums, bias, tokens, key_pool, value_pool)


def pack_rows(slots, strips):
    need = -(-slots // 8) * 8 + 3 * strips
    return -(-need // 16) * 16


def out_project(column_block, blocks, weight, pieces, slots):
    chips = len(blocks)
    depth, width = weight.shape
    high = -(-slots // 8) * 8
    rows = 2 * chips * slots
    piece = width // pieces

    def kernel(column_ref, *refs):
        block_refs = refs[:chips]
        weight_ref, keep_ref, send_ref, left = refs[chips:]

        @pl.when(pl.program_id(0) == 0)
        def _():
            gathered = jnp.concatenate(
                [block_refs[d][e, :high, :].astype(F32) for d in range(chips) for e in range(2)], axis=0
            )
            goal = gathered[:, PACK - 2 : PACK - 1].astype(jnp.int32)
            place = goal ^ lax.axis_index("req")
            row = (place % 2) * (chips * slots) + (place // 2) * slots + gathered[:, PACK - 1 :].astype(jnp.int32)
            row = jnp.where(goal < 0, -1, row)
            size = (gathered.shape[0], rows)
            order = jnp.where(lax.broadcasted_iota(jnp.int32, size, 1) == row, 1.0, 0.0)
            left[...] = lax.dot_general(
                order.astype(BF16), gathered.astype(BF16), (((0,), (0,)), ((), ())), preferred_element_type=F32
            )

        total = jnp.dot(left[:, :depth].astype(BF16), weight_ref[...], preferred_element_type=F32)
        for d in range(chips):
            keep_ref[d, 0] = total[d * slots : (d + 1) * slots]
            send_ref[d, 0] = total[(chips + d) * slots : (chips + d + 1) * slots].astype(BF16)

    shape = (chips, pieces, slots, piece)
    out_spec = pl.BlockSpec((chips, 1, slots, piece), lambda j, c: (0, j, 0, 0))
    whole = lambda shape: pl.BlockSpec(shape, lambda j, c: (0,) * len(shape))
    return pl.pallas_call(
        kernel,
        out_shape=(jax.ShapeDtypeStruct(shape, F32), jax.ShapeDtypeStruct(shape, BF16)),
        grid_spec=pltpu.PrefetchScalarGridSpec(
            num_scalar_prefetch=1,
            grid=(pieces,),
            in_specs=[whole(block.shape) for block in blocks]
            + [pl.BlockSpec((depth, piece), lambda j, c: (0, j ^ c[0]))],
            out_specs=(out_spec, out_spec),
            scratch_shapes=[pltpu.VMEM((rows, PACK), F32)],
        ),
        compiler_params=pltpu.CompilerParams(vmem_limit_bytes=8 * MIB),
        cost_estimate=cost(2 * rows * weight.size, 2 * weight.size),
        name="out_project",
    )(column_block, *blocks, weight)


def place_page(new_slot, spread, packs, tokens, out_bias, candidates, key_out, value_out):
    chips = len(spread)
    count = len(candidates)
    page, width = key_out.shape[1:]
    slots = tokens.shape[0]
    high = -(-slots // 8) * 8
    strips = width // PACK

    def kernel(slot_ref, *refs):
        block_refs, pack_refs = refs[:chips], refs[chips : 2 * chips]
        token_ref, bias_ref = refs[2 * chips : 2 * chips + 2]
        candidate_refs = refs[2 * chips + 2 : 2 * chips + 2 + count]
        _, _, base_ref, key_ref, value_ref, buffer, arrived, sem, out_sems = refs[2 * chips + 2 + count :]
        here = lax.axis_index("req")
        column = pl.multiple_of(lax.axis_index("head") * width, LANES)
        source, page_at, offset = arrivals(block_refs, here, 0)
        which = jnp.where(source % 2 == 0, source // 2, chips)
        for n in range(count):

            @pl.when(which == n)
            def _():
                copy = pltpu.make_async_copy(candidate_refs[n], buffer, sem)
                copy.start()

        for d in range(chips):
            for e in range(2):

                @pl.when(source == 2 * d + e)
                def _():
                    arrived[...] = pack_refs[d][e].astype(F32)

        def fresh(n):
            strip = high + n * strips
            return jnp.concatenate([arrived[strip + i : strip + i + 1, :] for i in range(strips)], axis=1)

        at = lax.broadcasted_iota(jnp.int32, (slots, width), 0)
        token = jnp.where(
            at == leaving_slot(slot_ref, slots, here),
            jnp.broadcast_to(fresh(2), (slots, width)),
            token_ref[:, pl.ds(column, width)].astype(F32),
        )
        base_ref[...] = token + bias_ref[:, pl.ds(column, width)]
        pltpu.make_async_copy(candidate_refs[0], buffer, sem).wait()
        first = pl.multiple_of(offset // 16 * 16, 16)
        row = lax.broadcasted_iota(jnp.int32, (16, width), 0)
        for n in range(2):
            old = buffer[n, pl.ds(first, 16), :].astype(F32)
            new = jnp.broadcast_to(fresh(n), (16, width))
            buffer[n, pl.ds(first, 16), :] = jnp.where(row == offset - first, new, old).astype(BF16)
        copies = [
            pltpu.make_async_copy(buffer.at[n], target.at[page_at], out_sems.at[n])
            for n, target in enumerate((key_ref, value_ref))
        ]
        for copy in copies:
            copy.start()
        for copy in copies:
            copy.wait()

    shape = jax.ShapeDtypeStruct(key_out.shape, key_out.dtype)
    return pl.pallas_call(
        kernel,
        out_shape=(jax.ShapeDtypeStruct((slots, width), F32), shape, shape),
        in_specs=[SMEM] + [VMEM] * (2 * chips + 2) + [ANY] * count + [HBM] * 2,
        out_specs=(VMEM, HBM, HBM),
        scratch_shapes=[
            pltpu.VMEM((2, page, width), BF16),
            pltpu.VMEM(packs[0].shape[1:], F32),
            pltpu.SemaphoreType.DMA,
            pltpu.SemaphoreType.DMA((2,)),
        ],
        input_output_aliases={2 * chips + 3 + count: 1, 2 * chips + 4 + count: 2},
        compiler_params=pltpu.CompilerParams(vmem_limit_bytes=4 * MIB),
        cost_estimate=cost(0, 8 * page * width),
        name="place_page",
    )(new_slot, *spread, *packs, tokens, out_bias, *candidates, key_out, value_out)


def body(
    tokens,
    norm_gain,
    norm_shift,
    qkv_weight,
    qkv_bias,
    out_weight,
    out_bias,
    key_pool,
    value_pool,
    lengths,
    page_table,
    new_slot,
    new_page,
):
    groups = lax.axis_size("req")
    head_groups = lax.axis_size("head")
    column_block = lax.axis_index("head")
    slots = tokens.shape[0]
    chips = groups // 2

    keep, send, mine = prepare(
        tokens, norm_gain[None], norm_shift[None], lengths, page_table, new_slot, new_page, key_pool, value_pool
    )
    got = swap(send, "req", 1)
    spread = [jnp.stack([keep[0], got[0]])] + [
        swap(jnp.stack([keep[d], got[d]]), "req", 2 * d) for d in range(1, chips)
    ]
    (weight,) = stage([jnp.transpose(qkv_weight, (1, 0, 2))], got, "stage_weight")
    candidates = [mine] + [swap(mine, "req", 2 * d) for d in range(1, chips)]

    keep, send = project(spread, weight)
    got = swap(send, "req", 1)
    own, *messages = combine(keep, got)
    sums = [own] + [swap(messages[d - 1], "req", 2 * d) for d in range(1, chips)]
    keys, values = stage([key_pool, value_pool], own, "stage_pools")

    pack_keep, pack_send, patches = attend(
        lengths,
        new_slot,
        page_table,
        sums,
        qkv_bias.reshape(1, -1),
        tokens,
        keys,
        values,
    )
    packs = spread_pairs(pack_keep, pack_send)

    from_other = swap(choose_page(spread, candidates), "req", 1)

    keep, send = out_project(
        column_block[None], packs, out_weight.reshape(-1, out_weight.shape[2]), head_groups, slots
    )
    total = keep + swap(send, "req", 1).astype(F32)
    key_out, value_out = write_pools(lengths, new_slot, page_table, patches, keys, values, total)
    base, key_out, value_out = place_page(
        new_slot, spread, packs, tokens, out_bias[None], candidates + [from_other], key_out, value_out
    )
    summed = total[0]
    for d in range(1, chips):
        summed = summed + swap(total[d].astype(BF16), "req", 2 * d).astype(F32)
    hidden = summed[0]
    for j in range(1, head_groups):
        hidden = hidden + swap(summed[j].astype(BF16), "head", j).astype(F32)
    hidden_out = (hidden + base).astype(BF16)
    return (hidden_out, key_out, value_out)


def solution(mesh):
    in_specs = (
        P("req", None),
        P(),
        P(),
        P("req", "head", None),
        P("head", None),
        P("head", "req", None),
        P(),
        P("req", None, "head"),
        P("req", None, "head"),
        P("req"),
        P("req", None),
        P("req"),
        P("req"),
    )
    out_specs = (P("req", "head"), P("req", None, "head"), P("req", None, "head"))
    return jax.shard_map(body, mesh=mesh, in_specs=in_specs, out_specs=out_specs, check_vma=False)
```

```python
import functools

import jax
import jax.numpy as jnp
from jax import lax
from jax.experimental import pallas as pl
from jax.experimental.pallas import tpu as pltpu
from jax.sharding import PartitionSpec as P

EPSILON = 1e-05
F32 = jnp.float32
BF16 = jnp.bfloat16
LANES = 128
META = 128
PACK = 256
VMEM = pl.BlockSpec(memory_space=pltpu.VMEM)
SMEM = pl.BlockSpec(memory_space=pltpu.SMEM)
ANY = pl.BlockSpec(memory_space=pl.ANY)
HBM = pl.BlockSpec(memory_space=pltpu.HBM)
MIB = 1024 * 1024


def cost(flops, moved):
    del flops, moved
    return pl.CostEstimate(flops=0, bytes_accessed=0, transcendentals=0)


def swap(value, axis, step):
    size = lax.axis_size(axis)
    return lax.ppermute(value, axis, [(i, i ^ step) for i in range(size)])


def spread_pairs(keep, got):
    chips = keep.shape[0]
    return [jnp.stack([keep[0], got[0]])] + [
        swap(jnp.stack([keep[d], got[d]]), "req", 2 * d) for d in range(1, chips)
    ]


def in_hbm(*arrays):
    return [pltpu.with_memory_space_constraint(array, pltpu.HBM) for array in arrays]


def stage(arrays, after, name):
    count = len(arrays)
    parts = 4

    def kernel(*refs):
        sources, targets, sems = refs[:count], refs[count + 1 : 2 * count + 1], refs[-1]
        copies = []
        for n in range(count):
            step = -(-arrays[n].shape[0] // parts)
            for i, first in enumerate(range(0, arrays[n].shape[0], step)):
                place = pl.ds(first, min(step, arrays[n].shape[0] - first))
                copies.append(pltpu.make_async_copy(sources[n].at[place], targets[n].at[place], sems.at[n, i]))
        for copy in copies:
            copy.start()
        for copy in copies:
            copy.wait()

    size = sum(array.size * 2 for array in arrays)
    return pl.pallas_call(
        kernel,
        out_shape=tuple(jax.ShapeDtypeStruct(array.shape, array.dtype) for array in arrays),
        in_specs=[HBM] * count + [ANY],
        out_specs=(VMEM,) * count,
        scratch_shapes=[pltpu.SemaphoreType.DMA((count, parts))],
        compiler_params=pltpu.CompilerParams(vmem_limit_bytes=size + 2 * MIB),
        cost_estimate=cost(0, size),
        name=name,
    )(*in_hbm(*arrays), after)


def write_pool(lengths, new_slot, page_table, patches, pool, after, part):
    pages, page, width = pool.shape
    slots, tall = patches.shape[1:3]
    parts = 4
    step = pages // parts

    def kernel(length_ref, slot_ref, table_ref, patch_ref, pool_ref, _, out_ref, sems, patch_sems):
        leaving = leaving_slot(slot_ref, slots, lax.axis_index("req"))
        places = [pl.ds(i * step, step) for i in range(parts)]
        copies = [
            pltpu.make_async_copy(pool_ref.at[place], out_ref.at[place], sems.at[i]) for i, place in enumerate(places)
        ]
        for copy in copies:
            copy.start()
        for copy in copies:
            copy.wait()

        def patch(s):
            length = length_ref[s]
            first = pl.multiple_of(length % page // tall * tall, tall)
            return pltpu.make_async_copy(
                patch_ref.at[part, s], out_ref.at[table_ref[s, length // page], pl.ds(first, tall)], patch_sems.at[s]
            )

        for act in ("start", "wait"):
            for s in range(slots):

                @pl.when(leaving != s)
                def _():
                    copy = patch(s)
                    copy.start() if act == "start" else copy.wait()

    return pl.pallas_call(
        kernel,
        out_shape=jax.ShapeDtypeStruct(pool.shape, pool.dtype),
        in_specs=[SMEM] * 3 + [VMEM] * 2 + [ANY],
        out_specs=HBM,
        scratch_shapes=[pltpu.SemaphoreType.DMA((parts,)), pltpu.SemaphoreType.DMA((slots,))],
        compiler_params=pltpu.CompilerParams(vmem_limit_bytes=8 * MIB),
        cost_estimate=cost(0, 2 * pool.size),
        name="write_pool",
    )(lengths, new_slot, page_table, patches, pool, after)


def leaving_slot(new_slot_ref, slots, here):
    leaving = jnp.int32(0)
    for s in range(slots):
        leaving = jnp.where(new_slot_ref[s] // slots != here, s, leaving)
    return leaving


def prepare(tokens, gain, shift, lengths, page_table, new_slot, new_page, key_pool, value_pool):
    groups = lax.axis_size("req")
    chips = groups // 2
    slots, model = tokens.shape
    depth = model // groups
    page, width = key_pool.shape[1:]
    half = page // 2

    def kernel(
        token_ref, gain_ref, shift_ref, length_ref, table_ref, slot_ref, page_ref, key_ref, value_ref,
        keep_ref, send_ref, keep_half, send_half, normed, sems,
    ):
        here = lax.axis_index("req")
        leaving = leaving_slot(slot_ref, slots, here)
        copies = []
        for n, source in enumerate((key_ref, value_ref)):
            for e, target in enumerate((keep_half, send_half)):
                rows = pl.ds(pl.multiple_of((here % 2 ^ e) * half, half), half)
                copies.append(
                    pltpu.make_async_copy(source.at[table_ref[leaving, 0], rows], target.at[n], sems.at[n, e])
                )
        for copy in copies:
            copy.start()
        values = token_ref[...].astype(F32)
        average = jnp.mean(values, axis=1, keepdims=True)
        centered = values - average
        variance = jnp.mean(centered * centered, axis=1, keepdims=True)
        rows = centered * lax.rsqrt(variance + EPSILON) * gain_ref[...] + shift_ref[...]
        normed[...] = rows.astype(BF16).astype(F32)
        row = lax.broadcasted_iota(jnp.int32, (slots, META), 0)
        lane = lax.broadcasted_iota(jnp.int32, (slots, META), 1)
        told = jnp.zeros((slots, META), F32)
        for s in range(slots):
            slot = slot_ref[s]
            numbers = (slot // slots, slot % slots, page_ref[s], length_ref[s] % page)
            for j, number in enumerate(numbers):
                told = jnp.where((row == s) & (lane == j), number.astype(F32), told)
        told = told.astype(BF16)
        for k in range(groups):
            first = (here ^ k) * depth
            if depth % LANES == 0:
                block = normed[:, pl.ds(pl.multiple_of(first, LANES), depth)]
            else:
                block = pltpu.roll(normed[...], lax.rem(model - first, model), 1)[:, :depth]
            target = (keep_ref, send_ref)[k % 2]
            target[k // 2, :, :META] = told
            target[k // 2, :, META:] = block.astype(BF16)
        for copy in copies:
            copy.wait()

    blocks = jax.ShapeDtypeStruct((chips, slots, META + depth), BF16)
    halves = jax.ShapeDtypeStruct((2, half, width), key_pool.dtype)
    return pl.pallas_call(
        kernel,
        out_shape=(blocks, blocks, halves, halves),
        in_specs=[VMEM] * 3 + [SMEM] * 4 + [HBM] * 2,
        out_specs=(VMEM,) * 4,
        scratch_shapes=[pltpu.VMEM((slots, model), F32), pltpu.SemaphoreType.DMA((2, 2))],
        compiler_params=pltpu.CompilerParams(vmem_limit_bytes=4 * MIB),
        cost_estimate=cost(0, 8 * page * width),
        name="prepare",
    )(*in_hbm(tokens, gain, shift, lengths, page_table, new_slot, new_page, key_pool, value_pool))


def arrivals(block_refs, here, wanted):
    slots = block_refs[0].shape[1]
    lane = lax.broadcasted_iota(jnp.int32, (slots, META), 1)
    found = jnp.zeros((slots, META), F32)
    goal = (here ^ wanted).astype(F32)
    for d, ref in enumerate(block_refs):
        for e in range(2):
            k = 2 * d + e
            if k == wanted:
                continue
            told = ref[e, :, :META].astype(F32)
            numbered = jnp.where(lane == 4, float(k), told)
            found = jnp.where(told[:, :1] == goal, numbered, found)
    return lambda j: jnp.sum(jnp.where(lane == j, found, 0.0)).astype(jnp.int32)


def row_length(chips):
    return 1 << (chips.bit_length() // 2)


def turn_pages(spread, halves):
    chips = len(spread)
    across = row_length(chips)
    down = chips // across
    shape = halves[0].shape

    def kernel(*refs):
        block_refs, half_refs = refs[:chips], refs[chips : chips + across]
        out_refs, sems = refs[chips + across : -1], refs[-1]
        here = lax.axis_index("req")
        waits = []
        for row in range(1, down):
            for j in range(2):
                source = arrivals(block_refs, here, 2 * across * row + j)(4)
                place = jnp.where(source < 2 * across, source, 0)
                for d in range(across):
                    for e in range(2):
                        copy = pltpu.make_async_copy(half_refs[d].at[e], out_refs[row - 1].at[j], sems.at[row - 1, j])

                        @pl.when(place == 2 * d + e)
                        def _():
                            copy.start()

                waits.append(copy)
        for copy in waits:
            copy.wait()

    one = jax.ShapeDtypeStruct(shape, halves[0].dtype)
    return pl.pallas_call(
        kernel,
        out_shape=(one,) * (down - 1),
        in_specs=[VMEM] * chips + [ANY] * across,
        out_specs=(VMEM,) * (down - 1),
        scratch_shapes=[pltpu.SemaphoreType.DMA((down - 1, 2))],
        compiler_params=pltpu.CompilerParams(vmem_limit_bytes=down * 2 * MIB),
        cost_estimate=cost(0, 4 * halves[0].size),
        name="turn_pages",
    )(*spread, *halves)


def start_half(source, across, core, half_refs, turned_refs, target, sem):
    place = jnp.where(source < 2 * across, source, 2 * across + source // (2 * across))
    for d, ref in enumerate(half_refs):
        for e in range(2):

            @pl.when(place == 2 * d + e)
            def _():
                pltpu.make_async_copy(ref.at[e], target, sem).start()

    for row, ref in enumerate(turned_refs):

        @pl.when(place == 2 * across + row + 1)
        def _():
            pltpu.make_async_copy(ref.at[core], target, sem).start()


def choose_half(spread, halves, turned):
    chips, across, rows = len(spread), len(halves), len(turned)

    def kernel(*refs):
        block_refs, half_refs = refs[:chips], refs[chips : chips + across]
        turned_refs = refs[chips + across : chips + across + rows]
        out_ref, sem = refs[chips + across + rows :]
        source = arrivals(block_refs, lax.axis_index("req"), 1)(4)
        start_half(source, across, 1, half_refs, turned_refs, out_ref, sem)
        pltpu.make_async_copy(half_refs[0].at[0], out_ref, sem).wait()

    shape = halves[0].shape[1:]
    return pl.pallas_call(
        kernel,
        out_shape=jax.ShapeDtypeStruct(shape, halves[0].dtype),
        in_specs=[VMEM] * chips + [ANY] * (across + rows),
        out_specs=VMEM,
        scratch_shapes=[pltpu.SemaphoreType.DMA],
        compiler_params=pltpu.CompilerParams(vmem_limit_bytes=2 * MIB),
        cost_estimate=cost(0, 2 * halves[0].size),
        name="choose_half",
    )(*spread, *halves, *turned)


def project(blocks, weight):
    chips = len(blocks)
    slots = blocks[0].shape[1]
    heads, depth, width = weight.shape
    per = 2 if heads % 2 == 0 else 1
    rows = chips * 2 * slots

    def kernel(*refs):
        block_refs = refs[:chips]
        weight_ref, keep_ref, send_ref, left = refs[chips:]
        for d in range(chips):
            for e in range(2):
                row = (d * 2 + e) * slots
                left[row : row + slots, :] = block_refs[d][e, :, META:].astype(F32)
        lhs = left[...].astype(BF16)

        @pl.loop(0, heads // per)
        def _(i):
            right = jnp.concatenate([weight_ref[i * per + j] for j in range(per)], axis=1)
            total = jnp.dot(lhs, right, preferred_element_type=F32)
            columns = pl.ds(pl.multiple_of(i * (per * width), per * width), per * width)
            for d in range(chips):
                row = d * 2 * slots
                keep_ref[d, :, columns] = total[row : row + slots]
                send_ref[d, :, columns] = total[row + slots : row + 2 * slots]

    shape = jax.ShapeDtypeStruct((chips, slots, heads * width), F32)
    return pl.pallas_call(
        kernel,
        out_shape=(shape, shape),
        in_specs=[VMEM] * (chips + 1),
        out_specs=(VMEM, VMEM),
        scratch_shapes=[pltpu.VMEM((rows, depth), F32)],
        compiler_params=pltpu.CompilerParams(vmem_limit_bytes=weight.size * 2 + 8 * MIB),
        cost_estimate=cost(2 * rows * weight.size, 2 * weight.size),
        name="project",
    )(*blocks, weight)


def combine(keep, got):
    chips, slots, width = keep.shape
    heads = width // (3 * LANES)

    def kernel(keep_ref, got_ref, own_ref, *message_refs):
        own_ref[...] = keep_ref[0] + got_ref[0]
        for d in range(1, chips):
            for h in range(heads):
                total = keep_ref[d, :, 3 * h * LANES : 3 * (h + 1) * LANES] + got_ref[d, :, 3 * h * LANES : 3 * (h + 1) * LANES]
                query = total[:, :LANES]
                high = query.astype(BF16)
                low = (query - high.astype(F32)).astype(BF16)
                base = 4 * h * LANES
                message_refs[d - 1][:, base : base + LANES] = high
                message_refs[d - 1][:, base + LANES : base + 2 * LANES] = low
                message_refs[d - 1][:, base + 2 * LANES : base + 4 * LANES] = total[:, LANES:].astype(BF16)

    message = jax.ShapeDtypeStruct((slots, 4 * heads * LANES), BF16)
    return pl.pallas_call(
        kernel,
        out_shape=(jax.ShapeDtypeStruct((slots, width), F32),) + (message,) * (chips - 1),
        in_specs=[VMEM, VMEM],
        out_specs=(VMEM,) * chips,
        compiler_params=pltpu.CompilerParams(vmem_limit_bytes=8 * MIB),
        cost_estimate=cost(0, 8 * keep.size),
        name="combine",
    )(keep, got)


def attend(lengths, new_slot, page_table, sums, bias, tokens, key_pool, value_pool, after):
    parts = len(sums)
    slots = sums[0].shape[0]
    pages, page, width = key_pool.shape
    head = LANES
    heads = width // head
    max_pages = page_table.shape[1]
    chunk_pages = 4
    chunk = chunk_pages * page
    chunks = max_pages // chunk_pages
    long_rows = max_pages * page
    short_rows = slots * page
    groups = 2 * parts
    share = head // groups
    per = LANES // share
    tall = 16
    strips = width // PACK
    scale = head ** (-0.5)

    def kernel(*refs):
        length_ref, slot_ref, table_ref = refs[:3]
        sum_refs = refs[3 : 3 + parts]
        (bias_ref, token_ref, key_ref, value_ref, _, pack_keep, pack_send, patch_ref, score_buffer, mix_buffer) = refs[
            3 + parts :
        ]
        here = lax.axis_index("req")
        column_block = lax.axis_index("head")
        leaving = leaving_slot(slot_ref, slots, here)
        lengths = [length_ref[s] for s in range(slots)]
        long_slot = jnp.int32(0)
        long_length = jnp.int32(0)
        for s in range(slots):
            is_long = lengths[s] >= page
            long_slot = jnp.where(is_long, s, long_slot)
            long_length = jnp.where(is_long, lengths[s], long_length)
        turns = (long_length + chunk - 1) // chunk

        total = sum_refs[0][...] + bias_ref[...]

        def third(k):
            columns = []
            for h in range(heads):
                one = total[:, (3 * h + k) * head : (3 * h + k + 1) * head]
                for ref in sum_refs[1:]:
                    base = 4 * h * head
                    if k == 0:
                        one = one + ref[:, base : base + head].astype(F32) + ref[:, base + head : base + 2 * head].astype(F32)
                    else:
                        one = one + ref[:, base + (k + 1) * head : base + (k + 2) * head].astype(F32)
                columns.append(one)
            return jnp.concatenate(columns, axis=1)

        query = (third(0) * scale).astype(BF16).astype(F32)
        new_rows = (third(1).astype(BF16).astype(F32), third(2).astype(BF16).astype(F32))

        lane_head = lax.broadcasted_iota(jnp.int32, (tall, width), 1) // head
        on_head = lane_head == lax.broadcasted_iota(jnp.int32, (tall, width), 0)

        def blocked(row):
            return jnp.where(on_head, jnp.broadcast_to(row, (tall, width)), 0.0).astype(BF16)

        def for_slot(which, rows):
            found = rows[0]
            for s in range(1, slots):
                found = jnp.where(which == s, rows[s], found)
            return found

        def softmax(scores, valid, new_score):
            masked = jnp.where(valid, scores, -1e30)
            peak = jnp.maximum(jnp.max(masked, axis=1, keepdims=True), new_score)
            weights = jnp.where(valid, jnp.exp(masked - peak), 0.0)
            new_weight = jnp.exp(new_score - peak)
            denom = jnp.sum(weights, axis=1, keepdims=True) + new_weight
            return weights.astype(BF16), new_weight.astype(BF16).astype(F32), denom

        across = (((1,), (1,)), ((), ()))
        short_query = jnp.concatenate([blocked(query[s : s + 1]) for s in range(slots)], axis=0)
        new_keys = jnp.concatenate([new_rows[0], jnp.zeros((tall - slots, width), F32)], axis=0).astype(BF16)
        new_scores = lax.dot_general(short_query, new_keys, across, preferred_element_type=F32)
        size = (slots * tall, tall)
        own_column = lax.broadcasted_iota(jnp.int32, size, 0) // tall == lax.broadcasted_iota(jnp.int32, size, 1)
        new_score = jnp.sum(jnp.where(own_column, new_scores, 0.0), axis=1, keepdims=True)

        first_pages = lambda ref: jnp.concatenate([ref[table_ref[s, 0]] for s in range(slots)], axis=0)
        short_scores = lax.dot_general(short_query, first_pages(key_ref), across, preferred_element_type=F32)
        size = (slots * tall, short_rows)
        row_slot = lax.broadcasted_iota(jnp.int32, size, 0) // tall
        column = lax.broadcasted_iota(jnp.int32, size, 1)
        limit = jnp.zeros(size, jnp.int32)
        for s in range(slots):
            limit = jnp.where(row_slot == s, lengths[s], limit)
        valid = (row_slot == column // page) & (column % page < limit)
        short_probs, new_prob, short_denom = softmax(short_scores, valid, new_score)
        new_values = jnp.concatenate(
            [jnp.broadcast_to(new_rows[1][s : s + 1], (tall, width)) for s in range(slots)], axis=0
        )
        short_mix = jnp.dot(short_probs, first_pages(value_ref), preferred_element_type=F32)
        short_mix = (short_mix + new_prob * new_values) / short_denom

        mix_buffer[...] = jnp.zeros(mix_buffer.shape, F32)

        @pl.when(turns > 0)
        def _():
            some_pages = lambda ref, c: jnp.concatenate(
                [ref[table_ref[long_slot, c * chunk_pages + i]] for i in range(chunk_pages)], axis=0
            )
            long_query = blocked(for_slot(long_slot, [query[s : s + 1] for s in range(slots)]))
            long_new = for_slot(long_slot, [new_score[s * tall : (s + 1) * tall] for s in range(slots)])
            long_value = for_slot(long_slot, [new_rows[1][s : s + 1] for s in range(slots)])
            for c in range(chunks):

                @pl.when(c < turns)
                def _():
                    score_buffer[:, c * chunk : (c + 1) * chunk] = lax.dot_general(
                        long_query, some_pages(key_ref, c), across, preferred_element_type=F32
                    )

                @pl.when(c >= turns)
                def _():
                    score_buffer[:, c * chunk : (c + 1) * chunk] = jnp.zeros((tall, chunk), F32)

            position = lax.broadcasted_iota(jnp.int32, (tall, long_rows), 1)
            long_probs, long_prob, long_denom = softmax(score_buffer[...], position < long_length, long_new)
            for c in range(chunks):

                @pl.when(c < turns)
                def _():
                    mix_buffer[...] += jnp.dot(
                        long_probs[:, c * chunk : (c + 1) * chunk], some_pages(value_ref, c), preferred_element_type=F32
                    )

            mix_buffer[...] = (mix_buffer[...] + long_prob * long_value) / long_denom

        def fold(mixed):
            return jnp.sum(jnp.where(on_head, mixed, 0.0), axis=0, keepdims=True)

        long_mix = fold(mix_buffer[...])
        rows = []
        for s in range(slots):
            row = fold(short_mix[s * tall : (s + 1) * tall])
            rows.append(jnp.where(lengths[s] >= page, long_mix, row))
        high = -(-slots // 8) * 8
        attended = jnp.concatenate(rows + [jnp.zeros((high - slots, width), F32)], axis=0).astype(BF16).astype(F32)

        token = token_ref[:, pl.ds(pl.multiple_of(column_block * width, LANES), width)].astype(F32)
        extra = []
        for source in new_rows + (token,):
            one = jnp.zeros((1, width), F32)
            for s in range(slots):
                one = jnp.where(leaving == s, source[s : s + 1], one)
            extra += [one[:, i * PACK : (i + 1) * PACK] for i in range(strips)]
        extra = jnp.concatenate(extra + [jnp.zeros((pack_rows(slots, strips) - high - 3 * strips, PACK), F32)], axis=0)

        row_at = lax.broadcasted_iota(jnp.int32, (high, LANES), 0)
        lane_at = lax.broadcasted_iota(jnp.int32, (high, LANES), 1)
        goal_device = jnp.full((high, LANES), -1.0, F32)
        goal_slot = jnp.zeros((high, LANES), F32)
        for s in range(slots):
            goal_device = jnp.where(row_at == s, (slot_ref[s] // slots).astype(F32), goal_device)
            goal_slot = jnp.where(row_at == s, (slot_ref[s] % slots).astype(F32), goal_slot)
        lane = lane_at // share
        for k in range(groups):
            wanted = here ^ k
            tiles = [jnp.zeros((high, LANES), F32) for _ in range(PACK // LANES)]
            for h in range(heads):
                place = h % per
                shift = lax.rem((place - wanted) * share + 2 * LANES, LANES)
                turned = pltpu.roll(attended[:, h * head : (h + 1) * head], shift, 1)
                tiles[h // per] = jnp.where(lane == place, turned, tiles[h // per])
            tiles[-1] = jnp.where(lane_at == LANES - 2, goal_device, jnp.where(lane_at == LANES - 1, goal_slot, tiles[-1]))
            block = jnp.concatenate([jnp.concatenate(tiles, axis=1), extra], axis=0).astype(BF16)
            (pack_keep, pack_send)[k % 2][k // 2] = block

        at = lax.broadcasted_iota(jnp.int32, (tall, width), 0)
        for n, ref in enumerate((key_ref, value_ref)):
            for s in range(slots):
                offset = lengths[s] % page
                first = pl.multiple_of(offset // tall * tall, tall)
                old = ref[table_ref[s, lengths[s] // page], pl.ds(first, tall), :].astype(F32)
                new = jnp.broadcast_to(new_rows[n][s : s + 1], (tall, width))
                patch_ref[n, s] = jnp.where(at == offset - first, new, old).astype(BF16)

    packed = jax.ShapeDtypeStruct((parts, pack_rows(slots, strips), PACK), BF16)
    return pl.pallas_call(
        kernel,
        out_shape=(packed, packed, jax.ShapeDtypeStruct((2, slots, tall, width), BF16)),
        in_specs=[SMEM] * 3 + [VMEM] * (parts + 4) + [ANY],
        out_specs=(VMEM, VMEM, VMEM),
        scratch_shapes=[pltpu.VMEM((tall, long_rows), F32), pltpu.VMEM((tall, width), F32)],
        compiler_params=pltpu.CompilerParams(vmem_limit_bytes=18 * MIB),
        cost_estimate=cost(4 * tall * (long_rows + short_rows) * width, 4 * (long_rows + short_rows) * width),
        name="attend",
    )(lengths, new_slot, page_table, *sums, bias, tokens, key_pool, value_pool, after)


def pack_rows(slots, strips):
    need = -(-slots // 8) * 8 + 3 * strips
    return -(-need // 16) * 16


def out_project(column_block, blocks, weight, pieces, slots, *after):
    chips = len(blocks)
    depth, width = weight.shape
    high = -(-slots // 8) * 8
    rows = 2 * chips * slots
    piece = width // pieces

    def kernel(column_ref, *refs):
        block_refs = refs[:chips]
        weight_ref = refs[chips]
        keep_ref, send_ref, left = refs[chips + 1 + len(after) :]

        @pl.when(pl.program_id(0) == 0)
        def _():
            gathered = jnp.concatenate(
                [block_refs[d][e, :high, :].astype(F32) for d in range(chips) for e in range(2)], axis=0
            )
            goal = gathered[:, PACK - 2 : PACK - 1].astype(jnp.int32)
            place = goal ^ lax.axis_index("req")
            row = (place % 2) * (chips * slots) + (place // 2) * slots + gathered[:, PACK - 1 :].astype(jnp.int32)
            row = jnp.where(goal < 0, -1, row)
            size = (gathered.shape[0], rows)
            order = jnp.where(lax.broadcasted_iota(jnp.int32, size, 1) == row, 1.0, 0.0)
            left[...] = lax.dot_general(
                order.astype(BF16), gathered.astype(BF16), (((0,), (0,)), ((), ())), preferred_element_type=F32
            )

        total = jnp.dot(left[:, :depth].astype(BF16), weight_ref[...], preferred_element_type=F32)
        for d in range(chips):
            keep_ref[d, 0] = total[d * slots : (d + 1) * slots]
            send_ref[d, 0] = total[(chips + d) * slots : (chips + d + 1) * slots].astype(BF16)

    shape = (chips, pieces, slots, piece)
    out_spec = pl.BlockSpec((chips, 1, slots, piece), lambda j, c: (0, j, 0, 0))
    whole = lambda shape: pl.BlockSpec(shape, lambda j, c: (0,) * len(shape))
    return pl.pallas_call(
        kernel,
        out_shape=(jax.ShapeDtypeStruct(shape, F32), jax.ShapeDtypeStruct(shape, BF16)),
        grid_spec=pltpu.PrefetchScalarGridSpec(
            num_scalar_prefetch=1,
            grid=(pieces,),
            in_specs=[whole(block.shape) for block in blocks]
            + [pl.BlockSpec((depth, piece), lambda j, c: (0, j ^ c[0]))]
            + [HBM] * min(1, len(after)) + [ANY] * (len(after) - 1),
            out_specs=(out_spec, out_spec),
            scratch_shapes=[pltpu.VMEM((rows, PACK), F32)],
        ),
        compiler_params=pltpu.CompilerParams(vmem_limit_bytes=8 * MIB),
        cost_estimate=cost(2 * rows * weight.size, 2 * weight.size),
        name="out_project",
    )(column_block, *blocks, weight, *after)


def place_page(new_slot, spread, packs, tokens, out_bias, halves, turned, from_other, key_out, value_out):
    chips, across, rows = len(spread), len(halves), len(turned)
    count = across + rows + 1
    page, width = key_out.shape[1:]
    half = page // 2
    slots = tokens.shape[0]
    high = -(-slots // 8) * 8
    strips = width // PACK

    def kernel(slot_ref, *refs):
        block_refs, pack_refs = refs[:chips], refs[chips : 2 * chips]
        token_ref, bias_ref = refs[2 * chips : 2 * chips + 2]
        half_refs = refs[2 * chips + 2 : 2 * chips + 2 + across]
        turned_refs = refs[2 * chips + 2 + across : 2 * chips + 2 + across + rows]
        other_ref = refs[2 * chips + 1 + count]
        _, _, base_ref, key_ref, value_ref, buffer, arrived, sems, out_sems = refs[2 * chips + 2 + count :]
        here = lax.axis_index("req")
        column = pl.multiple_of(lax.axis_index("head") * width, LANES)
        pick = arrivals(block_refs, here, 0)
        source, page_at, offset = pick(4), pick(2), pick(3)
        targets = [
            buffer.at[:, pl.ds(pl.multiple_of((here % 2 ^ e) * half, half), half)] for e in range(2)
        ]
        start_half(source, across, 0, half_refs, turned_refs, targets[0], sems.at[0])
        from_core = pltpu.make_async_copy(other_ref, targets[1], sems.at[1])
        from_core.start()

        for d in range(chips):
            for e in range(2):

                @pl.when(source == 2 * d + e)
                def _():
                    arrived[...] = pack_refs[d][e].astype(F32)

        def fresh(n):
            strip = high + n * strips
            return jnp.concatenate([arrived[strip + i : strip + i + 1, :] for i in range(strips)], axis=1)

        at = lax.broadcasted_iota(jnp.int32, (slots, width), 0)
        token = jnp.where(
            at == leaving_slot(slot_ref, slots, here),
            jnp.broadcast_to(fresh(2), (slots, width)),
            token_ref[:, pl.ds(column, width)].astype(F32),
        )
        base_ref[...] = token + bias_ref[:, pl.ds(column, width)]
        pltpu.make_async_copy(half_refs[0].at[0], targets[0], sems.at[0]).wait()
        from_core.wait()
        first = pl.multiple_of(offset // 16 * 16, 16)
        row = lax.broadcasted_iota(jnp.int32, (16, width), 0)
        for n in range(2):
            old = buffer[n, pl.ds(first, 16), :].astype(F32)
            new = jnp.broadcast_to(fresh(n), (16, width))
            buffer[n, pl.ds(first, 16), :] = jnp.where(row == offset - first, new, old).astype(BF16)
        copies = [
            pltpu.make_async_copy(buffer.at[n], target.at[page_at], out_sems.at[n])
            for n, target in enumerate((key_ref, value_ref))
        ]
        for copy in copies:
            copy.start()
        for copy in copies:
            copy.wait()

    shape = jax.ShapeDtypeStruct(key_out.shape, key_out.dtype)
    return pl.pallas_call(
        kernel,
        out_shape=(jax.ShapeDtypeStruct((slots, width), F32), shape, shape),
        in_specs=[SMEM] + [VMEM] * (2 * chips + 2) + [ANY] * count + [HBM] * 2,
        out_specs=(VMEM, HBM, HBM),
        scratch_shapes=[
            pltpu.VMEM((2, page, width), BF16),
            pltpu.VMEM(packs[0].shape[1:], F32),
            pltpu.SemaphoreType.DMA((2,)),
            pltpu.SemaphoreType.DMA((2,)),
        ],
        input_output_aliases={2 * chips + 3 + count: 1, 2 * chips + 4 + count: 2},
        compiler_params=pltpu.CompilerParams(vmem_limit_bytes=4 * MIB),
        cost_estimate=cost(0, 8 * page * width),
        name="place_page",
    )(new_slot, *spread, *packs, tokens, out_bias, *halves, *turned, from_other, key_out, value_out)


def body(
    tokens,
    norm_gain,
    norm_shift,
    qkv_weight,
    qkv_bias,
    out_weight,
    out_bias,
    key_pool,
    value_pool,
    lengths,
    page_table,
    new_slot,
    new_page,
):
    groups = lax.axis_size("req")
    head_groups = lax.axis_size("head")
    column_block = lax.axis_index("head")
    slots = tokens.shape[0]
    chips = groups // 2

    keep, send, keep_half, send_half = prepare(
        tokens, norm_gain[None], norm_shift[None], lengths, page_table, new_slot, new_page, key_pool, value_pool
    )
    got = swap(send, "req", 1)
    spread = spread_pairs(keep, got)
    (weight,) = stage([jnp.transpose(qkv_weight, (1, 0, 2))], got, "stage_weight")
    across = row_length(chips)
    halves = [jnp.stack([keep_half, swap(send_half, "req", 1)])]
    halves += [swap(halves[0], "req", 2 * d) for d in range(1, across)]
    turning = turn_pages(spread, halves)
    turned = [swap(one, "req", 2 * across * (row + 1)) for row, one in enumerate(turning)]

    keep, send = project(spread, weight)
    got = swap(send, "req", 1)
    own, *messages = combine(keep, got)
    sums = [own] + [swap(messages[d - 1], "req", 2 * d) for d in range(1, chips)]
    keys, values = stage([key_pool, value_pool], own, "stage_pools")

    pack_keep, pack_send, patches = attend(
        lengths,
        new_slot,
        page_table,
        sums,
        qkv_bias.reshape(1, -1),
        tokens,
        keys,
        values,
        turning[0],
    )
    packs_got = swap(pack_send, "req", 1)
    packs = spread_pairs(pack_keep, packs_got)

    from_other = swap(choose_half(spread, halves, turned), "req", 1)
    key_out = write_pool(lengths, new_slot, page_table, patches, keys, packs_got, 0)

    keep, send = out_project(
        column_block[None], packs, out_weight.reshape(-1, out_weight.shape[2]), head_groups, slots, *in_hbm(key_out), turned[0]
    )
    total = keep + swap(send, "req", 1).astype(F32)
    value_out = write_pool(lengths, new_slot, page_table, patches, values, total, 1)
    summed = total[0]
    for d in range(1, chips):
        summed = summed + swap(total[d].astype(BF16), "req", 2 * d).astype(F32)
    summed, value_out = lax.optimization_barrier((summed, value_out))
    base, key_out, value_out = place_page(
        new_slot, spread, packs, tokens, out_bias[None], halves, turned, from_other, key_out, value_out
    )
    hidden = summed[0]
    for j in range(1, head_groups):
        hidden = hidden + swap(summed[j].astype(BF16), "head", j).astype(F32)
    hidden_out = (hidden + base).astype(BF16)
    return (hidden_out, key_out, value_out)


def solution(mesh):
    in_specs = (
        P("req", None),
        P(),
        P(),
        P("req", "head", None),
        P("head", None),
        P("head", "req", None),
        P(),
        P("req", None, "head"),
        P("req", None, "head"),
        P("req"),
        P("req", None),
        P("req"),
        P("req"),
    )
    out_specs = (P("req", "head"), P("req", None, "head"), P("req", None, "head"))
    return jax.shard_map(body, mesh=mesh, in_specs=in_specs, out_specs=out_specs, check_vma=False)
```

```python
import functools

import jax
import jax.numpy as jnp
from jax import lax
from jax.experimental import pallas as pl
from jax.experimental.pallas import tpu as pltpu
from jax.sharding import PartitionSpec as P

EPSILON = 1e-05
F32 = jnp.float32
BF16 = jnp.bfloat16
LANES = 128
META = 128
PACK = 256
VMEM = pl.BlockSpec(memory_space=pltpu.VMEM)
SMEM = pl.BlockSpec(memory_space=pltpu.SMEM)
ANY = pl.BlockSpec(memory_space=pl.ANY)
HBM = pl.BlockSpec(memory_space=pltpu.HBM)
MIB = 1024 * 1024


def cost(flops, moved):
    del flops, moved
    return pl.CostEstimate(flops=0, bytes_accessed=0, transcendentals=0)


def swap(value, axis, step):
    size = lax.axis_size(axis)
    return lax.ppermute(value, axis, [(i, i ^ step) for i in range(size)])


def spread_pairs(keep, got):
    chips = keep.shape[0]
    return [jnp.stack([keep[0], got[0]])] + [
        swap(jnp.stack([keep[d], got[d]]), "req", 2 * d) for d in range(1, chips)
    ]


def in_hbm(*arrays):
    return [pltpu.with_memory_space_constraint(array, pltpu.HBM) for array in arrays]


def write_pool(pool, after):
    parts = 4
    step = pool.shape[0] // parts

    def kernel(pool_ref, _, out_ref, sems):
        places = [pl.ds(i * step, step) for i in range(parts)]
        copies = [
            pltpu.make_async_copy(pool_ref.at[place], out_ref.at[place], sems.at[i]) for i, place in enumerate(places)
        ]
        for copy in copies:
            copy.start()
        for copy in copies:
            copy.wait()

    return pl.pallas_call(
        kernel,
        out_shape=jax.ShapeDtypeStruct(pool.shape, pool.dtype),
        in_specs=[VMEM, ANY],
        out_specs=HBM,
        scratch_shapes=[pltpu.SemaphoreType.DMA((parts,))],
        compiler_params=pltpu.CompilerParams(vmem_limit_bytes=8 * MIB),
        cost_estimate=cost(0, 2 * pool.size),
        name="write_pool",
    )(pool, after)


def leaving_slot(new_slot_ref, slots, here):
    leaving = jnp.int32(0)
    for s in range(slots):
        leaving = jnp.where(new_slot_ref[s] // slots != here, s, leaving)
    return leaving


def prepare(tokens, gain, shift, lengths, page_table, new_slot, new_page, key_pool, value_pool):
    groups = lax.axis_size("req")
    chips = groups // 2
    slots, model = tokens.shape
    depth = model // groups
    page, width = key_pool.shape[1:]
    half = page // 2

    def kernel(
        token_ref, gain_ref, shift_ref, length_ref, table_ref, slot_ref, page_ref, key_ref, value_ref,
        keep_ref, send_ref, keep_half, send_half, normed, sems,
    ):
        here = lax.axis_index("req")
        leaving = leaving_slot(slot_ref, slots, here)
        copies = []
        for n, source in enumerate((key_ref, value_ref)):
            for e, target in enumerate((keep_half, send_half)):
                rows = pl.ds(pl.multiple_of((here % 2 ^ e) * half, half), half)
                copies.append(
                    pltpu.make_async_copy(source.at[table_ref[leaving, 0], rows], target.at[n], sems.at[n, e])
                )
        for copy in copies:
            copy.start()
        values = token_ref[...].astype(F32)
        average = jnp.mean(values, axis=1, keepdims=True)
        centered = values - average
        variance = jnp.mean(centered * centered, axis=1, keepdims=True)
        rows = centered * lax.rsqrt(variance + EPSILON) * gain_ref[...] + shift_ref[...]
        normed[...] = rows.astype(BF16).astype(F32)
        row = lax.broadcasted_iota(jnp.int32, (slots, META), 0)
        lane = lax.broadcasted_iota(jnp.int32, (slots, META), 1)
        told = jnp.zeros((slots, META), F32)
        for s in range(slots):
            slot = slot_ref[s]
            numbers = (slot // slots, slot % slots, page_ref[s], length_ref[s] % page)
            for j, number in enumerate(numbers):
                told = jnp.where((row == s) & (lane == j), number.astype(F32), told)
        told = told.astype(BF16)
        for k in range(groups):
            first = (here ^ k) * depth
            if depth % LANES == 0:
                block = normed[:, pl.ds(pl.multiple_of(first, LANES), depth)]
            else:
                block = pltpu.roll(normed[...], lax.rem(model - first, model), 1)[:, :depth]
            target = (keep_ref, send_ref)[k % 2]
            target[k // 2, :, :META] = told
            target[k // 2, :, META:] = block.astype(BF16)
        for copy in copies:
            copy.wait()

    blocks = jax.ShapeDtypeStruct((chips, slots, META + depth), BF16)
    halves = jax.ShapeDtypeStruct((2, half, width), key_pool.dtype)
    return pl.pallas_call(
        kernel,
        out_shape=(blocks, blocks, halves, halves),
        in_specs=[VMEM] * 3 + [SMEM] * 4 + [HBM] * 2,
        out_specs=(VMEM,) * 4,
        scratch_shapes=[pltpu.VMEM((slots, model), F32), pltpu.SemaphoreType.DMA((2, 2))],
        compiler_params=pltpu.CompilerParams(vmem_limit_bytes=4 * MIB),
        cost_estimate=cost(0, 8 * page * width),
        name="prepare",
    )(*in_hbm(tokens, gain, shift, lengths, page_table, new_slot, new_page, key_pool, value_pool))


def arrivals(block_refs, here, wanted):
    slots = block_refs[0].shape[1]
    lane = lax.broadcasted_iota(jnp.int32, (slots, META), 1)
    found = jnp.zeros((slots, META), F32)
    goal = (here ^ wanted).astype(F32)
    for d, ref in enumerate(block_refs):
        for e in range(2):
            k = 2 * d + e
            if k == wanted:
                continue
            told = ref[e, :, :META].astype(F32)
            numbered = jnp.where(lane == 4, float(k), told)
            found = jnp.where(told[:, :1] == goal, numbered, found)
    return lambda j: jnp.sum(jnp.where(lane == j, found, 0.0)).astype(jnp.int32)


def row_length(chips):
    return 1 << (chips.bit_length() // 2)


def turn_pages(spread, halves):
    chips = len(spread)
    across = row_length(chips)
    down = chips // across
    shape = halves[0].shape

    def kernel(*refs):
        block_refs, half_refs = refs[:chips], refs[chips : chips + across]
        out_refs, sems = refs[chips + across : -1], refs[-1]
        here = lax.axis_index("req")
        waits = []
        for row in range(1, down):
            for j in range(2):
                source = arrivals(block_refs, here, 2 * across * row + j)(4)
                place = jnp.where(source < 2 * across, source, 0)
                for d in range(across):
                    for e in range(2):
                        copy = pltpu.make_async_copy(half_refs[d].at[e], out_refs[row - 1].at[j], sems.at[row - 1, j])

                        @pl.when(place == 2 * d + e)
                        def _():
                            copy.start()

                waits.append(copy)
        for copy in waits:
            copy.wait()

    one = jax.ShapeDtypeStruct(shape, halves[0].dtype)
    return pl.pallas_call(
        kernel,
        out_shape=(one,) * (down - 1),
        in_specs=[VMEM] * chips + [ANY] * across,
        out_specs=(VMEM,) * (down - 1),
        scratch_shapes=[pltpu.SemaphoreType.DMA((down - 1, 2))],
        compiler_params=pltpu.CompilerParams(vmem_limit_bytes=down * 2 * MIB),
        cost_estimate=cost(0, 4 * halves[0].size),
        name="turn_pages",
    )(*spread, *halves)


def start_half(source, across, core, half_refs, turned_refs, target, sem):
    place = jnp.where(source < 2 * across, source, 2 * across + source // (2 * across))
    for d, ref in enumerate(half_refs):
        for e in range(2):

            @pl.when(place == 2 * d + e)
            def _():
                pltpu.make_async_copy(ref.at[e], target, sem).start()

    for row, ref in enumerate(turned_refs):

        @pl.when(place == 2 * across + row + 1)
        def _():
            pltpu.make_async_copy(ref.at[core], target, sem).start()


def choose_half(spread, halves, turned):
    chips, across, rows = len(spread), len(halves), len(turned)

    def kernel(*refs):
        block_refs, half_refs = refs[:chips], refs[chips : chips + across]
        turned_refs = refs[chips + across : chips + across + rows]
        out_ref, sem = refs[chips + across + rows :]
        source = arrivals(block_refs, lax.axis_index("req"), 1)(4)
        start_half(source, across, 1, half_refs, turned_refs, out_ref, sem)
        pltpu.make_async_copy(half_refs[0].at[0], out_ref, sem).wait()

    shape = halves[0].shape[1:]
    return pl.pallas_call(
        kernel,
        out_shape=jax.ShapeDtypeStruct(shape, halves[0].dtype),
        in_specs=[VMEM] * chips + [ANY] * (across + rows),
        out_specs=VMEM,
        scratch_shapes=[pltpu.SemaphoreType.DMA],
        compiler_params=pltpu.CompilerParams(vmem_limit_bytes=2 * MIB),
        cost_estimate=cost(0, 2 * halves[0].size),
        name="choose_half",
    )(*spread, *halves, *turned)


def project(blocks, weight):
    chips = len(blocks)
    slots = blocks[0].shape[1]
    heads, depth, width = weight.shape
    per = 2 if heads % 2 == 0 else 1
    rows = chips * 2 * slots

    def kernel(*refs):
        block_refs = refs[:chips]
        weight_ref, keep_ref, send_ref, left = refs[chips:]
        for d in range(chips):
            for e in range(2):
                row = (d * 2 + e) * slots
                left[row : row + slots, :] = block_refs[d][e, :, META:].astype(F32)
        lhs = left[...].astype(BF16)

        @pl.loop(0, heads // per)
        def _(i):
            right = jnp.concatenate([weight_ref[i * per + j] for j in range(per)], axis=1)
            total = jnp.dot(lhs, right, preferred_element_type=F32)
            columns = pl.ds(pl.multiple_of(i * (per * width), per * width), per * width)
            for d in range(chips):
                row = d * 2 * slots
                keep_ref[d, :, columns] = total[row : row + slots]
                send_ref[d, :, columns] = total[row + slots : row + 2 * slots]

    shape = jax.ShapeDtypeStruct((chips, slots, heads * width), F32)
    return pl.pallas_call(
        kernel,
        out_shape=(shape, shape),
        in_specs=[VMEM] * (chips + 1),
        out_specs=(VMEM, VMEM),
        scratch_shapes=[pltpu.VMEM((rows, depth), F32)],
        compiler_params=pltpu.CompilerParams(vmem_limit_bytes=weight.size * 2 + 8 * MIB),
        cost_estimate=cost(2 * rows * weight.size, 2 * weight.size),
        name="project",
    )(*blocks, weight)


def combine(keep, got):
    chips, slots, width = keep.shape
    heads = width // (3 * LANES)

    def kernel(keep_ref, got_ref, own_ref, *message_refs):
        own_ref[...] = keep_ref[0] + got_ref[0]
        for d in range(1, chips):
            for h in range(heads):
                total = keep_ref[d, :, 3 * h * LANES : 3 * (h + 1) * LANES] + got_ref[d, :, 3 * h * LANES : 3 * (h + 1) * LANES]
                query = total[:, :LANES]
                high = query.astype(BF16)
                low = (query - high.astype(F32)).astype(BF16)
                base = 4 * h * LANES
                message_refs[d - 1][:, base : base + LANES] = high
                message_refs[d - 1][:, base + LANES : base + 2 * LANES] = low
                message_refs[d - 1][:, base + 2 * LANES : base + 4 * LANES] = total[:, LANES:].astype(BF16)

    message = jax.ShapeDtypeStruct((slots, 4 * heads * LANES), BF16)
    return pl.pallas_call(
        kernel,
        out_shape=(jax.ShapeDtypeStruct((slots, width), F32),) + (message,) * (chips - 1),
        in_specs=[VMEM, VMEM],
        out_specs=(VMEM,) * chips,
        compiler_params=pltpu.CompilerParams(vmem_limit_bytes=8 * MIB),
        cost_estimate=cost(0, 8 * keep.size),
        name="combine",
    )(keep, got)


def attend(lengths, new_slot, page_table, sums, bias, tokens, key_pool, value_pool, after):
    parts = len(sums)
    slots = sums[0].shape[0]
    pages, page, width = key_pool.shape
    head = LANES
    heads = width // head
    max_pages = page_table.shape[1]
    chunk_pages = 4
    chunk = chunk_pages * page
    chunks = max_pages // chunk_pages
    long_rows = max_pages * page
    short_rows = slots * page
    groups = 2 * parts
    share = head // groups
    per = LANES // share
    tall = 16
    strips = width // PACK
    scale = head ** (-0.5)

    def kernel(*refs):
        length_ref, slot_ref, table_ref = refs[:3]
        sum_refs = refs[3 : 3 + parts]
        (bias_ref, token_ref, key_ref, value_ref, _, pack_keep, pack_send, patch_ref, score_buffer, mix_buffer) = refs[
            3 + parts :
        ]
        here = lax.axis_index("req")
        column_block = lax.axis_index("head")
        leaving = leaving_slot(slot_ref, slots, here)
        lengths = [length_ref[s] for s in range(slots)]
        long_slot = jnp.int32(0)
        long_length = jnp.int32(0)
        for s in range(slots):
            is_long = lengths[s] >= page
            long_slot = jnp.where(is_long, s, long_slot)
            long_length = jnp.where(is_long, lengths[s], long_length)
        turns = (long_length + chunk - 1) // chunk

        total = sum_refs[0][...] + bias_ref[...]

        def third(k):
            columns = []
            for h in range(heads):
                one = total[:, (3 * h + k) * head : (3 * h + k + 1) * head]
                for ref in sum_refs[1:]:
                    base = 4 * h * head
                    if k == 0:
                        one = one + ref[:, base : base + head].astype(F32) + ref[:, base + head : base + 2 * head].astype(F32)
                    else:
                        one = one + ref[:, base + (k + 1) * head : base + (k + 2) * head].astype(F32)
                columns.append(one)
            return jnp.concatenate(columns, axis=1)

        query = (third(0) * scale).astype(BF16).astype(F32)
        new_rows = (third(1).astype(BF16).astype(F32), third(2).astype(BF16).astype(F32))

        lane_head = lax.broadcasted_iota(jnp.int32, (tall, width), 1) // head
        on_head = lane_head == lax.broadcasted_iota(jnp.int32, (tall, width), 0)

        def blocked(row):
            return jnp.where(on_head, jnp.broadcast_to(row, (tall, width)), 0.0).astype(BF16)

        def for_slot(which, rows):
            found = rows[0]
            for s in range(1, slots):
                found = jnp.where(which == s, rows[s], found)
            return found

        def softmax(scores, valid, new_score):
            masked = jnp.where(valid, scores, -1e30)
            peak = jnp.maximum(jnp.max(masked, axis=1, keepdims=True), new_score)
            weights = jnp.where(valid, jnp.exp(masked - peak), 0.0)
            new_weight = jnp.exp(new_score - peak)
            denom = jnp.sum(weights, axis=1, keepdims=True) + new_weight
            return weights.astype(BF16), new_weight.astype(BF16).astype(F32), denom

        across = (((1,), (1,)), ((), ()))
        short_query = jnp.concatenate([blocked(query[s : s + 1]) for s in range(slots)], axis=0)
        new_keys = jnp.concatenate([new_rows[0], jnp.zeros((tall - slots, width), F32)], axis=0).astype(BF16)
        new_scores = lax.dot_general(short_query, new_keys, across, preferred_element_type=F32)
        size = (slots * tall, tall)
        own_column = lax.broadcasted_iota(jnp.int32, size, 0) // tall == lax.broadcasted_iota(jnp.int32, size, 1)
        new_score = jnp.sum(jnp.where(own_column, new_scores, 0.0), axis=1, keepdims=True)

        first_pages = lambda ref: jnp.concatenate([ref[table_ref[s, 0]] for s in range(slots)], axis=0)
        short_scores = lax.dot_general(short_query, first_pages(key_ref), across, preferred_element_type=F32)
        size = (slots * tall, short_rows)
        row_slot = lax.broadcasted_iota(jnp.int32, size, 0) // tall
        column = lax.broadcasted_iota(jnp.int32, size, 1)
        limit = jnp.zeros(size, jnp.int32)
        for s in range(slots):
            limit = jnp.where(row_slot == s, lengths[s], limit)
        valid = (row_slot == column // page) & (column % page < limit)
        short_probs, new_prob, short_denom = softmax(short_scores, valid, new_score)
        new_values = jnp.concatenate(
            [jnp.broadcast_to(new_rows[1][s : s + 1], (tall, width)) for s in range(slots)], axis=0
        )
        short_mix = jnp.dot(short_probs, first_pages(value_ref), preferred_element_type=F32)
        short_mix = (short_mix + new_prob * new_values) / short_denom

        mix_buffer[...] = jnp.zeros(mix_buffer.shape, F32)

        @pl.when(turns > 0)
        def _():
            some_pages = lambda ref, c: jnp.concatenate(
                [ref[table_ref[long_slot, c * chunk_pages + i]] for i in range(chunk_pages)], axis=0
            )
            long_query = blocked(for_slot(long_slot, [query[s : s + 1] for s in range(slots)]))
            long_new = for_slot(long_slot, [new_score[s * tall : (s + 1) * tall] for s in range(slots)])
            long_value = for_slot(long_slot, [new_rows[1][s : s + 1] for s in range(slots)])
            for c in range(chunks):

                @pl.when(c < turns)
                def _():
                    score_buffer[:, c * chunk : (c + 1) * chunk] = lax.dot_general(
                        long_query, some_pages(key_ref, c), across, preferred_element_type=F32
                    )

                @pl.when(c >= turns)
                def _():
                    score_buffer[:, c * chunk : (c + 1) * chunk] = jnp.zeros((tall, chunk), F32)

            position = lax.broadcasted_iota(jnp.int32, (tall, long_rows), 1)
            long_probs, long_prob, long_denom = softmax(score_buffer[...], position < long_length, long_new)
            for c in range(chunks):

                @pl.when(c < turns)
                def _():
                    mix_buffer[...] += jnp.dot(
                        long_probs[:, c * chunk : (c + 1) * chunk], some_pages(value_ref, c), preferred_element_type=F32
                    )

            mix_buffer[...] = (mix_buffer[...] + long_prob * long_value) / long_denom

        def fold(mixed):
            return jnp.sum(jnp.where(on_head, mixed, 0.0), axis=0, keepdims=True)

        long_mix = fold(mix_buffer[...])
        rows = []
        for s in range(slots):
            row = fold(short_mix[s * tall : (s + 1) * tall])
            rows.append(jnp.where(lengths[s] >= page, long_mix, row))
        high = -(-slots // 8) * 8
        attended = jnp.concatenate(rows + [jnp.zeros((high - slots, width), F32)], axis=0).astype(BF16).astype(F32)

        token = token_ref[:, pl.ds(pl.multiple_of(column_block * width, LANES), width)].astype(F32)
        extra = []
        for source in new_rows + (token,):
            one = jnp.zeros((1, width), F32)
            for s in range(slots):
                one = jnp.where(leaving == s, source[s : s + 1], one)
            extra += [one[:, i * PACK : (i + 1) * PACK] for i in range(strips)]
        extra = jnp.concatenate(extra + [jnp.zeros((pack_rows(slots, strips) - high - 3 * strips, PACK), F32)], axis=0)

        row_at = lax.broadcasted_iota(jnp.int32, (high, LANES), 0)
        lane_at = lax.broadcasted_iota(jnp.int32, (high, LANES), 1)
        goal_device = jnp.full((high, LANES), -1.0, F32)
        goal_slot = jnp.zeros((high, LANES), F32)
        for s in range(slots):
            goal_device = jnp.where(row_at == s, (slot_ref[s] // slots).astype(F32), goal_device)
            goal_slot = jnp.where(row_at == s, (slot_ref[s] % slots).astype(F32), goal_slot)
        lane = lane_at // share
        for k in range(groups):
            wanted = here ^ k
            tiles = [jnp.zeros((high, LANES), F32) for _ in range(PACK // LANES)]
            for h in range(heads):
                place = h % per
                shift = lax.rem((place - wanted) * share + 2 * LANES, LANES)
                turned = pltpu.roll(attended[:, h * head : (h + 1) * head], shift, 1)
                tiles[h // per] = jnp.where(lane == place, turned, tiles[h // per])
            tiles[-1] = jnp.where(lane_at == LANES - 2, goal_device, jnp.where(lane_at == LANES - 1, goal_slot, tiles[-1]))
            block = jnp.concatenate([jnp.concatenate(tiles, axis=1), extra], axis=0).astype(BF16)
            (pack_keep, pack_send)[k % 2][k // 2] = block

        at = lax.broadcasted_iota(jnp.int32, (tall, width), 0)
        for n, ref in enumerate((key_ref, value_ref)):
            for s in range(slots):
                offset = lengths[s] % page
                first = pl.multiple_of(offset // tall * tall, tall)
                old = ref[table_ref[s, lengths[s] // page], pl.ds(first, tall), :].astype(F32)
                new = jnp.broadcast_to(new_rows[n][s : s + 1], (tall, width))
                patch_ref[n, s] = jnp.where(at == offset - first, new, old).astype(BF16)

    packed = jax.ShapeDtypeStruct((parts, pack_rows(slots, strips), PACK), BF16)
    return pl.pallas_call(
        kernel,
        out_shape=(packed, packed, jax.ShapeDtypeStruct((2, slots, tall, width), BF16)),
        in_specs=[SMEM] * 3 + [VMEM] * (parts + 4) + [ANY],
        out_specs=(VMEM, VMEM, VMEM),
        scratch_shapes=[pltpu.VMEM((tall, long_rows), F32), pltpu.VMEM((tall, width), F32)],
        compiler_params=pltpu.CompilerParams(vmem_limit_bytes=18 * MIB),
        cost_estimate=cost(4 * tall * (long_rows + short_rows) * width, 4 * (long_rows + short_rows) * width),
        name="attend",
    )(lengths, new_slot, page_table, *sums, bias, tokens, key_pool, value_pool, after)


def pack_rows(slots, strips):
    need = -(-slots // 8) * 8 + 3 * strips
    return -(-need // 16) * 16


def out_project(blocks, weight, pieces, slots, *after):
    chips = len(blocks)
    depth, width = weight.shape
    high = -(-slots // 8) * 8
    rows = 2 * chips * slots
    piece = width // pieces

    def kernel(*refs):
        block_refs, weight_ref = refs[:chips], refs[chips]
        keep_ref, send_ref = refs[chips + 1 + len(after) :]
        gathered = jnp.concatenate(
            [block_refs[d][e, :high, :].astype(F32) for d in range(chips) for e in range(2)], axis=0
        )
        goal = gathered[:, PACK - 2 : PACK - 1].astype(jnp.int32)
        place = goal ^ lax.axis_index("req")
        row = (place % 2) * (chips * slots) + (place // 2) * slots + gathered[:, PACK - 1 :].astype(jnp.int32)
        row = jnp.where(goal < 0, -1, row)
        size = (gathered.shape[0], rows)
        order = jnp.where(lax.broadcasted_iota(jnp.int32, size, 1) == row, 1.0, 0.0)
        left = lax.dot_general(
            order.astype(BF16), gathered.astype(BF16), (((0,), (0,)), ((), ())), preferred_element_type=F32
        )
        left = left[:, :depth].astype(BF16)
        for j in range(pieces):
            first = (lax.axis_index("head") ^ j) * piece
            total = jnp.dot(
                left, weight_ref[:, pl.ds(pl.multiple_of(first, LANES), piece)], preferred_element_type=F32
            )
            for d in range(chips):
                keep_ref[d, j] = total[d * slots : (d + 1) * slots]
                send_ref[d, j] = total[(chips + d) * slots : (chips + d + 1) * slots].astype(BF16)

    shape = (chips, pieces, slots, piece)
    return pl.pallas_call(
        kernel,
        out_shape=(jax.ShapeDtypeStruct(shape, F32), jax.ShapeDtypeStruct(shape, BF16)),
        in_specs=[VMEM] * (chips + 1) + [HBM] * min(1, len(after)) + [ANY] * (len(after) - 1),
        out_specs=(VMEM, VMEM),
        compiler_params=pltpu.CompilerParams(vmem_limit_bytes=10 * MIB),
        cost_estimate=cost(2 * rows * weight.size, 2 * weight.size),
        name="out_project",
    )(*blocks, weight, *after)


def place_page(lengths, new_slot, page_table, patches, spread, packs, tokens, out_bias, halves, turned, from_other, key_out, value_out):
    chips, across, rows = len(spread), len(halves), len(turned)
    count = across + rows + 1
    page, width = key_out.shape[1:]
    half = page // 2
    slots = tokens.shape[0]
    high = -(-slots // 8) * 8
    strips = width // PACK

    tall = patches.shape[2]

    def kernel(length_ref, slot_ref, table_ref, patch_ref, *refs):
        block_refs, pack_refs = refs[:chips], refs[chips : 2 * chips]
        token_ref, bias_ref = refs[2 * chips : 2 * chips + 2]
        half_refs = refs[2 * chips + 2 : 2 * chips + 2 + across]
        turned_refs = refs[2 * chips + 2 + across : 2 * chips + 2 + across + rows]
        other_ref = refs[2 * chips + 1 + count]
        _, _, base_ref, key_ref, value_ref, buffer, arrived, sems, out_sems, patch_sems = refs[2 * chips + 2 + count :]
        here = lax.axis_index("req")
        leaving = leaving_slot(slot_ref, slots, here)

        def patch(n, s):
            length = length_ref[s]
            first = pl.multiple_of(length % page // tall * tall, tall)
            target = (key_ref, value_ref)[n].at[table_ref[s, length // page], pl.ds(first, tall)]
            return pltpu.make_async_copy(patch_ref.at[n, s], target, patch_sems.at[n, s])

        for n in range(2):
            for s in range(slots):

                @pl.when(leaving != s)
                def _():
                    patch(n, s).start()

        column = pl.multiple_of(lax.axis_index("head") * width, LANES)
        pick = arrivals(block_refs, here, 0)
        source, page_at, offset = pick(4), pick(2), pick(3)
        targets = [
            buffer.at[:, pl.ds(pl.multiple_of((here % 2 ^ e) * half, half), half)] for e in range(2)
        ]
        start_half(source, across, 0, half_refs, turned_refs, targets[0], sems.at[0])
        from_core = pltpu.make_async_copy(other_ref, targets[1], sems.at[1])
        from_core.start()

        for d in range(chips):
            for e in range(2):

                @pl.when(source == 2 * d + e)
                def _():
                    arrived[...] = pack_refs[d][e].astype(F32)

        def fresh(n):
            strip = high + n * strips
            return jnp.concatenate([arrived[strip + i : strip + i + 1, :] for i in range(strips)], axis=1)

        at = lax.broadcasted_iota(jnp.int32, (slots, width), 0)
        token = jnp.where(
            at == leaving,
            jnp.broadcast_to(fresh(2), (slots, width)),
            token_ref[:, pl.ds(column, width)].astype(F32),
        )
        base_ref[...] = token + bias_ref[:, pl.ds(column, width)]
        pltpu.make_async_copy(half_refs[0].at[0], targets[0], sems.at[0]).wait()
        from_core.wait()
        first = pl.multiple_of(offset // 16 * 16, 16)
        row = lax.broadcasted_iota(jnp.int32, (16, width), 0)
        for n in range(2):
            old = buffer[n, pl.ds(first, 16), :].astype(F32)
            new = jnp.broadcast_to(fresh(n), (16, width))
            buffer[n, pl.ds(first, 16), :] = jnp.where(row == offset - first, new, old).astype(BF16)
        copies = [
            pltpu.make_async_copy(buffer.at[n], target.at[page_at], out_sems.at[n])
            for n, target in enumerate((key_ref, value_ref))
        ]
        for copy in copies:
            copy.start()
        for n in range(2):
            for s in range(slots):

                @pl.when(leaving != s)
                def _():
                    patch(n, s).wait()

        for copy in copies:
            copy.wait()

    shape = jax.ShapeDtypeStruct(key_out.shape, key_out.dtype)
    return pl.pallas_call(
        kernel,
        out_shape=(jax.ShapeDtypeStruct((slots, width), F32), shape, shape),
        in_specs=[SMEM] * 3 + [VMEM] * (2 * chips + 3) + [ANY] * count + [HBM] * 2,
        out_specs=(VMEM, HBM, HBM),
        scratch_shapes=[
            pltpu.VMEM((2, page, width), BF16),
            pltpu.VMEM(packs[0].shape[1:], F32),
            pltpu.SemaphoreType.DMA((2,)),
            pltpu.SemaphoreType.DMA((2,)),
            pltpu.SemaphoreType.DMA((2, slots)),
        ],
        input_output_aliases={2 * chips + 6 + count: 1, 2 * chips + 7 + count: 2},
        compiler_params=pltpu.CompilerParams(vmem_limit_bytes=4 * MIB),
        cost_estimate=cost(0, 8 * page * width),
        name="place_page",
    )(
        lengths, new_slot, page_table, patches, *spread, *packs, tokens, out_bias, *halves, *turned, from_other, key_out, value_out
    )


def body(
    tokens,
    norm_gain,
    norm_shift,
    qkv_weight,
    qkv_bias,
    out_weight,
    out_bias,
    key_pool,
    value_pool,
    lengths,
    page_table,
    new_slot,
    new_page,
):
    groups = lax.axis_size("req")
    head_groups = lax.axis_size("head")
    slots = tokens.shape[0]
    chips = groups // 2

    keep, send, keep_half, send_half = prepare(
        tokens, norm_gain[None], norm_shift[None], lengths, page_table, new_slot, new_page, key_pool, value_pool
    )
    got = swap(send, "req", 1)
    spread = spread_pairs(keep, got)
    across = row_length(chips)
    halves = [jnp.stack([keep_half, swap(send_half, "req", 1)])]
    halves += [swap(halves[0], "req", 2 * d) for d in range(1, across)]
    turning = turn_pages(spread, halves)
    turned = [swap(one, "req", 2 * across * (row + 1)) for row, one in enumerate(turning)]

    keep, send = project(spread, jnp.transpose(qkv_weight, (1, 0, 2)))
    got = swap(send, "req", 1)
    own, *messages = combine(keep, got)
    sums = [own] + [swap(messages[d - 1], "req", 2 * d) for d in range(1, chips)]

    pack_keep, pack_send, patches = attend(
        lengths,
        new_slot,
        page_table,
        sums,
        qkv_bias.reshape(1, -1),
        tokens,
        key_pool,
        value_pool,
        turning[0],
    )
    packs_got = swap(pack_send, "req", 1)
    packs = spread_pairs(pack_keep, packs_got)

    from_other = swap(choose_half(spread, halves, turned), "req", 1)
    key_out = write_pool(key_pool, packs_got)

    keep, send = out_project(
        packs, out_weight.reshape(-1, out_weight.shape[2]), head_groups, slots, *in_hbm(key_out), turned[0]
    )
    total = keep + swap(send, "req", 1).astype(F32)
    value_out = write_pool(value_pool, total)
    summed = total[0]
    for d in range(1, chips):
        summed = summed + swap(total[d].astype(BF16), "req", 2 * d).astype(F32)
    summed, value_out = lax.optimization_barrier((summed, value_out))
    base, key_out, value_out = place_page(
        lengths,
        new_slot,
        page_table,
        patches,
        spread,
        packs,
        tokens,
        out_bias[None],
        halves,
        turned,
        from_other,
        key_out,
        value_out,
    )
    hidden = summed[0]
    for j in range(1, head_groups):
        hidden = hidden + swap(summed[j].astype(BF16), "head", j).astype(F32)
    hidden_out = (hidden + base).astype(BF16)
    return (hidden_out, key_out, value_out)


def solution(mesh):
    in_specs = (
        P("req", None),
        P(),
        P(),
        P("req", "head", None),
        P("head", None),
        P("head", "req", None),
        P(),
        P("req", None, "head"),
        P("req", None, "head"),
        P("req"),
        P("req", None),
        P("req"),
        P("req"),
    )
    out_specs = (P("req", "head"), P("req", None, "head"), P("req", None, "head"))
    return jax.shard_map(body, mesh=mesh, in_specs=in_specs, out_specs=out_specs, check_vma=False)
```

```python
import functools

import jax
import jax.numpy as jnp
from jax import lax
from jax.experimental import pallas as pl
from jax.experimental.pallas import tpu as pltpu
from jax.sharding import PartitionSpec as P

EPSILON = 1e-05
F32 = jnp.float32
BF16 = jnp.bfloat16
LANES = 128
META = 128
PACK = 256
VMEM = pl.BlockSpec(memory_space=pltpu.VMEM)
SMEM = pl.BlockSpec(memory_space=pltpu.SMEM)
ANY = pl.BlockSpec(memory_space=pl.ANY)
HBM = pl.BlockSpec(memory_space=pltpu.HBM)
MIB = 1024 * 1024


def cost(flops, moved):
    del flops, moved
    return pl.CostEstimate(flops=0, bytes_accessed=0, transcendentals=0)


def swap(value, axis, step):
    size = lax.axis_size(axis)
    return lax.ppermute(value, axis, [(i, i ^ step) for i in range(size)])


def spread_pairs(keep, got):
    chips = keep.shape[0]
    return [jnp.stack([keep[0], got[0]])] + [
        swap(jnp.stack([keep[d], got[d]]), "req", 2 * d) for d in range(1, chips)
    ]


def in_hbm(*arrays):
    return [pltpu.with_memory_space_constraint(array, pltpu.HBM) for array in arrays]


def leaving_slot(new_slot_ref, slots, here):
    leaving = jnp.int32(0)
    for s in range(slots):
        leaving = jnp.where(new_slot_ref[s] // slots != here, s, leaving)
    return leaving


def prepare(tokens, gain, shift, lengths, page_table, new_slot, new_page, key_pool, value_pool):
    groups = lax.axis_size("req")
    chips = groups // 2
    slots, model = tokens.shape
    depth = model // groups
    page, width = key_pool.shape[1:]
    half = page // 2

    def kernel(
        token_ref, gain_ref, shift_ref, length_ref, table_ref, slot_ref, page_ref, key_ref, value_ref,
        keep_ref, send_ref, keep_half, send_half, normed, sems,
    ):
        here = lax.axis_index("req")
        leaving = leaving_slot(slot_ref, slots, here)
        copies = []
        for n, source in enumerate((key_ref, value_ref)):
            for e, target in enumerate((keep_half, send_half)):
                rows = pl.ds(pl.multiple_of((here % 2 ^ e) * half, half), half)
                copies.append(
                    pltpu.make_async_copy(source.at[table_ref[leaving, 0], rows], target.at[n], sems.at[n, e])
                )
        for copy in copies:
            copy.start()
        values = token_ref[...].astype(F32)
        average = jnp.mean(values, axis=1, keepdims=True)
        centered = values - average
        variance = jnp.mean(centered * centered, axis=1, keepdims=True)
        rows = centered * lax.rsqrt(variance + EPSILON) * gain_ref[...] + shift_ref[...]
        normed[...] = rows.astype(BF16).astype(F32)
        row = lax.broadcasted_iota(jnp.int32, (slots, META), 0)
        lane = lax.broadcasted_iota(jnp.int32, (slots, META), 1)
        told = jnp.zeros((slots, META), F32)
        for s in range(slots):
            slot = slot_ref[s]
            numbers = (slot // slots, slot % slots, page_ref[s], length_ref[s] % page)
            for j, number in enumerate(numbers):
                told = jnp.where((row == s) & (lane == j), number.astype(F32), told)
        told = told.astype(BF16)
        for k in range(groups):
            first = (here ^ k) * depth
            if depth % LANES == 0:
                block = normed[:, pl.ds(pl.multiple_of(first, LANES), depth)]
            else:
                block = pltpu.roll(normed[...], lax.rem(model - first, model), 1)[:, :depth]
            target = (keep_ref, send_ref)[k % 2]
            target[k // 2, :, :META] = told
            target[k // 2, :, META:] = block.astype(BF16)
        for copy in copies:
            copy.wait()

    blocks = jax.ShapeDtypeStruct((chips, slots, META + depth), BF16)
    halves = jax.ShapeDtypeStruct((2, half, width), key_pool.dtype)
    return pl.pallas_call(
        kernel,
        out_shape=(blocks, blocks, halves, halves),
        in_specs=[VMEM] * 3 + [SMEM] * 4 + [HBM] * 2,
        out_specs=(VMEM,) * 4,
        scratch_shapes=[pltpu.VMEM((slots, model), F32), pltpu.SemaphoreType.DMA((2, 2))],
        compiler_params=pltpu.CompilerParams(vmem_limit_bytes=4 * MIB),
        cost_estimate=cost(0, 8 * page * width),
        name="prepare",
    )(*in_hbm(tokens, gain, shift, lengths, page_table, new_slot, new_page, key_pool, value_pool))


def arrivals(block_refs, here, wanted):
    slots = block_refs[0].shape[1]
    lane = lax.broadcasted_iota(jnp.int32, (slots, META), 1)
    found = jnp.zeros((slots, META), F32)
    goal = here ^ wanted
    for d, ref in enumerate(block_refs):
        for e in range(2):
            k = 2 * d + e
            told = ref[e, :, :META].astype(F32)
            numbered = jnp.where(lane == 4, float(k), told)
            found = jnp.where(told[:, :1] == jnp.where(wanted == k, -1, goal).astype(F32), numbered, found)
    return lambda j: jnp.sum(jnp.where(lane == j, found, 0.0)).astype(jnp.int32)


def row_length(chips):
    return 1 << (chips.bit_length() // 2)


def swap_pages(value, chips, along_row, step):
    across = row_length(chips)
    square = across * across == chips
    steps = [2 * step if along_row == (device % 2 == 0 or not square) else 2 * across * step for device in range(2 * chips)]
    return lax.ppermute(value, "req", [(i, i ^ steps[i]) for i in range(2 * chips)])


def find_sources(spread, after):
    chips = len(spread)
    across = row_length(chips)
    down = chips // across

    def kernel(*refs):
        block_refs, out_ref = refs[:chips], refs[-1]
        here = lax.axis_index("req")
        turned = (here % 2 == 1) & (across == down)
        for row in range(down):
            for j in range(2):
                pick = arrivals(block_refs, here, jnp.where(turned, 2 * row, 2 * across * row) + j)
                source = pick(4)
                chip = source // 2
                chip = jnp.where(turned, chip % across * across + chip // across, chip)
                out_ref[2 * row + j] = 2 * chip + source % 2
                if row == 0 and j == 0:
                    out_ref[2 * down] = pick(2)
                    out_ref[2 * down + 1] = pick(3)
                    out_ref[2 * down + 2] = source

    return pl.pallas_call(
        kernel,
        out_shape=jax.ShapeDtypeStruct((2 * down + 3,), jnp.int32),
        in_specs=[VMEM] * chips + [ANY],
        out_specs=SMEM,
        compiler_params=pltpu.CompilerParams(vmem_limit_bytes=2 * MIB),
        cost_estimate=cost(0, 0),
        name="find_sources",
    )(*spread, after)


def turn_pages(sources, halves, chips):
    across = len(halves)
    down = chips // across
    shape = halves[0].shape

    def kernel(source_ref, *refs):
        half_refs, out_refs, sems = refs[:across], refs[across:-1], refs[-1]
        waits = []
        for row in range(1, down):
            for j in range(2):
                source = source_ref[2 * row + j]
                place = jnp.where(source < 2 * across, source, 0)
                for d in range(across):
                    for e in range(2):
                        copy = pltpu.make_async_copy(half_refs[d].at[e], out_refs[row - 1].at[j], sems.at[row - 1, j])

                        @pl.when(place == 2 * d + e)
                        def _():
                            copy.start()

                waits.append(copy)
        for copy in waits:
            copy.wait()

    one = jax.ShapeDtypeStruct(shape, halves[0].dtype)
    return pl.pallas_call(
        kernel,
        out_shape=(one,) * (down - 1),
        in_specs=[SMEM] + [ANY] * across,
        out_specs=(VMEM,) * (down - 1),
        scratch_shapes=[pltpu.SemaphoreType.DMA((down - 1, 2))],
        compiler_params=pltpu.CompilerParams(vmem_limit_bytes=down * 2 * MIB),
        cost_estimate=cost(0, 4 * halves[0].size),
        name="turn_pages",
    )(sources, *halves)


def start_half(source, across, core, half_refs, turned_refs, target, sem):
    place = jnp.where(source < 2 * across, source, 2 * across + source // (2 * across))
    for d, ref in enumerate(half_refs):
        for e in range(2):

            @pl.when(place == 2 * d + e)
            def _():
                pltpu.make_async_copy(ref.at[e], target, sem).start()

    for row, ref in enumerate(turned_refs):

        @pl.when(place == 2 * across + row + 1)
        def _():
            pltpu.make_async_copy(ref.at[core], target, sem).start()


def choose_half(sources, halves, turned):
    across, rows = len(halves), len(turned)

    def kernel(source_ref, *refs):
        half_refs, turned_refs = refs[:across], refs[across : across + rows]
        out_ref, sem = refs[across + rows :]
        start_half(source_ref[1], across, 1, half_refs, turned_refs, out_ref, sem)
        pltpu.make_async_copy(half_refs[0].at[0], out_ref, sem).wait()

    shape = halves[0].shape[1:]
    return pl.pallas_call(
        kernel,
        out_shape=jax.ShapeDtypeStruct(shape, halves[0].dtype),
        in_specs=[SMEM] + [ANY] * (across + rows),
        out_specs=VMEM,
        scratch_shapes=[pltpu.SemaphoreType.DMA],
        compiler_params=pltpu.CompilerParams(vmem_limit_bytes=2 * MIB),
        cost_estimate=cost(0, 2 * halves[0].size),
        name="choose_half",
    )(sources, *halves, *turned)


def project(blocks, weight, later):
    chips = len(blocks)
    slots = blocks[0].shape[1]
    heads, depth, width = weight.shape
    per = 2 if heads % 2 == 0 else 1
    rows = chips * 2 * slots

    def kernel(*refs):
        block_refs = refs[:chips]
        weight_ref, later_ref, keep_ref, send_ref, later_out, left, sem = refs[chips:]
        copy = pltpu.make_async_copy(later_ref, later_out, sem)
        copy.start()
        for d in range(chips):
            for e in range(2):
                row = (d * 2 + e) * slots
                left[row : row + slots, :] = block_refs[d][e, :, META:].astype(F32)
        lhs = left[...].astype(BF16)

        @pl.loop(0, heads // per)
        def _(i):
            right = jnp.concatenate([weight_ref[i * per + j] for j in range(per)], axis=1)
            total = jnp.dot(lhs, right, preferred_element_type=F32)
            columns = pl.ds(pl.multiple_of(i * (per * width), per * width), per * width)
            for d in range(chips):
                row = d * 2 * slots
                keep_ref[d, :, columns] = total[row : row + slots]
                send_ref[d, :, columns] = total[row + slots : row + 2 * slots]

        copy.wait()

    shape = jax.ShapeDtypeStruct((chips, slots, heads * width), F32)
    return pl.pallas_call(
        kernel,
        out_shape=(shape, shape, jax.ShapeDtypeStruct(later.shape, later.dtype)),
        in_specs=[VMEM] * (chips + 1) + [HBM],
        out_specs=(VMEM, VMEM, VMEM),
        scratch_shapes=[pltpu.VMEM((rows, depth), F32), pltpu.SemaphoreType.DMA],
        compiler_params=pltpu.CompilerParams(vmem_limit_bytes=weight.size * 2 + 12 * MIB),
        cost_estimate=cost(2 * rows * weight.size, 2 * weight.size),
        name="project",
    )(*blocks, weight, *in_hbm(later))


def combine(keep, got, after):
    chips, slots, width = keep.shape
    heads = width // (3 * LANES)

    def kernel(keep_ref, got_ref, _, own_ref, *message_refs):
        own_ref[...] = keep_ref[0] + got_ref[0]
        for d in range(1, chips):
            for h in range(heads):
                total = keep_ref[d, :, 3 * h * LANES : 3 * (h + 1) * LANES] + got_ref[d, :, 3 * h * LANES : 3 * (h + 1) * LANES]
                query = total[:, :LANES]
                high = query.astype(BF16)
                low = (query - high.astype(F32)).astype(BF16)
                base = 4 * h * LANES
                message_refs[d - 1][:, base : base + LANES] = high
                message_refs[d - 1][:, base + LANES : base + 2 * LANES] = low
                message_refs[d - 1][:, base + 2 * LANES : base + 4 * LANES] = total[:, LANES:].astype(BF16)

    message = jax.ShapeDtypeStruct((slots, 4 * heads * LANES), BF16)
    return pl.pallas_call(
        kernel,
        out_shape=(jax.ShapeDtypeStruct((slots, width), F32),) + (message,) * (chips - 1),
        in_specs=[VMEM, VMEM, ANY],
        out_specs=(VMEM,) * chips,
        compiler_params=pltpu.CompilerParams(vmem_limit_bytes=8 * MIB),
        cost_estimate=cost(0, 8 * keep.size),
        name="combine",
    )(keep, got, after)


def attend(lengths, new_slot, page_table, sums, bias, tokens, key_pool, value_pool, after):
    parts = len(sums)
    slots = sums[0].shape[0]
    pages, page, width = key_pool.shape
    head = LANES
    heads = width // head
    max_pages = page_table.shape[1]
    chunk_pages = 4
    chunk = chunk_pages * page
    chunks = max_pages // chunk_pages
    long_rows = max_pages * page
    short_rows = slots * page
    groups = 2 * parts
    share = head // groups
    per = LANES // share
    tall = 16
    strips = width // PACK
    scale = head ** (-0.5)

    def kernel(*refs):
        length_ref, slot_ref, table_ref = refs[:3]
        sum_refs = refs[3 : 3 + parts]
        (bias_ref, token_ref, key_ref, value_ref, _, pack_keep, pack_send, patch_ref, key_out, value_out) = refs[
            3 + parts : 13 + parts
        ]
        score_buffer, mix_buffer, out_sems = refs[13 + parts :]
        step = pages // 4
        writes = [
            pltpu.make_async_copy(source.at[pl.ds(i * step, step)], target.at[pl.ds(i * step, step)], out_sems.at[n, i])
            for n, (source, target) in enumerate(((key_ref, key_out), (value_ref, value_out)))
            for i in range(4)
        ]
        for write in writes:
            write.start()
        here = lax.axis_index("req")
        column_block = lax.axis_index("head")
        leaving = leaving_slot(slot_ref, slots, here)
        lengths = [length_ref[s] for s in range(slots)]
        long_slot = jnp.int32(0)
        long_length = jnp.int32(0)
        for s in range(slots):
            is_long = lengths[s] >= page
            long_slot = jnp.where(is_long, s, long_slot)
            long_length = jnp.where(is_long, lengths[s], long_length)
        turns = (long_length + chunk - 1) // chunk

        total = sum_refs[0][...] + bias_ref[...]

        def third(k):
            columns = []
            for h in range(heads):
                one = total[:, (3 * h + k) * head : (3 * h + k + 1) * head]
                for ref in sum_refs[1:]:
                    base = 4 * h * head
                    if k == 0:
                        one = one + ref[:, base : base + head].astype(F32) + ref[:, base + head : base + 2 * head].astype(F32)
                    else:
                        one = one + ref[:, base + (k + 1) * head : base + (k + 2) * head].astype(F32)
                columns.append(one)
            return jnp.concatenate(columns, axis=1)

        query = (third(0) * scale).astype(BF16).astype(F32)
        new_rows = (third(1).astype(BF16).astype(F32), third(2).astype(BF16).astype(F32))

        lane_head = lax.broadcasted_iota(jnp.int32, (tall, width), 1) // head
        on_head = lane_head == lax.broadcasted_iota(jnp.int32, (tall, width), 0)

        def blocked(row):
            return jnp.where(on_head, jnp.broadcast_to(row, (tall, width)), 0.0).astype(BF16)

        def for_slot(which, rows):
            found = rows[0]
            for s in range(1, slots):
                found = jnp.where(which == s, rows[s], found)
            return found

        def softmax(scores, valid, new_score):
            masked = jnp.where(valid, scores, -1e30)
            peak = jnp.maximum(jnp.max(masked, axis=1, keepdims=True), new_score)
            weights = jnp.where(valid, jnp.exp(masked - peak), 0.0)
            new_weight = jnp.exp(new_score - peak)
            denom = jnp.sum(weights, axis=1, keepdims=True) + new_weight
            return weights.astype(BF16), new_weight.astype(BF16).astype(F32), denom

        across = (((1,), (1,)), ((), ()))
        short_query = jnp.concatenate([blocked(query[s : s + 1]) for s in range(slots)], axis=0)
        new_keys = jnp.concatenate([new_rows[0], jnp.zeros((tall - slots, width), F32)], axis=0).astype(BF16)
        new_scores = lax.dot_general(short_query, new_keys, across, preferred_element_type=F32)
        size = (slots * tall, tall)
        own_column = lax.broadcasted_iota(jnp.int32, size, 0) // tall == lax.broadcasted_iota(jnp.int32, size, 1)
        new_score = jnp.sum(jnp.where(own_column, new_scores, 0.0), axis=1, keepdims=True)

        first_pages = lambda ref: jnp.concatenate([ref[table_ref[s, 0]] for s in range(slots)], axis=0)
        short_scores = lax.dot_general(short_query, first_pages(key_ref), across, preferred_element_type=F32)
        size = (slots * tall, short_rows)
        row_slot = lax.broadcasted_iota(jnp.int32, size, 0) // tall
        column = lax.broadcasted_iota(jnp.int32, size, 1)
        limit = jnp.zeros(size, jnp.int32)
        for s in range(slots):
            limit = jnp.where(row_slot == s, lengths[s], limit)
        valid = (row_slot == column // page) & (column % page < limit)
        short_probs, new_prob, short_denom = softmax(short_scores, valid, new_score)
        new_values = jnp.concatenate(
            [jnp.broadcast_to(new_rows[1][s : s + 1], (tall, width)) for s in range(slots)], axis=0
        )
        short_mix = jnp.dot(short_probs, first_pages(value_ref), preferred_element_type=F32)
        short_mix = (short_mix + new_prob * new_values) / short_denom

        mix_buffer[...] = jnp.zeros(mix_buffer.shape, F32)

        @pl.when(turns > 0)
        def _():
            some_pages = lambda ref, c: jnp.concatenate(
                [ref[table_ref[long_slot, c * chunk_pages + i]] for i in range(chunk_pages)], axis=0
            )
            long_query = blocked(for_slot(long_slot, [query[s : s + 1] for s in range(slots)]))
            long_new = for_slot(long_slot, [new_score[s * tall : (s + 1) * tall] for s in range(slots)])
            long_value = for_slot(long_slot, [new_rows[1][s : s + 1] for s in range(slots)])
            for c in range(chunks):

                @pl.when(c < turns)
                def _():
                    score_buffer[:, c * chunk : (c + 1) * chunk] = lax.dot_general(
                        long_query, some_pages(key_ref, c), across, preferred_element_type=F32
                    )

                @pl.when(c >= turns)
                def _():
                    score_buffer[:, c * chunk : (c + 1) * chunk] = jnp.zeros((tall, chunk), F32)

            position = lax.broadcasted_iota(jnp.int32, (tall, long_rows), 1)
            long_probs, long_prob, long_denom = softmax(score_buffer[...], position < long_length, long_new)
            for c in range(chunks):

                @pl.when(c < turns)
                def _():
                    mix_buffer[...] += jnp.dot(
                        long_probs[:, c * chunk : (c + 1) * chunk], some_pages(value_ref, c), preferred_element_type=F32
                    )

            mix_buffer[...] = (mix_buffer[...] + long_prob * long_value) / long_denom

        def fold(mixed):
            return jnp.sum(jnp.where(on_head, mixed, 0.0), axis=0, keepdims=True)

        long_mix = fold(mix_buffer[...])
        rows = []
        for s in range(slots):
            row = fold(short_mix[s * tall : (s + 1) * tall])
            rows.append(jnp.where(lengths[s] >= page, long_mix, row))
        high = -(-slots // 8) * 8
        attended = jnp.concatenate(rows + [jnp.zeros((high - slots, width), F32)], axis=0).astype(BF16).astype(F32)

        token = token_ref[:, pl.ds(pl.multiple_of(column_block * width, LANES), width)].astype(F32)
        extra = []
        for source in new_rows + (token,):
            one = jnp.zeros((1, width), F32)
            for s in range(slots):
                one = jnp.where(leaving == s, source[s : s + 1], one)
            extra += [one[:, i * PACK : (i + 1) * PACK] for i in range(strips)]
        extra = jnp.concatenate(extra + [jnp.zeros((pack_rows(slots, strips) - high - 3 * strips, PACK), F32)], axis=0)

        lane = lax.broadcasted_iota(jnp.int32, (high, LANES), 1)
        row_at = lax.broadcasted_iota(jnp.int32, (high, LANES), 0)
        goal = jnp.full((high, LANES), -1.0, F32)
        for s in range(slots):
            device, slot = slot_ref[s] // slots, slot_ref[s] % slots
            number = jnp.where(lane % share == share - 1, slot, device).astype(F32)
            goal = jnp.where(row_at == s, number, goal)
        turned = [
            pltpu.roll(attended[:, h * head : (h + 1) * head], h % per * share, 1) if h % per else attended[:, h * head : (h + 1) * head]
            for h in range(heads)
        ]
        for k in range(groups):
            count = lax.rem(lane // share - (here ^ k) + per, per)
            tiles = [jnp.zeros((high, LANES), F32) for _ in range(PACK // LANES)]
            for h in range(heads):
                tiles[h // per] = jnp.where(count == h % per, turned[h], tiles[h // per])
            tiles[-1] = jnp.where((count == per - 1) & (lane % share >= share - 2), goal, tiles[-1])
            block = jnp.concatenate([jnp.concatenate(tiles, axis=1), extra], axis=0).astype(BF16)
            (pack_keep, pack_send)[k % 2][k // 2] = block

        at = lax.broadcasted_iota(jnp.int32, (tall, width), 0)
        for n, ref in enumerate((key_ref, value_ref)):
            for s in range(slots):
                offset = lengths[s] % page
                first = pl.multiple_of(offset // tall * tall, tall)
                old = ref[table_ref[s, lengths[s] // page], pl.ds(first, tall), :].astype(F32)
                new = jnp.broadcast_to(new_rows[n][s : s + 1], (tall, width))
                patch_ref[n, s] = jnp.where(at == offset - first, new, old).astype(BF16)

        for write in writes:
            write.wait()

    packed = jax.ShapeDtypeStruct((parts, pack_rows(slots, strips), PACK), BF16)
    pool = jax.ShapeDtypeStruct(key_pool.shape, key_pool.dtype)
    return pl.pallas_call(
        kernel,
        out_shape=(packed, packed, jax.ShapeDtypeStruct((2, slots, tall, width), BF16), pool, pool),
        in_specs=[SMEM] * 3 + [VMEM] * (parts + 4) + [ANY],
        out_specs=(VMEM, VMEM, VMEM, HBM, HBM),
        scratch_shapes=[
            pltpu.VMEM((tall, long_rows), F32),
            pltpu.VMEM((tall, width), F32),
            pltpu.SemaphoreType.DMA((2, 4)),
        ],
        compiler_params=pltpu.CompilerParams(vmem_limit_bytes=18 * MIB),
        cost_estimate=cost(4 * tall * (long_rows + short_rows) * width, 4 * (long_rows + short_rows) * width),
        name="attend",
    )(lengths, new_slot, page_table, *sums, bias, tokens, key_pool, value_pool, after)


def pack_rows(slots, strips):
    need = -(-slots // 8) * 8 + 3 * strips
    return -(-need // 16) * 16


def out_project(blocks, weight, pieces, slots, *after):
    chips = len(blocks)
    depth, width = weight.shape
    high = -(-slots // 8) * 8
    rows = 2 * chips * slots
    piece = width // pieces

    def kernel(*refs):
        block_refs, weight_ref = refs[:chips], refs[chips]
        keep_ref, send_ref = refs[chips + 1 + len(after) :]
        gathered = jnp.concatenate(
            [block_refs[d][e, :high, :].astype(F32) for d in range(chips) for e in range(2)], axis=0
        )
        here = lax.axis_index("req")
        share = LANES // (2 * chips)
        back = lax.rem(LANES - here * share, LANES)
        gathered = jnp.concatenate(
            [pltpu.roll(gathered[:, first : first + LANES], back, 1) for first in range(0, PACK, LANES)], axis=1
        )
        goal = gathered[:, PACK - 2 : PACK - 1].astype(jnp.int32)
        place = goal ^ here
        row = (place % 2) * (chips * slots) + (place // 2) * slots + gathered[:, PACK - 1 :].astype(jnp.int32)
        row = jnp.where(goal < 0, -1, row)
        size = (gathered.shape[0], rows)
        order = jnp.where(lax.broadcasted_iota(jnp.int32, size, 1) == row, 1.0, 0.0)
        left = lax.dot_general(
            order.astype(BF16), gathered.astype(BF16), (((0,), (0,)), ((), ())), preferred_element_type=F32
        )
        left = left[:, :depth].astype(BF16)
        for j in range(pieces):
            first = (lax.axis_index("head") ^ j) * piece
            total = jnp.dot(
                left, weight_ref[:, pl.ds(pl.multiple_of(first, LANES), piece)], preferred_element_type=F32
            )
            for d in range(chips):
                keep_ref[d, j] = total[d * slots : (d + 1) * slots]
                send_ref[d, j] = total[(chips + d) * slots : (chips + d + 1) * slots].astype(BF16)

    shape = (chips, pieces, slots, piece)
    return pl.pallas_call(
        kernel,
        out_shape=(jax.ShapeDtypeStruct(shape, F32), jax.ShapeDtypeStruct(shape, BF16)),
        in_specs=[VMEM] * (chips + 1) + [ANY] * len(after),
        out_specs=(VMEM, VMEM),
        compiler_params=pltpu.CompilerParams(vmem_limit_bytes=10 * MIB),
        cost_estimate=cost(2 * rows * weight.size, 2 * weight.size),
        name="out_project",
    )(*blocks, weight, *after)


def place_page(lengths, new_slot, page_table, sources, patches, packs, tokens, out_bias, halves, turned, from_other, key_out, value_out):
    chips, across, rows = len(packs), len(halves), len(turned)
    down = chips // across
    count = across + rows + 1
    page, width = key_out.shape[1:]
    half = page // 2
    slots = tokens.shape[0]
    high = -(-slots // 8) * 8
    strips = width // PACK

    tall = patches.shape[2]

    def kernel(length_ref, slot_ref, table_ref, source_ref, patch_ref, *refs):
        pack_refs = refs[:chips]
        token_ref, bias_ref = refs[chips : chips + 2]
        half_refs = refs[chips + 2 : chips + 2 + across]
        turned_refs = refs[chips + 2 + across : chips + 2 + across + rows]
        other_ref = refs[chips + 1 + count]
        _, _, base_ref, key_ref, value_ref, buffer, arrived, sems, out_sems, patch_sems = refs[chips + 2 + count :]
        here = lax.axis_index("req")
        leaving = leaving_slot(slot_ref, slots, here)

        def patch(n, s):
            length = length_ref[s]
            first = pl.multiple_of(length % page // tall * tall, tall)
            target = (key_ref, value_ref)[n].at[table_ref[s, length // page], pl.ds(first, tall)]
            return pltpu.make_async_copy(patch_ref.at[n, s], target, patch_sems.at[n, s])

        for n in range(2):
            for s in range(slots):

                @pl.when(leaving != s)
                def _():
                    patch(n, s).start()

        column = pl.multiple_of(lax.axis_index("head") * width, LANES)
        page_at, offset, source = source_ref[2 * down], source_ref[2 * down + 1], source_ref[2 * down + 2]
        targets = [
            buffer.at[:, pl.ds(pl.multiple_of((here % 2 ^ e) * half, half), half)] for e in range(2)
        ]
        start_half(source_ref[0], across, 0, half_refs, turned_refs, targets[0], sems.at[0])
        from_core = pltpu.make_async_copy(other_ref, targets[1], sems.at[1])
        from_core.start()

        for d in range(chips):
            for e in range(2):

                @pl.when(source == 2 * d + e)
                def _():
                    arrived[...] = pack_refs[d][e].astype(F32)

        def fresh(n):
            strip = high + n * strips
            return jnp.concatenate([arrived[strip + i : strip + i + 1, :] for i in range(strips)], axis=1)

        at = lax.broadcasted_iota(jnp.int32, (slots, width), 0)
        token = jnp.where(
            at == leaving,
            jnp.broadcast_to(fresh(2), (slots, width)),
            token_ref[:, pl.ds(column, width)].astype(F32),
        )
        base_ref[...] = token + bias_ref[:, pl.ds(column, width)]
        pltpu.make_async_copy(half_refs[0].at[0], targets[0], sems.at[0]).wait()
        from_core.wait()
        first = pl.multiple_of(offset // 16 * 16, 16)
        row = lax.broadcasted_iota(jnp.int32, (16, width), 0)
        for n in range(2):
            old = buffer[n, pl.ds(first, 16), :].astype(F32)
            new = jnp.broadcast_to(fresh(n), (16, width))
            buffer[n, pl.ds(first, 16), :] = jnp.where(row == offset - first, new, old).astype(BF16)
        copies = [
            pltpu.make_async_copy(buffer.at[n], target.at[page_at], out_sems.at[n])
            for n, target in enumerate((key_ref, value_ref))
        ]
        for copy in copies:
            copy.start()
        for n in range(2):
            for s in range(slots):

                @pl.when(leaving != s)
                def _():
                    patch(n, s).wait()

        for copy in copies:
            copy.wait()

    shape = jax.ShapeDtypeStruct(key_out.shape, key_out.dtype)
    return pl.pallas_call(
        kernel,
        out_shape=(jax.ShapeDtypeStruct((slots, width), F32), shape, shape),
        in_specs=[SMEM] * 4 + [VMEM] * (chips + 3) + [ANY] * count + [HBM] * 2,
        out_specs=(VMEM, HBM, HBM),
        scratch_shapes=[
            pltpu.VMEM((2, page, width), BF16),
            pltpu.VMEM(packs[0].shape[1:], F32),
            pltpu.SemaphoreType.DMA((2,)),
            pltpu.SemaphoreType.DMA((2,)),
            pltpu.SemaphoreType.DMA((2, slots)),
        ],
        input_output_aliases={chips + 7 + count: 1, chips + 8 + count: 2},
        compiler_params=pltpu.CompilerParams(vmem_limit_bytes=4 * MIB),
        cost_estimate=cost(0, 8 * page * width),
        name="place_page",
    )(
        lengths, new_slot, page_table, sources, patches, *packs, tokens, out_bias, *halves, *turned, from_other, key_out, value_out
    )


def body(
    tokens,
    norm_gain,
    norm_shift,
    qkv_weight,
    qkv_bias,
    out_weight,
    out_bias,
    key_pool,
    value_pool,
    lengths,
    page_table,
    new_slot,
    new_page,
):
    groups = lax.axis_size("req")
    head_groups = lax.axis_size("head")
    slots = tokens.shape[0]
    chips = groups // 2

    keep, send, keep_half, send_half = prepare(
        tokens, norm_gain[None], norm_shift[None], lengths, page_table, new_slot, new_page, key_pool, value_pool
    )
    got = swap(send, "req", 1)
    spread = spread_pairs(keep, got)
    across = row_length(chips)
    halves = [jnp.stack([keep_half, swap(send_half, "req", 1)])]
    halves += [swap_pages(halves[0], chips, True, d) for d in range(1, across)]
    flat = out_weight.reshape(-1, out_weight.shape[2])
    keep, send, staged = project(spread, jnp.transpose(qkv_weight, (1, 0, 2)), flat)
    got = swap(send, "req", 1)
    sources = find_sources(spread, keep)
    own, *messages = combine(keep, got, sources)
    turning = turn_pages(sources, halves, chips)
    turned = [swap_pages(one, chips, False, row + 1) for row, one in enumerate(turning)]
    sums = [own] + [swap(messages[d - 1], "req", 2 * d) for d in range(1, chips)]

    pack_keep, pack_send, patches, key_out, value_out = attend(
        lengths,
        new_slot,
        page_table,
        sums,
        qkv_bias.reshape(1, -1),
        tokens,
        key_pool,
        value_pool,
        turning[0],
    )
    packs_got = swap(pack_send, "req", 1)
    packs = spread_pairs(pack_keep, packs_got)

    from_other = swap(choose_half(sources, halves, turned), "req", 1)

    keep, send = out_project(
        packs, staged, head_groups, slots, turned[0]
    )
    total = keep + swap(send, "req", 1).astype(F32)
    summed = total[0]
    for d in range(1, chips):
        summed = summed + swap(total[d].astype(BF16), "req", 2 * d).astype(F32)
    base, key_out, value_out = place_page(
        lengths,
        new_slot,
        page_table,
        sources,
        patches,
        packs,
        tokens,
        out_bias[None],
        halves,
        turned,
        from_other,
        key_out,
        value_out,
    )
    hidden = summed[0]
    for j in range(1, head_groups):
        hidden = hidden + swap(summed[j].astype(BF16), "head", j).astype(F32)
    hidden_out = (hidden + base).astype(BF16)
    return (hidden_out, key_out, value_out)


def solution(mesh):
    in_specs = (
        P("req", None),
        P(),
        P(),
        P("req", "head", None),
        P("head", None),
        P("head", "req", None),
        P(),
        P("req", None, "head"),
        P("req", None, "head"),
        P("req"),
        P("req", None),
        P("req"),
        P("req"),
    )
    out_specs = (P("req", "head"), P("req", None, "head"), P("req", None, "head"))
    return jax.shard_map(body, mesh=mesh, in_specs=in_specs, out_specs=out_specs, check_vma=False)
```

```python
import functools

import jax
import jax.numpy as jnp
from jax import lax
from jax.experimental import pallas as pl
from jax.experimental.pallas import tpu as pltpu
from jax.sharding import PartitionSpec as P

EPSILON = 1e-05
F32 = jnp.float32
BF16 = jnp.bfloat16
LANES = 128
META = 128
PACK = 256
VMEM = pl.BlockSpec(memory_space=pltpu.VMEM)
SMEM = pl.BlockSpec(memory_space=pltpu.SMEM)
ANY = pl.BlockSpec(memory_space=pl.ANY)
HBM = pl.BlockSpec(memory_space=pltpu.HBM)
MIB = 1024 * 1024


def cost(flops, moved):
    del flops, moved
    return pl.CostEstimate(flops=0, bytes_accessed=0, transcendentals=0)


def swap(value, axis, step):
    size = lax.axis_size(axis)
    return lax.ppermute(value, axis, [(i, i ^ step) for i in range(size)])


def spread_pairs(keep, got):
    chips = keep.shape[0]
    return [jnp.stack([keep[0], got[0]])] + [
        swap(jnp.stack([keep[d], got[d]]), "req", 2 * d) for d in range(1, chips)
    ]


def in_hbm(*arrays):
    return [pltpu.with_memory_space_constraint(array, pltpu.HBM) for array in arrays]


def write_pool(pool, after):
    parts = 4
    step = pool.shape[0] // parts

    def kernel(pool_ref, _, out_ref, sems):
        places = [pl.ds(i * step, step) for i in range(parts)]
        copies = [
            pltpu.make_async_copy(pool_ref.at[place], out_ref.at[place], sems.at[i]) for i, place in enumerate(places)
        ]
        for copy in copies:
            copy.start()
        for copy in copies:
            copy.wait()

    return pl.pallas_call(
        kernel,
        out_shape=jax.ShapeDtypeStruct(pool.shape, pool.dtype),
        in_specs=[VMEM, ANY],
        out_specs=HBM,
        scratch_shapes=[pltpu.SemaphoreType.DMA((parts,))],
        compiler_params=pltpu.CompilerParams(vmem_limit_bytes=8 * MIB),
        cost_estimate=cost(0, 2 * pool.size),
        name="write_pool",
    )(pool, after)


def leaving_slot(new_slot_ref, slots, here):
    leaving = jnp.int32(0)
    for s in range(slots):
        leaving = jnp.where(new_slot_ref[s] // slots != here, s, leaving)
    return leaving


def prepare(tokens, gain, shift, lengths, page_table, new_slot, new_page, key_pool, value_pool):
    groups = lax.axis_size("req")
    chips = groups // 2
    slots, model = tokens.shape
    depth = model // groups
    page, width = key_pool.shape[1:]
    half = page // 2

    def kernel(
        token_ref, gain_ref, shift_ref, length_ref, table_ref, slot_ref, page_ref, key_ref, value_ref,
        keep_ref, send_ref, keep_half, send_half, normed, sems,
    ):
        here = lax.axis_index("req")
        leaving = leaving_slot(slot_ref, slots, here)
        copies = []
        for n, source in enumerate((key_ref, value_ref)):
            for e, target in enumerate((keep_half, send_half)):
                rows = pl.ds(pl.multiple_of((here % 2 ^ e) * half, half), half)
                copies.append(
                    pltpu.make_async_copy(source.at[table_ref[leaving, 0], rows], target.at[n], sems.at[n, e])
                )
        for copy in copies:
            copy.start()
        values = token_ref[...].astype(F32)
        average = jnp.mean(values, axis=1, keepdims=True)
        centered = values - average
        variance = jnp.mean(centered * centered, axis=1, keepdims=True)
        rows = centered * lax.rsqrt(variance + EPSILON) * gain_ref[...] + shift_ref[...]
        normed[...] = rows.astype(BF16).astype(F32)
        row = lax.broadcasted_iota(jnp.int32, (slots, META), 0)
        lane = lax.broadcasted_iota(jnp.int32, (slots, META), 1)
        told = jnp.zeros((slots, META), F32)
        for s in range(slots):
            slot = slot_ref[s]
            numbers = (slot // slots, slot % slots, page_ref[s], length_ref[s] % page)
            for j, number in enumerate(numbers):
                told = jnp.where((row == s) & (lane == j), number.astype(F32), told)
        told = told.astype(BF16)
        for k in range(groups):
            first = (here ^ k) * depth
            if depth % LANES == 0:
                block = normed[:, pl.ds(pl.multiple_of(first, LANES), depth)]
            else:
                block = pltpu.roll(normed[...], lax.rem(model - first, model), 1)[:, :depth]
            target = (keep_ref, send_ref)[k % 2]
            target[k // 2, :, :META] = told
            target[k // 2, :, META:] = block.astype(BF16)
        for copy in copies:
            copy.wait()

    blocks = jax.ShapeDtypeStruct((chips, slots, META + depth), BF16)
    halves = jax.ShapeDtypeStruct((2, half, width), key_pool.dtype)
    return pl.pallas_call(
        kernel,
        out_shape=(blocks, blocks, halves, halves),
        in_specs=[VMEM] * 3 + [SMEM] * 4 + [HBM] * 2,
        out_specs=(VMEM,) * 4,
        scratch_shapes=[pltpu.VMEM((slots, model), F32), pltpu.SemaphoreType.DMA((2, 2))],
        compiler_params=pltpu.CompilerParams(vmem_limit_bytes=4 * MIB),
        cost_estimate=cost(0, 8 * page * width),
        name="prepare",
    )(*in_hbm(tokens, gain, shift, lengths, page_table, new_slot, new_page, key_pool, value_pool))


def arrivals(block_refs, here, wanted):
    slots = block_refs[0].shape[1]
    lane = lax.broadcasted_iota(jnp.int32, (slots, META), 1)
    found = jnp.zeros((slots, META), F32)
    goal = here ^ wanted
    for d, ref in enumerate(block_refs):
        for e in range(2):
            k = 2 * d + e
            told = ref[e, :, :META].astype(F32)
            numbered = jnp.where(lane == 4, float(k), told)
            found = jnp.where(told[:, :1] == jnp.where(wanted == k, -1, goal).astype(F32), numbered, found)
    return lambda j: jnp.sum(jnp.where(lane == j, found, 0.0)).astype(jnp.int32)


def row_length(chips):
    return 1 << (chips.bit_length() // 2)


def swap_pages(value, chips, along_row, step):
    across = row_length(chips)
    square = across * across == chips
    steps = [2 * step if along_row == (device % 2 == 0 or not square) else 2 * across * step for device in range(2 * chips)]
    return lax.ppermute(value, "req", [(i, i ^ steps[i]) for i in range(2 * chips)])


def find_sources(spread, after):
    chips = len(spread)
    across = row_length(chips)
    down = chips // across

    def kernel(*refs):
        block_refs, out_ref = refs[:chips], refs[-1]
        here = lax.axis_index("req")
        lane = lax.broadcasted_iota(jnp.int32, (8, LANES), 1)
        found = jnp.zeros((8, LANES), F32)
        put = lambda j, number: jnp.where(lane == j, number.astype(F32), found)
        turned = (here % 2 == 1) & (across == down)
        for row in range(down):
            for j in range(2):
                pick = arrivals(block_refs, here, jnp.where(turned, 2 * row, 2 * across * row) + j)
                source = pick(4)
                chip = source // 2
                chip = jnp.where(turned, chip % across * across + chip // across, chip)
                found = put(2 * row + j, 2 * chip + source % 2)
                if row == 0 and j == 0:
                    found = put(2 * down, pick(2))
                    found = put(2 * down + 1, pick(3))
                    found = put(2 * down + 2, source)
        out_ref[...] = found

    return pl.pallas_call(
        kernel,
        out_shape=jax.ShapeDtypeStruct((8, LANES), F32),
        in_specs=[VMEM] * chips + [ANY],
        out_specs=VMEM,
        compiler_params=pltpu.CompilerParams(vmem_limit_bytes=2 * MIB),
        cost_estimate=cost(0, 0),
        name="find_sources",
    )(*spread, after)


def number_at(source_ref, j):
    lane = lax.broadcasted_iota(jnp.int32, (1, LANES), 1)
    return jnp.sum(jnp.where(lane == j, source_ref[:1, :], 0.0)).astype(jnp.int32)


def turn_pages(sources, halves, chips):
    across = len(halves)
    down = chips // across
    shape = halves[0].shape

    def kernel(source_ref, *refs):
        half_refs, out_refs = refs[:across], refs[across:]
        for row in range(1, down):
            for j in range(2):
                source = number_at(source_ref, 2 * row + j)
                place = jnp.where(source < 2 * across, source, 0)
                for d in range(across):
                    for e in range(2):

                        @pl.when(place == 2 * d + e)
                        def _():
                            out_refs[row - 1][j] = half_refs[d][e]

    one = jax.ShapeDtypeStruct(shape, halves[0].dtype)
    return pl.pallas_call(
        kernel,
        out_shape=(one,) * (down - 1),
        in_specs=[VMEM] * (1 + across),
        out_specs=(VMEM,) * (down - 1),
        compiler_params=pltpu.CompilerParams(vmem_limit_bytes=(across + down) * MIB),
        cost_estimate=cost(0, 4 * halves[0].size),
        name="turn_pages",
    )(sources, *halves)


def with_half(source, across, core, half_refs, turned_refs, use):
    place = jnp.where(source < 2 * across, source, 2 * across + source // (2 * across))
    for d, ref in enumerate(half_refs):
        for e in range(2):

            @pl.when(place == 2 * d + e)
            def _():
                use(ref.at[e])

    for row, ref in enumerate(turned_refs):

        @pl.when(place == 2 * across + row + 1)
        def _():
            use(ref.at[core])


def choose_half(sources, halves, turned, after):
    across, rows = len(halves), len(turned)

    def kernel(source_ref, *refs):
        half_refs, turned_refs = refs[:across], refs[across : across + rows]
        out_ref = refs[-1]

        def use(ref):
            out_ref[...] = ref[...]

        with_half(number_at(source_ref, 1), across, 1, half_refs, turned_refs, use)

    shape = halves[0].shape[1:]
    return pl.pallas_call(
        kernel,
        out_shape=jax.ShapeDtypeStruct(shape, halves[0].dtype),
        in_specs=[VMEM] * (1 + across + rows) + [ANY],
        out_specs=VMEM,
        compiler_params=pltpu.CompilerParams(vmem_limit_bytes=(1 + across + rows) * MIB),
        cost_estimate=cost(0, 2 * halves[0].size),
        name="choose_half",
    )(sources, *halves, *turned, after)


def project(blocks, weight, later):
    chips = len(blocks)
    slots = blocks[0].shape[1]
    heads, depth, width = weight.shape
    per = 2 if heads % 2 == 0 else 1
    rows = chips * 2 * slots

    def kernel(*refs):
        block_refs = refs[:chips]
        weight_ref, later_ref, keep_ref, send_ref, later_out, left, sem = refs[chips:]
        copy = pltpu.make_async_copy(later_ref, later_out, sem)
        copy.start()
        for d in range(chips):
            for e in range(2):
                row = (d * 2 + e) * slots
                left[row : row + slots, :] = block_refs[d][e, :, META:].astype(F32)
        lhs = left[...].astype(BF16)

        @pl.loop(0, heads // per)
        def _(i):
            right = jnp.concatenate([weight_ref[i * per + j] for j in range(per)], axis=1)
            total = jnp.dot(lhs, right, preferred_element_type=F32)
            columns = pl.ds(pl.multiple_of(i * (per * width), per * width), per * width)
            for d in range(chips):
                row = d * 2 * slots
                keep_ref[d, :, columns] = total[row : row + slots]
                send_ref[d, :, columns] = total[row + slots : row + 2 * slots]

        copy.wait()

    shape = jax.ShapeDtypeStruct((chips, slots, heads * width), F32)
    return pl.pallas_call(
        kernel,
        out_shape=(shape, shape, jax.ShapeDtypeStruct(later.shape, later.dtype)),
        in_specs=[VMEM] * (chips + 1) + [HBM],
        out_specs=(VMEM, VMEM, VMEM),
        scratch_shapes=[pltpu.VMEM((rows, depth), F32), pltpu.SemaphoreType.DMA],
        compiler_params=pltpu.CompilerParams(vmem_limit_bytes=weight.size * 2 + 12 * MIB),
        cost_estimate=cost(2 * rows * weight.size, 2 * weight.size),
        name="project",
    )(*blocks, weight, *in_hbm(later))


def combine(keep, got, after):
    chips, slots, width = keep.shape
    heads = width // (3 * LANES)

    def kernel(keep_ref, got_ref, _, own_ref, *message_refs):
        own_ref[...] = keep_ref[0] + got_ref[0]
        for d in range(1, chips):
            for h in range(heads):
                total = keep_ref[d, :, 3 * h * LANES : 3 * (h + 1) * LANES] + got_ref[d, :, 3 * h * LANES : 3 * (h + 1) * LANES]
                query = total[:, :LANES]
                high = query.astype(BF16)
                low = (query - high.astype(F32)).astype(BF16)
                base = 4 * h * LANES
                message_refs[d - 1][:, base : base + LANES] = high
                message_refs[d - 1][:, base + LANES : base + 2 * LANES] = low
                message_refs[d - 1][:, base + 2 * LANES : base + 4 * LANES] = total[:, LANES:].astype(BF16)

    message = jax.ShapeDtypeStruct((slots, 4 * heads * LANES), BF16)
    return pl.pallas_call(
        kernel,
        out_shape=(jax.ShapeDtypeStruct((slots, width), F32),) + (message,) * (chips - 1),
        in_specs=[VMEM, VMEM, ANY],
        out_specs=(VMEM,) * chips,
        compiler_params=pltpu.CompilerParams(vmem_limit_bytes=8 * MIB),
        cost_estimate=cost(0, 8 * keep.size),
        name="combine",
    )(keep, got, after)


def attend(lengths, new_slot, page_table, sums, bias, tokens, key_pool, value_pool, after):
    parts = len(sums)
    slots = sums[0].shape[0]
    pages, page, width = key_pool.shape
    head = LANES
    heads = width // head
    max_pages = page_table.shape[1]
    chunk_pages = 4
    chunk = chunk_pages * page
    chunks = max_pages // chunk_pages
    long_rows = max_pages * page
    short_rows = slots * page
    groups = 2 * parts
    share = head // groups
    per = LANES // share
    tall = 16
    strips = width // PACK
    scale = head ** (-0.5)

    def kernel(*refs):
        length_ref, slot_ref, table_ref = refs[:3]
        sum_refs = refs[3 : 3 + parts]
        (bias_ref, token_ref, key_ref, value_ref, _, pack_keep, pack_send, patch_ref, value_out) = refs[
            3 + parts : 12 + parts
        ]
        score_buffer, mix_buffer, out_sems = refs[12 + parts :]
        step = pages // 4
        writes = [
            pltpu.make_async_copy(value_ref.at[pl.ds(i * step, step)], value_out.at[pl.ds(i * step, step)], out_sems.at[i])
            for i in range(4)
        ]
        for write in writes:
            write.start()
        here = lax.axis_index("req")
        column_block = lax.axis_index("head")
        leaving = leaving_slot(slot_ref, slots, here)
        lengths = [length_ref[s] for s in range(slots)]
        long_slot = jnp.int32(0)
        long_length = jnp.int32(0)
        for s in range(slots):
            is_long = lengths[s] >= page
            long_slot = jnp.where(is_long, s, long_slot)
            long_length = jnp.where(is_long, lengths[s], long_length)
        turns = (long_length + chunk - 1) // chunk

        total = sum_refs[0][...] + bias_ref[...]

        def third(k):
            columns = []
            for h in range(heads):
                one = total[:, (3 * h + k) * head : (3 * h + k + 1) * head]
                for ref in sum_refs[1:]:
                    base = 4 * h * head
                    if k == 0:
                        one = one + ref[:, base : base + head].astype(F32) + ref[:, base + head : base + 2 * head].astype(F32)
                    else:
                        one = one + ref[:, base + (k + 1) * head : base + (k + 2) * head].astype(F32)
                columns.append(one)
            return jnp.concatenate(columns, axis=1)

        query = (third(0) * scale).astype(BF16).astype(F32)
        new_rows = (third(1).astype(BF16).astype(F32), third(2).astype(BF16).astype(F32))

        lane_head = lax.broadcasted_iota(jnp.int32, (tall, width), 1) // head
        on_head = lane_head == lax.broadcasted_iota(jnp.int32, (tall, width), 0)

        def blocked(row):
            return jnp.where(on_head, jnp.broadcast_to(row, (tall, width)), 0.0).astype(BF16)

        def for_slot(which, rows):
            found = rows[0]
            for s in range(1, slots):
                found = jnp.where(which == s, rows[s], found)
            return found

        def softmax(scores, valid, new_score):
            masked = jnp.where(valid, scores, -1e30)
            peak = jnp.maximum(jnp.max(masked, axis=1, keepdims=True), new_score)
            weights = jnp.where(valid, jnp.exp(masked - peak), 0.0)
            new_weight = jnp.exp(new_score - peak)
            denom = jnp.sum(weights, axis=1, keepdims=True) + new_weight
            return weights.astype(BF16), new_weight.astype(BF16).astype(F32), denom

        across = (((1,), (1,)), ((), ()))
        short_query = jnp.concatenate([blocked(query[s : s + 1]) for s in range(slots)], axis=0)
        new_keys = jnp.concatenate([new_rows[0], jnp.zeros((tall - slots, width), F32)], axis=0).astype(BF16)
        new_scores = lax.dot_general(short_query, new_keys, across, preferred_element_type=F32)
        size = (slots * tall, tall)
        own_column = lax.broadcasted_iota(jnp.int32, size, 0) // tall == lax.broadcasted_iota(jnp.int32, size, 1)
        new_score = jnp.sum(jnp.where(own_column, new_scores, 0.0), axis=1, keepdims=True)

        first_pages = lambda ref: jnp.concatenate([ref[table_ref[s, 0]] for s in range(slots)], axis=0)
        short_scores = lax.dot_general(short_query, first_pages(key_ref), across, preferred_element_type=F32)
        size = (slots * tall, short_rows)
        row_slot = lax.broadcasted_iota(jnp.int32, size, 0) // tall
        column = lax.broadcasted_iota(jnp.int32, size, 1)
        limit = jnp.zeros(size, jnp.int32)
        for s in range(slots):
            limit = jnp.where(row_slot == s, lengths[s], limit)
        valid = (row_slot == column // page) & (column % page < limit)
        short_probs, new_prob, short_denom = softmax(short_scores, valid, new_score)
        new_values = jnp.concatenate(
            [jnp.broadcast_to(new_rows[1][s : s + 1], (tall, width)) for s in range(slots)], axis=0
        )
        short_mix = jnp.dot(short_probs, first_pages(value_ref), preferred_element_type=F32)
        short_mix = (short_mix + new_prob * new_values) / short_denom

        mix_buffer[...] = jnp.zeros(mix_buffer.shape, F32)

        @pl.when(turns > 0)
        def _():
            some_pages = lambda ref, c: jnp.concatenate(
                [ref[table_ref[long_slot, c * chunk_pages + i]] for i in range(chunk_pages)], axis=0
            )
            long_query = blocked(for_slot(long_slot, [query[s : s + 1] for s in range(slots)]))
            long_new = for_slot(long_slot, [new_score[s * tall : (s + 1) * tall] for s in range(slots)])
            long_value = for_slot(long_slot, [new_rows[1][s : s + 1] for s in range(slots)])
            for c in range(chunks):

                @pl.when(c < turns)
                def _():
                    score_buffer[:, c * chunk : (c + 1) * chunk] = lax.dot_general(
                        long_query, some_pages(key_ref, c), across, preferred_element_type=F32
                    )

                @pl.when(c >= turns)
                def _():
                    score_buffer[:, c * chunk : (c + 1) * chunk] = jnp.zeros((tall, chunk), F32)

            position = lax.broadcasted_iota(jnp.int32, (tall, long_rows), 1)
            long_probs, long_prob, long_denom = softmax(score_buffer[...], position < long_length, long_new)
            for c in range(chunks):

                @pl.when(c < turns)
                def _():
                    mix_buffer[...] += jnp.dot(
                        long_probs[:, c * chunk : (c + 1) * chunk], some_pages(value_ref, c), preferred_element_type=F32
                    )

            mix_buffer[...] = (mix_buffer[...] + long_prob * long_value) / long_denom

        def fold(mixed):
            return jnp.sum(jnp.where(on_head, mixed, 0.0), axis=0, keepdims=True)

        long_mix = fold(mix_buffer[...])
        rows = []
        for s in range(slots):
            row = fold(short_mix[s * tall : (s + 1) * tall])
            rows.append(jnp.where(lengths[s] >= page, long_mix, row))
        high = -(-slots // 8) * 8
        attended = jnp.concatenate(rows + [jnp.zeros((high - slots, width), F32)], axis=0).astype(BF16).astype(F32)

        token = token_ref[:, pl.ds(pl.multiple_of(column_block * width, LANES), width)].astype(F32)
        extra = []
        for source in new_rows + (token,):
            one = jnp.zeros((1, width), F32)
            for s in range(slots):
                one = jnp.where(leaving == s, source[s : s + 1], one)
            extra += [one[:, i * PACK : (i + 1) * PACK] for i in range(strips)]
        extra = jnp.concatenate(extra + [jnp.zeros((pack_rows(slots, strips) - high - 3 * strips, PACK), F32)], axis=0)

        lane = lax.broadcasted_iota(jnp.int32, (high, LANES), 1)
        row_at = lax.broadcasted_iota(jnp.int32, (high, LANES), 0)
        goal = jnp.full((high, LANES), -1.0, F32)
        for s in range(slots):
            device, slot = slot_ref[s] // slots, slot_ref[s] % slots
            number = jnp.where(lane % share == share - 1, slot, device).astype(F32)
            goal = jnp.where(row_at == s, number, goal)
        turned = [
            pltpu.roll(attended[:, h * head : (h + 1) * head], h % per * share, 1) if h % per else attended[:, h * head : (h + 1) * head]
            for h in range(heads)
        ]
        for k in range(groups):
            count = lax.rem(lane // share - (here ^ k) + per, per)
            tiles = [jnp.zeros((high, LANES), F32) for _ in range(PACK // LANES)]
            for h in range(heads):
                tiles[h // per] = jnp.where(count == h % per, turned[h], tiles[h // per])
            tiles[-1] = jnp.where((count == per - 1) & (lane % share >= share - 2), goal, tiles[-1])
            block = jnp.concatenate([jnp.concatenate(tiles, axis=1), extra], axis=0).astype(BF16)
            (pack_keep, pack_send)[k % 2][k // 2] = block

        at = lax.broadcasted_iota(jnp.int32, (tall, width), 0)
        for n, ref in enumerate((key_ref, value_ref)):
            for s in range(slots):
                offset = lengths[s] % page
                first = pl.multiple_of(offset // tall * tall, tall)
                old = ref[table_ref[s, lengths[s] // page], pl.ds(first, tall), :].astype(F32)
                new = jnp.broadcast_to(new_rows[n][s : s + 1], (tall, width))
                patch_ref[n, s] = jnp.where(at == offset - first, new, old).astype(BF16)

        for write in writes:
            write.wait()

    packed = jax.ShapeDtypeStruct((parts, pack_rows(slots, strips), PACK), BF16)
    pool = jax.ShapeDtypeStruct(key_pool.shape, key_pool.dtype)
    return pl.pallas_call(
        kernel,
        out_shape=(packed, packed, jax.ShapeDtypeStruct((2, slots, tall, width), BF16), pool),
        in_specs=[SMEM] * 3 + [VMEM] * (parts + 4) + [ANY],
        out_specs=(VMEM, VMEM, VMEM, HBM),
        scratch_shapes=[
            pltpu.VMEM((tall, long_rows), F32),
            pltpu.VMEM((tall, width), F32),
            pltpu.SemaphoreType.DMA((4,)),
        ],
        compiler_params=pltpu.CompilerParams(vmem_limit_bytes=18 * MIB),
        cost_estimate=cost(4 * tall * (long_rows + short_rows) * width, 4 * (long_rows + short_rows) * width),
        name="attend",
    )(lengths, new_slot, page_table, *sums, bias, tokens, key_pool, value_pool, after)


def pack_rows(slots, strips):
    need = -(-slots // 8) * 8 + 3 * strips
    return -(-need // 16) * 16


def out_project(blocks, weight, pieces, slots, *after):
    chips = len(blocks)
    depth, width = weight.shape
    high = -(-slots // 8) * 8
    rows = 2 * chips * slots
    piece = width // pieces

    def kernel(*refs):
        block_refs, weight_ref = refs[:chips], refs[chips]
        keep_ref, send_ref = refs[chips + 1 + len(after) :]
        gathered = jnp.concatenate(
            [block_refs[d][e, :high, :].astype(F32) for d in range(chips) for e in range(2)], axis=0
        )
        here = lax.axis_index("req")
        share = LANES // (2 * chips)
        back = lax.rem(LANES - here * share, LANES)
        gathered = jnp.concatenate(
            [pltpu.roll(gathered[:, first : first + LANES], back, 1) for first in range(0, PACK, LANES)], axis=1
        )
        goal = gathered[:, PACK - 2 : PACK - 1].astype(jnp.int32)
        place = goal ^ here
        row = (place % 2) * (chips * slots) + (place // 2) * slots + gathered[:, PACK - 1 :].astype(jnp.int32)
        row = jnp.where(goal < 0, -1, row)
        size = (gathered.shape[0], rows)
        order = jnp.where(lax.broadcasted_iota(jnp.int32, size, 1) == row, 1.0, 0.0)
        left = lax.dot_general(
            order.astype(BF16), gathered.astype(BF16), (((0,), (0,)), ((), ())), preferred_element_type=F32
        )
        left = left[:, :depth].astype(BF16)
        for j in range(pieces):
            first = (lax.axis_index("head") ^ j) * piece
            total = jnp.dot(
                left, weight_ref[:, pl.ds(pl.multiple_of(first, LANES), piece)], preferred_element_type=F32
            )
            for d in range(chips):
                keep_ref[d, j] = total[d * slots : (d + 1) * slots]
                send_ref[d, j] = total[(chips + d) * slots : (chips + d + 1) * slots].astype(BF16)

    shape = (chips, pieces, slots, piece)
    return pl.pallas_call(
        kernel,
        out_shape=(jax.ShapeDtypeStruct(shape, F32), jax.ShapeDtypeStruct(shape, BF16)),
        in_specs=[VMEM] * (chips + 1) + [HBM] * min(1, len(after)) + [ANY] * (len(after) - 1),
        out_specs=(VMEM, VMEM),
        compiler_params=pltpu.CompilerParams(vmem_limit_bytes=10 * MIB),
        cost_estimate=cost(2 * rows * weight.size, 2 * weight.size),
        name="out_project",
    )(*blocks, weight, *after)


def place_page(lengths, new_slot, page_table, sources, patches, packs, tokens, out_bias, halves, turned, from_other, key_out, value_out):
    chips, across, rows = len(packs), len(halves), len(turned)
    down = chips // across
    count = across + rows + 1
    page, width = key_out.shape[1:]
    half = page // 2
    slots = tokens.shape[0]
    high = -(-slots // 8) * 8
    strips = width // PACK

    tall = patches.shape[2]

    def kernel(length_ref, slot_ref, table_ref, source_ref, patch_ref, *refs):
        pack_refs = refs[:chips]
        token_ref, bias_ref = refs[chips : chips + 2]
        half_refs = refs[chips + 2 : chips + 2 + across]
        turned_refs = refs[chips + 2 + across : chips + 2 + across + rows]
        other_ref = refs[chips + 1 + count]
        _, _, base_ref, key_ref, value_ref, buffer, arrived, out_sems, patch_sems = refs[chips + 2 + count :]
        here = lax.axis_index("req")
        leaving = leaving_slot(slot_ref, slots, here)

        def patch(n, s):
            length = length_ref[s]
            first = pl.multiple_of(length % page // tall * tall, tall)
            target = (key_ref, value_ref)[n].at[table_ref[s, length // page], pl.ds(first, tall)]
            return pltpu.make_async_copy(patch_ref.at[n, s], target, patch_sems.at[n, s])

        for n in range(2):
            for s in range(slots):

                @pl.when(leaving != s)
                def _():
                    patch(n, s).start()

        column = pl.multiple_of(lax.axis_index("head") * width, LANES)
        page_at, offset, source = [number_at(source_ref, 2 * down + j) for j in range(3)]
        own_rows, other_rows = [pl.ds(pl.multiple_of((here % 2 ^ e) * half, half), half) for e in range(2)]

        def use(ref):
            buffer[:, own_rows, :] = ref[...]

        with_half(number_at(source_ref, 0), across, 0, half_refs, turned_refs, use)
        buffer[:, other_rows, :] = other_ref[...]
        for d in range(chips):
            for e in range(2):

                @pl.when(source == 2 * d + e)
                def _():
                    arrived[...] = pack_refs[d][e].astype(F32)

        def fresh(n):
            strip = high + n * strips
            return jnp.concatenate([arrived[strip + i : strip + i + 1, :] for i in range(strips)], axis=1)

        at = lax.broadcasted_iota(jnp.int32, (slots, width), 0)
        token = jnp.where(
            at == leaving,
            jnp.broadcast_to(fresh(2), (slots, width)),
            token_ref[:, pl.ds(column, width)].astype(F32),
        )
        base_ref[...] = token + bias_ref[:, pl.ds(column, width)]
        first = pl.multiple_of(offset // 16 * 16, 16)
        row = lax.broadcasted_iota(jnp.int32, (16, width), 0)
        for n in range(2):
            old = buffer[n, pl.ds(first, 16), :].astype(F32)
            new = jnp.broadcast_to(fresh(n), (16, width))
            buffer[n, pl.ds(first, 16), :] = jnp.where(row == offset - first, new, old).astype(BF16)
        copies = [
            pltpu.make_async_copy(buffer.at[n], target.at[page_at], out_sems.at[n])
            for n, target in enumerate((key_ref, value_ref))
        ]
        for copy in copies:
            copy.start()
        for n in range(2):
            for s in range(slots):

                @pl.when(leaving != s)
                def _():
                    patch(n, s).wait()

        for copy in copies:
            copy.wait()

    shape = jax.ShapeDtypeStruct(key_out.shape, key_out.dtype)
    return pl.pallas_call(
        kernel,
        out_shape=(jax.ShapeDtypeStruct((slots, width), F32), shape, shape),
        in_specs=[SMEM] * 3 + [VMEM] * (chips + 4 + count) + [HBM] * 2,
        out_specs=(VMEM, HBM, HBM),
        scratch_shapes=[
            pltpu.VMEM((2, page, width), BF16),
            pltpu.VMEM(packs[0].shape[1:], F32),
            pltpu.SemaphoreType.DMA((2,)),
            pltpu.SemaphoreType.DMA((2, slots)),
        ],
        input_output_aliases={chips + 7 + count: 1, chips + 8 + count: 2},
        compiler_params=pltpu.CompilerParams(vmem_limit_bytes=(6 + count) * MIB),
        cost_estimate=cost(0, 8 * page * width),
        name="place_page",
    )(
        lengths, new_slot, page_table, sources, patches, *packs, tokens, out_bias, *halves, *turned, from_other, key_out, value_out
    )


def body(
    tokens,
    norm_gain,
    norm_shift,
    qkv_weight,
    qkv_bias,
    out_weight,
    out_bias,
    key_pool,
    value_pool,
    lengths,
    page_table,
    new_slot,
    new_page,
):
    groups = lax.axis_size("req")
    head_groups = lax.axis_size("head")
    slots = tokens.shape[0]
    chips = groups // 2

    keep, send, keep_half, send_half = prepare(
        tokens, norm_gain[None], norm_shift[None], lengths, page_table, new_slot, new_page, key_pool, value_pool
    )
    got = swap(send, "req", 1)
    spread = spread_pairs(keep, got)
    across = row_length(chips)
    halves = [jnp.stack([keep_half, swap(send_half, "req", 1)])]
    halves += [swap_pages(halves[0], chips, True, d) for d in range(1, across)]
    flat = out_weight.reshape(-1, out_weight.shape[2])
    keep, send, staged = project(spread, jnp.transpose(qkv_weight, (1, 0, 2)), flat)
    got = swap(send, "req", 1)
    sources = find_sources(spread, keep)
    own, *messages = combine(keep, got, sources)
    turning = turn_pages(sources, halves, chips)
    turned = [swap_pages(one, chips, False, row + 1) for row, one in enumerate(turning)]
    sums = [own] + [swap(messages[d - 1], "req", 2 * d) for d in range(1, chips)]

    pack_keep, pack_send, patches, value_out = attend(
        lengths,
        new_slot,
        page_table,
        sums,
        qkv_bias.reshape(1, -1),
        tokens,
        key_pool,
        value_pool,
        turning[0],
    )
    packs_got = swap(pack_send, "req", 1)
    packs = spread_pairs(pack_keep, packs_got)
    key_out = write_pool(key_pool, packs_got)


    keep, send = out_project(
        packs, staged, head_groups, slots, *in_hbm(key_out), turned[0]
    )
    total = keep + swap(send, "req", 1).astype(F32)
    from_other = swap(choose_half(sources, halves, turned, keep), "req", 1)
    summed = total[0]
    for d in range(1, chips):
        summed = summed + swap(total[d].astype(BF16), "req", 2 * d).astype(F32)
    base, key_out, value_out = place_page(
        lengths,
        new_slot,
        page_table,
        sources,
        patches,
        packs,
        tokens,
        out_bias[None],
        halves,
        turned,
        from_other,
        key_out,
        value_out,
    )
    summed, base = lax.optimization_barrier((summed, base))
    hidden = summed[0]
    for j in range(1, head_groups):
        hidden = hidden + swap(summed[j].astype(BF16), "head", j).astype(F32)
    hidden_out = (hidden + base).astype(BF16)
    return (hidden_out, key_out, value_out)


def solution(mesh):
    in_specs = (
        P("req", None),
        P(),
        P(),
        P("req", "head", None),
        P("head", None),
        P("head", "req", None),
        P(),
        P("req", None, "head"),
        P("req", None, "head"),
        P("req"),
        P("req", None),
        P("req"),
        P("req"),
    )
    out_specs = (P("req", "head"), P("req", None, "head"), P("req", None, "head"))
    return jax.shard_map(body, mesh=mesh, in_specs=in_specs, out_specs=out_specs, check_vma=False)
```

```python
import functools

import jax
import jax.numpy as jnp
from jax import lax
from jax.experimental import pallas as pl
from jax.experimental.pallas import tpu as pltpu
from jax.sharding import PartitionSpec as P

EPSILON = 1e-05
F32 = jnp.float32
BF16 = jnp.bfloat16
LANES = 128
META = 128
PACK = 256
VMEM = pl.BlockSpec(memory_space=pltpu.VMEM)
SMEM = pl.BlockSpec(memory_space=pltpu.SMEM)
ANY = pl.BlockSpec(memory_space=pl.ANY)
HBM = pl.BlockSpec(memory_space=pltpu.HBM)
MIB = 1024 * 1024


def cost(flops, moved):
    del flops, moved
    return pl.CostEstimate(flops=0, bytes_accessed=0, transcendentals=0)


def swap(value, axis, step):
    size = lax.axis_size(axis)
    return lax.ppermute(value, axis, [(i, i ^ step) for i in range(size)])


def spread_pairs(keep, got):
    chips = keep.shape[0]
    return [jnp.stack([keep[0], got[0]])] + [
        swap(jnp.stack([keep[d], got[d]]), "req", 2 * d) for d in range(1, chips)
    ]


def in_hbm(*arrays):
    return [pltpu.with_memory_space_constraint(array, pltpu.HBM) for array in arrays]


def write_pool(pool, after):
    parts = 4
    step = pool.shape[0] // parts

    def kernel(pool_ref, _, out_ref, sems):
        places = [pl.ds(i * step, step) for i in range(parts)]
        copies = [
            pltpu.make_async_copy(pool_ref.at[place], out_ref.at[place], sems.at[i]) for i, place in enumerate(places)
        ]
        for copy in copies:
            copy.start()
        for copy in copies:
            copy.wait()

    return pl.pallas_call(
        kernel,
        out_shape=jax.ShapeDtypeStruct(pool.shape, pool.dtype),
        in_specs=[VMEM, ANY],
        out_specs=HBM,
        scratch_shapes=[pltpu.SemaphoreType.DMA((parts,))],
        compiler_params=pltpu.CompilerParams(vmem_limit_bytes=8 * MIB),
        cost_estimate=cost(0, 2 * pool.size),
        name="write_pool",
    )(pool, after)


def leaving_slot(new_slot_ref, slots, here):
    leaving = jnp.int32(0)
    for s in range(slots):
        leaving = jnp.where(new_slot_ref[s] // slots != here, s, leaving)
    return leaving


def prepare(tokens, gain, shift, lengths, page_table, new_slot, new_page, key_pool, value_pool):
    groups = lax.axis_size("req")
    chips = groups // 2
    slots, model = tokens.shape
    depth = model // groups
    page, width = key_pool.shape[1:]
    half = page // 2

    def kernel(
        token_ref, gain_ref, shift_ref, length_ref, table_ref, slot_ref, page_ref, key_ref, value_ref,
        keep_ref, send_ref, keep_half, send_half, normed, sems,
    ):
        here = lax.axis_index("req")
        leaving = leaving_slot(slot_ref, slots, here)
        copies = []
        for n, source in enumerate((key_ref, value_ref)):
            for e, target in enumerate((keep_half, send_half)):
                rows = pl.ds(pl.multiple_of((here % 2 ^ e) * half, half), half)
                copies.append(
                    pltpu.make_async_copy(source.at[table_ref[leaving, 0], rows], target.at[n], sems.at[n, e])
                )
        for copy in copies:
            copy.start()
        values = token_ref[...].astype(F32)
        average = jnp.mean(values, axis=1, keepdims=True)
        centered = values - average
        variance = jnp.mean(centered * centered, axis=1, keepdims=True)
        rows = centered * lax.rsqrt(variance + EPSILON) * gain_ref[...] + shift_ref[...]
        normed[...] = rows.astype(BF16).astype(F32)
        row = lax.broadcasted_iota(jnp.int32, (slots, META), 0)
        lane = lax.broadcasted_iota(jnp.int32, (slots, META), 1)
        told = jnp.zeros((slots, META), F32)
        for s in range(slots):
            slot = slot_ref[s]
            numbers = (slot // slots, slot % slots, page_ref[s], length_ref[s] % page)
            for j, number in enumerate(numbers):
                told = jnp.where((row == s) & (lane == j), number.astype(F32), told)
        told = told.astype(BF16)
        for k in range(groups):
            first = (here ^ k) * depth
            if depth % LANES == 0:
                block = normed[:, pl.ds(pl.multiple_of(first, LANES), depth)]
            else:
                block = pltpu.roll(normed[...], lax.rem(model - first, model), 1)[:, :depth]
            target = (keep_ref, send_ref)[k % 2]
            target[k // 2, :, :META] = told
            target[k // 2, :, META:] = block.astype(BF16)
        for copy in copies:
            copy.wait()

    blocks = jax.ShapeDtypeStruct((chips, slots, META + depth), BF16)
    halves = jax.ShapeDtypeStruct((2, half, width), key_pool.dtype)
    return pl.pallas_call(
        kernel,
        out_shape=(blocks, blocks, halves, halves),
        in_specs=[VMEM] * 3 + [SMEM] * 4 + [HBM] * 2,
        out_specs=(VMEM,) * 4,
        scratch_shapes=[pltpu.VMEM((slots, model), F32), pltpu.SemaphoreType.DMA((2, 2))],
        compiler_params=pltpu.CompilerParams(vmem_limit_bytes=4 * MIB),
        cost_estimate=cost(0, 8 * page * width),
        name="prepare",
    )(*in_hbm(tokens, gain, shift, lengths, page_table, new_slot, new_page, key_pool, value_pool))


def arrivals(block_refs, here, wanted):
    slots = block_refs[0].shape[1]
    lane = lax.broadcasted_iota(jnp.int32, (slots, META), 1)
    found = jnp.zeros((slots, META), F32)
    goal = here ^ wanted
    for d, ref in enumerate(block_refs):
        for e in range(2):
            k = 2 * d + e
            told = ref[e, :, :META].astype(F32)
            numbered = jnp.where(lane == 4, float(k), told)
            found = jnp.where(told[:, :1] == jnp.where(wanted == k, -1, goal).astype(F32), numbered, found)
    return lambda j: jnp.sum(jnp.where(lane == j, found, 0.0)).astype(jnp.int32)


def row_length(chips):
    return 1 << (chips.bit_length() // 2)


def swap_pages(value, chips, along_row, step):
    across = row_length(chips)
    square = across * across == chips
    steps = [2 * step if along_row == (device % 2 == 0 or not square) else 2 * across * step for device in range(2 * chips)]
    return lax.ppermute(value, "req", [(i, i ^ steps[i]) for i in range(2 * chips)])


def find_sources(spread, after):
    chips = len(spread)
    across = row_length(chips)
    down = chips // across

    def kernel(*refs):
        block_refs, out_ref = refs[:chips], refs[-1]
        here = lax.axis_index("req")
        lane = lax.broadcasted_iota(jnp.int32, (8, LANES), 1)
        found = jnp.zeros((8, LANES), F32)
        put = lambda j, number: jnp.where(lane == j, number.astype(F32), found)
        turned = (here % 2 == 1) & (across == down)
        for row in range(down):
            for j in range(2):
                pick = arrivals(block_refs, here, jnp.where(turned, 2 * row, 2 * across * row) + j)
                source = pick(4)
                chip = source // 2
                chip = jnp.where(turned, chip % across * across + chip // across, chip)
                found = put(2 * row + j, 2 * chip + source % 2)
                if row == 0 and j == 0:
                    found = put(2 * down, pick(2))
                    found = put(2 * down + 1, pick(3))
                    found = put(2 * down + 2, source)
        out_ref[...] = found

    return pl.pallas_call(
        kernel,
        out_shape=jax.ShapeDtypeStruct((8, LANES), F32),
        in_specs=[VMEM] * chips + [ANY],
        out_specs=VMEM,
        compiler_params=pltpu.CompilerParams(vmem_limit_bytes=2 * MIB),
        cost_estimate=cost(0, 0),
        name="find_sources",
    )(*spread, after)


def number_at(source_ref, j):
    lane = lax.broadcasted_iota(jnp.int32, (1, LANES), 1)
    return jnp.sum(jnp.where(lane == j, source_ref[:1, :], 0.0)).astype(jnp.int32)


def turn_pages(sources, halves, chips, after):
    across = len(halves)
    down = chips // across
    shape = halves[0].shape

    def kernel(source_ref, *refs):
        half_refs, out_refs = refs[:across], refs[across + len(after) :]
        for row in range(1, down):
            for j in range(2):
                source = number_at(source_ref, 2 * row + j)
                place = jnp.where(source < 2 * across, source, 0)
                for d in range(across):
                    for e in range(2):

                        @pl.when(place == 2 * d + e)
                        def _():
                            out_refs[row - 1][j] = half_refs[d][e]

    one = jax.ShapeDtypeStruct(shape, halves[0].dtype)
    return pl.pallas_call(
        kernel,
        out_shape=(one,) * (down - 1),
        in_specs=[VMEM] * (1 + across) + [ANY] * len(after),
        out_specs=(VMEM,) * (down - 1),
        compiler_params=pltpu.CompilerParams(vmem_limit_bytes=(across + down) * MIB),
        cost_estimate=cost(0, 4 * halves[0].size),
        name="turn_pages",
    )(sources, *halves, *after)


def with_half(source, across, core, half_refs, turned_refs, use):
    place = jnp.where(source < 2 * across, source, 2 * across + source // (2 * across))
    for d, ref in enumerate(half_refs):
        for e in range(2):

            @pl.when(place == 2 * d + e)
            def _():
                use(ref.at[e])

    for row, ref in enumerate(turned_refs):

        @pl.when(place == 2 * across + row + 1)
        def _():
            use(ref.at[core])


def choose_half(sources, halves, turned, after):
    across, rows = len(halves), len(turned)

    def kernel(source_ref, *refs):
        half_refs, turned_refs = refs[:across], refs[across : across + rows]
        out_ref = refs[-1]

        def use(ref):
            out_ref[...] = ref[...]

        with_half(number_at(source_ref, 1), across, 1, half_refs, turned_refs, use)

    shape = halves[0].shape[1:]
    return pl.pallas_call(
        kernel,
        out_shape=jax.ShapeDtypeStruct(shape, halves[0].dtype),
        in_specs=[VMEM] * (1 + across + rows) + [ANY],
        out_specs=VMEM,
        compiler_params=pltpu.CompilerParams(vmem_limit_bytes=(1 + across + rows) * MIB),
        cost_estimate=cost(0, 2 * halves[0].size),
        name="choose_half",
    )(sources, *halves, *turned, after)


def project(blocks, weight, later):
    chips = len(blocks)
    slots = blocks[0].shape[1]
    heads, depth, width = weight.shape
    per = 2 if heads % 2 == 0 else 1
    rows = chips * 2 * slots

    def kernel(*refs):
        block_refs = refs[:chips]
        weight_ref, later_ref, keep_ref, send_ref, later_out, left, sem = refs[chips:]
        copy = pltpu.make_async_copy(later_ref, later_out, sem)
        copy.start()
        for d in range(chips):
            for e in range(2):
                row = (d * 2 + e) * slots
                left[row : row + slots, :] = block_refs[d][e, :, META:].astype(F32)
        lhs = left[...].astype(BF16)

        @pl.loop(0, heads // per)
        def _(i):
            right = jnp.concatenate([weight_ref[i * per + j] for j in range(per)], axis=1)
            total = jnp.dot(lhs, right, preferred_element_type=F32)
            columns = pl.ds(pl.multiple_of(i * (per * width), per * width), per * width)
            for d in range(chips):
                row = d * 2 * slots
                keep_ref[d, :, columns] = total[row : row + slots]
                send_ref[d, :, columns] = total[row + slots : row + 2 * slots]

        copy.wait()

    shape = jax.ShapeDtypeStruct((chips, slots, heads * width), F32)
    return pl.pallas_call(
        kernel,
        out_shape=(shape, shape, jax.ShapeDtypeStruct(later.shape, later.dtype)),
        in_specs=[VMEM] * (chips + 1) + [HBM],
        out_specs=(VMEM, VMEM, VMEM),
        scratch_shapes=[pltpu.VMEM((rows, depth), F32), pltpu.SemaphoreType.DMA],
        compiler_params=pltpu.CompilerParams(vmem_limit_bytes=weight.size * 2 + 12 * MIB),
        cost_estimate=cost(2 * rows * weight.size, 2 * weight.size),
        name="project",
    )(*blocks, weight, *in_hbm(later))


def combine(keep, got, after):
    chips, slots, width = keep.shape
    heads = width // (3 * LANES)

    def kernel(keep_ref, got_ref, _, own_ref, *message_refs):
        own_ref[...] = keep_ref[0] + got_ref[0]
        for d in range(1, chips):
            for h in range(heads):
                total = keep_ref[d, :, 3 * h * LANES : 3 * (h + 1) * LANES] + got_ref[d, :, 3 * h * LANES : 3 * (h + 1) * LANES]
                query = total[:, :LANES]
                high = query.astype(BF16)
                low = (query - high.astype(F32)).astype(BF16)
                base = 4 * h * LANES
                message_refs[d - 1][:, base : base + LANES] = high
                message_refs[d - 1][:, base + LANES : base + 2 * LANES] = low
                message_refs[d - 1][:, base + 2 * LANES : base + 4 * LANES] = total[:, LANES:].astype(BF16)

    message = jax.ShapeDtypeStruct((slots, 4 * heads * LANES), BF16)
    return pl.pallas_call(
        kernel,
        out_shape=(jax.ShapeDtypeStruct((slots, width), F32),) + (message,) * (chips - 1),
        in_specs=[VMEM, VMEM, ANY],
        out_specs=(VMEM,) * chips,
        compiler_params=pltpu.CompilerParams(vmem_limit_bytes=8 * MIB),
        cost_estimate=cost(0, 8 * keep.size),
        name="combine",
    )(keep, got, after)


def attend(lengths, new_slot, page_table, sums, bias, tokens, key_pool, value_pool, written, after):
    parts = len(sums)
    slots = sums[0].shape[0]
    pages, page, width = key_pool.shape
    head = LANES
    heads = width // head
    max_pages = page_table.shape[1]
    chunk_pages = 4
    chunk = chunk_pages * page
    chunks = max_pages // chunk_pages
    long_rows = max_pages * page
    short_rows = slots * page
    groups = 2 * parts
    share = head // groups
    per = LANES // share
    tall = 16
    strips = width // PACK
    scale = head ** (-0.5)

    def kernel(*refs):
        length_ref, slot_ref, table_ref = refs[:3]
        sum_refs = refs[3 : 3 + parts]
        (bias_ref, token_ref, key_ref, value_ref, _, _, pack_keep, pack_send, patch_ref, score_buffer, mix_buffer) = refs[
            3 + parts :
        ]
        here = lax.axis_index("req")
        column_block = lax.axis_index("head")
        leaving = leaving_slot(slot_ref, slots, here)
        lengths = [length_ref[s] for s in range(slots)]
        long_slot = jnp.int32(0)
        long_length = jnp.int32(0)
        for s in range(slots):
            is_long = lengths[s] >= page
            long_slot = jnp.where(is_long, s, long_slot)
            long_length = jnp.where(is_long, lengths[s], long_length)
        turns = (long_length + chunk - 1) // chunk

        total = sum_refs[0][...] + bias_ref[...]

        def third(k):
            columns = []
            for h in range(heads):
                one = total[:, (3 * h + k) * head : (3 * h + k + 1) * head]
                for ref in sum_refs[1:]:
                    base = 4 * h * head
                    if k == 0:
                        one = one + ref[:, base : base + head].astype(F32) + ref[:, base + head : base + 2 * head].astype(F32)
                    else:
                        one = one + ref[:, base + (k + 1) * head : base + (k + 2) * head].astype(F32)
                columns.append(one)
            return jnp.concatenate(columns, axis=1)

        query = (third(0) * scale).astype(BF16).astype(F32)
        new_rows = (third(1).astype(BF16).astype(F32), third(2).astype(BF16).astype(F32))

        lane_head = lax.broadcasted_iota(jnp.int32, (tall, width), 1) // head
        on_head = lane_head == lax.broadcasted_iota(jnp.int32, (tall, width), 0)

        def blocked(row):
            return jnp.where(on_head, jnp.broadcast_to(row, (tall, width)), 0.0).astype(BF16)

        def for_slot(which, rows):
            found = rows[0]
            for s in range(1, slots):
                found = jnp.where(which == s, rows[s], found)
            return found

        def softmax(scores, valid, new_score):
            masked = jnp.where(valid, scores, -1e30)
            peak = jnp.maximum(jnp.max(masked, axis=1, keepdims=True), new_score)
            weights = jnp.where(valid, jnp.exp(masked - peak), 0.0)
            new_weight = jnp.exp(new_score - peak)
            denom = jnp.sum(weights, axis=1, keepdims=True) + new_weight
            return weights.astype(BF16), new_weight.astype(BF16).astype(F32), denom

        across = (((1,), (1,)), ((), ()))
        short_query = jnp.concatenate([blocked(query[s : s + 1]) for s in range(slots)], axis=0)
        new_keys = jnp.concatenate([new_rows[0], jnp.zeros((tall - slots, width), F32)], axis=0).astype(BF16)
        new_scores = lax.dot_general(short_query, new_keys, across, preferred_element_type=F32)
        size = (slots * tall, tall)
        own_column = lax.broadcasted_iota(jnp.int32, size, 0) // tall == lax.broadcasted_iota(jnp.int32, size, 1)
        new_score = jnp.sum(jnp.where(own_column, new_scores, 0.0), axis=1, keepdims=True)

        first_pages = lambda ref: jnp.concatenate([ref[table_ref[s, 0]] for s in range(slots)], axis=0)
        short_scores = lax.dot_general(short_query, first_pages(key_ref), across, preferred_element_type=F32)
        size = (slots * tall, short_rows)
        row_slot = lax.broadcasted_iota(jnp.int32, size, 0) // tall
        column = lax.broadcasted_iota(jnp.int32, size, 1)
        limit = jnp.zeros(size, jnp.int32)
        for s in range(slots):
            limit = jnp.where(row_slot == s, lengths[s], limit)
        valid = (row_slot == column // page) & (column % page < limit)
        short_probs, new_prob, short_denom = softmax(short_scores, valid, new_score)
        new_values = jnp.concatenate(
            [jnp.broadcast_to(new_rows[1][s : s + 1], (tall, width)) for s in range(slots)], axis=0
        )
        short_mix = jnp.dot(short_probs, first_pages(value_ref), preferred_element_type=F32)
        short_mix = (short_mix + new_prob * new_values) / short_denom

        mix_buffer[...] = jnp.zeros(mix_buffer.shape, F32)

        @pl.when(turns > 0)
        def _():
            some_pages = lambda ref, c: jnp.concatenate(
                [ref[table_ref[long_slot, c * chunk_pages + i]] for i in range(chunk_pages)], axis=0
            )
            long_query = blocked(for_slot(long_slot, [query[s : s + 1] for s in range(slots)]))
            long_new = for_slot(long_slot, [new_score[s * tall : (s + 1) * tall] for s in range(slots)])
            long_value = for_slot(long_slot, [new_rows[1][s : s + 1] for s in range(slots)])
            for c in range(chunks):

                @pl.when(c < turns)
                def _():
                    score_buffer[:, c * chunk : (c + 1) * chunk] = lax.dot_general(
                        long_query, some_pages(key_ref, c), across, preferred_element_type=F32
                    )

                @pl.when(c >= turns)
                def _():
                    score_buffer[:, c * chunk : (c + 1) * chunk] = jnp.zeros((tall, chunk), F32)

            position = lax.broadcasted_iota(jnp.int32, (tall, long_rows), 1)
            long_probs, long_prob, long_denom = softmax(score_buffer[...], position < long_length, long_new)
            for c in range(chunks):

                @pl.when(c < turns)
                def _():
                    mix_buffer[...] += jnp.dot(
                        long_probs[:, c * chunk : (c + 1) * chunk], some_pages(value_ref, c), preferred_element_type=F32
                    )

            mix_buffer[...] = (mix_buffer[...] + long_prob * long_value) / long_denom

        def fold(mixed):
            return jnp.sum(jnp.where(on_head, mixed, 0.0), axis=0, keepdims=True)

        long_mix = fold(mix_buffer[...])
        rows = []
        for s in range(slots):
            row = fold(short_mix[s * tall : (s + 1) * tall])
            rows.append(jnp.where(lengths[s] >= page, long_mix, row))
        high = -(-slots // 8) * 8
        attended = jnp.concatenate(rows + [jnp.zeros((high - slots, width), F32)], axis=0).astype(BF16).astype(F32)

        token = token_ref[:, pl.ds(pl.multiple_of(column_block * width, LANES), width)].astype(F32)
        extra = []
        for source in new_rows + (token,):
            one = jnp.zeros((1, width), F32)
            for s in range(slots):
                one = jnp.where(leaving == s, source[s : s + 1], one)
            extra += [one[:, i * PACK : (i + 1) * PACK] for i in range(strips)]
        extra = jnp.concatenate(extra + [jnp.zeros((pack_rows(slots, strips) - high - 3 * strips, PACK), F32)], axis=0)

        lane = lax.broadcasted_iota(jnp.int32, (high, LANES), 1)
        row_at = lax.broadcasted_iota(jnp.int32, (high, LANES), 0)
        goal = jnp.full((high, LANES), -1.0, F32)
        for s in range(slots):
            device, slot = slot_ref[s] // slots, slot_ref[s] % slots
            number = jnp.where(lane % share == share - 1, slot, device).astype(F32)
            goal = jnp.where(row_at == s, number, goal)
        turned = [
            pltpu.roll(attended[:, h * head : (h + 1) * head], h % per * share, 1) if h % per else attended[:, h * head : (h + 1) * head]
            for h in range(heads)
        ]
        for k in range(groups):
            count = lax.rem(lane // share - (here ^ k) + per, per)
            tiles = [jnp.zeros((high, LANES), F32) for _ in range(PACK // LANES)]
            for h in range(heads):
                tiles[h // per] = jnp.where(count == h % per, turned[h], tiles[h // per])
            tiles[-1] = jnp.where((count == per - 1) & (lane % share >= share - 2), goal, tiles[-1])
            block = jnp.concatenate([jnp.concatenate(tiles, axis=1), extra], axis=0).astype(BF16)
            (pack_keep, pack_send)[k % 2][k // 2] = block

        at = lax.broadcasted_iota(jnp.int32, (tall, width), 0)
        for n, ref in enumerate((key_ref, value_ref)):
            for s in range(slots):
                offset = lengths[s] % page
                first = pl.multiple_of(offset // tall * tall, tall)
                old = ref[table_ref[s, lengths[s] // page], pl.ds(first, tall), :].astype(F32)
                new = jnp.broadcast_to(new_rows[n][s : s + 1], (tall, width))
                patch_ref[n, s] = jnp.where(at == offset - first, new, old).astype(BF16)

    packed = jax.ShapeDtypeStruct((parts, pack_rows(slots, strips), PACK), BF16)
    return pl.pallas_call(
        kernel,
        out_shape=(packed, packed, jax.ShapeDtypeStruct((2, slots, tall, width), BF16)),
        in_specs=[SMEM] * 3 + [VMEM] * (parts + 4) + [HBM, ANY],
        out_specs=(VMEM, VMEM, VMEM),
        scratch_shapes=[
            pltpu.VMEM((tall, long_rows), F32),
            pltpu.VMEM((tall, width), F32),
        ],
        compiler_params=pltpu.CompilerParams(vmem_limit_bytes=18 * MIB),
        cost_estimate=cost(4 * tall * (long_rows + short_rows) * width, 4 * (long_rows + short_rows) * width),
        name="attend",
    )(lengths, new_slot, page_table, *sums, bias, tokens, key_pool, value_pool, *in_hbm(written), after)


def pack_rows(slots, strips):
    need = -(-slots // 8) * 8 + 3 * strips
    return -(-need // 16) * 16


def out_project(blocks, weight, pieces, slots, *after):
    chips = len(blocks)
    depth, width = weight.shape
    high = -(-slots // 8) * 8
    rows = 2 * chips * slots
    piece = width // pieces

    def kernel(*refs):
        block_refs, weight_ref = refs[:chips], refs[chips]
        keep_ref, send_ref = refs[chips + 1 + len(after) :]
        gathered = jnp.concatenate(
            [block_refs[d][e, :high, :].astype(F32) for d in range(chips) for e in range(2)], axis=0
        )
        here = lax.axis_index("req")
        share = LANES // (2 * chips)
        back = lax.rem(LANES - here * share, LANES)
        gathered = jnp.concatenate(
            [pltpu.roll(gathered[:, first : first + LANES], back, 1) for first in range(0, PACK, LANES)], axis=1
        )
        goal = gathered[:, PACK - 2 : PACK - 1].astype(jnp.int32)
        place = goal ^ here
        row = (place % 2) * (chips * slots) + (place // 2) * slots + gathered[:, PACK - 1 :].astype(jnp.int32)
        row = jnp.where(goal < 0, -1, row)
        size = (gathered.shape[0], rows)
        order = jnp.where(lax.broadcasted_iota(jnp.int32, size, 1) == row, 1.0, 0.0)
        left = lax.dot_general(
            order.astype(BF16), gathered.astype(BF16), (((0,), (0,)), ((), ())), preferred_element_type=F32
        )
        left = left[:, :depth].astype(BF16)
        for j in range(pieces):
            first = (lax.axis_index("head") ^ j) * piece
            total = jnp.dot(
                left, weight_ref[:, pl.ds(pl.multiple_of(first, LANES), piece)], preferred_element_type=F32
            )
            for d in range(chips):
                keep_ref[d, j] = total[d * slots : (d + 1) * slots]
                send_ref[d, j] = total[(chips + d) * slots : (chips + d + 1) * slots].astype(BF16)

    shape = (chips, pieces, slots, piece)
    return pl.pallas_call(
        kernel,
        out_shape=(jax.ShapeDtypeStruct(shape, F32), jax.ShapeDtypeStruct(shape, BF16)),
        in_specs=[VMEM] * (chips + 1) + [HBM] * min(1, len(after)) + [ANY] * (len(after) - 1),
        out_specs=(VMEM, VMEM),
        compiler_params=pltpu.CompilerParams(vmem_limit_bytes=10 * MIB),
        cost_estimate=cost(2 * rows * weight.size, 2 * weight.size),
        name="out_project",
    )(*blocks, weight, *after)


def place_page(lengths, new_slot, page_table, sources, patches, packs, tokens, out_bias, halves, turned, from_other, key_out, value_out):
    chips, across, rows = len(packs), len(halves), len(turned)
    down = chips // across
    count = across + rows + 1
    page, width = key_out.shape[1:]
    half = page // 2
    slots = tokens.shape[0]
    high = -(-slots // 8) * 8
    strips = width // PACK

    tall = patches.shape[2]

    def kernel(length_ref, slot_ref, table_ref, source_ref, patch_ref, *refs):
        pack_refs = refs[:chips]
        token_ref, bias_ref = refs[chips : chips + 2]
        half_refs = refs[chips + 2 : chips + 2 + across]
        turned_refs = refs[chips + 2 + across : chips + 2 + across + rows]
        other_ref = refs[chips + 1 + count]
        _, _, base_ref, key_ref, value_ref, buffer, arrived, out_sems, patch_sems = refs[chips + 2 + count :]
        here = lax.axis_index("req")
        leaving = leaving_slot(slot_ref, slots, here)

        def patch(n, s):
            length = length_ref[s]
            first = pl.multiple_of(length % page // tall * tall, tall)
            target = (key_ref, value_ref)[n].at[table_ref[s, length // page], pl.ds(first, tall)]
            return pltpu.make_async_copy(patch_ref.at[n, s], target, patch_sems.at[n, s])

        for n in range(2):
            for s in range(slots):

                @pl.when(leaving != s)
                def _():
                    patch(n, s).start()

        column = pl.multiple_of(lax.axis_index("head") * width, LANES)
        page_at, offset, source = [number_at(source_ref, 2 * down + j) for j in range(3)]
        own_rows, other_rows = [pl.ds(pl.multiple_of((here % 2 ^ e) * half, half), half) for e in range(2)]

        def use(ref):
            buffer[:, own_rows, :] = ref[...]

        with_half(number_at(source_ref, 0), across, 0, half_refs, turned_refs, use)
        buffer[:, other_rows, :] = other_ref[...]
        for d in range(chips):
            for e in range(2):

                @pl.when(source == 2 * d + e)
                def _():
                    arrived[...] = pack_refs[d][e].astype(F32)

        def fresh(n):
            strip = high + n * strips
            return jnp.concatenate([arrived[strip + i : strip + i + 1, :] for i in range(strips)], axis=1)

        at = lax.broadcasted_iota(jnp.int32, (slots, width), 0)
        token = jnp.where(
            at == leaving,
            jnp.broadcast_to(fresh(2), (slots, width)),
            token_ref[:, pl.ds(column, width)].astype(F32),
        )
        base_ref[...] = token + bias_ref[:, pl.ds(column, width)]
        first = pl.multiple_of(offset // 16 * 16, 16)
        row = lax.broadcasted_iota(jnp.int32, (16, width), 0)
        for n in range(2):
            old = buffer[n, pl.ds(first, 16), :].astype(F32)
            new = jnp.broadcast_to(fresh(n), (16, width))
            buffer[n, pl.ds(first, 16), :] = jnp.where(row == offset - first, new, old).astype(BF16)
        copies = [
            pltpu.make_async_copy(buffer.at[n], target.at[page_at], out_sems.at[n])
            for n, target in enumerate((key_ref, value_ref))
        ]
        for copy in copies:
            copy.start()
        for n in range(2):
            for s in range(slots):

                @pl.when(leaving != s)
                def _():
                    patch(n, s).wait()

        for copy in copies:
            copy.wait()

    shape = jax.ShapeDtypeStruct(key_out.shape, key_out.dtype)
    return pl.pallas_call(
        kernel,
        out_shape=(jax.ShapeDtypeStruct((slots, width), F32), shape, shape),
        in_specs=[SMEM] * 3 + [VMEM] * (chips + 4 + count) + [HBM] * 2,
        out_specs=(VMEM, HBM, HBM),
        scratch_shapes=[
            pltpu.VMEM((2, page, width), BF16),
            pltpu.VMEM(packs[0].shape[1:], F32),
            pltpu.SemaphoreType.DMA((2,)),
            pltpu.SemaphoreType.DMA((2, slots)),
        ],
        input_output_aliases={chips + 7 + count: 1, chips + 8 + count: 2},
        compiler_params=pltpu.CompilerParams(vmem_limit_bytes=(6 + count) * MIB),
        cost_estimate=cost(0, 8 * page * width),
        name="place_page",
    )(
        lengths, new_slot, page_table, sources, patches, *packs, tokens, out_bias, *halves, *turned, from_other, key_out, value_out
    )


def body(
    tokens,
    norm_gain,
    norm_shift,
    qkv_weight,
    qkv_bias,
    out_weight,
    out_bias,
    key_pool,
    value_pool,
    lengths,
    page_table,
    new_slot,
    new_page,
):
    groups = lax.axis_size("req")
    head_groups = lax.axis_size("head")
    slots = tokens.shape[0]
    chips = groups // 2

    keep, send, keep_half, send_half = prepare(
        tokens, norm_gain[None], norm_shift[None], lengths, page_table, new_slot, new_page, key_pool, value_pool
    )
    got = swap(send, "req", 1)
    across = row_length(chips)
    send_half, got = lax.optimization_barrier((send_half, got))
    spread = spread_pairs(keep, got)
    halves = [jnp.stack([keep_half, swap(send_half, "req", 1)])]
    halves[0], *spread = lax.optimization_barrier((halves[0], *spread))
    halves += [swap_pages(halves[0], chips, True, d) for d in range(1, across)]
    flat = out_weight.reshape(-1, out_weight.shape[2])
    keep, send, staged = project(spread, jnp.transpose(qkv_weight, (1, 0, 2)), flat)
    got = swap(send, "req", 1)
    sources = find_sources(spread, keep)
    own, *messages = combine(keep, got, sources)
    sums = [own] + [swap(messages[d - 1], "req", 2 * d) for d in range(1, chips)]
    value_out = write_pool(value_pool, own)
    turning = turn_pages(sources, halves, chips, sums[1:])
    turned = [swap_pages(one, chips, False, row + 1) for row, one in enumerate(turning)]

    pack_keep, pack_send, patches = attend(
        lengths,
        new_slot,
        page_table,
        sums,
        qkv_bias.reshape(1, -1),
        tokens,
        key_pool,
        value_pool,
        value_out,
        turning[0],
    )
    packs_got = swap(pack_send, "req", 1)
    packs = spread_pairs(pack_keep, packs_got)
    key_out = write_pool(key_pool, packs_got)


    keep, send = out_project(
        packs, staged, head_groups, slots, *in_hbm(key_out), turned[0]
    )
    total = keep + swap(send, "req", 1).astype(F32)
    from_other = swap(choose_half(sources, halves, turned, keep), "req", 1)
    summed = total[0]
    for d in range(1, chips):
        summed = summed + swap(total[d].astype(BF16), "req", 2 * d).astype(F32)
    base, key_out, value_out = place_page(
        lengths,
        new_slot,
        page_table,
        sources,
        patches,
        packs,
        tokens,
        out_bias[None],
        halves,
        turned,
        from_other,
        key_out,
        value_out,
    )
    summed, base = lax.optimization_barrier((summed, base))
    count = head_groups
    while count > 1:
        count //= 2
        summed = summed[:count] + swap(summed[count : 2 * count].astype(BF16), "head", count).astype(F32)
    hidden = summed[0]
    hidden_out = (hidden + base).astype(BF16)
    return (hidden_out, key_out, value_out)


def solution(mesh):
    in_specs = (
        P("req", None),
        P(),
        P(),
        P("req", "head", None),
        P("head", None),
        P("head", "req", None),
        P(),
        P("req", None, "head"),
        P("req", None, "head"),
        P("req"),
        P("req", None),
        P("req"),
        P("req"),
    )
    out_specs = (P("req", "head"), P("req", None, "head"), P("req", None, "head"))
    return jax.shard_map(body, mesh=mesh, in_specs=in_specs, out_specs=out_specs, check_vma=False)
```

```python
import functools

import jax
import jax.numpy as jnp
from jax import lax
from jax.experimental import pallas as pl
from jax.experimental.pallas import tpu as pltpu
from jax.sharding import PartitionSpec as P

EPSILON = 1e-05
F32 = jnp.float32
BF16 = jnp.bfloat16
LANES = 128
META = 128
PACK = 256
VMEM = pl.BlockSpec(memory_space=pltpu.VMEM)
SMEM = pl.BlockSpec(memory_space=pltpu.SMEM)
ANY = pl.BlockSpec(memory_space=pl.ANY)
HBM = pl.BlockSpec(memory_space=pltpu.HBM)
MIB = 1024 * 1024


def cost(flops, moved):
    del flops, moved
    return pl.CostEstimate(flops=0, bytes_accessed=0, transcendentals=0)


def swap(value, axis, step):
    size = lax.axis_size(axis)
    return lax.ppermute(value, axis, [(i, i ^ step) for i in range(size)])


def spread_pairs(keep, got):
    chips = keep.shape[0]
    return [jnp.stack([keep[0], got[0]])] + [
        swap(jnp.stack([keep[d], got[d]]), "req", 2 * d) for d in range(1, chips)
    ]


def in_hbm(*arrays):
    return [pltpu.with_memory_space_constraint(array, pltpu.HBM) for array in arrays]


def write_pool(pool, after):
    parts = 4
    step = pool.shape[0] // parts

    def kernel(pool_ref, _, out_ref, sems):
        places = [pl.ds(i * step, step) for i in range(parts)]
        copies = [
            pltpu.make_async_copy(pool_ref.at[place], out_ref.at[place], sems.at[i]) for i, place in enumerate(places)
        ]
        for copy in copies:
            copy.start()
        for copy in copies:
            copy.wait()

    return pl.pallas_call(
        kernel,
        out_shape=jax.ShapeDtypeStruct(pool.shape, pool.dtype),
        in_specs=[VMEM, ANY],
        out_specs=HBM,
        scratch_shapes=[pltpu.SemaphoreType.DMA((parts,))],
        compiler_params=pltpu.CompilerParams(vmem_limit_bytes=8 * MIB),
        cost_estimate=cost(0, 2 * pool.size),
        name="write_pool",
    )(pool, after)


def leaving_slot(new_slot_ref, slots, here):
    leaving = jnp.int32(0)
    for s in range(slots):
        leaving = jnp.where(new_slot_ref[s] // slots != here, s, leaving)
    return leaving


def prepare(tokens, gain, shift, lengths, page_table, new_slot, new_page, key_pool, value_pool):
    groups = lax.axis_size("req")
    chips = groups // 2
    slots, model = tokens.shape
    depth = model // groups
    page, width = key_pool.shape[1:]
    half = page // 2

    def kernel(
        token_ref, gain_ref, shift_ref, length_ref, table_ref, slot_ref, page_ref, key_ref, value_ref,
        keep_ref, send_ref, keep_half, send_half, normed, sems,
    ):
        here = lax.axis_index("req")
        leaving = leaving_slot(slot_ref, slots, here)
        copies = []
        for n, source in enumerate((key_ref, value_ref)):
            for e, target in enumerate((keep_half, send_half)):
                rows = pl.ds(pl.multiple_of((here % 2 ^ e) * half, half), half)
                copies.append(
                    pltpu.make_async_copy(source.at[table_ref[leaving, 0], rows], target.at[n], sems.at[n, e])
                )
        for copy in copies:
            copy.start()
        values = token_ref[...].astype(F32)
        average = jnp.mean(values, axis=1, keepdims=True)
        centered = values - average
        variance = jnp.mean(centered * centered, axis=1, keepdims=True)
        rows = centered * lax.rsqrt(variance + EPSILON) * gain_ref[...] + shift_ref[...]
        normed[...] = rows.astype(BF16).astype(F32)
        row = lax.broadcasted_iota(jnp.int32, (slots, META), 0)
        lane = lax.broadcasted_iota(jnp.int32, (slots, META), 1)
        told = jnp.zeros((slots, META), F32)
        for s in range(slots):
            slot = slot_ref[s]
            numbers = (slot // slots, slot % slots, page_ref[s], length_ref[s] % page)
            for j, number in enumerate(numbers):
                told = jnp.where((row == s) & (lane == j), number.astype(F32), told)
        told = told.astype(BF16)
        for k in range(groups):
            first = (here ^ k) * depth
            if depth % LANES == 0:
                block = normed[:, pl.ds(pl.multiple_of(first, LANES), depth)]
            else:
                block = pltpu.roll(normed[...], lax.rem(model - first, model), 1)[:, :depth]
            target = (keep_ref, send_ref)[k % 2]
            target[k // 2, :, :META] = told
            target[k // 2, :, META:] = block.astype(BF16)
        for copy in copies:
            copy.wait()

    blocks = jax.ShapeDtypeStruct((chips, slots, META + depth), BF16)
    halves = jax.ShapeDtypeStruct((2, half, width), key_pool.dtype)
    return pl.pallas_call(
        kernel,
        out_shape=(blocks, blocks, halves, halves),
        in_specs=[VMEM] * 3 + [SMEM] * 4 + [HBM] * 2,
        out_specs=(VMEM,) * 4,
        scratch_shapes=[pltpu.VMEM((slots, model), F32), pltpu.SemaphoreType.DMA((2, 2))],
        compiler_params=pltpu.CompilerParams(vmem_limit_bytes=4 * MIB),
        cost_estimate=cost(0, 8 * page * width),
        name="prepare",
    )(*in_hbm(tokens, gain, shift, lengths, page_table, new_slot, new_page, key_pool, value_pool))


def arrivals(block_refs, here, wanted):
    slots = block_refs[0].shape[1]
    lane = lax.broadcasted_iota(jnp.int32, (slots, META), 1)
    found = jnp.zeros((slots, META), F32)
    goal = here ^ wanted
    for d, ref in enumerate(block_refs):
        for e in range(2):
            k = 2 * d + e
            told = ref[e, :, :META].astype(F32)
            numbered = jnp.where(lane == 4, float(k), told)
            found = jnp.where(told[:, :1] == jnp.where(wanted == k, -1, goal).astype(F32), numbered, found)
    return lambda j: jnp.sum(jnp.where(lane == j, found, 0.0)).astype(jnp.int32)


def row_length(chips):
    return 1 << (chips.bit_length() // 2)


def swap_pages(value, chips, along_row, step):
    across = row_length(chips)
    square = across * across == chips
    steps = [2 * step if along_row == (device % 2 == 0 or not square) else 2 * across * step for device in range(2 * chips)]
    return lax.ppermute(value, "req", [(i, i ^ steps[i]) for i in range(2 * chips)])


def find_sources(spread, after):
    chips = len(spread)
    across = row_length(chips)
    down = chips // across

    def kernel(*refs):
        block_refs, out_ref = refs[:chips][::-1], refs[-1]
        here = lax.axis_index("req")
        lane = lax.broadcasted_iota(jnp.int32, (8, LANES), 1)
        found = jnp.zeros((8, LANES), F32)
        put = lambda j, number: jnp.where(lane == j, number.astype(F32), found)
        turned = (here % 2 == 1) & (across == down)
        for row in range(down):
            for j in range(2):
                pick = arrivals(block_refs, here, jnp.where(turned, 2 * row, 2 * across * row) + j)
                source = pick(4)
                chip = source // 2
                chip = jnp.where(turned, chip % across * across + chip // across, chip)
                found = put(2 * row + j, 2 * chip + source % 2)
                if row == 0 and j == 0:
                    found = put(2 * down, pick(2))
                    found = put(2 * down + 1, pick(3))
                    found = put(2 * down + 2, source)
        out_ref[...] = found

    return pl.pallas_call(
        kernel,
        out_shape=jax.ShapeDtypeStruct((8, LANES), F32),
        in_specs=[VMEM] * chips + [ANY],
        out_specs=VMEM,
        compiler_params=pltpu.CompilerParams(vmem_limit_bytes=2 * MIB),
        cost_estimate=cost(0, 0),
        name="find_sources",
    )(*spread[::-1], after)


def number_at(source_ref, j):
    lane = lax.broadcasted_iota(jnp.int32, (1, LANES), 1)
    return jnp.sum(jnp.where(lane == j, source_ref[:1, :], 0.0)).astype(jnp.int32)


def turn_pages(sources, halves, chips):
    across = len(halves)
    down = chips // across
    shape = halves[0].shape

    def kernel(source_ref, *refs):
        half_refs, out_refs = refs[:across], refs[across:]
        for row in range(1, down):
            for j in range(2):
                source = number_at(source_ref, 2 * row + j)
                place = jnp.where(source < 2 * across, source, 0)
                for d in range(across):
                    for e in range(2):

                        @pl.when(place == 2 * d + e)
                        def _():
                            out_refs[row - 1][j] = half_refs[d][e]

    one = jax.ShapeDtypeStruct(shape, halves[0].dtype)
    return pl.pallas_call(
        kernel,
        out_shape=(one,) * (down - 1),
        in_specs=[VMEM] * (1 + across),
        out_specs=(VMEM,) * (down - 1),
        compiler_params=pltpu.CompilerParams(vmem_limit_bytes=(across + down) * MIB),
        cost_estimate=cost(0, 4 * halves[0].size),
        name="turn_pages",
    )(sources, *halves)


def with_half(source, across, core, half_refs, turned_refs, use):
    place = jnp.where(source < 2 * across, source, 2 * across + source // (2 * across))
    for d, ref in enumerate(half_refs):
        for e in range(2):

            @pl.when(place == 2 * d + e)
            def _():
                use(ref.at[e])

    for row, ref in enumerate(turned_refs):

        @pl.when(place == 2 * across + row + 1)
        def _():
            use(ref.at[core])


def choose_half(sources, halves, turned, after):
    across, rows = len(halves), len(turned)

    def kernel(source_ref, *refs):
        half_refs, turned_refs = refs[:across], refs[across : across + rows]
        out_ref = refs[-1]

        def use(ref):
            out_ref[...] = ref[...]

        with_half(number_at(source_ref, 1), across, 1, half_refs, turned_refs, use)

    shape = halves[0].shape[1:]
    return pl.pallas_call(
        kernel,
        out_shape=jax.ShapeDtypeStruct(shape, halves[0].dtype),
        in_specs=[VMEM] * (1 + across + rows) + [ANY],
        out_specs=VMEM,
        compiler_params=pltpu.CompilerParams(vmem_limit_bytes=(1 + across + rows) * MIB),
        cost_estimate=cost(0, 2 * halves[0].size),
        name="choose_half",
    )(sources, *halves, *turned, after)


def project(blocks, weight, later):
    chips = len(blocks)
    slots = blocks[0].shape[1]
    heads, depth, width = weight.shape
    per = 2 if heads % 2 == 0 else 1
    rows = chips * 2 * slots

    def kernel(*refs):
        block_refs = refs[:chips][::-1]
        weight_ref, later_ref, keep_ref, send_ref, later_out, left, sem = refs[chips:]
        copy = pltpu.make_async_copy(later_ref, later_out, sem)
        copy.start()
        for d in range(chips):
            for e in range(2):
                row = (d * 2 + e) * slots
                left[row : row + slots, :] = block_refs[d][e, :, META:].astype(F32)
        lhs = left[...].astype(BF16)

        @pl.loop(0, heads // per)
        def _(i):
            right = jnp.concatenate([weight_ref[i * per + j] for j in range(per)], axis=1)
            total = jnp.dot(lhs, right, preferred_element_type=F32)
            columns = pl.ds(pl.multiple_of(i * (per * width), per * width), per * width)
            for d in range(chips):
                row = d * 2 * slots
                keep_ref[d, :, columns] = total[row : row + slots]
                send_ref[d, :, columns] = total[row + slots : row + 2 * slots]

        copy.wait()

    shape = jax.ShapeDtypeStruct((chips, slots, heads * width), F32)
    return pl.pallas_call(
        kernel,
        out_shape=(shape, shape, jax.ShapeDtypeStruct(later.shape, later.dtype)),
        in_specs=[VMEM] * (chips + 1) + [HBM],
        out_specs=(VMEM, VMEM, VMEM),
        scratch_shapes=[pltpu.VMEM((rows, depth), F32), pltpu.SemaphoreType.DMA],
        compiler_params=pltpu.CompilerParams(vmem_limit_bytes=weight.size * 2 + 12 * MIB),
        cost_estimate=cost(2 * rows * weight.size, 2 * weight.size),
        name="project",
    )(*blocks[::-1], weight, *in_hbm(later))


def combine(keep, got, after):
    chips, slots, width = keep.shape
    heads = width // (3 * LANES)

    def kernel(keep_ref, got_ref, _, own_ref, *message_refs):
        own_ref[...] = keep_ref[0] + got_ref[0]
        for d in range(1, chips):
            for h in range(heads):
                total = keep_ref[d, :, 3 * h * LANES : 3 * (h + 1) * LANES] + got_ref[d, :, 3 * h * LANES : 3 * (h + 1) * LANES]
                query = total[:, :LANES]
                high = query.astype(BF16)
                low = (query - high.astype(F32)).astype(BF16)
                base = 4 * h * LANES
                message_refs[d - 1][:, base : base + LANES] = high
                message_refs[d - 1][:, base + LANES : base + 2 * LANES] = low
                message_refs[d - 1][:, base + 2 * LANES : base + 4 * LANES] = total[:, LANES:].astype(BF16)

    message = jax.ShapeDtypeStruct((slots, 4 * heads * LANES), BF16)
    return pl.pallas_call(
        kernel,
        out_shape=(jax.ShapeDtypeStruct((slots, width), F32),) + (message,) * (chips - 1),
        in_specs=[VMEM, VMEM, ANY],
        out_specs=(VMEM,) * chips,
        compiler_params=pltpu.CompilerParams(vmem_limit_bytes=8 * MIB),
        cost_estimate=cost(0, 8 * keep.size),
        name="combine",
    )(keep, got, after)


def attend(lengths, new_slot, page_table, sums, bias, tokens, key_pool, value_pool, after):
    parts = len(sums)
    slots = sums[0].shape[0]
    pages, page, width = key_pool.shape
    head = LANES
    heads = width // head
    max_pages = page_table.shape[1]
    short_rows = slots * page
    groups = 2 * parts
    share = head // groups
    per = LANES // share
    tall = 16
    strips = width // PACK
    scale = head ** (-0.5)

    def kernel(*refs):
        length_ref, slot_ref, table_ref = refs[:3]
        sum_refs = refs[3 : 3 + parts][::-1]
        (bias_ref, token_ref, key_ref, value_ref, _, pack_keep, pack_send, patch_ref, value_out) = refs[
            3 + parts : 12 + parts
        ]
        attended_ref, out_sems = refs[12 + parts :]
        step = pages // 4
        writes = [
            pltpu.make_async_copy(value_ref.at[pl.ds(i * step, step)], value_out.at[pl.ds(i * step, step)], out_sems.at[i])
            for i in range(4)
        ]
        for write in writes:
            write.start()
        here = lax.axis_index("req")
        column_block = lax.axis_index("head")
        leaving = leaving_slot(slot_ref, slots, here)
        lengths = [length_ref[s] for s in range(slots)]
        long_slot = jnp.int32(0)
        long_length = jnp.int32(0)
        for s in range(slots):
            is_long = lengths[s] >= page
            long_slot = jnp.where(is_long, s, long_slot)
            long_length = jnp.where(is_long, lengths[s], long_length)

        total = sum_refs[0][...] + bias_ref[...]

        def third(k):
            columns = []
            for h in range(heads):
                one = total[:, (3 * h + k) * head : (3 * h + k + 1) * head]
                for ref in sum_refs[1:]:
                    base = 4 * h * head
                    if k == 0:
                        one = one + ref[:, base : base + head].astype(F32) + ref[:, base + head : base + 2 * head].astype(F32)
                    else:
                        one = one + ref[:, base + (k + 1) * head : base + (k + 2) * head].astype(F32)
                columns.append(one)
            return jnp.concatenate(columns, axis=1)

        query = (third(0) * scale).astype(BF16).astype(F32)
        new_rows = (third(1).astype(BF16).astype(F32), third(2).astype(BF16).astype(F32))

        lane_head = lax.broadcasted_iota(jnp.int32, (tall, width), 1) // head
        on_head = lane_head == lax.broadcasted_iota(jnp.int32, (tall, width), 0)

        def blocked(row):
            return jnp.where(on_head, jnp.broadcast_to(row, (tall, width)), 0.0).astype(BF16)

        def for_slot(which, rows):
            found = rows[0]
            for s in range(1, slots):
                found = jnp.where(which == s, rows[s], found)
            return found

        def softmax(scores, valid, new_score):
            masked = jnp.where(valid, scores, -1e30)
            peak = jnp.maximum(jnp.max(masked, axis=1, keepdims=True), new_score)
            weights = jnp.where(valid, jnp.exp(masked - peak), 0.0)
            new_weight = jnp.exp(new_score - peak)
            denom = jnp.sum(weights, axis=1, keepdims=True) + new_weight
            return weights.astype(BF16), new_weight.astype(BF16).astype(F32), denom

        across = (((1,), (1,)), ((), ()))
        short_query = jnp.concatenate([blocked(query[s : s + 1]) for s in range(slots)], axis=0)
        new_keys = jnp.concatenate([new_rows[0], jnp.zeros((tall - slots, width), F32)], axis=0).astype(BF16)
        new_scores = lax.dot_general(short_query, new_keys, across, preferred_element_type=F32)
        size = (slots * tall, tall)
        own_column = lax.broadcasted_iota(jnp.int32, size, 0) // tall == lax.broadcasted_iota(jnp.int32, size, 1)
        new_score = jnp.sum(jnp.where(own_column, new_scores, 0.0), axis=1, keepdims=True)

        def fold(mixed):
            return jnp.sum(jnp.where(on_head, mixed, 0.0), axis=0, keepdims=True)

        high = -(-slots // 8) * 8

        def attend_all(long_pages):
            first_pages = lambda ref: jnp.concatenate([ref[table_ref[s, 0]] for s in range(slots)], axis=0)
            short_scores = lax.dot_general(short_query, first_pages(key_ref), across, preferred_element_type=F32)
            size = (slots * tall, short_rows)
            row_slot = lax.broadcasted_iota(jnp.int32, size, 0) // tall
            column = lax.broadcasted_iota(jnp.int32, size, 1)
            limit = jnp.zeros(size, jnp.int32)
            for s in range(slots):
                limit = jnp.where(row_slot == s, lengths[s], limit)
            valid = (row_slot == column // page) & (column % page < limit)
            short_probs, new_prob, short_denom = softmax(short_scores, valid, new_score)
            new_values = jnp.concatenate(
                [jnp.broadcast_to(new_rows[1][s : s + 1], (tall, width)) for s in range(slots)], axis=0
            )
            short_mix = jnp.dot(short_probs, first_pages(value_ref), preferred_element_type=F32)
            short_mix = (short_mix + new_prob * new_values) / short_denom

            rows = [fold(short_mix[s * tall : (s + 1) * tall]) for s in range(slots)]
            if long_pages:
                some_pages = lambda ref: jnp.concatenate(
                    [ref[table_ref[long_slot, i]] for i in range(long_pages)], axis=0
                )
                long_query = blocked(for_slot(long_slot, [query[s : s + 1] for s in range(slots)]))
                long_new = for_slot(long_slot, [new_score[s * tall : (s + 1) * tall] for s in range(slots)])
                long_value = for_slot(long_slot, [new_rows[1][s : s + 1] for s in range(slots)])
                scores = lax.dot_general(long_query, some_pages(key_ref), across, preferred_element_type=F32)
                position = lax.broadcasted_iota(jnp.int32, (tall, long_pages * page), 1)
                long_probs, long_prob, long_denom = softmax(scores, position < long_length, long_new)
                mixed = jnp.dot(long_probs, some_pages(value_ref), preferred_element_type=F32)
                long_mix = fold((mixed + long_prob * long_value) / long_denom)
                rows = [jnp.where(lengths[s] >= page, long_mix, row) for s, row in enumerate(rows)]
            rows += [jnp.zeros((high - slots, width), F32)]
            attended_ref[...] = jnp.concatenate(rows, axis=0).astype(BF16).astype(F32)

        half = max_pages // 2
        pl.when(long_length == 0)(lambda: attend_all(0))
        pl.when((long_length > 0) & (long_length <= half * page))(lambda: attend_all(half))
        pl.when(long_length > half * page)(lambda: attend_all(max_pages))
        attended = attended_ref[...]

        token = token_ref[:, pl.ds(pl.multiple_of(column_block * width, LANES), width)].astype(F32)
        extra = []
        for source in new_rows + (token,):
            one = jnp.zeros((1, width), F32)
            for s in range(slots):
                one = jnp.where(leaving == s, source[s : s + 1], one)
            extra += [one[:, i * PACK : (i + 1) * PACK] for i in range(strips)]
        extra = jnp.concatenate(extra + [jnp.zeros((pack_rows(slots, strips) - high - 3 * strips, PACK), F32)], axis=0)

        lane = lax.broadcasted_iota(jnp.int32, (high, LANES), 1)
        row_at = lax.broadcasted_iota(jnp.int32, (high, LANES), 0)
        goal = jnp.full((high, LANES), -1.0, F32)
        for s in range(slots):
            device, slot = slot_ref[s] // slots, slot_ref[s] % slots
            number = jnp.where(lane % share == share - 1, slot, device).astype(F32)
            goal = jnp.where(row_at == s, number, goal)
        turned = [
            pltpu.roll(attended[:, h * head : (h + 1) * head], h % per * share, 1) if h % per else attended[:, h * head : (h + 1) * head]
            for h in range(heads)
        ]
        for k in range(groups):
            count = lax.rem(lane // share - (here ^ k) + per, per)
            tiles = [jnp.zeros((high, LANES), F32) for _ in range(PACK // LANES)]
            for h in range(heads):
                tiles[h // per] = jnp.where(count == h % per, turned[h], tiles[h // per])
            tiles[-1] = jnp.where((count == per - 1) & (lane % share >= share - 2), goal, tiles[-1])
            block = jnp.concatenate([jnp.concatenate(tiles, axis=1), extra], axis=0).astype(BF16)
            (pack_keep, pack_send)[k % 2][k // 2] = block

        at = lax.broadcasted_iota(jnp.int32, (tall, width), 0)
        for n, ref in enumerate((key_ref, value_ref)):
            for s in range(slots):
                offset = lengths[s] % page
                first = pl.multiple_of(offset // tall * tall, tall)
                old = ref[table_ref[s, lengths[s] // page], pl.ds(first, tall), :].astype(F32)
                new = jnp.broadcast_to(new_rows[n][s : s + 1], (tall, width))
                patch_ref[n, s] = jnp.where(at == offset - first, new, old).astype(BF16)

        for write in writes:
            write.wait()

    packed = jax.ShapeDtypeStruct((parts, pack_rows(slots, strips), PACK), BF16)
    pool = jax.ShapeDtypeStruct(key_pool.shape, key_pool.dtype)
    return pl.pallas_call(
        kernel,
        out_shape=(packed, packed, jax.ShapeDtypeStruct((2, slots, tall, width), BF16), pool),
        in_specs=[SMEM] * 3 + [VMEM] * (parts + 4) + [ANY],
        out_specs=(VMEM, VMEM, VMEM, HBM),
        scratch_shapes=[
            pltpu.VMEM((-(-slots // 8) * 8, width), F32),
            pltpu.SemaphoreType.DMA((4,)),
        ],
        compiler_params=pltpu.CompilerParams(vmem_limit_bytes=18 * MIB),
        cost_estimate=cost(0, 0),
        name="attend",
    )(lengths, new_slot, page_table, *sums[::-1], bias, tokens, key_pool, value_pool, after)


def pack_rows(slots, strips):
    need = -(-slots // 8) * 8 + 3 * strips
    return -(-need // 16) * 16


def out_project(blocks, weight, pieces, slots, *after):
    chips = len(blocks)
    depth, width = weight.shape
    high = -(-slots // 8) * 8
    rows = 2 * chips * slots
    piece = width // pieces

    def kernel(*refs):
        block_refs, weight_ref = refs[:chips][::-1], refs[chips]
        keep_ref, send_ref = refs[chips + 1 + len(after) :]
        gathered = jnp.concatenate(
            [block_refs[d][e, :high, :].astype(F32) for d in range(chips) for e in range(2)], axis=0
        )
        here = lax.axis_index("req")
        share = LANES // (2 * chips)
        back = lax.rem(LANES - here * share, LANES)
        gathered = jnp.concatenate(
            [pltpu.roll(gathered[:, first : first + LANES], back, 1) for first in range(0, PACK, LANES)], axis=1
        )
        goal = gathered[:, PACK - 2 : PACK - 1].astype(jnp.int32)
        place = goal ^ here
        row = (place % 2) * (chips * slots) + (place // 2) * slots + gathered[:, PACK - 1 :].astype(jnp.int32)
        row = jnp.where(goal < 0, -1, row)
        size = (gathered.shape[0], rows)
        order = jnp.where(lax.broadcasted_iota(jnp.int32, size, 1) == row, 1.0, 0.0)
        left = lax.dot_general(
            order.astype(BF16), gathered.astype(BF16), (((0,), (0,)), ((), ())), preferred_element_type=F32
        )
        left = left[:, :depth].astype(BF16)
        for j in range(pieces):
            first = (lax.axis_index("head") ^ j) * piece
            total = jnp.dot(
                left, weight_ref[:, pl.ds(pl.multiple_of(first, LANES), piece)], preferred_element_type=F32
            )
            for d in range(chips):
                keep_ref[d, j] = total[d * slots : (d + 1) * slots]
                send_ref[d, j] = total[(chips + d) * slots : (chips + d + 1) * slots].astype(BF16)

    shape = (chips, pieces, slots, piece)
    return pl.pallas_call(
        kernel,
        out_shape=(jax.ShapeDtypeStruct(shape, F32), jax.ShapeDtypeStruct(shape, BF16)),
        in_specs=[VMEM] * (chips + 1) + [HBM] * min(1, len(after)) + [ANY] * (len(after) - 1),
        out_specs=(VMEM, VMEM),
        compiler_params=pltpu.CompilerParams(vmem_limit_bytes=10 * MIB),
        cost_estimate=cost(2 * rows * weight.size, 2 * weight.size),
        name="out_project",
    )(*blocks[::-1], weight, *after)


def place_page(lengths, new_slot, page_table, sources, patches, packs, tokens, out_bias, halves, turned, from_other, key_out, value_out):
    chips, across, rows = len(packs), len(halves), len(turned)
    down = chips // across
    count = across + rows + 1
    page, width = key_out.shape[1:]
    half = page // 2
    slots = tokens.shape[0]
    high = -(-slots // 8) * 8
    strips = width // PACK

    tall = patches.shape[2]

    def kernel(length_ref, slot_ref, table_ref, source_ref, patch_ref, *refs):
        pack_refs = refs[:chips][::-1]
        token_ref, bias_ref = refs[chips : chips + 2]
        half_refs = refs[chips + 2 : chips + 2 + across]
        turned_refs = refs[chips + 2 + across : chips + 2 + across + rows]
        other_ref = refs[chips + 1 + count]
        _, _, base_ref, key_ref, value_ref, buffer, arrived, out_sems, patch_sems = refs[chips + 2 + count :]
        here = lax.axis_index("req")
        leaving = leaving_slot(slot_ref, slots, here)

        def patch(n, s):
            length = length_ref[s]
            first = pl.multiple_of(length % page // tall * tall, tall)
            target = (key_ref, value_ref)[n].at[table_ref[s, length // page], pl.ds(first, tall)]
            return pltpu.make_async_copy(patch_ref.at[n, s], target, patch_sems.at[n, s])

        for n in range(2):
            for s in range(slots):

                @pl.when(leaving != s)
                def _():
                    patch(n, s).start()

        column = pl.multiple_of(lax.axis_index("head") * width, LANES)
        page_at, offset, source = [number_at(source_ref, 2 * down + j) for j in range(3)]
        own_rows, other_rows = [pl.ds(pl.multiple_of((here % 2 ^ e) * half, half), half) for e in range(2)]

        def use(ref):
            buffer[:, own_rows, :] = ref[...]

        with_half(number_at(source_ref, 0), across, 0, half_refs, turned_refs, use)
        buffer[:, other_rows, :] = other_ref[...]
        for d in range(chips):
            for e in range(2):

                @pl.when(source == 2 * d + e)
                def _():
                    arrived[...] = pack_refs[d][e].astype(F32)

        def fresh(n):
            strip = high + n * strips
            return jnp.concatenate([arrived[strip + i : strip + i + 1, :] for i in range(strips)], axis=1)

        at = lax.broadcasted_iota(jnp.int32, (slots, width), 0)
        token = jnp.where(
            at == leaving,
            jnp.broadcast_to(fresh(2), (slots, width)),
            token_ref[:, pl.ds(column, width)].astype(F32),
        )
        base_ref[...] = token + bias_ref[:, pl.ds(column, width)]
        first = pl.multiple_of(offset // 16 * 16, 16)
        row = lax.broadcasted_iota(jnp.int32, (16, width), 0)
        for n in range(2):
            old = buffer[n, pl.ds(first, 16), :].astype(F32)
            new = jnp.broadcast_to(fresh(n), (16, width))
            buffer[n, pl.ds(first, 16), :] = jnp.where(row == offset - first, new, old).astype(BF16)
        copies = [
            pltpu.make_async_copy(buffer.at[n], target.at[page_at], out_sems.at[n])
            for n, target in enumerate((key_ref, value_ref))
        ]
        for copy in copies:
            copy.start()
        for n in range(2):
            for s in range(slots):

                @pl.when(leaving != s)
                def _():
                    patch(n, s).wait()

        for copy in copies:
            copy.wait()

    shape = jax.ShapeDtypeStruct(key_out.shape, key_out.dtype)
    return pl.pallas_call(
        kernel,
        out_shape=(jax.ShapeDtypeStruct((slots, width), F32), shape, shape),
        in_specs=[SMEM] * 3 + [VMEM] * (chips + 4 + count) + [HBM] * 2,
        out_specs=(VMEM, HBM, HBM),
        scratch_shapes=[
            pltpu.VMEM((2, page, width), BF16),
            pltpu.VMEM(packs[0].shape[1:], F32),
            pltpu.SemaphoreType.DMA((2,)),
            pltpu.SemaphoreType.DMA((2, slots)),
        ],
        input_output_aliases={chips + 7 + count: 1, chips + 8 + count: 2},
        compiler_params=pltpu.CompilerParams(vmem_limit_bytes=(6 + count) * MIB),
        cost_estimate=cost(0, 8 * page * width),
        name="place_page",
    )(
        lengths, new_slot, page_table, sources, patches, *packs[::-1], tokens, out_bias, *halves, *turned, from_other, key_out, value_out
    )


def body(
    tokens,
    norm_gain,
    norm_shift,
    qkv_weight,
    qkv_bias,
    out_weight,
    out_bias,
    key_pool,
    value_pool,
    lengths,
    page_table,
    new_slot,
    new_page,
):
    groups = lax.axis_size("req")
    head_groups = lax.axis_size("head")
    slots = tokens.shape[0]
    chips = groups // 2

    keep, send, keep_half, send_half = prepare(
        tokens, norm_gain[None], norm_shift[None], lengths, page_table, new_slot, new_page, key_pool, value_pool
    )
    got = swap(send, "req", 1)
    spread = spread_pairs(keep, got)
    across = row_length(chips)
    halves = [jnp.stack([keep_half, swap(send_half, "req", 1)])]
    halves += [swap_pages(halves[0], chips, True, d) for d in range(1, across)]
    flat = out_weight.reshape(-1, out_weight.shape[2])
    keep, send, staged = project(spread, jnp.transpose(qkv_weight, (1, 0, 2)), flat)
    got = swap(send, "req", 1)
    sources = find_sources(spread, keep)
    own, *messages = combine(keep, got, sources)
    turning = turn_pages(sources, halves, chips)
    turned = [swap_pages(one, chips, False, row + 1) for row, one in enumerate(turning)]
    sums = [own] + [swap(messages[d - 1], "req", 2 * d) for d in range(1, chips)]

    pack_keep, pack_send, patches, value_out = attend(
        lengths,
        new_slot,
        page_table,
        sums,
        qkv_bias.reshape(1, -1),
        tokens,
        key_pool,
        value_pool,
        turning[0],
    )
    packs_got = swap(pack_send, "req", 1)
    packs = spread_pairs(pack_keep, packs_got)
    key_out = write_pool(key_pool, packs_got)


    keep, send = out_project(
        packs, staged, head_groups, slots, *in_hbm(key_out), turned[0]
    )
    total = keep + swap(send, "req", 1).astype(F32)
    from_other = swap(choose_half(sources, halves, turned, keep), "req", 1)
    summed = total[0]
    for d in range(1, chips):
        summed = summed + swap(total[d].astype(BF16), "req", 2 * d).astype(F32)
    base, key_out, value_out = place_page(
        lengths,
        new_slot,
        page_table,
        sources,
        patches,
        packs,
        tokens,
        out_bias[None],
        halves,
        turned,
        from_other,
        key_out,
        value_out,
    )
    summed, base = lax.optimization_barrier((summed, base))
    hidden = summed[0]
    for j in range(1, head_groups):
        hidden = hidden + swap(summed[j].astype(BF16), "head", j).astype(F32)
    hidden_out = (hidden + base).astype(BF16)
    return (hidden_out, key_out, value_out)


def solution(mesh):
    in_specs = (
        P("req", None),
        P(),
        P(),
        P("req", "head", None),
        P("head", None),
        P("head", "req", None),
        P(),
        P("req", None, "head"),
        P("req", None, "head"),
        P("req"),
        P("req", None),
        P("req"),
        P("req"),
    )
    out_specs = (P("req", "head"), P("req", None, "head"), P("req", None, "head"))
    return jax.shard_map(body, mesh=mesh, in_specs=in_specs, out_specs=out_specs, check_vma=False)
```

```python
import functools

import jax
import jax.numpy as jnp
from jax import lax
from jax.experimental import pallas as pl
from jax.experimental.pallas import tpu as pltpu
from jax.sharding import PartitionSpec as P

EPSILON = 1e-05
F32 = jnp.float32
BF16 = jnp.bfloat16
LANES = 128
META = 128
PACK = 256
VMEM = pl.BlockSpec(memory_space=pltpu.VMEM)
SMEM = pl.BlockSpec(memory_space=pltpu.SMEM)
ANY = pl.BlockSpec(memory_space=pl.ANY)
HBM = pl.BlockSpec(memory_space=pltpu.HBM)
MIB = 1024 * 1024


def cost(flops, moved):
    del flops, moved
    return pl.CostEstimate(flops=0, bytes_accessed=0, transcendentals=0)


def swap(value, axis, step):
    size = lax.axis_size(axis)
    return lax.ppermute(value, axis, [(i, i ^ step) for i in range(size)])


def spread_pairs(keep, got):
    chips = keep.shape[0]
    return [jnp.stack([keep[0], got[0]])] + [
        swap(jnp.stack([keep[d], got[d]]), "req", 2 * d) for d in range(1, chips)
    ]


def in_hbm(*arrays):
    return [pltpu.with_memory_space_constraint(array, pltpu.HBM) for array in arrays]


def write_pool(pool, after):
    parts = 4
    step = pool.shape[0] // parts

    def kernel(pool_ref, _, out_ref, sems):
        places = [pl.ds(i * step, step) for i in range(parts)]
        copies = [
            pltpu.make_async_copy(pool_ref.at[place], out_ref.at[place], sems.at[i]) for i, place in enumerate(places)
        ]
        for copy in copies:
            copy.start()
        for copy in copies:
            copy.wait()

    return pl.pallas_call(
        kernel,
        out_shape=jax.ShapeDtypeStruct(pool.shape, pool.dtype),
        in_specs=[VMEM, ANY],
        out_specs=HBM,
        scratch_shapes=[pltpu.SemaphoreType.DMA((parts,))],
        compiler_params=pltpu.CompilerParams(vmem_limit_bytes=8 * MIB),
        cost_estimate=cost(0, 2 * pool.size),
        name="write_pool",
    )(pool, after)


def leaving_slot(new_slot_ref, slots, here):
    leaving = jnp.int32(0)
    for s in range(slots):
        leaving = jnp.where(new_slot_ref[s] // slots != here, s, leaving)
    return leaving


def prepare(tokens, gain, shift, lengths, page_table, new_slot, new_page, key_pool, value_pool):
    groups = lax.axis_size("req")
    chips = groups // 2
    slots, model = tokens.shape
    depth = model // groups
    page, width = key_pool.shape[1:]
    half = page // 2

    def kernel(
        token_ref, gain_ref, shift_ref, length_ref, table_ref, slot_ref, page_ref, key_ref, value_ref,
        keep_ref, send_ref, keep_half, send_half, normed, sems,
    ):
        here = lax.axis_index("req")
        leaving = leaving_slot(slot_ref, slots, here)
        copies = []
        for n, source in enumerate((key_ref, value_ref)):
            for e, target in enumerate((keep_half, send_half)):
                rows = pl.ds(pl.multiple_of((here % 2 ^ e) * half, half), half)
                copies.append(
                    pltpu.make_async_copy(source.at[table_ref[leaving, 0], rows], target.at[n], sems.at[n, e])
                )
        for copy in copies:
            copy.start()
        values = token_ref[...].astype(F32)
        average = jnp.mean(values, axis=1, keepdims=True)
        centered = values - average
        variance = jnp.mean(centered * centered, axis=1, keepdims=True)
        rows = centered * lax.rsqrt(variance + EPSILON) * gain_ref[...] + shift_ref[...]
        normed[...] = rows.astype(BF16).astype(F32)
        row = lax.broadcasted_iota(jnp.int32, (slots, META), 0)
        lane = lax.broadcasted_iota(jnp.int32, (slots, META), 1)
        told = jnp.zeros((slots, META), F32)
        for s in range(slots):
            slot = slot_ref[s]
            numbers = (slot // slots, slot % slots, page_ref[s], length_ref[s] % page)
            for j, number in enumerate(numbers):
                told = jnp.where((row == s) & (lane == j), number.astype(F32), told)
        told = told.astype(BF16)
        for k in range(groups):
            first = (here ^ k) * depth
            if depth % LANES == 0:
                block = normed[:, pl.ds(pl.multiple_of(first, LANES), depth)]
            else:
                block = pltpu.roll(normed[...], lax.rem(model - first, model), 1)[:, :depth]
            target = (keep_ref, send_ref)[k % 2]
            target[k // 2, :, :META] = told
            target[k // 2, :, META:] = block.astype(BF16)
        for copy in copies:
            copy.wait()

    blocks = jax.ShapeDtypeStruct((chips, slots, META + depth), BF16)
    halves = jax.ShapeDtypeStruct((2, half, width), key_pool.dtype)
    return pl.pallas_call(
        kernel,
        out_shape=(blocks, blocks, halves, halves),
        in_specs=[VMEM] * 3 + [SMEM] * 4 + [HBM] * 2,
        out_specs=(VMEM,) * 4,
        scratch_shapes=[pltpu.VMEM((slots, model), F32), pltpu.SemaphoreType.DMA((2, 2))],
        compiler_params=pltpu.CompilerParams(vmem_limit_bytes=4 * MIB),
        cost_estimate=cost(0, 8 * page * width),
        name="prepare",
    )(*in_hbm(tokens, gain, shift, lengths, page_table, new_slot, new_page, key_pool, value_pool))


def arrivals(block_refs, here, wanted):
    slots = block_refs[0].shape[1]
    lane = lax.broadcasted_iota(jnp.int32, (slots, META), 1)
    found = jnp.zeros((slots, META), F32)
    goal = here ^ wanted
    for d, ref in enumerate(block_refs):
        for e in range(2):
            k = 2 * d + e
            told = ref[e, :, :META].astype(F32)
            numbered = jnp.where(lane == 4, float(k), told)
            found = jnp.where(told[:, :1] == jnp.where(wanted == k, -1, goal).astype(F32), numbered, found)
    return lambda j: jnp.sum(jnp.where(lane == j, found, 0.0)).astype(jnp.int32)


def row_length(chips):
    return 1 << (chips.bit_length() // 2)


def swap_pages(value, chips, along_row, step):
    across = row_length(chips)
    square = across * across == chips
    steps = [2 * step if along_row == (device % 2 == 0 or not square) else 2 * across * step for device in range(2 * chips)]
    return lax.ppermute(value, "req", [(i, i ^ steps[i]) for i in range(2 * chips)])


def find_sources(spread, after):
    chips = len(spread)
    across = row_length(chips)
    down = chips // across

    def kernel(*refs):
        block_refs, out_ref = refs[:chips][::-1], refs[-1]
        here = lax.axis_index("req")
        lane = lax.broadcasted_iota(jnp.int32, (8, LANES), 1)
        found = jnp.zeros((8, LANES), F32)
        put = lambda j, number: jnp.where(lane == j, number.astype(F32), found)
        turned = (here % 2 == 1) & (across == down)
        for row in range(down):
            for j in range(2):
                pick = arrivals(block_refs, here, jnp.where(turned, 2 * row, 2 * across * row) + j)
                source = pick(4)
                chip = source // 2
                chip = jnp.where(turned, chip % across * across + chip // across, chip)
                found = put(2 * row + j, 2 * chip + source % 2)
                if row == 0 and j == 0:
                    found = put(2 * down, pick(2))
                    found = put(2 * down + 1, pick(3))
        out_ref[...] = found

    return pl.pallas_call(
        kernel,
        out_shape=jax.ShapeDtypeStruct((8, LANES), F32),
        in_specs=[VMEM] * chips + [ANY],
        out_specs=VMEM,
        compiler_params=pltpu.CompilerParams(vmem_limit_bytes=2 * MIB),
        cost_estimate=cost(0, 0),
        name="find_sources",
    )(*spread[::-1], after)


def number_at(source_ref, j):
    lane = lax.broadcasted_iota(jnp.int32, (1, LANES), 1)
    return jnp.sum(jnp.where(lane == j, source_ref[:1, :], 0.0)).astype(jnp.int32)


def turn_pages(sources, halves, chips):
    across = len(halves)
    down = chips // across
    shape = halves[0].shape

    def kernel(source_ref, *refs):
        half_refs, out_refs = refs[:across], refs[across:]
        for row in range(1, down):
            for j in range(2):
                source = number_at(source_ref, 2 * row + j)
                place = jnp.where(source < 2 * across, source, 0)
                for d in range(across):
                    for e in range(2):

                        @pl.when(place == 2 * d + e)
                        def _():
                            out_refs[row - 1][j] = half_refs[d][e]

    one = jax.ShapeDtypeStruct(shape, halves[0].dtype)
    return pl.pallas_call(
        kernel,
        out_shape=(one,) * (down - 1),
        in_specs=[VMEM] * (1 + across),
        out_specs=(VMEM,) * (down - 1),
        compiler_params=pltpu.CompilerParams(vmem_limit_bytes=(across + down) * MIB),
        cost_estimate=cost(0, 4 * halves[0].size),
        name="turn_pages",
    )(sources, *halves)


def with_half(source, across, core, half_refs, turned_refs, use):
    place = jnp.where(source < 2 * across, source, 2 * across + source // (2 * across))
    for d, ref in enumerate(half_refs):
        for e in range(2):

            @pl.when(place == 2 * d + e)
            def _():
                use(ref.at[e])

    for row, ref in enumerate(turned_refs):

        @pl.when(place == 2 * across + row + 1)
        def _():
            use(ref.at[core])


def choose_half(sources, halves, turned, after):
    across, rows = len(halves), len(turned)

    def kernel(source_ref, *refs):
        half_refs, turned_refs = refs[:across], refs[across : across + rows]
        out_ref = refs[-1]

        def use(ref):
            out_ref[...] = ref[...]

        with_half(number_at(source_ref, 1), across, 1, half_refs, turned_refs, use)

    shape = halves[0].shape[1:]
    return pl.pallas_call(
        kernel,
        out_shape=jax.ShapeDtypeStruct(shape, halves[0].dtype),
        in_specs=[VMEM] * (1 + across + rows) + [ANY],
        out_specs=VMEM,
        compiler_params=pltpu.CompilerParams(vmem_limit_bytes=(1 + across + rows) * MIB),
        cost_estimate=cost(0, 2 * halves[0].size),
        name="choose_half",
    )(sources, *halves, *turned, after)


def project(blocks, weight, later):
    chips = len(blocks)
    slots = blocks[0].shape[1]
    heads, depth, width = weight.shape
    per = 2 if heads % 2 == 0 else 1
    rows = chips * 2 * slots

    def kernel(*refs):
        block_refs = refs[:chips][::-1]
        weight_ref, later_ref, keep_ref, send_ref, later_out, left, sem = refs[chips:]
        copy = pltpu.make_async_copy(later_ref, later_out, sem)
        copy.start()
        for d in range(chips):
            for e in range(2):
                row = (d * 2 + e) * slots
                left[row : row + slots, :] = block_refs[d][e, :, META:].astype(F32)
        lhs = left[...].astype(BF16)

        @pl.loop(0, heads // per)
        def _(i):
            right = jnp.concatenate([weight_ref[i * per + j] for j in range(per)], axis=1)
            total = jnp.dot(lhs, right, preferred_element_type=F32)
            columns = pl.ds(pl.multiple_of(i * (per * width), per * width), per * width)
            for d in range(chips):
                row = d * 2 * slots
                keep_ref[d, :, columns] = total[row : row + slots]
                send_ref[d, :, columns] = total[row + slots : row + 2 * slots]

        copy.wait()

    shape = jax.ShapeDtypeStruct((chips, slots, heads * width), F32)
    return pl.pallas_call(
        kernel,
        out_shape=(shape, shape, jax.ShapeDtypeStruct(later.shape, later.dtype)),
        in_specs=[VMEM] * (chips + 1) + [HBM],
        out_specs=(VMEM, VMEM, VMEM),
        scratch_shapes=[pltpu.VMEM((rows, depth), F32), pltpu.SemaphoreType.DMA],
        compiler_params=pltpu.CompilerParams(vmem_limit_bytes=weight.size * 2 + 12 * MIB),
        cost_estimate=cost(2 * rows * weight.size, 2 * weight.size),
        name="project",
    )(*blocks[::-1], weight, *in_hbm(later))


def combine(keep, got, after):
    chips, slots, width = keep.shape
    heads = width // (3 * LANES)

    def kernel(keep_ref, got_ref, _, own_ref, *message_refs):
        own_ref[...] = keep_ref[0] + got_ref[0]
        for d in range(1, chips):
            for h in range(heads):
                total = keep_ref[d, :, 3 * h * LANES : 3 * (h + 1) * LANES] + got_ref[d, :, 3 * h * LANES : 3 * (h + 1) * LANES]
                query = total[:, :LANES]
                high = query.astype(BF16)
                low = (query - high.astype(F32)).astype(BF16)
                base = 4 * h * LANES
                message_refs[d - 1][:, base : base + LANES] = high
                message_refs[d - 1][:, base + LANES : base + 2 * LANES] = low
                message_refs[d - 1][:, base + 2 * LANES : base + 4 * LANES] = total[:, LANES:].astype(BF16)

    message = jax.ShapeDtypeStruct((slots, 4 * heads * LANES), BF16)
    return pl.pallas_call(
        kernel,
        out_shape=(jax.ShapeDtypeStruct((slots, width), F32),) + (message,) * (chips - 1),
        in_specs=[VMEM, VMEM, ANY],
        out_specs=(VMEM,) * chips,
        compiler_params=pltpu.CompilerParams(vmem_limit_bytes=8 * MIB),
        cost_estimate=cost(0, 8 * keep.size),
        name="combine",
    )(keep, got, after)


def attend(lengths, new_slot, page_table, sums, bias, tokens, key_pool, value_pool, after):
    parts = len(sums)
    slots = sums[0].shape[0]
    pages, page, width = key_pool.shape
    head = LANES
    heads = width // head
    max_pages = page_table.shape[1]
    short_rows = slots * page
    groups = 2 * parts
    share = head // groups
    per = LANES // share
    tall = 16
    strips = width // PACK
    scale = head ** (-0.5)

    def kernel(*refs):
        length_ref, slot_ref, table_ref = refs[:3]
        sum_refs = refs[3 : 3 + parts][::-1]
        (bias_ref, token_ref, key_ref, value_ref, _, pack_keep, pack_send, patch_ref, value_out) = refs[
            3 + parts : 12 + parts
        ]
        attended_ref, out_sems = refs[12 + parts :]
        step = pages // 4
        writes = [
            pltpu.make_async_copy(value_ref.at[pl.ds(i * step, step)], value_out.at[pl.ds(i * step, step)], out_sems.at[i])
            for i in range(4)
        ]
        for write in writes:
            write.start()
        here = lax.axis_index("req")
        column_block = lax.axis_index("head")
        leaving = leaving_slot(slot_ref, slots, here)
        lengths = [length_ref[s] for s in range(slots)]
        long_slot = jnp.int32(0)
        long_length = jnp.int32(0)
        for s in range(slots):
            is_long = lengths[s] >= page
            long_slot = jnp.where(is_long, s, long_slot)
            long_length = jnp.where(is_long, lengths[s], long_length)

        total = sum_refs[0][...] + bias_ref[...]

        def third(k):
            columns = []
            for h in range(heads):
                one = total[:, (3 * h + k) * head : (3 * h + k + 1) * head]
                for ref in sum_refs[1:]:
                    base = 4 * h * head
                    if k == 0:
                        one = one + ref[:, base : base + head].astype(F32) + ref[:, base + head : base + 2 * head].astype(F32)
                    else:
                        one = one + ref[:, base + (k + 1) * head : base + (k + 2) * head].astype(F32)
                columns.append(one)
            return jnp.concatenate(columns, axis=1)

        query = (third(0) * scale).astype(BF16).astype(F32)
        new_rows = (third(1).astype(BF16).astype(F32), third(2).astype(BF16).astype(F32))

        lane_head = lax.broadcasted_iota(jnp.int32, (tall, width), 1) // head
        on_head = lane_head == lax.broadcasted_iota(jnp.int32, (tall, width), 0)

        def blocked(row):
            return jnp.where(on_head, jnp.broadcast_to(row, (tall, width)), 0.0).astype(BF16)

        def for_slot(which, rows):
            found = rows[0]
            for s in range(1, slots):
                found = jnp.where(which == s, rows[s], found)
            return found

        def softmax(scores, valid, new_score):
            masked = jnp.where(valid, scores, -1e30)
            peak = jnp.maximum(jnp.max(masked, axis=1, keepdims=True), new_score)
            weights = jnp.where(valid, jnp.exp(masked - peak), 0.0)
            new_weight = jnp.exp(new_score - peak)
            denom = jnp.sum(weights, axis=1, keepdims=True) + new_weight
            return weights.astype(BF16), new_weight.astype(BF16).astype(F32), denom

        across = (((1,), (1,)), ((), ()))
        short_query = jnp.concatenate([blocked(query[s : s + 1]) for s in range(slots)], axis=0)
        new_keys = jnp.concatenate([new_rows[0], jnp.zeros((tall - slots, width), F32)], axis=0).astype(BF16)
        new_scores = lax.dot_general(short_query, new_keys, across, preferred_element_type=F32)
        size = (slots * tall, tall)
        own_column = lax.broadcasted_iota(jnp.int32, size, 0) // tall == lax.broadcasted_iota(jnp.int32, size, 1)
        new_score = jnp.sum(jnp.where(own_column, new_scores, 0.0), axis=1, keepdims=True)

        def fold(mixed):
            return jnp.sum(jnp.where(on_head, mixed, 0.0), axis=0, keepdims=True)

        high = -(-slots // 8) * 8

        def attend_all(long_pages):
            first_pages = lambda ref: jnp.concatenate([ref[table_ref[s, 0]] for s in range(slots)], axis=0)
            short_scores = lax.dot_general(short_query, first_pages(key_ref), across, preferred_element_type=F32)
            size = (slots * tall, short_rows)
            row_slot = lax.broadcasted_iota(jnp.int32, size, 0) // tall
            column = lax.broadcasted_iota(jnp.int32, size, 1)
            limit = jnp.zeros(size, jnp.int32)
            for s in range(slots):
                limit = jnp.where(row_slot == s, lengths[s], limit)
            valid = (row_slot == column // page) & (column % page < limit)
            short_probs, new_prob, short_denom = softmax(short_scores, valid, new_score)
            new_values = jnp.concatenate(
                [jnp.broadcast_to(new_rows[1][s : s + 1], (tall, width)) for s in range(slots)], axis=0
            )
            short_mix = jnp.dot(short_probs, first_pages(value_ref), preferred_element_type=F32)
            short_mix = (short_mix + new_prob * new_values) / short_denom

            rows = [fold(short_mix[s * tall : (s + 1) * tall]) for s in range(slots)]
            if long_pages:
                some_pages = lambda ref: jnp.concatenate(
                    [ref[table_ref[long_slot, i]] for i in range(long_pages)], axis=0
                )
                long_query = blocked(for_slot(long_slot, [query[s : s + 1] for s in range(slots)]))
                long_new = for_slot(long_slot, [new_score[s * tall : (s + 1) * tall] for s in range(slots)])
                long_value = for_slot(long_slot, [new_rows[1][s : s + 1] for s in range(slots)])
                scores = lax.dot_general(long_query, some_pages(key_ref), across, preferred_element_type=F32)
                position = lax.broadcasted_iota(jnp.int32, (tall, long_pages * page), 1)
                long_probs, long_prob, long_denom = softmax(scores, position < long_length, long_new)
                mixed = jnp.dot(long_probs, some_pages(value_ref), preferred_element_type=F32)
                long_mix = fold((mixed + long_prob * long_value) / long_denom)
                rows = [jnp.where(lengths[s] >= page, long_mix, row) for s, row in enumerate(rows)]
            rows += [jnp.zeros((high - slots, width), F32)]
            attended_ref[...] = jnp.concatenate(rows, axis=0).astype(BF16).astype(F32)

        half = max_pages // 2
        pl.when(long_length == 0)(lambda: attend_all(0))
        pl.when((long_length > 0) & (long_length <= half * page))(lambda: attend_all(half))
        pl.when(long_length > half * page)(lambda: attend_all(max_pages))
        attended = attended_ref[...]

        toward = jnp.int32(0)
        for s in range(slots):
            toward = jnp.where(leaving == s, slot_ref[s] // slots ^ here, toward)
        token = token_ref[:, pl.ds(pl.multiple_of(column_block * width, LANES), width)].astype(F32)
        extra = []
        for source in new_rows + (token,):
            one = jnp.zeros((1, width), F32)
            for s in range(slots):
                one = jnp.where(leaving == s, source[s : s + 1], one)
            extra += [one[:, i * PACK : (i + 1) * PACK] for i in range(strips)]
        extra = jnp.concatenate(extra + [jnp.zeros((pack_rows(slots, strips) - high - 3 * strips, PACK), F32)], axis=0)

        lane = lax.broadcasted_iota(jnp.int32, (high, LANES), 1)
        row_at = lax.broadcasted_iota(jnp.int32, (high, LANES), 0)
        goal = jnp.full((high, LANES), -1.0, F32)
        for s in range(slots):
            device, slot = slot_ref[s] // slots, slot_ref[s] % slots
            number = jnp.where(lane % share == share - 1, slot, device).astype(F32)
            goal = jnp.where(row_at == s, number, goal)
        turned = [
            pltpu.roll(attended[:, h * head : (h + 1) * head], h % per * share, 1) if h % per else attended[:, h * head : (h + 1) * head]
            for h in range(heads)
        ]
        for k in range(groups):
            count = lax.rem(lane // share - (here ^ k) + per, per)
            tiles = [jnp.zeros((high, LANES), F32) for _ in range(PACK // LANES)]
            for h in range(heads):
                tiles[h // per] = jnp.where(count == h % per, turned[h], tiles[h // per])
            tiles[-1] = jnp.where((count == per - 1) & (lane % share >= share - 2), goal, tiles[-1])
            block = jnp.concatenate([jnp.concatenate(tiles, axis=1), jnp.where(toward == k, extra, 0.0)], axis=0).astype(BF16)
            (pack_keep, pack_send)[k % 2][k // 2] = block

        at = lax.broadcasted_iota(jnp.int32, (tall, width), 0)
        for n, ref in enumerate((key_ref, value_ref)):
            for s in range(slots):
                offset = lengths[s] % page
                first = pl.multiple_of(offset // tall * tall, tall)
                old = ref[table_ref[s, lengths[s] // page], pl.ds(first, tall), :].astype(F32)
                new = jnp.broadcast_to(new_rows[n][s : s + 1], (tall, width))
                patch_ref[n, s] = jnp.where(at == offset - first, new, old).astype(BF16)

        for write in writes:
            write.wait()

    packed = jax.ShapeDtypeStruct((parts, pack_rows(slots, strips), PACK), BF16)
    pool = jax.ShapeDtypeStruct(key_pool.shape, key_pool.dtype)
    return pl.pallas_call(
        kernel,
        out_shape=(packed, packed, jax.ShapeDtypeStruct((2, slots, tall, width), BF16), pool),
        in_specs=[SMEM] * 3 + [VMEM] * (parts + 4) + [ANY],
        out_specs=(VMEM, VMEM, VMEM, HBM),
        scratch_shapes=[
            pltpu.VMEM((-(-slots // 8) * 8, width), F32),
            pltpu.SemaphoreType.DMA((4,)),
        ],
        compiler_params=pltpu.CompilerParams(vmem_limit_bytes=18 * MIB),
        cost_estimate=cost(0, 0),
        name="attend",
    )(lengths, new_slot, page_table, *sums[::-1], bias, tokens, key_pool, value_pool, after)


def pack_rows(slots, strips):
    need = -(-slots // 8) * 8 + 3 * strips
    return -(-need // 16) * 16


def out_project(blocks, weight, pieces, slots, *after):
    chips = len(blocks)
    depth, width = weight.shape
    rows = 2 * chips * slots
    piece = width // pieces

    def kernel(*refs):
        block_refs, weight_ref = refs[:chips][::-1], refs[chips]
        keep_ref, send_ref = refs[chips + 1 + len(after) :]
        gathered = jnp.concatenate(
            [block_refs[d][: 2 * slots, :].astype(F32) for d in range(chips)], axis=0
        )
        here = lax.axis_index("req")
        share = LANES // (2 * chips)
        back = lax.rem(LANES - here * share, LANES)
        gathered = jnp.concatenate(
            [pltpu.roll(gathered[:, first : first + LANES], back, 1) for first in range(0, PACK, LANES)], axis=1
        )
        goal = gathered[:, PACK - 2 : PACK - 1].astype(jnp.int32)
        place = goal ^ here
        row = (place % 2) * (chips * slots) + (place // 2) * slots + gathered[:, PACK - 1 :].astype(jnp.int32)
        row = jnp.where(goal < 0, -1, row)
        size = (gathered.shape[0], rows)
        order = jnp.where(lax.broadcasted_iota(jnp.int32, size, 1) == row, 1.0, 0.0)
        left = lax.dot_general(
            order.astype(BF16), gathered.astype(BF16), (((0,), (0,)), ((), ())), preferred_element_type=F32
        )
        left = left[:, :depth].astype(BF16)
        for j in range(pieces):
            first = (lax.axis_index("head") ^ j) * piece
            total = jnp.dot(
                left, weight_ref[:, pl.ds(pl.multiple_of(first, LANES), piece)], preferred_element_type=F32
            )
            for d in range(chips):
                keep_ref[d, j] = total[d * slots : (d + 1) * slots]
                send_ref[d, j] = total[(chips + d) * slots : (chips + d + 1) * slots].astype(BF16)

    shape = (chips, pieces, slots, piece)
    return pl.pallas_call(
        kernel,
        out_shape=(jax.ShapeDtypeStruct(shape, F32), jax.ShapeDtypeStruct(shape, BF16)),
        in_specs=[VMEM] * (chips + 1) + [ANY] * len(after),
        out_specs=(VMEM, VMEM),
        compiler_params=pltpu.CompilerParams(vmem_limit_bytes=10 * MIB),
        cost_estimate=cost(2 * rows * weight.size, 2 * weight.size),
        name="out_project",
    )(*blocks[::-1], weight, *after)


def place_page(lengths, new_slot, page_table, sources, patches, packs, tokens, out_bias, halves, turned, from_other, key_out, value_out):
    chips, across, rows = len(packs), len(halves), len(turned)
    down = chips // across
    count = across + rows + 1
    page, width = key_out.shape[1:]
    half = page // 2
    slots = tokens.shape[0]
    strips = width // PACK
    tall = patches.shape[2]

    def kernel(length_ref, slot_ref, table_ref, source_ref, patch_ref, *refs):
        pack_refs = refs[:chips][::-1]
        token_ref, bias_ref = refs[chips : chips + 2]
        half_refs = refs[chips + 2 : chips + 2 + across]
        turned_refs = refs[chips + 2 + across : chips + 2 + across + rows]
        other_ref = refs[chips + 1 + count]
        _, _, base_ref, key_ref, value_ref, buffer, out_sems, patch_sems = refs[chips + 2 + count :]
        here = lax.axis_index("req")
        leaving = leaving_slot(slot_ref, slots, here)

        def patch(n, s):
            length = length_ref[s]
            first = pl.multiple_of(length % page // tall * tall, tall)
            target = (key_ref, value_ref)[n].at[table_ref[s, length // page], pl.ds(first, tall)]
            return pltpu.make_async_copy(patch_ref.at[n, s], target, patch_sems.at[n, s])

        for n in range(2):
            for s in range(slots):

                @pl.when(leaving != s)
                def _():
                    patch(n, s).start()

        column = pl.multiple_of(lax.axis_index("head") * width, LANES)
        page_at, offset = [number_at(source_ref, 2 * down + j) for j in range(2)]
        own_rows, other_rows = [pl.ds(pl.multiple_of((here % 2 ^ e) * half, half), half) for e in range(2)]

        def use(ref):
            buffer[:, own_rows, :] = ref[...]

        with_half(number_at(source_ref, 0), across, 0, half_refs, turned_refs, use)
        buffer[:, other_rows, :] = other_ref[...]
        arrived = pack_refs[0][2 * slots :, :].astype(F32)
        for ref in pack_refs[1:]:
            arrived = arrived + ref[2 * slots :, :].astype(F32)

        def fresh(n):
            return jnp.concatenate([arrived[n * strips + i : n * strips + i + 1, :] for i in range(strips)], axis=1)

        at = lax.broadcasted_iota(jnp.int32, (slots, width), 0)
        token = jnp.where(
            at == leaving,
            jnp.broadcast_to(fresh(2), (slots, width)),
            token_ref[:, pl.ds(column, width)].astype(F32),
        )
        base_ref[...] = token + bias_ref[:, pl.ds(column, width)]
        first = pl.multiple_of(offset // 16 * 16, 16)
        row = lax.broadcasted_iota(jnp.int32, (16, width), 0)
        for n in range(2):
            old = buffer[n, pl.ds(first, 16), :].astype(F32)
            new = jnp.broadcast_to(fresh(n), (16, width))
            buffer[n, pl.ds(first, 16), :] = jnp.where(row == offset - first, new, old).astype(BF16)
        copies = [
            pltpu.make_async_copy(buffer.at[n], target.at[page_at], out_sems.at[n])
            for n, target in enumerate((key_ref, value_ref))
        ]
        for copy in copies:
            copy.start()
        for n in range(2):
            for s in range(slots):

                @pl.when(leaving != s)
                def _():
                    patch(n, s).wait()

        for copy in copies:
            copy.wait()

    shape = jax.ShapeDtypeStruct(key_out.shape, key_out.dtype)
    return pl.pallas_call(
        kernel,
        out_shape=(jax.ShapeDtypeStruct((slots, width), F32), shape, shape),
        in_specs=[SMEM] * 3 + [VMEM] * (chips + 4 + count) + [HBM] * 2,
        out_specs=(VMEM, HBM, HBM),
        scratch_shapes=[
            pltpu.VMEM((2, page, width), BF16),
            pltpu.SemaphoreType.DMA((2,)),
            pltpu.SemaphoreType.DMA((2, slots)),
        ],
        input_output_aliases={chips + 7 + count: 1, chips + 8 + count: 2},
        compiler_params=pltpu.CompilerParams(vmem_limit_bytes=(6 + count) * MIB),
        cost_estimate=cost(0, 8 * page * width),
        name="place_page",
    )(
        lengths, new_slot, page_table, sources, patches, *packs[::-1], tokens, out_bias, *halves, *turned, from_other, key_out, value_out
    )


def body(
    tokens,
    norm_gain,
    norm_shift,
    qkv_weight,
    qkv_bias,
    out_weight,
    out_bias,
    key_pool,
    value_pool,
    lengths,
    page_table,
    new_slot,
    new_page,
):
    groups = lax.axis_size("req")
    head_groups = lax.axis_size("head")
    slots = tokens.shape[0]
    chips = groups // 2

    keep, send, keep_half, send_half = prepare(
        tokens, norm_gain[None], norm_shift[None], lengths, page_table, new_slot, new_page, key_pool, value_pool
    )
    got = swap(send, "req", 1)
    spread = spread_pairs(keep, got)
    across = row_length(chips)
    halves = [jnp.stack([keep_half, swap(send_half, "req", 1)])]
    halves += [swap_pages(halves[0], chips, True, d) for d in range(1, across)]
    flat = out_weight.reshape(-1, out_weight.shape[2])
    keep, send, staged = project(spread, jnp.transpose(qkv_weight, (1, 0, 2)), flat)
    got = swap(send, "req", 1)
    sources = find_sources(spread, keep)
    own, *messages = combine(keep, got, sources)
    turning = turn_pages(sources, halves, chips)
    turned = [swap_pages(one, chips, False, row + 1) for row, one in enumerate(turning)]
    sums = [own] + [swap(messages[d - 1], "req", 2 * d) for d in range(1, chips)]

    pack_keep, pack_send, patches, value_out = attend(
        lengths,
        new_slot,
        page_table,
        sums,
        qkv_bias.reshape(1, -1),
        tokens,
        key_pool,
        value_pool,
        turning[0],
    )
    packs_got = swap(pack_send, "req", 1)
    high = -(-slots // 8) * 8
    merged = [
        jnp.concatenate([pack_keep[d, :slots], packs_got[d, :slots], pack_keep[d, high:] + packs_got[d, high:]], axis=0)
        for d in range(chips)
    ]
    packs = [merged[0]] + [swap(merged[d], "req", 2 * d) for d in range(1, chips)]

    keep, send = out_project(
        packs, staged, head_groups, slots, turned[0]
    )
    total = keep + swap(send, "req", 1).astype(F32)
    from_other = swap(choose_half(sources, halves, turned, keep), "req", 1)
    summed = total[0]
    for d in reversed(range(1, chips)):
        summed = summed + swap(total[d].astype(BF16), "req", 2 * d).astype(F32)
    key_out = write_pool(key_pool, from_other)
    summed, key_out = lax.optimization_barrier((summed, key_out))
    base, key_out, value_out = place_page(
        lengths,
        new_slot,
        page_table,
        sources,
        patches,
        packs,
        tokens,
        out_bias[None],
        halves,
        turned,
        from_other,
        key_out,
        value_out,
    )
    hidden = summed[0]
    for j in [head_groups - 1, *range(1, head_groups - 1)]:
        hidden = hidden + swap(summed[j].astype(BF16), "head", j).astype(F32)
    hidden_out = (hidden + base).astype(BF16)
    return (hidden_out, key_out, value_out)


def solution(mesh):
    in_specs = (
        P("req", None),
        P(),
        P(),
        P("req", "head", None),
        P("head", None),
        P("head", "req", None),
        P(),
        P("req", None, "head"),
        P("req", None, "head"),
        P("req"),
        P("req", None),
        P("req"),
        P("req"),
    )
    out_specs = (P("req", "head"), P("req", None, "head"), P("req", None, "head"))
    return jax.shard_map(body, mesh=mesh, in_specs=in_specs, out_specs=out_specs, check_vma=False)
```

```python
import functools

import jax
import jax.numpy as jnp
from jax import lax
from jax.experimental import pallas as pl
from jax.experimental.pallas import tpu as pltpu
from jax.sharding import PartitionSpec as P

EPSILON = 1e-05
F32 = jnp.float32
BF16 = jnp.bfloat16
LANES = 128
META = 128
PACK = 256
VMEM = pl.BlockSpec(memory_space=pltpu.VMEM)
SMEM = pl.BlockSpec(memory_space=pltpu.SMEM)
ANY = pl.BlockSpec(memory_space=pl.ANY)
HBM = pl.BlockSpec(memory_space=pltpu.HBM)
MIB = 1024 * 1024


def cost(flops, moved):
    del flops, moved
    return pl.CostEstimate(flops=0, bytes_accessed=0, transcendentals=0)


def swap(value, axis, step):
    size = lax.axis_size(axis)
    return lax.ppermute(value, axis, [(i, i ^ step) for i in range(size)])


def in_hbm(*arrays):
    return [pltpu.with_memory_space_constraint(array, pltpu.HBM) for array in arrays]


def write_pool(pool, after):
    parts = 4
    step = pool.shape[0] // parts

    def kernel(pool_ref, _, out_ref, sems):
        places = [pl.ds(i * step, step) for i in range(parts)]
        copies = [
            pltpu.make_async_copy(pool_ref.at[place], out_ref.at[place], sems.at[i]) for i, place in enumerate(places)
        ]
        for copy in copies:
            copy.start()
        for copy in copies:
            copy.wait()

    return pl.pallas_call(
        kernel,
        out_shape=jax.ShapeDtypeStruct(pool.shape, pool.dtype),
        in_specs=[VMEM, ANY],
        out_specs=HBM,
        scratch_shapes=[pltpu.SemaphoreType.DMA((parts,))],
        compiler_params=pltpu.CompilerParams(vmem_limit_bytes=8 * MIB),
        cost_estimate=cost(0, 2 * pool.size),
        name="write_pool",
    )(pool, after)


def leaving_slot(new_slot_ref, slots, here):
    leaving = jnp.int32(0)
    for s in range(slots):
        leaving = jnp.where(new_slot_ref[s] // slots != here, s, leaving)
    return leaving


def pick_halves(lengths, page_table, new_slot, new_page, tokens, key_pool, value_pool):
    slots = new_slot.shape[0]
    page, width = key_pool.shape[1:]
    half = page // 2

    def kernel(
        length_ref, table_ref, slot_ref, page_ref, token_ref, key_ref, value_ref,
        keep_half, send_half, told_ref, token_out, sems,
    ):
        here = lax.axis_index("req")
        leaving = leaving_slot(slot_ref, slots, here)
        copies = []
        for n, source in enumerate((key_ref, value_ref)):
            for e, target in enumerate((keep_half, send_half)):
                rows = pl.ds(pl.multiple_of((here % 2 ^ e) * half, half), half)
                copies.append(
                    pltpu.make_async_copy(source.at[table_ref[leaving, 0], rows], target.at[n], sems.at[n, e])
                )
        for copy in copies:
            copy.start()
        row = lax.broadcasted_iota(jnp.int32, (slots, META), 0)
        lane = lax.broadcasted_iota(jnp.int32, (slots, META), 1)
        told = jnp.zeros((slots, META), F32)
        for s in range(slots):
            slot = slot_ref[s]
            numbers = (slot // slots, slot % slots, page_ref[s], length_ref[s] % page)
            for j, number in enumerate(numbers):
                told = jnp.where((row == s) & (lane == j), number.astype(F32), told)
        told_ref[...] = told
        token_out[...] = token_ref[...]
        for copy in copies:
            copy.wait()

    halves = jax.ShapeDtypeStruct((2, half, width), key_pool.dtype)
    return pl.pallas_call(
        kernel,
        out_shape=(
            halves,
            halves,
            jax.ShapeDtypeStruct((slots, META), F32),
            jax.ShapeDtypeStruct(tokens.shape, tokens.dtype),
        ),
        in_specs=[SMEM] * 4 + [VMEM] + [HBM] * 2,
        out_specs=(VMEM,) * 4,
        scratch_shapes=[pltpu.SemaphoreType.DMA((2, 2))],
        compiler_params=pltpu.CompilerParams(vmem_limit_bytes=2 * MIB),
        cost_estimate=cost(0, 8 * page * width),
        name="pick_halves",
    )(*in_hbm(lengths, page_table, new_slot, new_page, tokens, key_pool, value_pool))


def prepare(tokens, other_tokens, gain, shift, told):
    groups = lax.axis_size("req")
    chips = groups // 2
    slots, model = tokens.shape
    depth = model // groups

    def kernel(token_ref, other_ref, gain_ref, shift_ref, told_ref, *refs):
        out_refs, normed = refs[:chips], refs[chips]
        here = lax.axis_index("req")
        values = jnp.concatenate([token_ref[...].astype(F32), other_ref[...].astype(F32)], axis=0)
        average = jnp.mean(values, axis=1, keepdims=True)
        centered = values - average
        variance = jnp.mean(centered * centered, axis=1, keepdims=True)
        rows = centered * lax.rsqrt(variance + EPSILON) * gain_ref[...] + shift_ref[...]
        normed[...] = rows.astype(BF16).astype(F32)
        for d in range(chips):
            first = (here ^ 2 * d) * depth
            if depth % LANES == 0:
                block = normed[:, pl.ds(pl.multiple_of(first, LANES), depth)]
            else:
                block = pltpu.roll(normed[...], lax.rem(model - first, model), 1)[:, :depth]
            for e in range(2):
                out_refs[d][e, :, META:] = block[e * slots : (e + 1) * slots].astype(BF16)
            out_refs[d][0, :, :META] = told_ref[...].astype(BF16)
            out_refs[d][1, :, :META] = jnp.zeros((slots, META), BF16)

    return pl.pallas_call(
        kernel,
        out_shape=(jax.ShapeDtypeStruct((2, slots, META + depth), BF16),) * chips,
        in_specs=[VMEM] * 5,
        out_specs=(VMEM,) * chips,
        scratch_shapes=[pltpu.VMEM((2 * slots, model), F32)],
        compiler_params=pltpu.CompilerParams(vmem_limit_bytes=4 * MIB),
        cost_estimate=cost(0, 0),
        name="prepare",
    )(tokens, other_tokens, gain, shift, told)


def arrivals(tables, here, wanted):
    slots = tables[0].shape[0]
    lane = lax.broadcasted_iota(jnp.int32, (slots, META), 1)
    found = jnp.zeros((slots, META), F32)
    goal = here ^ wanted
    for k, told in enumerate(tables):
        numbered = jnp.where(lane == 4, float(k), told)
        found = jnp.where(told[:, :1] == jnp.where(wanted == k, -1, goal).astype(F32), numbered, found)
    return lambda j: jnp.sum(jnp.where(lane == j, found, 0.0)).astype(jnp.int32)


def row_length(chips):
    return 1 << (chips.bit_length() // 2)


def swap_pages(value, chips, along_row, step):
    across = row_length(chips)
    square = across * across == chips
    steps = [2 * step if along_row == (device % 2 == 0 or not square) else 2 * across * step for device in range(2 * chips)]
    return lax.ppermute(value, "req", [(i, i ^ steps[i]) for i in range(2 * chips)])


def find_sources(spread, got):
    chips = len(spread)
    across = row_length(chips)
    down = chips // across

    def kernel(*refs):
        block_refs, got_ref, out_ref = refs[:chips][::-1], refs[-2], refs[-1]
        here = lax.axis_index("req")
        tables = []
        for d in range(chips):
            tables += [block_refs[d][0, :, :META].astype(F32), got_ref[d, :, got_ref.shape[2] - META :]]
        lane = lax.broadcasted_iota(jnp.int32, (8, LANES), 1)
        found = jnp.zeros((8, LANES), F32)
        put = lambda j, number: jnp.where(lane == j, number.astype(F32), found)
        turned = (here % 2 == 1) & (across == down)
        for row in range(down):
            for j in range(2):
                pick = arrivals(tables, here, jnp.where(turned, 2 * row, 2 * across * row) + j)
                source = pick(4)
                chip = source // 2
                chip = jnp.where(turned, chip % across * across + chip // across, chip)
                found = put(2 * row + j, 2 * chip + source % 2)
                if row == 0 and j == 0:
                    found = put(2 * down, pick(2))
                    found = put(2 * down + 1, pick(3))
        out_ref[...] = found

    return pl.pallas_call(
        kernel,
        out_shape=jax.ShapeDtypeStruct((8, LANES), F32),
        in_specs=[VMEM] * (chips + 1),
        out_specs=VMEM,
        compiler_params=pltpu.CompilerParams(vmem_limit_bytes=4 * MIB),
        cost_estimate=cost(0, 0),
        name="find_sources",
    )(*spread[::-1], got)


def number_at(source_ref, j):
    lane = lax.broadcasted_iota(jnp.int32, (1, LANES), 1)
    return jnp.sum(jnp.where(lane == j, source_ref[:1, :], 0.0)).astype(jnp.int32)


def turn_pages(sources, halves, chips):
    across = len(halves)
    down = chips // across
    shape = halves[0].shape

    def kernel(source_ref, *refs):
        half_refs, out_refs = refs[:across], refs[across:]
        for row in range(1, down):
            for j in range(2):
                source = number_at(source_ref, 2 * row + j)
                place = jnp.where(source < 2 * across, source, 0)
                for d in range(across):
                    for e in range(2):

                        @pl.when(place == 2 * d + e)
                        def _():
                            out_refs[row - 1][j] = half_refs[d][e]

    one = jax.ShapeDtypeStruct(shape, halves[0].dtype)
    return pl.pallas_call(
        kernel,
        out_shape=(one,) * (down - 1),
        in_specs=[VMEM] * (1 + across),
        out_specs=(VMEM,) * (down - 1),
        compiler_params=pltpu.CompilerParams(vmem_limit_bytes=(across + down) * MIB),
        cost_estimate=cost(0, 4 * halves[0].size),
        name="turn_pages",
    )(sources, *halves)


def with_half(source, across, core, half_refs, turned_refs, use):
    place = jnp.where(source < 2 * across, source, 2 * across + source // (2 * across))
    for d, ref in enumerate(half_refs):
        for e in range(2):

            @pl.when(place == 2 * d + e)
            def _():
                use(ref.at[e])

    for row, ref in enumerate(turned_refs):

        @pl.when(place == 2 * across + row + 1)
        def _():
            use(ref.at[core])


def choose_half(sources, halves, turned, after):
    across, rows = len(halves), len(turned)

    def kernel(source_ref, *refs):
        half_refs, turned_refs = refs[:across], refs[across : across + rows]
        out_ref = refs[-1]

        def use(ref):
            out_ref[...] = ref[...]

        with_half(number_at(source_ref, 1), across, 1, half_refs, turned_refs, use)

    shape = halves[0].shape[1:]
    return pl.pallas_call(
        kernel,
        out_shape=jax.ShapeDtypeStruct(shape, halves[0].dtype),
        in_specs=[VMEM] * (1 + across + rows) + [ANY],
        out_specs=VMEM,
        compiler_params=pltpu.CompilerParams(vmem_limit_bytes=(1 + across + rows) * MIB),
        cost_estimate=cost(0, 2 * halves[0].size),
        name="choose_half",
    )(sources, *halves, *turned, after)


def project(blocks, weight, later):
    chips = len(blocks)
    slots = blocks[0].shape[1]
    heads, depth, width = weight.shape
    per = 2 if heads % 2 == 0 else 1
    rows = chips * 2 * slots

    def kernel(*refs):
        block_refs = refs[:chips][::-1]
        weight_ref, later_ref, keep_ref, send_ref, later_out, left, sem = refs[chips:]
        copy = pltpu.make_async_copy(later_ref, later_out, sem)
        copy.start()
        for d in range(chips):
            for e in range(2):
                row = (d * 2 + e) * slots
                left[row : row + slots, :] = block_refs[d][e, :, META:].astype(F32)
        lhs = left[...].astype(BF16)

        @pl.loop(0, heads // per)
        def _(i):
            right = jnp.concatenate([weight_ref[i * per + j] for j in range(per)], axis=1)
            total = jnp.dot(lhs, right, preferred_element_type=F32)
            columns = pl.ds(pl.multiple_of(i * (per * width), per * width), per * width)
            for d in range(chips):
                row = d * 2 * slots
                keep_ref[d, :, columns] = total[row : row + slots]
                send_ref[d, :, columns] = total[row + slots : row + 2 * slots]

        for d in range(chips):
            send_ref[d, :, heads * width :] = block_refs[d][0, :, :META].astype(F32)
        copy.wait()

    shape = jax.ShapeDtypeStruct((chips, slots, heads * width), F32)
    wider = jax.ShapeDtypeStruct((chips, slots, heads * width + META), F32)
    return pl.pallas_call(
        kernel,
        out_shape=(shape, wider, jax.ShapeDtypeStruct(later.shape, later.dtype)),
        in_specs=[VMEM] * (chips + 1) + [HBM],
        out_specs=(VMEM, VMEM, VMEM),
        scratch_shapes=[pltpu.VMEM((rows, depth), F32), pltpu.SemaphoreType.DMA],
        compiler_params=pltpu.CompilerParams(vmem_limit_bytes=weight.size * 2 + 12 * MIB),
        cost_estimate=cost(2 * rows * weight.size, 2 * weight.size),
        name="project",
    )(*blocks[::-1], weight, *in_hbm(later))


def combine(keep, got):
    chips, slots, width = keep.shape
    heads = width // (3 * LANES)

    def kernel(keep_ref, got_ref, own_ref, *message_refs):
        own_ref[...] = keep_ref[0] + got_ref[0, :, :width]
        for d in range(1, chips):
            for h in range(heads):
                total = keep_ref[d, :, 3 * h * LANES : 3 * (h + 1) * LANES] + got_ref[d, :, 3 * h * LANES : 3 * (h + 1) * LANES]
                query = total[:, :LANES]
                high = query.astype(BF16)
                low = (query - high.astype(F32)).astype(BF16)
                base = 4 * h * LANES
                message_refs[d - 1][:, base : base + LANES] = high
                message_refs[d - 1][:, base + LANES : base + 2 * LANES] = low
                message_refs[d - 1][:, base + 2 * LANES : base + 4 * LANES] = total[:, LANES:].astype(BF16)

    message = jax.ShapeDtypeStruct((slots, 4 * heads * LANES), BF16)
    return pl.pallas_call(
        kernel,
        out_shape=(jax.ShapeDtypeStruct((slots, width), F32),) + (message,) * (chips - 1),
        in_specs=[VMEM, VMEM],
        out_specs=(VMEM,) * chips,
        compiler_params=pltpu.CompilerParams(vmem_limit_bytes=8 * MIB),
        cost_estimate=cost(0, 8 * keep.size),
        name="combine",
    )(keep, got)


def attend(lengths, new_slot, page_table, sums, bias, tokens, key_pool, value_pool, written, after):
    parts = len(sums)
    slots = sums[0].shape[0]
    pages, page, width = key_pool.shape
    head = LANES
    heads = width // head
    max_pages = page_table.shape[1]
    short_rows = slots * page
    groups = 2 * parts
    share = head // groups
    per = LANES // share
    tall = 16
    strips = width // PACK
    scale = head ** (-0.5)

    def kernel(*refs):
        length_ref, slot_ref, table_ref = refs[:3]
        sum_refs = refs[3 : 3 + parts][::-1]
        (bias_ref, token_ref, key_ref, value_ref, _, _, pack_keep, pack_send, patch_ref, attended_ref) = refs[3 + parts :]
        here = lax.axis_index("req")
        column_block = lax.axis_index("head")
        leaving = leaving_slot(slot_ref, slots, here)
        lengths = [length_ref[s] for s in range(slots)]
        long_slot = jnp.int32(0)
        long_length = jnp.int32(0)
        for s in range(slots):
            is_long = lengths[s] >= page
            long_slot = jnp.where(is_long, s, long_slot)
            long_length = jnp.where(is_long, lengths[s], long_length)

        total = sum_refs[0][...] + bias_ref[...]

        def third(k):
            columns = []
            for h in range(heads):
                one = total[:, (3 * h + k) * head : (3 * h + k + 1) * head]
                for ref in sum_refs[1:]:
                    base = 4 * h * head
                    if k == 0:
                        one = one + ref[:, base : base + head].astype(F32) + ref[:, base + head : base + 2 * head].astype(F32)
                    else:
                        one = one + ref[:, base + (k + 1) * head : base + (k + 2) * head].astype(F32)
                columns.append(one)
            return jnp.concatenate(columns, axis=1)

        query = (third(0) * scale).astype(BF16).astype(F32)
        new_rows = (third(1).astype(BF16).astype(F32), third(2).astype(BF16).astype(F32))

        lane_head = lax.broadcasted_iota(jnp.int32, (tall, width), 1) // head
        on_head = lane_head == lax.broadcasted_iota(jnp.int32, (tall, width), 0)

        def blocked(row):
            return jnp.where(on_head, jnp.broadcast_to(row, (tall, width)), 0.0).astype(BF16)

        def for_slot(which, rows):
            found = rows[0]
            for s in range(1, slots):
                found = jnp.where(which == s, rows[s], found)
            return found

        def softmax(scores, valid, new_score):
            masked = jnp.where(valid, scores, -1e30)
            peak = jnp.maximum(jnp.max(masked, axis=1, keepdims=True), new_score)
            weights = jnp.where(valid, jnp.exp(masked - peak), 0.0)
            new_weight = jnp.exp(new_score - peak)
            denom = jnp.sum(weights, axis=1, keepdims=True) + new_weight
            return weights.astype(BF16), new_weight.astype(BF16).astype(F32), denom

        across = (((1,), (1,)), ((), ()))
        short_query = jnp.concatenate([blocked(query[s : s + 1]) for s in range(slots)], axis=0)
        new_keys = jnp.concatenate([new_rows[0], jnp.zeros((tall - slots, width), F32)], axis=0).astype(BF16)
        new_scores = lax.dot_general(short_query, new_keys, across, preferred_element_type=F32)
        size = (slots * tall, tall)
        own_column = lax.broadcasted_iota(jnp.int32, size, 0) // tall == lax.broadcasted_iota(jnp.int32, size, 1)
        new_score = jnp.sum(jnp.where(own_column, new_scores, 0.0), axis=1, keepdims=True)

        def fold(mixed):
            return jnp.sum(jnp.where(on_head, mixed, 0.0), axis=0, keepdims=True)

        high = -(-slots // 8) * 8

        def attend_all(long_pages):
            first_pages = lambda ref: jnp.concatenate([ref[table_ref[s, 0]] for s in range(slots)], axis=0)
            short_scores = lax.dot_general(short_query, first_pages(key_ref), across, preferred_element_type=F32)
            size = (slots * tall, short_rows)
            row_slot = lax.broadcasted_iota(jnp.int32, size, 0) // tall
            column = lax.broadcasted_iota(jnp.int32, size, 1)
            limit = jnp.zeros(size, jnp.int32)
            for s in range(slots):
                limit = jnp.where(row_slot == s, lengths[s], limit)
            valid = (row_slot == column // page) & (column % page < limit)
            short_probs, new_prob, short_denom = softmax(short_scores, valid, new_score)
            new_values = jnp.concatenate(
                [jnp.broadcast_to(new_rows[1][s : s + 1], (tall, width)) for s in range(slots)], axis=0
            )
            short_mix = jnp.dot(short_probs, first_pages(value_ref), preferred_element_type=F32)
            short_mix = (short_mix + new_prob * new_values) / short_denom

            rows = [fold(short_mix[s * tall : (s + 1) * tall]) for s in range(slots)]
            if long_pages:
                some_pages = lambda ref: jnp.concatenate(
                    [ref[table_ref[long_slot, i]] for i in range(long_pages)], axis=0
                )
                long_query = blocked(for_slot(long_slot, [query[s : s + 1] for s in range(slots)]))
                long_new = for_slot(long_slot, [new_score[s * tall : (s + 1) * tall] for s in range(slots)])
                long_value = for_slot(long_slot, [new_rows[1][s : s + 1] for s in range(slots)])
                scores = lax.dot_general(long_query, some_pages(key_ref), across, preferred_element_type=F32)
                position = lax.broadcasted_iota(jnp.int32, (tall, long_pages * page), 1)
                long_probs, long_prob, long_denom = softmax(scores, position < long_length, long_new)
                mixed = jnp.dot(long_probs, some_pages(value_ref), preferred_element_type=F32)
                long_mix = fold((mixed + long_prob * long_value) / long_denom)
                rows = [jnp.where(lengths[s] >= page, long_mix, row) for s, row in enumerate(rows)]
            rows += [jnp.zeros((high - slots, width), F32)]
            attended_ref[...] = jnp.concatenate(rows, axis=0).astype(BF16).astype(F32)

        half = max_pages // 2
        pl.when(long_length == 0)(lambda: attend_all(0))
        pl.when((long_length > 0) & (long_length <= half * page))(lambda: attend_all(half))
        pl.when(long_length > half * page)(lambda: attend_all(max_pages))
        attended = attended_ref[...]

        toward = jnp.int32(0)
        for s in range(slots):
            toward = jnp.where(leaving == s, slot_ref[s] // slots ^ here, toward)
        token = token_ref[:, pl.ds(pl.multiple_of(column_block * width, LANES), width)].astype(F32)
        extra = []
        for source in new_rows + (token,):
            one = jnp.zeros((1, width), F32)
            for s in range(slots):
                one = jnp.where(leaving == s, source[s : s + 1], one)
            extra += [one[:, i * PACK : (i + 1) * PACK] for i in range(strips)]
        extra = jnp.concatenate(extra + [jnp.zeros((pack_rows(slots, strips) - high - 3 * strips, PACK), F32)], axis=0)

        lane = lax.broadcasted_iota(jnp.int32, (high, LANES), 1)
        row_at = lax.broadcasted_iota(jnp.int32, (high, LANES), 0)
        goal = jnp.full((high, LANES), -1.0, F32)
        for s in range(slots):
            device, slot = slot_ref[s] // slots, slot_ref[s] % slots
            number = jnp.where(lane % share == share - 1, slot, device).astype(F32)
            goal = jnp.where(row_at == s, number, goal)
        turned = [
            pltpu.roll(attended[:, h * head : (h + 1) * head], h % per * share, 1) if h % per else attended[:, h * head : (h + 1) * head]
            for h in range(heads)
        ]
        for k in range(groups):
            count = lax.rem(lane // share - (here ^ k) + per, per)
            tiles = [jnp.zeros((high, LANES), F32) for _ in range(PACK // LANES)]
            for h in range(heads):
                tiles[h // per] = jnp.where(count == h % per, turned[h], tiles[h // per])
            tiles[-1] = jnp.where((count == per - 1) & (lane % share >= share - 2), goal, tiles[-1])
            block = jnp.concatenate([jnp.concatenate(tiles, axis=1), jnp.where(toward == k, extra, 0.0)], axis=0).astype(BF16)
            (pack_keep, pack_send)[k % 2][k // 2] = block

        at = lax.broadcasted_iota(jnp.int32, (tall, width), 0)
        for n, ref in enumerate((key_ref, value_ref)):
            for s in range(slots):
                offset = lengths[s] % page
                first = pl.multiple_of(offset // tall * tall, tall)
                old = ref[table_ref[s, lengths[s] // page], pl.ds(first, tall), :].astype(F32)
                new = jnp.broadcast_to(new_rows[n][s : s + 1], (tall, width))
                patch_ref[n, s] = jnp.where(at == offset - first, new, old).astype(BF16)

    packed = jax.ShapeDtypeStruct((parts, pack_rows(slots, strips), PACK), BF16)
    return pl.pallas_call(
        kernel,
        out_shape=(packed, packed, jax.ShapeDtypeStruct((2, slots, tall, width), BF16)),
        in_specs=[SMEM] * 3 + [VMEM] * (parts + 4) + [HBM, ANY],
        out_specs=(VMEM, VMEM, VMEM),
        scratch_shapes=[pltpu.VMEM((-(-slots // 8) * 8, width), F32)],
        compiler_params=pltpu.CompilerParams(vmem_limit_bytes=18 * MIB),
        cost_estimate=cost(0, 0),
        name="attend",
    )(lengths, new_slot, page_table, *sums[::-1], bias, tokens, key_pool, value_pool, *in_hbm(written), after)


def pack_rows(slots, strips):
    need = -(-slots // 8) * 8 + 3 * strips
    return -(-need // 16) * 16


def out_project(blocks, weight, pieces, slots, *after):
    chips = len(blocks)
    depth, width = weight.shape
    rows = 2 * chips * slots
    piece = width // pieces

    def kernel(*refs):
        block_refs, weight_ref = refs[:chips][::-1], refs[chips]
        keep_ref, send_ref = refs[chips + 1 + len(after) :]
        gathered = jnp.concatenate(
            [block_refs[d][: 2 * slots, :].astype(F32) for d in range(chips)], axis=0
        )
        here = lax.axis_index("req")
        share = LANES // (2 * chips)
        back = lax.rem(LANES - here * share, LANES)
        gathered = jnp.concatenate(
            [pltpu.roll(gathered[:, first : first + LANES], back, 1) for first in range(0, PACK, LANES)], axis=1
        )
        goal = gathered[:, PACK - 2 : PACK - 1].astype(jnp.int32)
        place = goal ^ here
        row = (place % 2) * (chips * slots) + (place // 2) * slots + gathered[:, PACK - 1 :].astype(jnp.int32)
        row = jnp.where(goal < 0, -1, row)
        size = (gathered.shape[0], rows)
        order = jnp.where(lax.broadcasted_iota(jnp.int32, size, 1) == row, 1.0, 0.0)
        left = lax.dot_general(
            order.astype(BF16), gathered.astype(BF16), (((0,), (0,)), ((), ())), preferred_element_type=F32
        )
        left = left[:, :depth].astype(BF16)
        for j in range(pieces):
            first = (lax.axis_index("head") ^ j) * piece
            total = jnp.dot(
                left, weight_ref[:, pl.ds(pl.multiple_of(first, LANES), piece)], preferred_element_type=F32
            )
            for d in range(chips):
                keep_ref[d, j] = total[d * slots : (d + 1) * slots]
                send_ref[d, j] = total[(chips + d) * slots : (chips + d + 1) * slots].astype(BF16)

    shape = (chips, pieces, slots, piece)
    return pl.pallas_call(
        kernel,
        out_shape=(jax.ShapeDtypeStruct(shape, F32), jax.ShapeDtypeStruct(shape, BF16)),
        in_specs=[VMEM] * (chips + 1) + [ANY] * len(after),
        out_specs=(VMEM, VMEM),
        compiler_params=pltpu.CompilerParams(vmem_limit_bytes=10 * MIB),
        cost_estimate=cost(2 * rows * weight.size, 2 * weight.size),
        name="out_project",
    )(*blocks[::-1], weight, *after)


def place_page(lengths, new_slot, page_table, sources, patches, packs, tokens, out_bias, halves, turned, from_other, key_out, value_out):
    chips, across, rows = len(packs), len(halves), len(turned)
    down = chips // across
    count = across + rows + 1
    page, width = key_out.shape[1:]
    half = page // 2
    slots = tokens.shape[0]
    strips = width // PACK
    tall = patches.shape[2]

    def kernel(length_ref, slot_ref, table_ref, source_ref, patch_ref, *refs):
        pack_refs = refs[:chips][::-1]
        token_ref, bias_ref = refs[chips : chips + 2]
        half_refs = refs[chips + 2 : chips + 2 + across]
        turned_refs = refs[chips + 2 + across : chips + 2 + across + rows]
        other_ref = refs[chips + 1 + count]
        _, _, base_ref, key_ref, value_ref, buffer, out_sems, patch_sems = refs[chips + 2 + count :]
        here = lax.axis_index("req")
        leaving = leaving_slot(slot_ref, slots, here)

        def patch(n, s):
            length = length_ref[s]
            first = pl.multiple_of(length % page // tall * tall, tall)
            target = (key_ref, value_ref)[n].at[table_ref[s, length // page], pl.ds(first, tall)]
            return pltpu.make_async_copy(patch_ref.at[n, s], target, patch_sems.at[n, s])

        for n in range(2):
            for s in range(slots):

                @pl.when(leaving != s)
                def _():
                    patch(n, s).start()

        column = pl.multiple_of(lax.axis_index("head") * width, LANES)
        page_at, offset = [number_at(source_ref, 2 * down + j) for j in range(2)]
        own_rows, other_rows = [pl.ds(pl.multiple_of((here % 2 ^ e) * half, half), half) for e in range(2)]

        def use(ref):
            buffer[:, own_rows, :] = ref[...]

        with_half(number_at(source_ref, 0), across, 0, half_refs, turned_refs, use)
        buffer[:, other_rows, :] = other_ref[...]
        arrived = pack_refs[0][2 * slots :, :].astype(F32)
        for ref in pack_refs[1:]:
            arrived = arrived + ref[2 * slots :, :].astype(F32)

        def fresh(n):
            return jnp.concatenate([arrived[n * strips + i : n * strips + i + 1, :] for i in range(strips)], axis=1)

        at = lax.broadcasted_iota(jnp.int32, (slots, width), 0)
        token = jnp.where(
            at == leaving,
            jnp.broadcast_to(fresh(2), (slots, width)),
            token_ref[:, pl.ds(column, width)].astype(F32),
        )
        base_ref[...] = token + bias_ref[:, pl.ds(column, width)]
        first = pl.multiple_of(offset // 16 * 16, 16)
        row = lax.broadcasted_iota(jnp.int32, (16, width), 0)
        for n in range(2):
            old = buffer[n, pl.ds(first, 16), :].astype(F32)
            new = jnp.broadcast_to(fresh(n), (16, width))
            buffer[n, pl.ds(first, 16), :] = jnp.where(row == offset - first, new, old).astype(BF16)
        copies = [
            pltpu.make_async_copy(buffer.at[n], target.at[page_at], out_sems.at[n])
            for n, target in enumerate((key_ref, value_ref))
        ]
        for copy in copies:
            copy.start()
        for n in range(2):
            for s in range(slots):

                @pl.when(leaving != s)
                def _():
                    patch(n, s).wait()

        for copy in copies:
            copy.wait()

    shape = jax.ShapeDtypeStruct(key_out.shape, key_out.dtype)
    return pl.pallas_call(
        kernel,
        out_shape=(jax.ShapeDtypeStruct((slots, width), F32), shape, shape),
        in_specs=[SMEM] * 3 + [VMEM] * (chips + 4 + count) + [HBM] * 2,
        out_specs=(VMEM, HBM, HBM),
        scratch_shapes=[
            pltpu.VMEM((2, page, width), BF16),
            pltpu.SemaphoreType.DMA((2,)),
            pltpu.SemaphoreType.DMA((2, slots)),
        ],
        input_output_aliases={chips + 7 + count: 1, chips + 8 + count: 2},
        compiler_params=pltpu.CompilerParams(vmem_limit_bytes=(6 + count) * MIB),
        cost_estimate=cost(0, 8 * page * width),
        name="place_page",
    )(
        lengths, new_slot, page_table, sources, patches, *packs[::-1], tokens, out_bias, *halves, *turned, from_other, key_out, value_out
    )


def body(
    tokens,
    norm_gain,
    norm_shift,
    qkv_weight,
    qkv_bias,
    out_weight,
    out_bias,
    key_pool,
    value_pool,
    lengths,
    page_table,
    new_slot,
    new_page,
):
    groups = lax.axis_size("req")
    head_groups = lax.axis_size("head")
    slots = tokens.shape[0]
    chips = groups // 2

    other_tokens = swap(tokens, "req", 1)
    keep_half, send_half, told, own_tokens = pick_halves(
        lengths, page_table, new_slot, new_page, tokens, key_pool, value_pool
    )
    blocks = prepare(own_tokens, other_tokens, norm_gain[None], norm_shift[None], told)
    send_half, *blocks = lax.optimization_barrier((send_half, *blocks))
    across = row_length(chips)
    spread = [blocks[0]] + [swap(blocks[d], "req", 2 * d) for d in range(1, chips)]
    halves = [jnp.stack([keep_half, swap(send_half, "req", 1)])]
    halves[0], *spread = lax.optimization_barrier((halves[0], *spread[::-1]))
    spread = spread[::-1]
    halves += [swap_pages(halves[0], chips, True, d) for d in range(1, across)]
    flat = out_weight.reshape(-1, out_weight.shape[2])
    keep, send, staged = project(spread, jnp.transpose(qkv_weight, (1, 0, 2)), flat)
    got = swap(send, "req", 1)
    own, *messages = combine(keep, got)
    sources = find_sources(spread, got)
    value_out = write_pool(value_pool, own)
    turning = turn_pages(sources, halves, chips)
    turned = [swap_pages(one, chips, False, row + 1) for row, one in enumerate(turning)]
    sums = [own] + [swap(messages[d - 1], "req", 2 * d) for d in range(1, chips)]

    pack_keep, pack_send, patches = attend(
        lengths,
        new_slot,
        page_table,
        sums,
        qkv_bias.reshape(1, -1),
        own_tokens,
        key_pool,
        value_pool,
        value_out,
        turning[0],
    )
    packs_got = swap(pack_send, "req", 1)
    high = -(-slots // 8) * 8
    merged = [
        jnp.concatenate([pack_keep[d, :slots], packs_got[d, :slots], pack_keep[d, high:] + packs_got[d, high:]], axis=0)
        for d in range(chips)
    ]
    packs = [merged[0]] + [swap(merged[d], "req", 2 * d) for d in range(1, chips)]

    keep, send = out_project(
        packs, staged, head_groups, slots, turned[0]
    )
    total = keep + swap(send, "req", 1).astype(F32)
    from_other = swap(choose_half(sources, halves, turned, keep), "req", 1)
    summed = total[0]
    for d in reversed(range(1, chips)):
        summed = summed + swap(total[d].astype(BF16), "req", 2 * d).astype(F32)
    key_out = write_pool(key_pool, from_other)
    summed, key_out = lax.optimization_barrier((summed, key_out))
    base, key_out, value_out = place_page(
        lengths,
        new_slot,
        page_table,
        sources,
        patches,
        packs,
        own_tokens,
        out_bias[None],
        halves,
        turned,
        from_other,
        key_out,
        value_out,
    )
    hidden = summed[0]
    for j in [head_groups - 1, *range(1, head_groups - 1)]:
        hidden = hidden + swap(summed[j].astype(BF16), "head", j).astype(F32)
    hidden_out = (hidden + base).astype(BF16)
    return (hidden_out, key_out, value_out)


def solution(mesh):
    in_specs = (
        P("req", None),
        P(),
        P(),
        P("req", "head", None),
        P("head", None),
        P("head", "req", None),
        P(),
        P("req", None, "head"),
        P("req", None, "head"),
        P("req"),
        P("req", None),
        P("req"),
        P("req"),
    )
    out_specs = (P("req", "head"), P("req", None, "head"), P("req", None, "head"))
    return jax.shard_map(body, mesh=mesh, in_specs=in_specs, out_specs=out_specs, check_vma=False)
```

```python
import functools

import jax
import jax.numpy as jnp
from jax import lax
from jax.experimental import pallas as pl
from jax.experimental.pallas import tpu as pltpu
from jax.sharding import PartitionSpec as P

EPSILON = 1e-05
F32 = jnp.float32
BF16 = jnp.bfloat16
LANES = 128
META = 128
PACK = 256
VMEM = pl.BlockSpec(memory_space=pltpu.VMEM)
SMEM = pl.BlockSpec(memory_space=pltpu.SMEM)
ANY = pl.BlockSpec(memory_space=pl.ANY)
HBM = pl.BlockSpec(memory_space=pltpu.HBM)
MIB = 1024 * 1024


def cost(flops, moved):
    del flops, moved
    return pl.CostEstimate(flops=0, bytes_accessed=0, transcendentals=0)


def swap(value, axis, step):
    size = lax.axis_size(axis)
    return lax.ppermute(value, axis, [(i, i ^ step) for i in range(size)])


def in_hbm(*arrays):
    return [pltpu.with_memory_space_constraint(array, pltpu.HBM) for array in arrays]


def write_pool(pool, after):
    parts = 4
    step = pool.shape[0] // parts

    def kernel(pool_ref, _, out_ref, sems):
        places = [pl.ds(i * step, step) for i in range(parts)]
        copies = [
            pltpu.make_async_copy(pool_ref.at[place], out_ref.at[place], sems.at[i]) for i, place in enumerate(places)
        ]
        for copy in copies:
            copy.start()
        for copy in copies:
            copy.wait()

    return pl.pallas_call(
        kernel,
        out_shape=jax.ShapeDtypeStruct(pool.shape, pool.dtype),
        in_specs=[VMEM, ANY],
        out_specs=HBM,
        scratch_shapes=[pltpu.SemaphoreType.DMA((parts,))],
        compiler_params=pltpu.CompilerParams(vmem_limit_bytes=8 * MIB),
        cost_estimate=cost(0, 2 * pool.size),
        name="write_pool",
    )(pool, after)


def leaving_slot(new_slot_ref, slots, here):
    leaving = jnp.int32(0)
    for s in range(slots):
        leaving = jnp.where(new_slot_ref[s] // slots != here, s, leaving)
    return leaving


def tell(lengths, new_slot, new_page, tokens, page):
    slots = new_slot.shape[0]

    def kernel(length_ref, slot_ref, page_ref, token_ref, told_ref, token_out):
        row = lax.broadcasted_iota(jnp.int32, (slots, META), 0)
        lane = lax.broadcasted_iota(jnp.int32, (slots, META), 1)
        told = jnp.zeros((slots, META), F32)
        for s in range(slots):
            slot = slot_ref[s]
            numbers = (slot // slots, slot % slots, page_ref[s], length_ref[s] % page)
            for j, number in enumerate(numbers):
                told = jnp.where((row == s) & (lane == j), number.astype(F32), told)
        told_ref[...] = told
        token_out[...] = token_ref[...]

    return pl.pallas_call(
        kernel,
        out_shape=(
            jax.ShapeDtypeStruct((slots, META), F32),
            jax.ShapeDtypeStruct(tokens.shape, tokens.dtype),
        ),
        in_specs=[SMEM] * 3 + [VMEM],
        out_specs=(VMEM, VMEM),
        compiler_params=pltpu.CompilerParams(vmem_limit_bytes=2 * MIB),
        cost_estimate=cost(0, 0),
        name="tell",
    )(*in_hbm(lengths, new_slot, new_page, tokens))


def pick_page(new_slot, page_table, key_pool, value_pool, *after):
    slots = new_slot.shape[0]

    def kernel(slot_ref, table_ref, key_ref, value_ref, *refs):
        out_ref, sems = refs[len(after) :]
        leaving = leaving_slot(slot_ref, slots, lax.axis_index("req"))
        copies = [
            pltpu.make_async_copy(source.at[table_ref[leaving, 0]], out_ref.at[n], sems.at[n])
            for n, source in enumerate((key_ref, value_ref))
        ]
        for copy in copies:
            copy.start()
        for copy in copies:
            copy.wait()

    return pl.pallas_call(
        kernel,
        out_shape=jax.ShapeDtypeStruct((2,) + key_pool.shape[1:], key_pool.dtype),
        in_specs=[SMEM] * 2 + [HBM] * 2 + [ANY] * len(after),
        out_specs=VMEM,
        scratch_shapes=[pltpu.SemaphoreType.DMA((2,))],
        compiler_params=pltpu.CompilerParams(vmem_limit_bytes=2 * MIB),
        cost_estimate=cost(0, 0),
        name="pick_page",
    )(*in_hbm(new_slot, page_table, key_pool, value_pool), *after)


def prepare(tokens, other_tokens, gain, shift, told):
    groups = lax.axis_size("req")
    chips = groups // 2
    slots, model = tokens.shape
    depth = model // groups

    def kernel(token_ref, other_ref, gain_ref, shift_ref, told_ref, *refs):
        out_refs, normed = refs[:chips], refs[chips]
        here = lax.axis_index("req")
        values = jnp.concatenate([token_ref[...].astype(F32), other_ref[...].astype(F32)], axis=0)
        average = jnp.mean(values, axis=1, keepdims=True)
        centered = values - average
        variance = jnp.mean(centered * centered, axis=1, keepdims=True)
        rows = centered * lax.rsqrt(variance + EPSILON) * gain_ref[...] + shift_ref[...]
        normed[...] = rows.astype(BF16).astype(F32)
        for d in range(chips):
            first = (here ^ 2 * d) * depth
            if depth % LANES == 0:
                block = normed[:, pl.ds(pl.multiple_of(first, LANES), depth)]
            else:
                block = pltpu.roll(normed[...], lax.rem(model - first, model), 1)[:, :depth]
            for e in range(2):
                out_refs[d][e, :, META:] = block[e * slots : (e + 1) * slots].astype(BF16)
            out_refs[d][0, :, :META] = told_ref[...].astype(BF16)
            out_refs[d][1, :, :META] = jnp.zeros((slots, META), BF16)

    return pl.pallas_call(
        kernel,
        out_shape=(jax.ShapeDtypeStruct((2, slots, META + depth), BF16),) * chips,
        in_specs=[VMEM] * 5,
        out_specs=(VMEM,) * chips,
        scratch_shapes=[pltpu.VMEM((2 * slots, model), F32)],
        compiler_params=pltpu.CompilerParams(vmem_limit_bytes=4 * MIB),
        cost_estimate=cost(0, 0),
        name="prepare",
    )(tokens, other_tokens, gain, shift, told)


def arrivals(tables, here, wanted):
    slots = tables[0].shape[0]
    lane = lax.broadcasted_iota(jnp.int32, (slots, META), 1)
    found = jnp.zeros((slots, META), F32)
    goal = here ^ wanted
    for k, told in enumerate(tables):
        numbered = jnp.where(lane == 4, float(k), told)
        found = jnp.where(told[:, :1] == jnp.where(wanted == k, -1, goal).astype(F32), numbered, found)
    return lambda j: jnp.sum(jnp.where(lane == j, found, 0.0)).astype(jnp.int32)


def row_length(chips):
    return 1 << (chips.bit_length() // 2)


def swap_pages(value, chips, along_row, step):
    across = row_length(chips)
    square = across * across == chips
    steps = [2 * step if along_row == (device % 2 == 0 or not square) else 2 * across * step for device in range(2 * chips)]
    return lax.ppermute(value, "req", [(i, i ^ steps[i]) for i in range(2 * chips)])


def find_sources(spread, got):
    chips = len(spread)
    across = row_length(chips)
    down = chips // across

    def kernel(*refs):
        block_refs, got_ref, out_ref = refs[:chips][::-1], refs[-2], refs[-1]
        here = lax.axis_index("req")
        tables = []
        for d in range(chips):
            tables += [block_refs[d][0, :, :META].astype(F32), got_ref[d, :, got_ref.shape[2] - META :]]
        lane = lax.broadcasted_iota(jnp.int32, (8, LANES), 1)
        found = jnp.zeros((8, LANES), F32)
        put = lambda j, number: jnp.where(lane == j, number.astype(F32), found)
        turned = (here % 2 == 1) & (across == down)
        for row in range(down):
            for j in range(2):
                pick = arrivals(tables, here, jnp.where(turned, 2 * row, 2 * across * row) + j)
                source = pick(4)
                chip = source // 2
                chip = jnp.where(turned, chip % across * across + chip // across, chip)
                found = put(2 * row + j, 2 * chip + source % 2)
                if row == 0 and j == 0:
                    found = put(2 * down, pick(2))
                    found = put(2 * down + 1, pick(3))
        out_ref[...] = found

    return pl.pallas_call(
        kernel,
        out_shape=jax.ShapeDtypeStruct((8, LANES), F32),
        in_specs=[VMEM] * (chips + 1),
        out_specs=VMEM,
        compiler_params=pltpu.CompilerParams(vmem_limit_bytes=4 * MIB),
        cost_estimate=cost(0, 0),
        name="find_sources",
    )(*spread[::-1], got)


def number_at(source_ref, j):
    lane = lax.broadcasted_iota(jnp.int32, (1, LANES), 1)
    return jnp.sum(jnp.where(lane == j, source_ref[:1, :], 0.0)).astype(jnp.int32)


def turn_pages(sources, messages, chips):
    across = len(messages)
    down = chips // across
    shape = (2,) + messages[0].shape

    def kernel(source_ref, *refs):
        message_refs, out_refs = refs[:across], refs[across:]
        for row in range(1, down):
            for j in range(2):
                source = number_at(source_ref, 2 * row + j)
                place = jnp.where((source % 2 == 0) & (source < 2 * across), source // 2, 0)
                for d in range(across):

                    @pl.when(place == d)
                    def _():
                        out_refs[row - 1][j] = message_refs[d][...]

    one = jax.ShapeDtypeStruct(shape, messages[0].dtype)
    return pl.pallas_call(
        kernel,
        out_shape=(one,) * (down - 1),
        in_specs=[VMEM] * (1 + across),
        out_specs=(VMEM,) * (down - 1),
        compiler_params=pltpu.CompilerParams(vmem_limit_bytes=(across + 2 * down) * MIB),
        cost_estimate=cost(0, 0),
        name="turn_pages",
    )(sources, *messages)


def with_page(source, across, core, message_refs, turned_refs, use):
    place = jnp.where(source < 2 * across, source // 2, across - 1 + source // (2 * across))
    for d, ref in enumerate(message_refs):

        @pl.when(place == d)
        def _():
            use(ref)

    for row, ref in enumerate(turned_refs):

        @pl.when(place == across + row)
        def _():
            use(ref.at[core])


def choose_page(sources, messages, turned, after):
    across, rows = len(messages), len(turned)

    def kernel(source_ref, *refs):
        message_refs, turned_refs = refs[:across], refs[across : across + rows]
        out_ref = refs[-1]

        def use(ref):
            out_ref[...] = ref[...]

        with_page(number_at(source_ref, 1), across, 1, message_refs, turned_refs, use)

    one = messages[0]
    return pl.pallas_call(
        kernel,
        out_shape=jax.ShapeDtypeStruct(one.shape, one.dtype),
        in_specs=[VMEM] * (1 + across + rows) + [ANY],
        out_specs=VMEM,
        compiler_params=pltpu.CompilerParams(vmem_limit_bytes=(2 + across + 2 * rows) * MIB),
        cost_estimate=cost(0, 0),
        name="choose_page",
    )(sources, *messages, *turned, after)


def project(blocks, weight, later):
    chips = len(blocks)
    slots = blocks[0].shape[1]
    heads, depth, width = weight.shape
    per = 2 if heads % 2 == 0 else 1
    rows = chips * 2 * slots

    def kernel(*refs):
        block_refs = refs[:chips][::-1]
        weight_ref, later_ref, keep_ref, send_ref, later_out, left, sem = refs[chips:]
        copy = pltpu.make_async_copy(later_ref, later_out, sem)
        copy.start()
        for d in range(chips):
            for e in range(2):
                row = (d * 2 + e) * slots
                left[row : row + slots, :] = block_refs[d][e, :, META:].astype(F32)
        lhs = left[...].astype(BF16)

        @pl.loop(0, heads // per)
        def _(i):
            right = jnp.concatenate([weight_ref[i * per + j] for j in range(per)], axis=1)
            total = jnp.dot(lhs, right, preferred_element_type=F32)
            columns = pl.ds(pl.multiple_of(i * (per * width), per * width), per * width)
            for d in range(chips):
                row = d * 2 * slots
                keep_ref[d, :, columns] = total[row : row + slots]
                send_ref[d, :, columns] = total[row + slots : row + 2 * slots]

        for d in range(chips):
            send_ref[d, :, heads * width :] = block_refs[d][0, :, :META].astype(F32)
        copy.wait()

    shape = jax.ShapeDtypeStruct((chips, slots, heads * width), F32)
    wider = jax.ShapeDtypeStruct((chips, slots, heads * width + META), F32)
    return pl.pallas_call(
        kernel,
        out_shape=(shape, wider, jax.ShapeDtypeStruct(later.shape, later.dtype)),
        in_specs=[VMEM] * (chips + 1) + [HBM],
        out_specs=(VMEM, VMEM, VMEM),
        scratch_shapes=[pltpu.VMEM((rows, depth), F32), pltpu.SemaphoreType.DMA],
        compiler_params=pltpu.CompilerParams(vmem_limit_bytes=weight.size * 2 + 12 * MIB),
        cost_estimate=cost(2 * rows * weight.size, 2 * weight.size),
        name="project",
    )(*blocks[::-1], weight, *in_hbm(later))


def combine(keep, got):
    chips, slots, width = keep.shape
    heads = width // (3 * LANES)

    def kernel(keep_ref, got_ref, own_ref, *message_refs):
        own_ref[...] = keep_ref[0] + got_ref[0, :, :width]
        for d in range(1, chips):
            for h in range(heads):
                total = keep_ref[d, :, 3 * h * LANES : 3 * (h + 1) * LANES] + got_ref[d, :, 3 * h * LANES : 3 * (h + 1) * LANES]
                query = total[:, :LANES]
                high = query.astype(BF16)
                low = (query - high.astype(F32)).astype(BF16)
                base = 4 * h * LANES
                message_refs[d - 1][:, base : base + LANES] = high
                message_refs[d - 1][:, base + LANES : base + 2 * LANES] = low
                message_refs[d - 1][:, base + 2 * LANES : base + 4 * LANES] = total[:, LANES:].astype(BF16)

    message = jax.ShapeDtypeStruct((slots, 4 * heads * LANES), BF16)
    return pl.pallas_call(
        kernel,
        out_shape=(jax.ShapeDtypeStruct((slots, width), F32),) + (message,) * (chips - 1),
        in_specs=[VMEM, VMEM],
        out_specs=(VMEM,) * chips,
        compiler_params=pltpu.CompilerParams(vmem_limit_bytes=8 * MIB),
        cost_estimate=cost(0, 8 * keep.size),
        name="combine",
    )(keep, got)


def attend(lengths, new_slot, page_table, sums, bias, tokens, key_pool, value_pool, after):
    parts = len(sums)
    slots = sums[0].shape[0]
    pages, page, width = key_pool.shape
    head = LANES
    heads = width // head
    max_pages = page_table.shape[1]
    short_rows = slots * page
    groups = 2 * parts
    share = head // groups
    per = LANES // share
    tall = 16
    strips = width // PACK
    scale = head ** (-0.5)

    def kernel(*refs):
        length_ref, slot_ref, table_ref = refs[:3]
        sum_refs = refs[3 : 3 + parts][::-1]
        (bias_ref, token_ref, key_ref, value_ref, _, pack_keep, pack_send, patch_ref, value_out) = refs[
            3 + parts : 12 + parts
        ]
        attended_ref, out_sems = refs[12 + parts :]
        step = pages // 4
        writes = [
            pltpu.make_async_copy(value_ref.at[pl.ds(i * step, step)], value_out.at[pl.ds(i * step, step)], out_sems.at[i])
            for i in range(4)
        ]
        for write in writes:
            write.start()
        here = lax.axis_index("req")
        column_block = lax.axis_index("head")
        leaving = leaving_slot(slot_ref, slots, here)
        lengths = [length_ref[s] for s in range(slots)]
        long_slot = jnp.int32(0)
        long_length = jnp.int32(0)
        for s in range(slots):
            is_long = lengths[s] >= page
            long_slot = jnp.where(is_long, s, long_slot)
            long_length = jnp.where(is_long, lengths[s], long_length)

        total = sum_refs[0][...] + bias_ref[...]

        def third(k):
            columns = []
            for h in range(heads):
                one = total[:, (3 * h + k) * head : (3 * h + k + 1) * head]
                for ref in sum_refs[1:]:
                    base = 4 * h * head
                    if k == 0:
                        one = one + ref[:, base : base + head].astype(F32) + ref[:, base + head : base + 2 * head].astype(F32)
                    else:
                        one = one + ref[:, base + (k + 1) * head : base + (k + 2) * head].astype(F32)
                columns.append(one)
            return jnp.concatenate(columns, axis=1)

        query = (third(0) * scale).astype(BF16).astype(F32)
        new_rows = (third(1).astype(BF16).astype(F32), third(2).astype(BF16).astype(F32))

        lane_head = lax.broadcasted_iota(jnp.int32, (tall, width), 1) // head
        on_head = lane_head == lax.broadcasted_iota(jnp.int32, (tall, width), 0)

        def blocked(row):
            return jnp.where(on_head, jnp.broadcast_to(row, (tall, width)), 0.0).astype(BF16)

        def for_slot(which, rows):
            found = rows[0]
            for s in range(1, slots):
                found = jnp.where(which == s, rows[s], found)
            return found

        def softmax(scores, valid, new_score):
            masked = jnp.where(valid, scores, -1e30)
            peak = jnp.maximum(jnp.max(masked, axis=1, keepdims=True), new_score)
            weights = jnp.where(valid, jnp.exp(masked - peak), 0.0)
            new_weight = jnp.exp(new_score - peak)
            denom = jnp.sum(weights, axis=1, keepdims=True) + new_weight
            return weights.astype(BF16), new_weight.astype(BF16).astype(F32), denom

        across = (((1,), (1,)), ((), ()))
        short_query = jnp.concatenate([blocked(query[s : s + 1]) for s in range(slots)], axis=0)
        new_keys = jnp.concatenate([new_rows[0], jnp.zeros((tall - slots, width), F32)], axis=0).astype(BF16)
        new_scores = lax.dot_general(short_query, new_keys, across, preferred_element_type=F32)
        size = (slots * tall, tall)
        own_column = lax.broadcasted_iota(jnp.int32, size, 0) // tall == lax.broadcasted_iota(jnp.int32, size, 1)
        new_score = jnp.sum(jnp.where(own_column, new_scores, 0.0), axis=1, keepdims=True)

        def fold(mixed):
            return jnp.sum(jnp.where(on_head, mixed, 0.0), axis=0, keepdims=True)

        high = -(-slots // 8) * 8

        def attend_all(long_pages):
            first_pages = lambda ref: jnp.concatenate([ref[table_ref[s, 0]] for s in range(slots)], axis=0)
            short_scores = lax.dot_general(short_query, first_pages(key_ref), across, preferred_element_type=F32)
            size = (slots * tall, short_rows)
            row_slot = lax.broadcasted_iota(jnp.int32, size, 0) // tall
            column = lax.broadcasted_iota(jnp.int32, size, 1)
            limit = jnp.zeros(size, jnp.int32)
            for s in range(slots):
                limit = jnp.where(row_slot == s, lengths[s], limit)
            valid = (row_slot == column // page) & (column % page < limit)
            short_probs, new_prob, short_denom = softmax(short_scores, valid, new_score)
            new_values = jnp.concatenate(
                [jnp.broadcast_to(new_rows[1][s : s + 1], (tall, width)) for s in range(slots)], axis=0
            )
            short_mix = jnp.dot(short_probs, first_pages(value_ref), preferred_element_type=F32)
            short_mix = (short_mix + new_prob * new_values) / short_denom

            rows = [fold(short_mix[s * tall : (s + 1) * tall]) for s in range(slots)]
            if long_pages:
                some_pages = lambda ref: jnp.concatenate(
                    [ref[table_ref[long_slot, i]] for i in range(long_pages)], axis=0
                )
                long_query = blocked(for_slot(long_slot, [query[s : s + 1] for s in range(slots)]))
                long_new = for_slot(long_slot, [new_score[s * tall : (s + 1) * tall] for s in range(slots)])
                long_value = for_slot(long_slot, [new_rows[1][s : s + 1] for s in range(slots)])
                scores = lax.dot_general(long_query, some_pages(key_ref), across, preferred_element_type=F32)
                position = lax.broadcasted_iota(jnp.int32, (tall, long_pages * page), 1)
                long_probs, long_prob, long_denom = softmax(scores, position < long_length, long_new)
                mixed = jnp.dot(long_probs, some_pages(value_ref), preferred_element_type=F32)
                long_mix = fold((mixed + long_prob * long_value) / long_denom)
                rows = [jnp.where(lengths[s] >= page, long_mix, row) for s, row in enumerate(rows)]
            rows += [jnp.zeros((high - slots, width), F32)]
            attended_ref[...] = jnp.concatenate(rows, axis=0).astype(BF16).astype(F32)

        half = max_pages // 2
        pl.when(long_length == 0)(lambda: attend_all(0))
        pl.when((long_length > 0) & (long_length <= half * page))(lambda: attend_all(half))
        pl.when(long_length > half * page)(lambda: attend_all(max_pages))
        attended = attended_ref[...]

        toward = jnp.int32(0)
        for s in range(slots):
            toward = jnp.where(leaving == s, slot_ref[s] // slots ^ here, toward)
        token = token_ref[:, pl.ds(pl.multiple_of(column_block * width, LANES), width)].astype(F32)
        extra = []
        for source in new_rows + (token,):
            one = jnp.zeros((1, width), F32)
            for s in range(slots):
                one = jnp.where(leaving == s, source[s : s + 1], one)
            extra += [one[:, i * PACK : (i + 1) * PACK] for i in range(strips)]
        extra = jnp.concatenate(extra + [jnp.zeros((pack_rows(slots, strips) - high - 3 * strips, PACK), F32)], axis=0)

        lane = lax.broadcasted_iota(jnp.int32, (high, LANES), 1)
        row_at = lax.broadcasted_iota(jnp.int32, (high, LANES), 0)
        goal = jnp.full((high, LANES), -1.0, F32)
        for s in range(slots):
            device, slot = slot_ref[s] // slots, slot_ref[s] % slots
            number = jnp.where(lane % share == share - 1, slot, device).astype(F32)
            goal = jnp.where(row_at == s, number, goal)
        turned = [
            pltpu.roll(attended[:, h * head : (h + 1) * head], h % per * share, 1) if h % per else attended[:, h * head : (h + 1) * head]
            for h in range(heads)
        ]
        for k in range(groups):
            count = lax.rem(lane // share - (here ^ k) + per, per)
            tiles = [jnp.zeros((high, LANES), F32) for _ in range(PACK // LANES)]
            for h in range(heads):
                tiles[h // per] = jnp.where(count == h % per, turned[h], tiles[h // per])
            tiles[-1] = jnp.where((count == per - 1) & (lane % share >= share - 2), goal, tiles[-1])
            block = jnp.concatenate([jnp.concatenate(tiles, axis=1), jnp.where(toward == k, extra, 0.0)], axis=0).astype(BF16)
            (pack_keep, pack_send)[k % 2][k // 2] = block

        at = lax.broadcasted_iota(jnp.int32, (tall, width), 0)
        for n, ref in enumerate((key_ref, value_ref)):
            for s in range(slots):
                offset = lengths[s] % page
                first = pl.multiple_of(offset // tall * tall, tall)
                old = ref[table_ref[s, lengths[s] // page], pl.ds(first, tall), :].astype(F32)
                new = jnp.broadcast_to(new_rows[n][s : s + 1], (tall, width))
                patch_ref[n, s] = jnp.where(at == offset - first, new, old).astype(BF16)

        for write in writes:
            write.wait()

    packed = jax.ShapeDtypeStruct((parts, pack_rows(slots, strips), PACK), BF16)
    pool = jax.ShapeDtypeStruct(key_pool.shape, key_pool.dtype)
    return pl.pallas_call(
        kernel,
        out_shape=(packed, packed, jax.ShapeDtypeStruct((2, slots, tall, width), BF16), pool),
        in_specs=[SMEM] * 3 + [VMEM] * (parts + 4) + [ANY],
        out_specs=(VMEM, VMEM, VMEM, HBM),
        scratch_shapes=[
            pltpu.VMEM((-(-slots // 8) * 8, width), F32),
            pltpu.SemaphoreType.DMA((4,)),
        ],
        compiler_params=pltpu.CompilerParams(vmem_limit_bytes=18 * MIB),
        cost_estimate=cost(0, 0),
        name="attend",
    )(lengths, new_slot, page_table, *sums[::-1], bias, tokens, key_pool, value_pool, after)


def pack_rows(slots, strips):
    need = -(-slots // 8) * 8 + 3 * strips
    return -(-need // 16) * 16


def out_project(blocks, weight, pieces, slots, *after):
    chips = len(blocks)
    depth, width = weight.shape
    rows = 2 * chips * slots
    piece = width // pieces

    def kernel(*refs):
        block_refs, weight_ref = refs[:chips][::-1], refs[chips]
        keep_ref, send_ref = refs[chips + 1 + len(after) :]
        gathered = jnp.concatenate(
            [block_refs[d][: 2 * slots, :].astype(F32) for d in range(chips)], axis=0
        )
        here = lax.axis_index("req")
        share = LANES // (2 * chips)
        back = lax.rem(LANES - here * share, LANES)
        gathered = jnp.concatenate(
            [pltpu.roll(gathered[:, first : first + LANES], back, 1) for first in range(0, PACK, LANES)], axis=1
        )
        goal = gathered[:, PACK - 2 : PACK - 1].astype(jnp.int32)
        place = goal ^ here
        row = (place % 2) * (chips * slots) + (place // 2) * slots + gathered[:, PACK - 1 :].astype(jnp.int32)
        row = jnp.where(goal < 0, -1, row)
        size = (gathered.shape[0], rows)
        order = jnp.where(lax.broadcasted_iota(jnp.int32, size, 1) == row, 1.0, 0.0)
        left = lax.dot_general(
            order.astype(BF16), gathered.astype(BF16), (((0,), (0,)), ((), ())), preferred_element_type=F32
        )
        left = left[:, :depth].astype(BF16)
        for j in range(pieces):
            first = (lax.axis_index("head") ^ j) * piece
            total = jnp.dot(
                left, weight_ref[:, pl.ds(pl.multiple_of(first, LANES), piece)], preferred_element_type=F32
            )
            for d in range(chips):
                keep_ref[d, j] = total[d * slots : (d + 1) * slots]
                send_ref[d, j] = total[(chips + d) * slots : (chips + d + 1) * slots].astype(BF16)

    shape = (chips, pieces, slots, piece)
    return pl.pallas_call(
        kernel,
        out_shape=(jax.ShapeDtypeStruct(shape, F32), jax.ShapeDtypeStruct(shape, BF16)),
        in_specs=[VMEM] * (chips + 1) + [ANY] * len(after),
        out_specs=(VMEM, VMEM),
        compiler_params=pltpu.CompilerParams(vmem_limit_bytes=10 * MIB),
        cost_estimate=cost(2 * rows * weight.size, 2 * weight.size),
        name="out_project",
    )(*blocks[::-1], weight, *after)


def place_page(lengths, new_slot, page_table, sources, patches, packs, tokens, out_bias, messages, turned, from_other, key_out, value_out):
    chips, across, rows = len(packs), len(messages), len(turned)
    down = chips // across
    count = across + rows + 1
    page, width = key_out.shape[1:]
    slots = tokens.shape[0]
    strips = width // PACK
    tall = patches.shape[2]

    def kernel(length_ref, slot_ref, table_ref, source_ref, patch_ref, *refs):
        pack_refs = refs[:chips][::-1]
        token_ref, bias_ref = refs[chips : chips + 2]
        message_refs = refs[chips + 2 : chips + 2 + across]
        turned_refs = refs[chips + 2 + across : chips + 2 + across + rows]
        other_ref = refs[chips + 1 + count]
        _, _, base_ref, key_ref, value_ref, buffer, out_sems, patch_sems = refs[chips + 2 + count :]
        here = lax.axis_index("req")
        leaving = leaving_slot(slot_ref, slots, here)

        def patch(n, s):
            length = length_ref[s]
            first = pl.multiple_of(length % page // tall * tall, tall)
            target = (key_ref, value_ref)[n].at[table_ref[s, length // page], pl.ds(first, tall)]
            return pltpu.make_async_copy(patch_ref.at[n, s], target, patch_sems.at[n, s])

        for n in range(2):
            for s in range(slots):

                @pl.when(leaving != s)
                def _():
                    patch(n, s).start()

        column = pl.multiple_of(lax.axis_index("head") * width, LANES)
        page_at, offset = [number_at(source_ref, 2 * down + j) for j in range(2)]

        def use(ref):
            buffer[...] = ref[...]

        source = number_at(source_ref, 0)

        @pl.when(source % 2 == 0)
        def _():
            with_page(source, across, 0, message_refs, turned_refs, use)

        @pl.when(source % 2 == 1)
        def _():
            use(other_ref)

        arrived = pack_refs[0][2 * slots :, :].astype(F32)
        for ref in pack_refs[1:]:
            arrived = arrived + ref[2 * slots :, :].astype(F32)

        def fresh(n):
            return jnp.concatenate([arrived[n * strips + i : n * strips + i + 1, :] for i in range(strips)], axis=1)

        at = lax.broadcasted_iota(jnp.int32, (slots, width), 0)
        token = jnp.where(
            at == leaving,
            jnp.broadcast_to(fresh(2), (slots, width)),
            token_ref[:, pl.ds(column, width)].astype(F32),
        )
        base_ref[...] = token + bias_ref[:, pl.ds(column, width)]
        first = pl.multiple_of(offset // 16 * 16, 16)
        row = lax.broadcasted_iota(jnp.int32, (16, width), 0)
        for n in range(2):
            old = buffer[n, pl.ds(first, 16), :].astype(F32)
            new = jnp.broadcast_to(fresh(n), (16, width))
            buffer[n, pl.ds(first, 16), :] = jnp.where(row == offset - first, new, old).astype(BF16)
        copies = [
            pltpu.make_async_copy(buffer.at[n], target.at[page_at], out_sems.at[n])
            for n, target in enumerate((key_ref, value_ref))
        ]
        for copy in copies:
            copy.start()
        for n in range(2):
            for s in range(slots):

                @pl.when(leaving != s)
                def _():
                    patch(n, s).wait()

        for copy in copies:
            copy.wait()

    shape = jax.ShapeDtypeStruct(key_out.shape, key_out.dtype)
    return pl.pallas_call(
        kernel,
        out_shape=(jax.ShapeDtypeStruct((slots, width), F32), shape, shape),
        in_specs=[SMEM] * 3 + [VMEM] * (chips + 4 + count) + [HBM] * 2,
        out_specs=(VMEM, HBM, HBM),
        scratch_shapes=[
            pltpu.VMEM((2, page, width), BF16),
            pltpu.SemaphoreType.DMA((2,)),
            pltpu.SemaphoreType.DMA((2, slots)),
        ],
        input_output_aliases={chips + 7 + count: 1, chips + 8 + count: 2},
        compiler_params=pltpu.CompilerParams(vmem_limit_bytes=(6 + 2 * count) * MIB),
        cost_estimate=cost(0, 8 * page * width),
        name="place_page",
    )(
        lengths, new_slot, page_table, sources, patches, *packs[::-1], tokens, out_bias, *messages, *turned, from_other, key_out, value_out
    )


def body(
    tokens,
    norm_gain,
    norm_shift,
    qkv_weight,
    qkv_bias,
    out_weight,
    out_bias,
    key_pool,
    value_pool,
    lengths,
    page_table,
    new_slot,
    new_page,
):
    groups = lax.axis_size("req")
    head_groups = lax.axis_size("head")
    slots = tokens.shape[0]
    chips = groups // 2

    other_tokens = swap(tokens, "req", 1)
    told, own_tokens = tell(lengths, new_slot, new_page, tokens, key_pool.shape[1])
    blocks = prepare(own_tokens, other_tokens, norm_gain[None], norm_shift[None], told)
    across = row_length(chips)
    spread = [blocks[0]] + [swap(blocks[d], "req", 2 * d) for d in range(1, chips)]
    page = pick_page(new_slot, page_table, key_pool, value_pool, *blocks[::-1])
    page, *spread = lax.optimization_barrier((page, *spread))
    pages = [page] + [swap_pages(page, chips, True, d) for d in range(1, across)]

    flat = out_weight.reshape(-1, out_weight.shape[2])
    keep, send, staged = project(spread, jnp.transpose(qkv_weight, (1, 0, 2)), flat)
    got = swap(send, "req", 1)
    own, *messages = combine(keep, got)
    sources = find_sources(spread, got)
    sums = [own] + [swap(messages[d - 1], "req", 2 * d) for d in range(1, chips)]
    turning = turn_pages(sources, pages, chips)
    turned = [swap_pages(one, chips, False, row + 1) for row, one in enumerate(turning)]

    pack_keep, pack_send, patches, value_out = attend(
        lengths,
        new_slot,
        page_table,
        sums,
        qkv_bias.reshape(1, -1),
        own_tokens,
        key_pool,
        value_pool,
        turning[0],
    )
    packs_got = swap(pack_send, "req", 1)
    high = -(-slots // 8) * 8
    merged = [
        jnp.concatenate([pack_keep[d, :slots], packs_got[d, :slots], pack_keep[d, high:] + packs_got[d, high:]], axis=0)
        for d in range(chips)
    ]
    packs = [merged[0]] + [swap(merged[d], "req", 2 * d) for d in range(1, chips)]

    keep, send = out_project(
        packs, staged, head_groups, slots, turned[0]
    )
    total = keep + swap(send, "req", 1).astype(F32)
    from_other = swap(choose_page(sources, pages, turned, keep), "req", 1)
    summed = total[0]
    for d in reversed(range(1, chips)):
        summed = summed + swap(total[d].astype(BF16), "req", 2 * d).astype(F32)
    key_out = write_pool(key_pool, total)
    summed, key_out, from_other = lax.optimization_barrier((summed, key_out, from_other))
    base, key_out, value_out = place_page(
        lengths,
        new_slot,
        page_table,
        sources,
        patches,
        packs,
        own_tokens,
        out_bias[None],
        pages,
        turned,
        from_other,
        key_out,
        value_out,
    )
    hidden = summed[0]
    for j in [head_groups - 1, *range(1, head_groups - 1)]:
        hidden = hidden + swap(summed[j].astype(BF16), "head", j).astype(F32)
    hidden_out = (hidden + base).astype(BF16)
    return (hidden_out, key_out, value_out)


def solution(mesh):
    in_specs = (
        P("req", None),
        P(),
        P(),
        P("req", "head", None),
        P("head", None),
        P("head", "req", None),
        P(),
        P("req", None, "head"),
        P("req", None, "head"),
        P("req"),
        P("req", None),
        P("req"),
        P("req"),
    )
    out_specs = (P("req", "head"), P("req", None, "head"), P("req", None, "head"))
    return jax.shard_map(body, mesh=mesh, in_specs=in_specs, out_specs=out_specs, check_vma=False)
```

```python
import functools

import jax
import jax.numpy as jnp
from jax import lax
from jax.experimental import pallas as pl
from jax.experimental.pallas import tpu as pltpu
from jax.sharding import PartitionSpec as P

EPSILON = 1e-05
F32 = jnp.float32
BF16 = jnp.bfloat16
LANES = 128
META = 128
PACK = 256
VMEM = pl.BlockSpec(memory_space=pltpu.VMEM)
SMEM = pl.BlockSpec(memory_space=pltpu.SMEM)
ANY = pl.BlockSpec(memory_space=pl.ANY)
HBM = pl.BlockSpec(memory_space=pltpu.HBM)
MIB = 1024 * 1024


def cost(flops, moved):
    del flops, moved
    return pl.CostEstimate(flops=0, bytes_accessed=0, transcendentals=0)


def swap(value, axis, step):
    size = lax.axis_size(axis)
    return lax.ppermute(value, axis, [(i, i ^ step) for i in range(size)])


def in_hbm(*arrays):
    return [pltpu.with_memory_space_constraint(array, pltpu.HBM) for array in arrays]


def write_pool(pool, after):
    parts = 4
    step = pool.shape[0] // parts

    def kernel(pool_ref, _, out_ref, sems):
        places = [pl.ds(i * step, step) for i in range(parts)]
        copies = [
            pltpu.make_async_copy(pool_ref.at[place], out_ref.at[place], sems.at[i]) for i, place in enumerate(places)
        ]
        for copy in copies:
            copy.start()
        for copy in copies:
            copy.wait()

    return pl.pallas_call(
        kernel,
        out_shape=jax.ShapeDtypeStruct(pool.shape, pool.dtype),
        in_specs=[VMEM, ANY],
        out_specs=HBM,
        scratch_shapes=[pltpu.SemaphoreType.DMA((parts,))],
        compiler_params=pltpu.CompilerParams(vmem_limit_bytes=8 * MIB),
        cost_estimate=cost(0, 2 * pool.size),
        name="write_pool",
    )(pool, after)


def leaving_slot(new_slot_ref, slots, here):
    leaving = jnp.int32(0)
    for s in range(slots):
        leaving = jnp.where(new_slot_ref[s] // slots != here, s, leaving)
    return leaving


def tell(lengths, new_slot, new_page, tokens, gain, shift, page):
    slots = new_slot.shape[0]

    def kernel(length_ref, slot_ref, page_ref, token_ref, gain_ref, shift_ref, told_ref, token_out, gain_out, shift_out):
        row = lax.broadcasted_iota(jnp.int32, (slots, META), 0)
        lane = lax.broadcasted_iota(jnp.int32, (slots, META), 1)
        told = jnp.zeros((slots, META), F32)
        for s in range(slots):
            slot = slot_ref[s]
            numbers = (slot // slots, slot % slots, page_ref[s], length_ref[s] % page)
            for j, number in enumerate(numbers):
                told = jnp.where((row == s) & (lane == j), number.astype(F32), told)
        told_ref[...] = told
        token_out[...] = token_ref[...]
        gain_out[...] = gain_ref[...]
        shift_out[...] = shift_ref[...]

    return pl.pallas_call(
        kernel,
        out_shape=(
            jax.ShapeDtypeStruct((slots, META), F32),
            jax.ShapeDtypeStruct(tokens.shape, tokens.dtype),
            jax.ShapeDtypeStruct(gain.shape, gain.dtype),
            jax.ShapeDtypeStruct(shift.shape, shift.dtype),
        ),
        in_specs=[SMEM] * 3 + [VMEM] * 3,
        out_specs=(VMEM,) * 4,
        compiler_params=pltpu.CompilerParams(vmem_limit_bytes=2 * MIB),
        cost_estimate=cost(0, 0),
        name="tell",
    )(*in_hbm(lengths, new_slot, new_page, tokens, gain, shift))


def pick_page(new_slot, page_table, key_pool, value_pool, *after):
    slots = new_slot.shape[0]

    def kernel(slot_ref, table_ref, key_ref, value_ref, *refs):
        out_ref, sems = refs[len(after) :]
        leaving = leaving_slot(slot_ref, slots, lax.axis_index("req"))
        copies = [
            pltpu.make_async_copy(source.at[table_ref[leaving, 0]], out_ref.at[n], sems.at[n])
            for n, source in enumerate((key_ref, value_ref))
        ]
        for copy in copies:
            copy.start()
        for copy in copies:
            copy.wait()

    return pl.pallas_call(
        kernel,
        out_shape=jax.ShapeDtypeStruct((2,) + key_pool.shape[1:], key_pool.dtype),
        in_specs=[SMEM] * 2 + [HBM] * 2 + [ANY] * len(after),
        out_specs=VMEM,
        scratch_shapes=[pltpu.SemaphoreType.DMA((2,))],
        compiler_params=pltpu.CompilerParams(vmem_limit_bytes=2 * MIB),
        cost_estimate=cost(0, 0),
        name="pick_page",
    )(*in_hbm(new_slot, page_table, key_pool, value_pool), *after)


def prepare(tokens, other_tokens, gain, shift, told):
    groups = lax.axis_size("req")
    chips = groups // 2
    slots, model = tokens.shape
    depth = model // groups

    def kernel(token_ref, other_ref, gain_ref, shift_ref, told_ref, *refs):
        out_refs, normed = refs[:chips], refs[chips]
        here = lax.axis_index("req")
        values = jnp.concatenate([token_ref[...].astype(F32), other_ref[...].astype(F32)], axis=0)
        average = jnp.mean(values, axis=1, keepdims=True)
        centered = values - average
        variance = jnp.mean(centered * centered, axis=1, keepdims=True)
        rows = centered * lax.rsqrt(variance + EPSILON) * gain_ref[...] + shift_ref[...]
        normed[...] = rows.astype(BF16).astype(F32)
        for d in range(chips):
            first = (here ^ 2 * d) * depth
            if depth % LANES == 0:
                block = normed[:, pl.ds(pl.multiple_of(first, LANES), depth)]
            else:
                block = pltpu.roll(normed[...], lax.rem(model - first, model), 1)[:, :depth]
            for e in range(2):
                out_refs[d][e, :, META:] = block[e * slots : (e + 1) * slots].astype(BF16)
            out_refs[d][0, :, :META] = told_ref[...].astype(BF16)
            out_refs[d][1, :, :META] = jnp.zeros((slots, META), BF16)

    return pl.pallas_call(
        kernel,
        out_shape=(jax.ShapeDtypeStruct((2, slots, META + depth), BF16),) * chips,
        in_specs=[VMEM] * 5,
        out_specs=(VMEM,) * chips,
        scratch_shapes=[pltpu.VMEM((2 * slots, model), F32)],
        compiler_params=pltpu.CompilerParams(vmem_limit_bytes=4 * MIB),
        cost_estimate=cost(0, 0),
        name="prepare",
    )(tokens, other_tokens, gain, shift, told)


def arrivals(tables, here, wanted):
    slots = tables[0].shape[0]
    lane = lax.broadcasted_iota(jnp.int32, (slots, META), 1)
    found = jnp.zeros((slots, META), F32)
    goal = here ^ wanted
    for k, told in enumerate(tables):
        numbered = jnp.where(lane == 4, float(k), told)
        found = jnp.where(told[:, :1] == jnp.where(wanted == k, -1, goal).astype(F32), numbered, found)
    return lambda j: jnp.sum(jnp.where(lane == j, found, 0.0)).astype(jnp.int32)


def row_length(chips):
    return 1 << (chips.bit_length() // 2)


def swap_pages(value, chips, along_row, step):
    across = row_length(chips)
    square = across * across == chips
    steps = [2 * step if along_row == (device % 2 == 0 or not square) else 2 * across * step for device in range(2 * chips)]
    return lax.ppermute(value, "req", [(i, i ^ steps[i]) for i in range(2 * chips)])


def find_sources(spread, got):
    chips = len(spread)
    across = row_length(chips)
    down = chips // across

    def kernel(*refs):
        block_refs, got_ref, out_ref = refs[:chips][::-1], refs[-2], refs[-1]
        here = lax.axis_index("req")
        tables = []
        for d in range(chips):
            tables += [block_refs[d][0, :, :META].astype(F32), got_ref[d, :, got_ref.shape[2] - META :]]
        lane = lax.broadcasted_iota(jnp.int32, (8, LANES), 1)
        found = jnp.zeros((8, LANES), F32)
        put = lambda j, number: jnp.where(lane == j, number.astype(F32), found)
        turned = (here % 2 == 1) & (across == down)
        for row in range(down):
            for j in range(2):
                pick = arrivals(tables, here, jnp.where(turned, 2 * row, 2 * across * row) + j)
                source = pick(4)
                chip = source // 2
                chip = jnp.where(turned, chip % across * across + chip // across, chip)
                found = put(2 * row + j, 2 * chip + source % 2)
                if row == 0 and j == 0:
                    found = put(2 * down, pick(2))
                    found = put(2 * down + 1, pick(3))
        out_ref[...] = found

    return pl.pallas_call(
        kernel,
        out_shape=jax.ShapeDtypeStruct((8, LANES), F32),
        in_specs=[VMEM] * (chips + 1),
        out_specs=VMEM,
        compiler_params=pltpu.CompilerParams(vmem_limit_bytes=4 * MIB),
        cost_estimate=cost(0, 0),
        name="find_sources",
    )(*spread[::-1], got)


def number_at(source_ref, j):
    lane = lax.broadcasted_iota(jnp.int32, (1, LANES), 1)
    return jnp.sum(jnp.where(lane == j, source_ref[:1, :], 0.0)).astype(jnp.int32)


def turn_pages(sources, messages, chips):
    across = len(messages)
    down = chips // across
    shape = (2,) + messages[0].shape

    def kernel(source_ref, *refs):
        message_refs, out_refs = refs[:across], refs[across:]
        for row in range(1, down):
            for j in range(2):
                source = number_at(source_ref, 2 * row + j)
                place = jnp.where((source % 2 == 0) & (source < 2 * across), source // 2, 0)
                for d in range(across):

                    @pl.when(place == d)
                    def _():
                        out_refs[row - 1][j] = message_refs[d][...]

    one = jax.ShapeDtypeStruct(shape, messages[0].dtype)
    return pl.pallas_call(
        kernel,
        out_shape=(one,) * (down - 1),
        in_specs=[VMEM] * (1 + across),
        out_specs=(VMEM,) * (down - 1),
        compiler_params=pltpu.CompilerParams(vmem_limit_bytes=(across + 2 * down) * MIB),
        cost_estimate=cost(0, 0),
        name="turn_pages",
    )(sources, *messages)


def with_page(source, across, core, message_refs, turned_refs, use):
    place = jnp.where(source < 2 * across, source // 2, across - 1 + source // (2 * across))
    for d, ref in enumerate(message_refs):

        @pl.when(place == d)
        def _():
            use(ref)

    for row, ref in enumerate(turned_refs):

        @pl.when(place == across + row)
        def _():
            use(ref.at[core])


def choose_page(sources, messages, turned, after):
    across, rows = len(messages), len(turned)

    def kernel(source_ref, *refs):
        message_refs, turned_refs = refs[:across], refs[across : across + rows]
        out_ref = refs[-1]

        def use(ref):
            out_ref[...] = ref[...]

        with_page(number_at(source_ref, 1), across, 1, message_refs, turned_refs, use)

    one = messages[0]
    return pl.pallas_call(
        kernel,
        out_shape=jax.ShapeDtypeStruct(one.shape, one.dtype),
        in_specs=[VMEM] * (1 + across + rows) + [ANY],
        out_specs=VMEM,
        compiler_params=pltpu.CompilerParams(vmem_limit_bytes=(2 + across + 2 * rows) * MIB),
        cost_estimate=cost(0, 0),
        name="choose_page",
    )(sources, *messages, *turned, after)


def project(blocks, weight, later):
    chips = len(blocks)
    slots = blocks[0].shape[1]
    heads, depth, width = weight.shape
    per = 2 if heads % 2 == 0 else 1
    rows = chips * 2 * slots

    def kernel(*refs):
        block_refs = refs[:chips][::-1]
        weight_ref, later_ref, keep_ref, send_ref, later_out, left, sem = refs[chips:]
        copy = pltpu.make_async_copy(later_ref, later_out, sem)
        copy.start()
        for d in range(chips):
            for e in range(2):
                row = (d * 2 + e) * slots
                left[row : row + slots, :] = block_refs[d][e, :, META:].astype(F32)
        lhs = left[...].astype(BF16)

        @pl.loop(0, heads // per)
        def _(i):
            right = jnp.concatenate([weight_ref[i * per + j] for j in range(per)], axis=1)
            total = jnp.dot(lhs, right, preferred_element_type=F32)
            columns = pl.ds(pl.multiple_of(i * (per * width), per * width), per * width)
            for d in range(chips):
                row = d * 2 * slots
                keep_ref[d, :, columns] = total[row : row + slots]
                send_ref[d, :, columns] = total[row + slots : row + 2 * slots]

        for d in range(chips):
            send_ref[d, :, heads * width :] = block_refs[d][0, :, :META].astype(F32)
        copy.wait()

    shape = jax.ShapeDtypeStruct((chips, slots, heads * width), F32)
    wider = jax.ShapeDtypeStruct((chips, slots, heads * width + META), F32)
    return pl.pallas_call(
        kernel,
        out_shape=(shape, wider, jax.ShapeDtypeStruct(later.shape, later.dtype)),
        in_specs=[VMEM] * (chips + 1) + [HBM],
        out_specs=(VMEM, VMEM, VMEM),
        scratch_shapes=[pltpu.VMEM((rows, depth), F32), pltpu.SemaphoreType.DMA],
        compiler_params=pltpu.CompilerParams(vmem_limit_bytes=weight.size * 2 + 12 * MIB),
        cost_estimate=cost(2 * rows * weight.size, 2 * weight.size),
        name="project",
    )(*blocks[::-1], weight, *in_hbm(later))


def combine(keep, got):
    chips, slots, width = keep.shape
    heads = width // (3 * LANES)

    def kernel(keep_ref, got_ref, own_ref, *message_refs):
        own_ref[...] = keep_ref[0] + got_ref[0, :, :width]
        for d in range(1, chips):
            for h in range(heads):
                total = keep_ref[d, :, 3 * h * LANES : 3 * (h + 1) * LANES] + got_ref[d, :, 3 * h * LANES : 3 * (h + 1) * LANES]
                query = total[:, :LANES]
                high = query.astype(BF16)
                low = (query - high.astype(F32)).astype(BF16)
                base = 4 * h * LANES
                message_refs[d - 1][:, base : base + LANES] = high
                message_refs[d - 1][:, base + LANES : base + 2 * LANES] = low
                message_refs[d - 1][:, base + 2 * LANES : base + 4 * LANES] = total[:, LANES:].astype(BF16)

    message = jax.ShapeDtypeStruct((slots, 4 * heads * LANES), BF16)
    return pl.pallas_call(
        kernel,
        out_shape=(jax.ShapeDtypeStruct((slots, width), F32),) + (message,) * (chips - 1),
        in_specs=[VMEM, VMEM],
        out_specs=(VMEM,) * chips,
        compiler_params=pltpu.CompilerParams(vmem_limit_bytes=8 * MIB),
        cost_estimate=cost(0, 8 * keep.size),
        name="combine",
    )(keep, got)


def attend(lengths, new_slot, page_table, sums, bias, tokens, key_pool, value_pool, after):
    parts = len(sums)
    slots = sums[0].shape[0]
    pages, page, width = key_pool.shape
    head = LANES
    heads = width // head
    max_pages = page_table.shape[1]
    short_rows = slots * page
    groups = 2 * parts
    share = head // groups
    per = LANES // share
    tall = 16
    strips = width // PACK
    scale = head ** (-0.5)

    def kernel(*refs):
        length_ref, slot_ref, table_ref = refs[:3]
        sum_refs = refs[3 : 3 + parts][::-1]
        (bias_ref, token_ref, key_ref, value_ref, _, pack_keep, pack_send, patch_ref, value_out) = refs[
            3 + parts : 12 + parts
        ]
        attended_ref, out_sems = refs[12 + parts :]
        step = pages // 4
        writes = [
            pltpu.make_async_copy(value_ref.at[pl.ds(i * step, step)], value_out.at[pl.ds(i * step, step)], out_sems.at[i])
            for i in range(4)
        ]
        for write in writes:
            write.start()
        here = lax.axis_index("req")
        column_block = lax.axis_index("head")
        leaving = leaving_slot(slot_ref, slots, here)
        lengths = [length_ref[s] for s in range(slots)]
        long_slot = jnp.int32(0)
        long_length = jnp.int32(0)
        for s in range(slots):
            is_long = lengths[s] >= page
            long_slot = jnp.where(is_long, s, long_slot)
            long_length = jnp.where(is_long, lengths[s], long_length)

        total = sum_refs[0][...] + bias_ref[...]

        def third(k):
            columns = []
            for h in range(heads):
                one = total[:, (3 * h + k) * head : (3 * h + k + 1) * head]
                for ref in sum_refs[1:]:
                    base = 4 * h * head
                    if k == 0:
                        one = one + ref[:, base : base + head].astype(F32) + ref[:, base + head : base + 2 * head].astype(F32)
                    else:
                        one = one + ref[:, base + (k + 1) * head : base + (k + 2) * head].astype(F32)
                columns.append(one)
            return jnp.concatenate(columns, axis=1)

        query = (third(0) * scale).astype(BF16).astype(F32)
        new_rows = (third(1).astype(BF16).astype(F32), third(2).astype(BF16).astype(F32))

        lane_head = lax.broadcasted_iota(jnp.int32, (tall, width), 1) // head
        on_head = lane_head == lax.broadcasted_iota(jnp.int32, (tall, width), 0)

        def blocked(row):
            return jnp.where(on_head, jnp.broadcast_to(row, (tall, width)), 0.0).astype(BF16)

        def for_slot(which, rows):
            found = rows[0]
            for s in range(1, slots):
                found = jnp.where(which == s, rows[s], found)
            return found

        def softmax(scores, valid, new_score):
            masked = jnp.where(valid, scores, -1e30)
            peak = jnp.maximum(jnp.max(masked, axis=1, keepdims=True), new_score)
            weights = jnp.where(valid, jnp.exp(masked - peak), 0.0)
            new_weight = jnp.exp(new_score - peak)
            denom = jnp.sum(weights, axis=1, keepdims=True) + new_weight
            return weights.astype(BF16), new_weight.astype(BF16).astype(F32), denom

        across = (((1,), (1,)), ((), ()))
        short_query = jnp.concatenate([blocked(query[s : s + 1]) for s in range(slots)], axis=0)
        new_keys = jnp.concatenate([new_rows[0], jnp.zeros((tall - slots, width), F32)], axis=0).astype(BF16)
        new_scores = lax.dot_general(short_query, new_keys, across, preferred_element_type=F32)
        size = (slots * tall, tall)
        own_column = lax.broadcasted_iota(jnp.int32, size, 0) // tall == lax.broadcasted_iota(jnp.int32, size, 1)
        new_score = jnp.sum(jnp.where(own_column, new_scores, 0.0), axis=1, keepdims=True)

        def fold(mixed):
            return jnp.sum(jnp.where(on_head, mixed, 0.0), axis=0, keepdims=True)

        high = -(-slots // 8) * 8

        def attend_all(long_pages):
            first_pages = lambda ref: jnp.concatenate([ref[table_ref[s, 0]] for s in range(slots)], axis=0)
            short_scores = lax.dot_general(short_query, first_pages(key_ref), across, preferred_element_type=F32)
            size = (slots * tall, short_rows)
            row_slot = lax.broadcasted_iota(jnp.int32, size, 0) // tall
            column = lax.broadcasted_iota(jnp.int32, size, 1)
            limit = jnp.zeros(size, jnp.int32)
            for s in range(slots):
                limit = jnp.where(row_slot == s, lengths[s], limit)
            valid = (row_slot == column // page) & (column % page < limit)
            short_probs, new_prob, short_denom = softmax(short_scores, valid, new_score)
            new_values = jnp.concatenate(
                [jnp.broadcast_to(new_rows[1][s : s + 1], (tall, width)) for s in range(slots)], axis=0
            )
            short_mix = jnp.dot(short_probs, first_pages(value_ref), preferred_element_type=F32)
            short_mix = (short_mix + new_prob * new_values) / short_denom

            rows = [fold(short_mix[s * tall : (s + 1) * tall]) for s in range(slots)]
            if long_pages:
                some_pages = lambda ref: jnp.concatenate(
                    [ref[table_ref[long_slot, i]] for i in range(long_pages)], axis=0
                )
                long_query = blocked(for_slot(long_slot, [query[s : s + 1] for s in range(slots)]))
                long_new = for_slot(long_slot, [new_score[s * tall : (s + 1) * tall] for s in range(slots)])
                long_value = for_slot(long_slot, [new_rows[1][s : s + 1] for s in range(slots)])
                scores = lax.dot_general(long_query, some_pages(key_ref), across, preferred_element_type=F32)
                position = lax.broadcasted_iota(jnp.int32, (tall, long_pages * page), 1)
                long_probs, long_prob, long_denom = softmax(scores, position < long_length, long_new)
                mixed = jnp.dot(long_probs, some_pages(value_ref), preferred_element_type=F32)
                long_mix = fold((mixed + long_prob * long_value) / long_denom)
                rows = [jnp.where(lengths[s] >= page, long_mix, row) for s, row in enumerate(rows)]
            rows += [jnp.zeros((high - slots, width), F32)]
            attended_ref[...] = jnp.concatenate(rows, axis=0).astype(BF16).astype(F32)

        half = max_pages // 2
        pl.when(long_length == 0)(lambda: attend_all(0))
        pl.when((long_length > 0) & (long_length <= half * page))(lambda: attend_all(half))
        pl.when(long_length > half * page)(lambda: attend_all(max_pages))
        attended = attended_ref[...]

        toward = jnp.int32(0)
        for s in range(slots):
            toward = jnp.where(leaving == s, slot_ref[s] // slots ^ here, toward)
        token = token_ref[:, pl.ds(pl.multiple_of(column_block * width, LANES), width)].astype(F32)
        extra = []
        for source in new_rows + (token,):
            one = jnp.zeros((1, width), F32)
            for s in range(slots):
                one = jnp.where(leaving == s, source[s : s + 1], one)
            extra += [one[:, i * PACK : (i + 1) * PACK] for i in range(strips)]
        extra = jnp.concatenate(extra + [jnp.zeros((pack_rows(slots, strips) - high - 3 * strips, PACK), F32)], axis=0)

        lane = lax.broadcasted_iota(jnp.int32, (high, LANES), 1)
        row_at = lax.broadcasted_iota(jnp.int32, (high, LANES), 0)
        goal = jnp.full((high, LANES), -1.0, F32)
        for s in range(slots):
            device, slot = slot_ref[s] // slots, slot_ref[s] % slots
            number = jnp.where(lane % share == share - 1, slot, device).astype(F32)
            goal = jnp.where(row_at == s, number, goal)
        turned = [
            pltpu.roll(attended[:, h * head : (h + 1) * head], h % per * share, 1) if h % per else attended[:, h * head : (h + 1) * head]
            for h in range(heads)
        ]
        for k in range(groups):
            count = lax.rem(lane // share - (here ^ k) + per, per)
            tiles = [jnp.zeros((high, LANES), F32) for _ in range(PACK // LANES)]
            for h in range(heads):
                tiles[h // per] = jnp.where(count == h % per, turned[h], tiles[h // per])
            tiles[-1] = jnp.where((count == per - 1) & (lane % share >= share - 2), goal, tiles[-1])
            block = jnp.concatenate([jnp.concatenate(tiles, axis=1), jnp.where(toward == k, extra, 0.0)], axis=0).astype(BF16)
            (pack_keep, pack_send)[k % 2][k // 2] = block

        at = lax.broadcasted_iota(jnp.int32, (tall, width), 0)
        for n, ref in enumerate((key_ref, value_ref)):
            for s in range(slots):
                offset = lengths[s] % page
                first = pl.multiple_of(offset // tall * tall, tall)
                old = ref[table_ref[s, lengths[s] // page], pl.ds(first, tall), :].astype(F32)
                new = jnp.broadcast_to(new_rows[n][s : s + 1], (tall, width))
                patch_ref[n, s] = jnp.where(at == offset - first, new, old).astype(BF16)

        for write in writes:
            write.wait()

    packed = jax.ShapeDtypeStruct((parts, pack_rows(slots, strips), PACK), BF16)
    pool = jax.ShapeDtypeStruct(key_pool.shape, key_pool.dtype)
    return pl.pallas_call(
        kernel,
        out_shape=(packed, packed, jax.ShapeDtypeStruct((2, slots, tall, width), BF16), pool),
        in_specs=[SMEM] * 3 + [VMEM] * (parts + 4) + [ANY],
        out_specs=(VMEM, VMEM, VMEM, HBM),
        scratch_shapes=[
            pltpu.VMEM((-(-slots // 8) * 8, width), F32),
            pltpu.SemaphoreType.DMA((4,)),
        ],
        compiler_params=pltpu.CompilerParams(vmem_limit_bytes=18 * MIB),
        cost_estimate=cost(0, 0),
        name="attend",
    )(lengths, new_slot, page_table, *sums[::-1], bias, tokens, key_pool, value_pool, after)


def pack_rows(slots, strips):
    need = -(-slots // 8) * 8 + 3 * strips
    return -(-need // 16) * 16


def out_project(blocks, weight, pieces, slots, *after):
    chips = len(blocks)
    depth, width = weight.shape
    rows = 2 * chips * slots
    piece = width // pieces

    def kernel(*refs):
        block_refs, weight_ref = refs[:chips][::-1], refs[chips]
        keep_ref, send_ref = refs[chips + 1 + len(after) :]
        gathered = jnp.concatenate(
            [block_refs[d][: 2 * slots, :].astype(F32) for d in range(chips)], axis=0
        )
        here = lax.axis_index("req")
        share = LANES // (2 * chips)
        back = lax.rem(LANES - here * share, LANES)
        gathered = jnp.concatenate(
            [pltpu.roll(gathered[:, first : first + LANES], back, 1) for first in range(0, PACK, LANES)], axis=1
        )
        goal = gathered[:, PACK - 2 : PACK - 1].astype(jnp.int32)
        place = goal ^ here
        row = (place % 2) * (chips * slots) + (place // 2) * slots + gathered[:, PACK - 1 :].astype(jnp.int32)
        row = jnp.where(goal < 0, -1, row)
        size = (gathered.shape[0], rows)
        order = jnp.where(lax.broadcasted_iota(jnp.int32, size, 1) == row, 1.0, 0.0)
        left = lax.dot_general(
            order.astype(BF16), gathered.astype(BF16), (((0,), (0,)), ((), ())), preferred_element_type=F32
        )
        left = left[:, :depth].astype(BF16)
        for j in range(pieces):
            first = (lax.axis_index("head") ^ j) * piece
            total = jnp.dot(
                left, weight_ref[:, pl.ds(pl.multiple_of(first, LANES), piece)], preferred_element_type=F32
            )
            for d in range(chips):
                keep_ref[d, j] = total[d * slots : (d + 1) * slots]
                send_ref[d, j] = total[(chips + d) * slots : (chips + d + 1) * slots].astype(BF16)

    shape = (chips, pieces, slots, piece)
    return pl.pallas_call(
        kernel,
        out_shape=(jax.ShapeDtypeStruct(shape, F32), jax.ShapeDtypeStruct(shape, BF16)),
        in_specs=[VMEM] * (chips + 1) + [ANY] * len(after),
        out_specs=(VMEM, VMEM),
        compiler_params=pltpu.CompilerParams(vmem_limit_bytes=10 * MIB),
        cost_estimate=cost(2 * rows * weight.size, 2 * weight.size),
        name="out_project",
    )(*blocks[::-1], weight, *after)


def place_page(lengths, new_slot, page_table, sources, patches, packs, tokens, out_bias, messages, turned, from_other, key_out, value_out):
    chips, across, rows = len(packs), len(messages), len(turned)
    down = chips // across
    count = across + rows + 1
    page, width = key_out.shape[1:]
    slots = tokens.shape[0]
    strips = width // PACK
    tall = patches.shape[2]

    def kernel(length_ref, slot_ref, table_ref, source_ref, patch_ref, *refs):
        pack_refs = refs[:chips][::-1]
        token_ref, bias_ref = refs[chips : chips + 2]
        message_refs = refs[chips + 2 : chips + 2 + across]
        turned_refs = refs[chips + 2 + across : chips + 2 + across + rows]
        other_ref = refs[chips + 1 + count]
        _, _, base_ref, key_ref, value_ref, buffer, out_sems, patch_sems = refs[chips + 2 + count :]
        here = lax.axis_index("req")
        leaving = leaving_slot(slot_ref, slots, here)

        def patch(n, s):
            length = length_ref[s]
            first = pl.multiple_of(length % page // tall * tall, tall)
            target = (key_ref, value_ref)[n].at[table_ref[s, length // page], pl.ds(first, tall)]
            return pltpu.make_async_copy(patch_ref.at[n, s], target, patch_sems.at[n, s])

        for n in range(2):
            for s in range(slots):

                @pl.when(leaving != s)
                def _():
                    patch(n, s).start()

        column = pl.multiple_of(lax.axis_index("head") * width, LANES)
        page_at, offset = [number_at(source_ref, 2 * down + j) for j in range(2)]

        def use(ref):
            buffer[...] = ref[...]

        source = number_at(source_ref, 0)

        @pl.when(source % 2 == 0)
        def _():
            with_page(source, across, 0, message_refs, turned_refs, use)

        @pl.when(source % 2 == 1)
        def _():
            use(other_ref)

        arrived = pack_refs[0][2 * slots :, :].astype(F32)
        for ref in pack_refs[1:]:
            arrived = arrived + ref[2 * slots :, :].astype(F32)

        def fresh(n):
            return jnp.concatenate([arrived[n * strips + i : n * strips + i + 1, :] for i in range(strips)], axis=1)

        at = lax.broadcasted_iota(jnp.int32, (slots, width), 0)
        token = jnp.where(
            at == leaving,
            jnp.broadcast_to(fresh(2), (slots, width)),
            token_ref[:, pl.ds(column, width)].astype(F32),
        )
        base_ref[...] = token + bias_ref[:, pl.ds(column, width)]
        first = pl.multiple_of(offset // 16 * 16, 16)
        row = lax.broadcasted_iota(jnp.int32, (16, width), 0)
        for n in range(2):
            old = buffer[n, pl.ds(first, 16), :].astype(F32)
            new = jnp.broadcast_to(fresh(n), (16, width))
            buffer[n, pl.ds(first, 16), :] = jnp.where(row == offset - first, new, old).astype(BF16)
        copies = [
            pltpu.make_async_copy(buffer.at[n], target.at[page_at], out_sems.at[n])
            for n, target in enumerate((key_ref, value_ref))
        ]
        for copy in copies:
            copy.start()
        for n in range(2):
            for s in range(slots):

                @pl.when(leaving != s)
                def _():
                    patch(n, s).wait()

        for copy in copies:
            copy.wait()

    shape = jax.ShapeDtypeStruct(key_out.shape, key_out.dtype)
    return pl.pallas_call(
        kernel,
        out_shape=(jax.ShapeDtypeStruct((slots, width), F32), shape, shape),
        in_specs=[SMEM] * 3 + [VMEM] * (chips + 4 + count) + [HBM] * 2,
        out_specs=(VMEM, HBM, HBM),
        scratch_shapes=[
            pltpu.VMEM((2, page, width), BF16),
            pltpu.SemaphoreType.DMA((2,)),
            pltpu.SemaphoreType.DMA((2, slots)),
        ],
        input_output_aliases={chips + 7 + count: 1, chips + 8 + count: 2},
        compiler_params=pltpu.CompilerParams(vmem_limit_bytes=(6 + 2 * count) * MIB),
        cost_estimate=cost(0, 8 * page * width),
        name="place_page",
    )(
        lengths, new_slot, page_table, sources, patches, *packs[::-1], tokens, out_bias, *messages, *turned, from_other, key_out, value_out
    )


def body(
    tokens,
    norm_gain,
    norm_shift,
    qkv_weight,
    qkv_bias,
    out_weight,
    out_bias,
    key_pool,
    value_pool,
    lengths,
    page_table,
    new_slot,
    new_page,
):
    groups = lax.axis_size("req")
    head_groups = lax.axis_size("head")
    slots = tokens.shape[0]
    chips = groups // 2

    other_tokens = swap(tokens, "req", 1)
    told, own_tokens, gain, shift = tell(
        lengths, new_slot, new_page, tokens, norm_gain[None], norm_shift[None], key_pool.shape[1]
    )
    blocks = prepare(own_tokens, other_tokens, gain, shift, told)
    across = row_length(chips)
    spread = [blocks[0]] + [swap(blocks[d], "req", 2 * d) for d in range(1, chips)]
    page = pick_page(new_slot, page_table, key_pool, value_pool, *blocks[::-1])
    page, *spread = lax.optimization_barrier((page, *spread))
    pages = [page] + [swap_pages(page, chips, True, d) for d in range(1, across)]

    flat = out_weight.reshape(-1, out_weight.shape[2])
    keep, send, staged = project(spread, jnp.transpose(qkv_weight, (1, 0, 2)), flat)
    got = swap(send, "req", 1)
    own, *messages = combine(keep, got)
    sources = find_sources(spread, got)
    sums = [own] + [swap(messages[d - 1], "req", 2 * d) for d in range(1, chips)]
    turning = turn_pages(sources, pages, chips)
    turned = [swap_pages(one, chips, False, row + 1) for row, one in enumerate(turning)]

    pack_keep, pack_send, patches, value_out = attend(
        lengths,
        new_slot,
        page_table,
        sums,
        qkv_bias.reshape(1, -1),
        own_tokens,
        key_pool,
        value_pool,
        turning[0],
    )
    packs_got = swap(pack_send, "req", 1)
    high = -(-slots // 8) * 8
    merged = [
        jnp.concatenate([pack_keep[d, :slots], packs_got[d, :slots], pack_keep[d, high:] + packs_got[d, high:]], axis=0)
        for d in range(chips)
    ]
    packs = [merged[0]] + [swap(merged[d], "req", 2 * d) for d in range(1, chips)]

    keep, send = out_project(
        packs, staged, head_groups, slots, turned[0]
    )
    total = keep + swap(send, "req", 1).astype(F32)
    from_other = swap(choose_page(sources, pages, turned, keep), "req", 1)
    summed = total[0]
    for d in reversed(range(1, chips)):
        summed = summed + swap(total[d].astype(BF16), "req", 2 * d).astype(F32)
    key_out = write_pool(key_pool, total)
    summed, key_out, from_other = lax.optimization_barrier((summed, key_out, from_other))
    base, key_out, value_out = place_page(
        lengths,
        new_slot,
        page_table,
        sources,
        patches,
        packs,
        own_tokens,
        out_bias[None],
        pages,
        turned,
        from_other,
        key_out,
        value_out,
    )
    hidden = summed[0]
    for j in [head_groups - 1, *range(1, head_groups - 1)]:
        hidden = hidden + swap(summed[j].astype(BF16), "head", j).astype(F32)
    hidden_out = (hidden + base).astype(BF16)
    return (hidden_out, key_out, value_out)


def solution(mesh):
    in_specs = (
        P("req", None),
        P(),
        P(),
        P("req", "head", None),
        P("head", None),
        P("head", "req", None),
        P(),
        P("req", None, "head"),
        P("req", None, "head"),
        P("req"),
        P("req", None),
        P("req"),
        P("req"),
    )
    out_specs = (P("req", "head"), P("req", None, "head"), P("req", None, "head"))
    return jax.shard_map(body, mesh=mesh, in_specs=in_specs, out_specs=out_specs, check_vma=False)
```

```python
import functools

import jax
import jax.numpy as jnp
from jax import lax
from jax.experimental import pallas as pl
from jax.experimental.pallas import tpu as pltpu
from jax.sharding import PartitionSpec as P

EPSILON = 1e-05
F32 = jnp.float32
BF16 = jnp.bfloat16
LANES = 128
META = 128
PACK = 256
VMEM = pl.BlockSpec(memory_space=pltpu.VMEM)
SMEM = pl.BlockSpec(memory_space=pltpu.SMEM)
ANY = pl.BlockSpec(memory_space=pl.ANY)
HBM = pl.BlockSpec(memory_space=pltpu.HBM)
MIB = 1024 * 1024


def cost(flops, moved):
    del flops, moved
    return pl.CostEstimate(flops=0, bytes_accessed=0, transcendentals=0)


def swap(value, axis, step):
    size = lax.axis_size(axis)
    return lax.ppermute(value, axis, [(i, i ^ step) for i in range(size)])


def in_hbm(*arrays):
    return [pltpu.with_memory_space_constraint(array, pltpu.HBM) for array in arrays]


def write_pool(pool, after):
    parts = 4
    step = pool.shape[0] // parts

    def kernel(pool_ref, _, out_ref, sems):
        places = [pl.ds(i * step, step) for i in range(parts)]
        copies = [
            pltpu.make_async_copy(pool_ref.at[place], out_ref.at[place], sems.at[i]) for i, place in enumerate(places)
        ]
        for copy in copies:
            copy.start()
        for copy in copies:
            copy.wait()

    return pl.pallas_call(
        kernel,
        out_shape=jax.ShapeDtypeStruct(pool.shape, pool.dtype),
        in_specs=[VMEM, ANY],
        out_specs=HBM,
        scratch_shapes=[pltpu.SemaphoreType.DMA((parts,))],
        compiler_params=pltpu.CompilerParams(vmem_limit_bytes=8 * MIB),
        cost_estimate=cost(0, 2 * pool.size),
        name="write_pool",
    )(pool, after)


def leaving_slot(new_slot_ref, slots, here):
    leaving = jnp.int32(0)
    for s in range(slots):
        leaving = jnp.where(new_slot_ref[s] // slots != here, s, leaving)
    return leaving


def tell(lengths, new_slot, new_page, tokens, gain, shift, page):
    slots = new_slot.shape[0]

    def kernel(length_ref, slot_ref, page_ref, token_ref, gain_ref, shift_ref, told_ref, token_out, gain_out, shift_out):
        row = lax.broadcasted_iota(jnp.int32, (slots, META), 0)
        lane = lax.broadcasted_iota(jnp.int32, (slots, META), 1)
        told = jnp.zeros((slots, META), F32)
        for s in range(slots):
            slot = slot_ref[s]
            numbers = (slot // slots, slot % slots, page_ref[s], length_ref[s] % page)
            for j, number in enumerate(numbers):
                told = jnp.where((row == s) & (lane == j), number.astype(F32), told)
        told_ref[...] = told
        token_out[...] = token_ref[...]
        gain_out[...] = gain_ref[...]
        shift_out[...] = shift_ref[...]

    return pl.pallas_call(
        kernel,
        out_shape=(
            jax.ShapeDtypeStruct((slots, META), F32),
            jax.ShapeDtypeStruct(tokens.shape, tokens.dtype),
            jax.ShapeDtypeStruct(gain.shape, gain.dtype),
            jax.ShapeDtypeStruct(shift.shape, shift.dtype),
        ),
        in_specs=[SMEM] * 3 + [VMEM] * 3,
        out_specs=(VMEM,) * 4,
        compiler_params=pltpu.CompilerParams(vmem_limit_bytes=2 * MIB),
        cost_estimate=cost(0, 0),
        name="tell",
    )(*in_hbm(lengths, new_slot, new_page, tokens, gain, shift))


def pick_page(new_slot, page_table, key_pool, value_pool, *after):
    slots = new_slot.shape[0]

    def kernel(slot_ref, table_ref, key_ref, value_ref, *refs):
        out_ref, sems = refs[len(after) :]
        leaving = leaving_slot(slot_ref, slots, lax.axis_index("req"))
        copies = [
            pltpu.make_async_copy(source.at[table_ref[leaving, 0]], out_ref.at[n], sems.at[n])
            for n, source in enumerate((key_ref, value_ref))
        ]
        for copy in copies:
            copy.start()
        for copy in copies:
            copy.wait()

    return pl.pallas_call(
        kernel,
        out_shape=jax.ShapeDtypeStruct((2,) + key_pool.shape[1:], key_pool.dtype),
        in_specs=[SMEM] * 2 + [HBM] * 2 + [ANY] * len(after),
        out_specs=VMEM,
        scratch_shapes=[pltpu.SemaphoreType.DMA((2,))],
        compiler_params=pltpu.CompilerParams(vmem_limit_bytes=2 * MIB),
        cost_estimate=cost(0, 0),
        name="pick_page",
    )(*in_hbm(new_slot, page_table, key_pool, value_pool), *after)


def prepare(tokens, other_tokens, gain, shift, told):
    groups = lax.axis_size("req")
    chips = groups // 2
    slots, model = tokens.shape
    depth = model // groups

    def kernel(token_ref, other_ref, gain_ref, shift_ref, told_ref, *refs):
        out_refs, normed = refs[:chips], refs[chips]
        here = lax.axis_index("req")
        values = jnp.concatenate([token_ref[...].astype(F32), other_ref[...].astype(F32)], axis=0)
        average = jnp.mean(values, axis=1, keepdims=True)
        centered = values - average
        variance = jnp.mean(centered * centered, axis=1, keepdims=True)
        rows = centered * lax.rsqrt(variance + EPSILON) * gain_ref[...] + shift_ref[...]
        normed[...] = rows.astype(BF16).astype(F32)
        for d in range(chips):
            first = (here ^ 2 * d) * depth
            if depth % LANES == 0:
                block = normed[:, pl.ds(pl.multiple_of(first, LANES), depth)]
            else:
                block = pltpu.roll(normed[...], lax.rem(model - first, model), 1)[:, :depth]
            for e in range(2):
                out_refs[d][e, :, META:] = block[e * slots : (e + 1) * slots].astype(BF16)
            out_refs[d][0, :, :META] = told_ref[...].astype(BF16)
            out_refs[d][1, :, :META] = jnp.zeros((slots, META), BF16)

    return pl.pallas_call(
        kernel,
        out_shape=(jax.ShapeDtypeStruct((2, slots, META + depth), BF16),) * chips,
        in_specs=[VMEM] * 5,
        out_specs=(VMEM,) * chips,
        scratch_shapes=[pltpu.VMEM((2 * slots, model), F32)],
        compiler_params=pltpu.CompilerParams(vmem_limit_bytes=4 * MIB),
        cost_estimate=cost(0, 0),
        name="prepare",
    )(tokens, other_tokens, gain, shift, told)


def arrivals(tables, here, wanted):
    slots = tables[0].shape[0]
    lane = lax.broadcasted_iota(jnp.int32, (slots, META), 1)
    found = jnp.zeros((slots, META), F32)
    goal = here ^ wanted
    for k, told in enumerate(tables):
        numbered = jnp.where(lane == 4, float(k), told)
        found = jnp.where(told[:, :1] == jnp.where(wanted == k, -1, goal).astype(F32), numbered, found)
    return lambda j: jnp.sum(jnp.where(lane == j, found, 0.0)).astype(jnp.int32)


def row_length(chips):
    return 1 << (chips.bit_length() // 2)


def swap_pages(value, chips, along_row, step):
    across = row_length(chips)
    square = across * across == chips
    steps = [2 * step if along_row == (device % 2 == 0 or not square) else 2 * across * step for device in range(2 * chips)]
    return lax.ppermute(value, "req", [(i, i ^ steps[i]) for i in range(2 * chips)])


def find_sources(spread, got):
    chips = len(spread)
    across = row_length(chips)
    down = chips // across

    def kernel(*refs):
        block_refs, got_ref, out_ref = refs[:chips][::-1], refs[-2], refs[-1]
        here = lax.axis_index("req")
        tables = []
        for d in range(chips):
            tables += [block_refs[d][0, :, :META].astype(F32), got_ref[d, :, got_ref.shape[2] - META :]]
        lane = lax.broadcasted_iota(jnp.int32, (8, LANES), 1)
        found = jnp.zeros((8, LANES), F32)
        put = lambda j, number: jnp.where(lane == j, number.astype(F32), found)
        turned = (here % 2 == 1) & (across == down)
        for row in range(down):
            for j in range(2):
                pick = arrivals(tables, here, jnp.where(turned, 2 * row, 2 * across * row) + j)
                source = pick(4)
                chip = source // 2
                chip = jnp.where(turned, chip % across * across + chip // across, chip)
                found = put(2 * row + j, 2 * chip + source % 2)
                if row == 0 and j == 0:
                    found = put(2 * down, pick(2))
                    found = put(2 * down + 1, pick(3))
        out_ref[...] = found

    return pl.pallas_call(
        kernel,
        out_shape=jax.ShapeDtypeStruct((8, LANES), F32),
        in_specs=[VMEM] * (chips + 1),
        out_specs=VMEM,
        compiler_params=pltpu.CompilerParams(vmem_limit_bytes=4 * MIB),
        cost_estimate=cost(0, 0),
        name="find_sources",
    )(*spread[::-1], got)


def number_at(source_ref, j):
    lane = lax.broadcasted_iota(jnp.int32, (1, LANES), 1)
    return jnp.sum(jnp.where(lane == j, source_ref[:1, :], 0.0)).astype(jnp.int32)


def turn_pages(sources, messages, chips):
    across = len(messages)
    down = chips // across
    shape = (2,) + messages[0].shape

    def kernel(source_ref, *refs):
        message_refs, out_refs = refs[:across], refs[across:]
        for row in range(1, down):
            for j in range(2):
                source = number_at(source_ref, 2 * row + j)
                place = jnp.where((source % 2 == 0) & (source < 2 * across), source // 2, 0)
                for d in range(across):

                    @pl.when(place == d)
                    def _():
                        out_refs[row - 1][j] = message_refs[d][...]

    one = jax.ShapeDtypeStruct(shape, messages[0].dtype)
    return pl.pallas_call(
        kernel,
        out_shape=(one,) * (down - 1),
        in_specs=[VMEM] * (1 + across),
        out_specs=(VMEM,) * (down - 1),
        compiler_params=pltpu.CompilerParams(vmem_limit_bytes=(across + 2 * down) * MIB),
        cost_estimate=cost(0, 0),
        name="turn_pages",
    )(sources, *messages)


def with_page(source, across, core, message_refs, turned_refs, use):
    place = jnp.where(source < 2 * across, source // 2, across - 1 + source // (2 * across))
    for d, ref in enumerate(message_refs):

        @pl.when(place == d)
        def _():
            use(ref)

    for row, ref in enumerate(turned_refs):

        @pl.when(place == across + row)
        def _():
            use(ref.at[core])


def choose_page(sources, messages, turned, after):
    across, rows = len(messages), len(turned)

    def kernel(source_ref, *refs):
        message_refs, turned_refs = refs[:across], refs[across : across + rows]
        out_ref = refs[-1]

        def use(ref):
            out_ref[...] = ref[...]

        with_page(number_at(source_ref, 1), across, 1, message_refs, turned_refs, use)

    one = messages[0]
    return pl.pallas_call(
        kernel,
        out_shape=jax.ShapeDtypeStruct(one.shape, one.dtype),
        in_specs=[VMEM] * (1 + across + rows) + [ANY],
        out_specs=VMEM,
        compiler_params=pltpu.CompilerParams(vmem_limit_bytes=(2 + across + 2 * rows) * MIB),
        cost_estimate=cost(0, 0),
        name="choose_page",
    )(sources, *messages, *turned, after)


def project(blocks, weight, later):
    chips = len(blocks)
    slots = blocks[0].shape[1]
    heads, depth, width = weight.shape
    per = 2 if heads % 2 == 0 else 1
    rows = chips * 2 * slots

    def kernel(*refs):
        block_refs = refs[:chips][::-1]
        weight_ref, later_ref, keep_ref, send_ref, later_out, left, sem = refs[chips:]
        copy = pltpu.make_async_copy(later_ref, later_out, sem)
        copy.start()
        for d in range(chips):
            for e in range(2):
                row = (d * 2 + e) * slots
                left[row : row + slots, :] = block_refs[d][e, :, META:].astype(F32)
        lhs = left[...].astype(BF16)

        @pl.loop(0, heads // per)
        def _(i):
            right = jnp.concatenate([weight_ref[i * per + j] for j in range(per)], axis=1)
            total = jnp.dot(lhs, right, preferred_element_type=F32)
            columns = pl.ds(pl.multiple_of(i * (per * width), per * width), per * width)
            for d in range(chips):
                row = d * 2 * slots
                keep_ref[d, :, columns] = total[row : row + slots]
                send_ref[d, :, columns] = total[row + slots : row + 2 * slots]

        for d in range(chips):
            send_ref[d, :, heads * width :] = block_refs[d][0, :, :META].astype(F32)
        copy.wait()

    shape = jax.ShapeDtypeStruct((chips, slots, heads * width), F32)
    wider = jax.ShapeDtypeStruct((chips, slots, heads * width + META), F32)
    return pl.pallas_call(
        kernel,
        out_shape=(shape, wider, jax.ShapeDtypeStruct(later.shape, later.dtype)),
        in_specs=[VMEM] * (chips + 1) + [HBM],
        out_specs=(VMEM, VMEM, VMEM),
        scratch_shapes=[pltpu.VMEM((rows, depth), F32), pltpu.SemaphoreType.DMA],
        compiler_params=pltpu.CompilerParams(vmem_limit_bytes=weight.size * 2 + 12 * MIB),
        cost_estimate=cost(2 * rows * weight.size, 2 * weight.size),
        name="project",
    )(*blocks[::-1], weight, *in_hbm(later))


def combine(keep, got):
    chips, slots, width = keep.shape
    heads = width // (3 * LANES)

    def kernel(keep_ref, got_ref, own_ref, *message_refs):
        own_ref[...] = keep_ref[0] + got_ref[0, :, :width]
        for d in range(1, chips):
            for h in range(heads):
                total = keep_ref[d, :, 3 * h * LANES : 3 * (h + 1) * LANES] + got_ref[d, :, 3 * h * LANES : 3 * (h + 1) * LANES]
                query = total[:, :LANES]
                high = query.astype(BF16)
                low = (query - high.astype(F32)).astype(BF16)
                base = 4 * h * LANES
                message_refs[d - 1][:, base : base + LANES] = high
                message_refs[d - 1][:, base + LANES : base + 2 * LANES] = low
                message_refs[d - 1][:, base + 2 * LANES : base + 4 * LANES] = total[:, LANES:].astype(BF16)

    message = jax.ShapeDtypeStruct((slots, 4 * heads * LANES), BF16)
    return pl.pallas_call(
        kernel,
        out_shape=(jax.ShapeDtypeStruct((slots, width), F32),) + (message,) * (chips - 1),
        in_specs=[VMEM, VMEM],
        out_specs=(VMEM,) * chips,
        compiler_params=pltpu.CompilerParams(vmem_limit_bytes=8 * MIB),
        cost_estimate=cost(0, 8 * keep.size),
        name="combine",
    )(keep, got)


def attend(lengths, new_slot, page_table, sums, bias, tokens, key_pool, value_pool, after):
    parts = len(sums)
    slots = sums[0].shape[0]
    pages, page, width = key_pool.shape
    head = LANES
    heads = width // head
    max_pages = page_table.shape[1]
    short_rows = slots * page
    groups = 2 * parts
    share = head // groups
    per = LANES // share
    tall = 16
    strips = width // PACK
    scale = head ** (-0.5)

    def kernel(*refs):
        length_ref, slot_ref, table_ref = refs[:3]
        sum_refs = refs[3 : 3 + parts][::-1]
        (bias_ref, token_ref, key_ref, value_ref, _, pack_keep, pack_send, patch_ref, value_out) = refs[
            3 + parts : 12 + parts
        ]
        attended_ref, out_sems = refs[12 + parts :]
        step = pages // 4
        writes = [
            pltpu.make_async_copy(value_ref.at[pl.ds(i * step, step)], value_out.at[pl.ds(i * step, step)], out_sems.at[i])
            for i in range(4)
        ]
        for write in writes:
            write.start()
        here = lax.axis_index("req")
        column_block = lax.axis_index("head")
        leaving = leaving_slot(slot_ref, slots, here)
        lengths = [length_ref[s] for s in range(slots)]
        long_slot = jnp.int32(0)
        long_length = jnp.int32(0)
        for s in range(slots):
            is_long = lengths[s] >= page
            long_slot = jnp.where(is_long, s, long_slot)
            long_length = jnp.where(is_long, lengths[s], long_length)

        total = sum_refs[0][...] + bias_ref[...]

        def third(k):
            columns = []
            for h in range(heads):
                one = total[:, (3 * h + k) * head : (3 * h + k + 1) * head]
                for ref in sum_refs[1:]:
                    base = 4 * h * head
                    if k == 0:
                        one = one + ref[:, base : base + head].astype(F32) + ref[:, base + head : base + 2 * head].astype(F32)
                    else:
                        one = one + ref[:, base + (k + 1) * head : base + (k + 2) * head].astype(F32)
                columns.append(one)
            return jnp.concatenate(columns, axis=1)

        query = (third(0) * scale).astype(BF16).astype(F32)
        new_rows = (third(1).astype(BF16).astype(F32), third(2).astype(BF16).astype(F32))

        lane_head = lax.broadcasted_iota(jnp.int32, (tall, width), 1) // head
        on_head = lane_head == lax.broadcasted_iota(jnp.int32, (tall, width), 0)

        def blocked(row):
            return jnp.where(on_head, jnp.broadcast_to(row, (tall, width)), 0.0).astype(BF16)

        def for_slot(which, rows):
            found = rows[0]
            for s in range(1, slots):
                found = jnp.where(which == s, rows[s], found)
            return found

        def softmax(scores, valid, new_score):
            masked = jnp.where(valid, scores, -1e30)
            peak = jnp.maximum(jnp.max(masked, axis=1, keepdims=True), new_score)
            weights = jnp.where(valid, jnp.exp(masked - peak), 0.0)
            new_weight = jnp.exp(new_score - peak)
            denom = jnp.sum(weights, axis=1, keepdims=True) + new_weight
            return weights.astype(BF16), new_weight.astype(BF16).astype(F32), denom

        across = (((1,), (1,)), ((), ()))
        short_query = jnp.concatenate([blocked(query[s : s + 1]) for s in range(slots)], axis=0)
        new_keys = jnp.concatenate([new_rows[0], jnp.zeros((tall - slots, width), F32)], axis=0).astype(BF16)
        new_scores = lax.dot_general(short_query, new_keys, across, preferred_element_type=F32)
        size = (slots * tall, tall)
        own_column = lax.broadcasted_iota(jnp.int32, size, 0) // tall == lax.broadcasted_iota(jnp.int32, size, 1)
        new_score = jnp.sum(jnp.where(own_column, new_scores, 0.0), axis=1, keepdims=True)

        def fold(mixed):
            return jnp.sum(jnp.where(on_head, mixed, 0.0), axis=0, keepdims=True)

        high = -(-slots // 8) * 8

        def attend_all(long_pages):
            first_pages = lambda ref: jnp.concatenate([ref[table_ref[s, 0]] for s in range(slots)], axis=0)
            short_scores = lax.dot_general(short_query, first_pages(key_ref), across, preferred_element_type=F32)
            size = (slots * tall, short_rows)
            row_slot = lax.broadcasted_iota(jnp.int32, size, 0) // tall
            column = lax.broadcasted_iota(jnp.int32, size, 1)
            limit = jnp.zeros(size, jnp.int32)
            for s in range(slots):
                limit = jnp.where(row_slot == s, lengths[s], limit)
            valid = (row_slot == column // page) & (column % page < limit)
            short_probs, new_prob, short_denom = softmax(short_scores, valid, new_score)
            new_values = jnp.concatenate(
                [jnp.broadcast_to(new_rows[1][s : s + 1], (tall, width)) for s in range(slots)], axis=0
            )
            short_mix = jnp.dot(short_probs, first_pages(value_ref), preferred_element_type=F32)
            short_mix = (short_mix + new_prob * new_values) / short_denom

            rows = [fold(short_mix[s * tall : (s + 1) * tall]) for s in range(slots)]
            if long_pages:
                some_pages = lambda ref: jnp.concatenate(
                    [ref[table_ref[long_slot, i]] for i in range(long_pages)], axis=0
                )
                long_query = blocked(for_slot(long_slot, [query[s : s + 1] for s in range(slots)]))
                long_new = for_slot(long_slot, [new_score[s * tall : (s + 1) * tall] for s in range(slots)])
                long_value = for_slot(long_slot, [new_rows[1][s : s + 1] for s in range(slots)])
                scores = lax.dot_general(long_query, some_pages(key_ref), across, preferred_element_type=F32)
                position = lax.broadcasted_iota(jnp.int32, (tall, long_pages * page), 1)
                long_probs, long_prob, long_denom = softmax(scores, position < long_length, long_new)
                mixed = jnp.dot(long_probs, some_pages(value_ref), preferred_element_type=F32)
                long_mix = fold((mixed + long_prob * long_value) / long_denom)
                rows = [jnp.where(lengths[s] >= page, long_mix, row) for s, row in enumerate(rows)]
            rows += [jnp.zeros((high - slots, width), F32)]
            attended_ref[...] = jnp.concatenate(rows, axis=0).astype(BF16).astype(F32)

        half = max_pages // 2
        pl.when(long_length == 0)(lambda: attend_all(0))
        pl.when((long_length > 0) & (long_length <= half * page))(lambda: attend_all(half))
        pl.when(long_length > half * page)(lambda: attend_all(max_pages))
        attended = attended_ref[...]

        toward = jnp.int32(0)
        for s in range(slots):
            toward = jnp.where(leaving == s, slot_ref[s] // slots ^ here, toward)
        token = token_ref[:, pl.ds(pl.multiple_of(column_block * width, LANES), width)].astype(F32)
        extra = []
        for source in new_rows + (token,):
            one = jnp.zeros((1, width), F32)
            for s in range(slots):
                one = jnp.where(leaving == s, source[s : s + 1], one)
            extra += [one[:, i * PACK : (i + 1) * PACK] for i in range(strips)]
        extra = jnp.concatenate(extra + [jnp.zeros((pack_rows(slots, strips) - high - 3 * strips, PACK), F32)], axis=0)

        lane = lax.broadcasted_iota(jnp.int32, (high, LANES), 1)
        row_at = lax.broadcasted_iota(jnp.int32, (high, LANES), 0)
        goal = jnp.full((high, LANES), -1.0, F32)
        for s in range(slots):
            device, slot = slot_ref[s] // slots, slot_ref[s] % slots
            number = jnp.where(lane % share == share - 1, slot, device).astype(F32)
            goal = jnp.where(row_at == s, number, goal)
        turned = [
            pltpu.roll(attended[:, h * head : (h + 1) * head], h % per * share, 1) if h % per else attended[:, h * head : (h + 1) * head]
            for h in range(heads)
        ]
        for k in range(groups):
            count = lax.rem(lane // share - (here ^ k) + per, per)
            tiles = [jnp.zeros((high, LANES), F32) for _ in range(PACK // LANES)]
            for h in range(heads):
                tiles[h // per] = jnp.where(count == h % per, turned[h], tiles[h // per])
            tiles[-1] = jnp.where((count == per - 1) & (lane % share >= share - 2), goal, tiles[-1])
            block = jnp.concatenate([jnp.concatenate(tiles, axis=1), jnp.where(toward == k, extra, 0.0)], axis=0).astype(BF16)
            (pack_keep, pack_send)[k % 2][k // 2] = block

        at = lax.broadcasted_iota(jnp.int32, (tall, width), 0)
        for n, ref in enumerate((key_ref, value_ref)):
            for s in range(slots):
                offset = lengths[s] % page
                first = pl.multiple_of(offset // tall * tall, tall)
                old = ref[table_ref[s, lengths[s] // page], pl.ds(first, tall), :].astype(F32)
                new = jnp.broadcast_to(new_rows[n][s : s + 1], (tall, width))
                patch_ref[n, s] = jnp.where(at == offset - first, new, old).astype(BF16)

        for write in writes:
            write.wait()

    packed = jax.ShapeDtypeStruct((parts, pack_rows(slots, strips), PACK), BF16)
    pool = jax.ShapeDtypeStruct(key_pool.shape, key_pool.dtype)
    return pl.pallas_call(
        kernel,
        out_shape=(packed, packed, jax.ShapeDtypeStruct((2, slots, tall, width), BF16), pool),
        in_specs=[SMEM] * 3 + [VMEM] * (parts + 4) + [ANY],
        out_specs=(VMEM, VMEM, VMEM, HBM),
        scratch_shapes=[
            pltpu.VMEM((-(-slots // 8) * 8, width), F32),
            pltpu.SemaphoreType.DMA((4,)),
        ],
        compiler_params=pltpu.CompilerParams(vmem_limit_bytes=18 * MIB),
        cost_estimate=cost(0, 0),
        name="attend",
    )(lengths, new_slot, page_table, *sums[::-1], bias, tokens, key_pool, value_pool, after)


def pack_rows(slots, strips):
    need = -(-slots // 8) * 8 + 3 * strips
    return -(-need // 16) * 16


def out_project(blocks, weight, pieces, slots, *after):
    chips = len(blocks)
    depth, width = weight.shape
    rows = 2 * chips * slots
    piece = width // pieces

    def kernel(*refs):
        block_refs, weight_ref = refs[:chips], refs[chips]
        keep_ref, send_ref = refs[chips + 1 + len(after) :]
        gathered = jnp.concatenate(
            [block_refs[d][: 2 * slots, :].astype(F32) for d in range(chips)], axis=0
        )
        here = lax.axis_index("req")
        share = LANES // (2 * chips)
        back = lax.rem(LANES - here * share, LANES)
        gathered = jnp.concatenate(
            [pltpu.roll(gathered[:, first : first + LANES], back, 1) for first in range(0, PACK, LANES)], axis=1
        )
        goal = gathered[:, PACK - 2 : PACK - 1].astype(jnp.int32)
        place = goal ^ here
        row = (place % 2) * (chips * slots) + (place // 2) * slots + gathered[:, PACK - 1 :].astype(jnp.int32)
        row = jnp.where(goal < 0, -1, row)
        size = (gathered.shape[0], rows)
        order = jnp.where(lax.broadcasted_iota(jnp.int32, size, 1) == row, 1.0, 0.0)
        left = lax.dot_general(
            order.astype(BF16), gathered.astype(BF16), (((0,), (0,)), ((), ())), preferred_element_type=F32
        )
        left = left[:, :depth].astype(BF16)
        for j in range(pieces):
            first = (lax.axis_index("head") ^ j) * piece
            total = jnp.dot(
                left, weight_ref[:, pl.ds(pl.multiple_of(first, LANES), piece)], preferred_element_type=F32
            )
            for d in range(chips):
                keep_ref[d, j] = total[d * slots : (d + 1) * slots]
                send_ref[d, j] = total[(chips + d) * slots : (chips + d + 1) * slots].astype(BF16)

    shape = (chips, pieces, slots, piece)
    return pl.pallas_call(
        kernel,
        out_shape=(jax.ShapeDtypeStruct(shape, F32), jax.ShapeDtypeStruct(shape, BF16)),
        in_specs=[VMEM] * (chips + 1) + [ANY] * len(after),
        out_specs=(VMEM, VMEM),
        compiler_params=pltpu.CompilerParams(vmem_limit_bytes=10 * MIB),
        cost_estimate=cost(2 * rows * weight.size, 2 * weight.size),
        name="out_project",
    )(*blocks, weight, *after)


def place_page(lengths, new_slot, page_table, sources, patches, packs, tokens, out_bias, messages, turned, from_other, key_out, value_out):
    chips, across, rows = len(packs), len(messages), len(turned)
    down = chips // across
    count = across + rows + 1
    page, width = key_out.shape[1:]
    slots = tokens.shape[0]
    strips = width // PACK
    tall = patches.shape[2]

    def kernel(length_ref, slot_ref, table_ref, source_ref, patch_ref, *refs):
        pack_refs = refs[:chips][::-1]
        token_ref, bias_ref = refs[chips : chips + 2]
        message_refs = refs[chips + 2 : chips + 2 + across]
        turned_refs = refs[chips + 2 + across : chips + 2 + across + rows]
        other_ref = refs[chips + 1 + count]
        _, _, base_ref, key_ref, value_ref, buffer, out_sems, patch_sems = refs[chips + 2 + count :]
        here = lax.axis_index("req")
        leaving = leaving_slot(slot_ref, slots, here)

        def patch(n, s):
            length = length_ref[s]
            first = pl.multiple_of(length % page // tall * tall, tall)
            target = (key_ref, value_ref)[n].at[table_ref[s, length // page], pl.ds(first, tall)]
            return pltpu.make_async_copy(patch_ref.at[n, s], target, patch_sems.at[n, s])

        for n in range(2):
            for s in range(slots):

                @pl.when(leaving != s)
                def _():
                    patch(n, s).start()

        column = pl.multiple_of(lax.axis_index("head") * width, LANES)
        page_at, offset = [number_at(source_ref, 2 * down + j) for j in range(2)]

        def use(ref):
            buffer[...] = ref[...]

        source = number_at(source_ref, 0)

        @pl.when(source % 2 == 0)
        def _():
            with_page(source, across, 0, message_refs, turned_refs, use)

        @pl.when(source % 2 == 1)
        def _():
            use(other_ref)

        arrived = pack_refs[0][2 * slots :, :].astype(F32)
        for ref in pack_refs[1:]:
            arrived = arrived + ref[2 * slots :, :].astype(F32)

        def fresh(n):
            return jnp.concatenate([arrived[n * strips + i : n * strips + i + 1, :] for i in range(strips)], axis=1)

        at = lax.broadcasted_iota(jnp.int32, (slots, width), 0)
        token = jnp.where(
            at == leaving,
            jnp.broadcast_to(fresh(2), (slots, width)),
            token_ref[:, pl.ds(column, width)].astype(F32),
        )
        base_ref[...] = token + bias_ref[:, pl.ds(column, width)]
        first = pl.multiple_of(offset // 16 * 16, 16)
        row = lax.broadcasted_iota(jnp.int32, (16, width), 0)
        for n in range(2):
            old = buffer[n, pl.ds(first, 16), :].astype(F32)
            new = jnp.broadcast_to(fresh(n), (16, width))
            buffer[n, pl.ds(first, 16), :] = jnp.where(row == offset - first, new, old).astype(BF16)
        copies = [
            pltpu.make_async_copy(buffer.at[n], target.at[page_at], out_sems.at[n])
            for n, target in enumerate((key_ref, value_ref))
        ]
        for copy in copies:
            copy.start()
        for n in range(2):
            for s in range(slots):

                @pl.when(leaving != s)
                def _():
                    patch(n, s).wait()

        for copy in copies:
            copy.wait()

    shape = jax.ShapeDtypeStruct(key_out.shape, key_out.dtype)
    return pl.pallas_call(
        kernel,
        out_shape=(jax.ShapeDtypeStruct((slots, width), F32), shape, shape),
        in_specs=[SMEM] * 3 + [VMEM] * (chips + 4 + count) + [HBM] * 2,
        out_specs=(VMEM, HBM, HBM),
        scratch_shapes=[
            pltpu.VMEM((2, page, width), BF16),
            pltpu.SemaphoreType.DMA((2,)),
            pltpu.SemaphoreType.DMA((2, slots)),
        ],
        input_output_aliases={chips + 7 + count: 1, chips + 8 + count: 2},
        compiler_params=pltpu.CompilerParams(vmem_limit_bytes=(6 + 2 * count) * MIB),
        cost_estimate=cost(0, 8 * page * width),
        name="place_page",
    )(
        lengths, new_slot, page_table, sources, patches, *packs[::-1], tokens, out_bias, *messages, *turned, from_other, key_out, value_out
    )


def body(
    tokens,
    norm_gain,
    norm_shift,
    qkv_weight,
    qkv_bias,
    out_weight,
    out_bias,
    key_pool,
    value_pool,
    lengths,
    page_table,
    new_slot,
    new_page,
):
    groups = lax.axis_size("req")
    head_groups = lax.axis_size("head")
    slots = tokens.shape[0]
    chips = groups // 2

    other_tokens = swap(tokens, "req", 1)
    told, own_tokens, gain, shift = tell(
        lengths, new_slot, new_page, tokens, norm_gain[None], norm_shift[None], key_pool.shape[1]
    )
    blocks = prepare(own_tokens, other_tokens, gain, shift, told)
    across = row_length(chips)
    spread = [blocks[0]] + [swap(blocks[d], "req", 2 * d) for d in range(1, chips)]
    page = pick_page(new_slot, page_table, key_pool, value_pool, *blocks[::-1])
    page, *spread = lax.optimization_barrier((page, *spread))
    pages = [page] + [swap_pages(page, chips, True, d) for d in range(1, across)]

    flat = out_weight.reshape(-1, out_weight.shape[2])
    keep, send, staged = project(spread, jnp.transpose(qkv_weight, (1, 0, 2)), flat)
    got = swap(send, "req", 1)
    own, *messages = combine(keep, got)
    sources = find_sources(spread, got)
    sums = [own] + [swap(messages[d - 1], "req", 2 * d) for d in range(1, chips)]
    turning = turn_pages(sources, pages, chips)
    turned = [swap_pages(one, chips, False, row + 1) for row, one in enumerate(turning)]

    pack_keep, pack_send, patches, value_out = attend(
        lengths,
        new_slot,
        page_table,
        sums,
        qkv_bias.reshape(1, -1),
        own_tokens,
        key_pool,
        value_pool,
        turning[0],
    )
    packs_got = swap(pack_send, "req", 1)
    high = -(-slots // 8) * 8
    merged = [
        jnp.concatenate([pack_keep[d, :slots], packs_got[d, :slots], pack_keep[d, high:] + packs_got[d, high:]], axis=0)
        for d in range(chips)
    ]
    packs = [merged[0]] + [swap(merged[d], "req", 2 * d) for d in range(1, chips)]

    keep, send = out_project(
        packs, staged, head_groups, slots, turned[0]
    )
    total = keep + swap(send, "req", 1).astype(F32)
    from_other = swap(choose_page(sources, pages, turned, keep), "req", 1)
    summed = total[0]
    for d in reversed(range(1, chips)):
        summed = summed + swap(total[d].astype(BF16), "req", 2 * d).astype(F32)
    key_out = write_pool(key_pool, total)
    summed, key_out, from_other = lax.optimization_barrier((summed, key_out, from_other))
    base, key_out, value_out = place_page(
        lengths,
        new_slot,
        page_table,
        sources,
        patches,
        packs,
        own_tokens,
        out_bias[None],
        pages,
        turned,
        from_other,
        key_out,
        value_out,
    )
    hidden = summed[0]
    for j in [head_groups - 1, *range(1, head_groups - 1)]:
        hidden = hidden + swap(summed[j].astype(BF16), "head", j).astype(F32)
    hidden_out = (hidden + base).astype(BF16)
    return (hidden_out, key_out, value_out)


def solution(mesh):
    in_specs = (
        P("req", None),
        P(),
        P(),
        P("req", "head", None),
        P("head", None),
        P("head", "req", None),
        P(),
        P("req", None, "head"),
        P("req", None, "head"),
        P("req"),
        P("req", None),
        P("req"),
        P("req"),
    )
    out_specs = (P("req", "head"), P("req", None, "head"), P("req", None, "head"))
    return jax.shard_map(body, mesh=mesh, in_specs=in_specs, out_specs=out_specs, check_vma=False)
```
